32 devices in a mesh: sect: 4 (over y, x), node: 8 (over z, core).
Axes of the slice: x: 2, y: 2, z: 4, core: 2. Of those that a mesh axis runs over, the one named last changes fastest.
Arguments:
- grid_feat: bfloat16 [8192, 512], P(('sect', 'node')), may hold values from -6 to 6
- edge_len: float32 [8192, 2], P(('sect', 'node')), may hold values from 0.2 to 1.5
- g2m_owner: int32 [8192, 2], P(('sect', 'node')), may hold values from 0 to 7, all different within a row; in each aligned block of 256 rows (0 to 255, 256 to 511, ...) at most 128 rows name the same one
- g2m_dst: int32 [8192, 2], P(('sect', 'node')), may hold values from 0 to 511
- enc_weight: bfloat16 [512, 512], replicated, may hold values from -0.25 to 0.25
- enc_vec: float32 [512], replicated, may hold values from -5 to 5
- mesh_init: bfloat16 [8, 512, 512], P('node', 'sect'), may hold values from -1.11 to 1.11
- mesh_weight: bfloat16 [512, 512], replicated, may hold values from -0.015625 to 0.015625
- halo_send: int32 [4, 8, 4, 8, 2], P('sect', 'node'), may hold values from 0 to 127
- mesh_src: int32 [8, 512, 8], P('node', 'sect'), may hold values from 0 to 191
- proc_weight: bfloat16 [2, 4, 512, 512], replicated, may hold values from -0.25 to 0.25
- cot: bfloat16 [8, 512, 512], P('node', 'sect'), may hold values from -16 to 16
Outputs:
- mesh_out: bfloat16 [8, 512, 512], P('node', 'sect')
- grid_grad: bfloat16 [8192, 512], P(('sect', 'node'))
The draws below stay inside these ranges and needn't reach their ends.
Inputs may be any that keep to these rules, and one draw needn't show every extreme that they name: `g2m_owner`: within the 256 grid nodes of one device (aligned blocks), at most 128 edges name one mesh block, and some block is named by exactly 128 edges in some or all devices; the 2 edges of one grid node name different blocks. `mesh_src`: entries below 128 name own rows of the table, the others received rows.
All inputs are finite; a program needn't handle non-finite values.
Results may differ from the reference program's by a relative error of at most 0.009.
Values may be sent and summed in bfloat16 or wider, within the bound.
No kernel may reach another device: no remote copies, remote signals or barrier semaphores. Data moves between devices by JAX's collectives and lax.ppermute only.
A program may use at most 64 MiB of HBM per device.

```python
import math
import jax
import jax.numpy as jnp
import numpy as np
from jax import lax

D = 512
G_DEV = 256
Q_DEV = 128
KG = 2
KM = 8
HCAP = 2
LAYERS = 2
OWNERS = 8
SECTIONS = 4
M_DEV = 512
MESH = 4096
GRID = 8192
CAP = 128
TABLE = 192
N_SECT = 4
N_NODE = 8


def draw_mesh_init(key, part):
    key = jax.random.fold_in(key, 11)
    key_rows, key_vals = jax.random.split(key)
    row_scale = jnp.exp(jax.random.uniform(key_rows, (OWNERS, M_DEV, 1), jnp.float32, -3.0, -1.0))
    values = jnp.clip(jax.random.normal(key_vals, (OWNERS, M_DEV, D), jnp.float32), -3.0, 3.0)
    return (row_scale * values).astype(jnp.bfloat16)


def place_ends(entries, own_key, least, high):
    longest = entries.shape.index(max(entries.shape))
    spots = []
    for shift in (0, 1):
        where = [jax.random.randint(jax.random.fold_in(own_key, axis), (), 0, length) for axis, length in enumerate(entries.shape)]
        where[longest] = (where[longest] + shift) % entries.shape[longest]
        spots.append(tuple(where))
    return entries.at[spots[0]].set(least).at[spots[1]].set(high)


def level_of(own_key, shape, pieces, low, largest):
    level = 1.0
    for axis_at, blocks in pieces:
        steps = jax.random.uniform(jax.random.fold_in(jax.random.fold_in(own_key, 6), axis_at), (blocks,), jnp.float32, low / len(pieces), largest / len(pieces))
        level = level * jnp.repeat(jnp.exp(steps), shape[axis_at] // blocks).reshape((-1,) + (1,) * (len(shape) - 1 - axis_at))
    return level


def deal_out(rng, own, number, rows, count, top, most, skew):
    sequence = jax.random.permutation(rng, count)
    heavy_load, usual = shares(count, rows * top, most, skew, True), shares(count, rows * top, most, skew, False)
    places = jnp.arange(count)

    def named(sizes, turn):
        used = int((sizes > 0).sum())
        fixed = max(1, used // 4)
        passed = fixed + (places - fixed + turn * (used - fixed)) % max(1, count - fixed)
        return jnp.zeros((count,), jnp.int32).at[sequence[jnp.where(places < fixed, places, passed)]].set(jnp.asarray(sizes, jnp.int32))

    sizes = jnp.where(number % 4 == 0, named(heavy_load, number // 4), named(usual, number - number // 4 - 1))
    mixed = jax.random.permutation(jax.random.fold_in(own, 3), count)
    source_of, sink = mixed[0:count // 2 * 2:2], mixed[1:count // 2 * 2:2]
    margin = jnp.minimum(sizes[source_of] - 1, most - sizes[sink]) // 2
    margin = jnp.where((source_of == sequence[0]) | (sink == sequence[0]) | (sizes[sink] == 0), 0, jnp.maximum(margin, 0))
    passed = jax.random.randint(jax.random.fold_in(own, 4), (count // 2,), 0, 1 << 20) % (margin + 1)
    sizes = sizes.at[source_of].add(-passed).at[sink].add(passed)
    members = jnp.searchsorted(jnp.cumsum(sizes), jnp.arange(rows * top), side="right").astype(jnp.int32)
    listing = members.reshape(top, rows).T
    listing = listing[jax.random.permutation(jax.random.fold_in(own, 1), rows)]
    turn = jax.random.randint(jax.random.fold_in(own, 2), (rows, 1), 0, top)
    return jnp.take_along_axis(listing, (jnp.arange(top)[None, :] + turn) % top, axis=1)


def shares(amount, total, bound, skew, full):
    weights = [(1 << 20) // math.isqrt(standing ** skew) + 1 for standing in range(1, amount + 1)]
    largest = bound if full else min(bound, max(-(-total // amount), total * weights[0] // sum(weights)))
    least = 1 if total - largest >= amount - 1 else 0
    holding, rest = [largest] + [least] * (amount - 1), total - largest - least * (amount - 1)
    while rest > 0:
        free = [i for i in range(1, amount) if holding[i] < largest] or [i for i in range(1, amount) if holding[i] < bound]
        whole, left = sum([weights[i] for i in free]), rest
        for i in free:
            more = min(bound - holding[i], max(1, left * weights[i] // whole), rest)
            holding[i] = holding[i] + more
            rest = rest - more
    return np.array(holding)


def normal_values(own_key, dims, width, most, shards=(), kind=jnp.bfloat16):
    entries = jax.random.normal(own_key, dims, jnp.float32) * width
    if len(shards) > 0:
        entries = level_of(own_key, dims, shards, -0.22, 0.18) * entries
    return jnp.clip(entries, min=-most, max=most).astype(kind)


def setup_inputs(seed: int = 0) -> dict:
    splits = jax.random.split(jax.random.key(seed), 13)
    grid_feat = normal_values(splits[0], (GRID, D), 1.0, 6.0, ((0, 32),))
    edge_len = jnp.clip(0.2 + 1.3 * jax.random.uniform(splits[1], (GRID, KG), jnp.float32) ** level_of(splits[1], (GRID, KG), ((0, 32),), -0.2, 0.2), 0.2, 1.5)
    g2m_owner_keys = jax.random.split(jax.random.fold_in(splits[2], 1), GRID // G_DEV)
    g2m_owner_turns = jax.random.permutation(jax.random.fold_in(splits[2], 3), GRID // G_DEV)
    g2m_owner = jax.vmap(lambda own, number: deal_out(jax.random.fold_in(splits[2], 2), own, number, G_DEV, OWNERS, KG, CAP, 1))(g2m_owner_keys, g2m_owner_turns).reshape((GRID, KG))
    g2m_dst = place_ends(jax.random.randint(splits[3], (GRID, KG), 0, M_DEV), jax.random.fold_in(splits[3], 1), 0, M_DEV - 1).astype(jnp.int32)
    enc_weight = normal_values(splits[4], (D, D), D ** -0.5, 0.25)
    enc_vec = normal_values(splits[5], (D,), 1.0, 5.0, (), jnp.float32)
    mesh_init = draw_mesh_init(jax.random.fold_in(splits[12], 71), 0)
    mesh_weight = normal_values(splits[7], (D, D), (256 * D) ** -0.5, 0.015625)
    halo_send = place_ends(jax.random.randint(splits[8], (SECTIONS, OWNERS, SECTIONS, OWNERS, HCAP), 0, Q_DEV), jax.random.fold_in(splits[8], 1), 0, Q_DEV - 1).astype(jnp.int32)
    mesh_src = place_ends(jax.random.randint(splits[9], (OWNERS, M_DEV, KM), 0, TABLE), jax.random.fold_in(splits[9], 1), 0, TABLE - 1).astype(jnp.int32)
    proc_weight = normal_values(splits[10], (LAYERS, 4, D, D), D ** -0.5, 0.25)
    cot = normal_values(splits[11], (OWNERS, M_DEV, D), 4.0, 16.0, ((0, 8), (1, 4)))
    return dict(grid_feat=grid_feat, edge_len=edge_len, g2m_owner=g2m_owner, g2m_dst=g2m_dst, enc_weight=enc_weight, enc_vec=enc_vec, mesh_init=mesh_init, mesh_weight=mesh_weight, halo_send=halo_send, mesh_src=mesh_src, proc_weight=proc_weight, cot=cot)


HIGH = lax.Precision.HIGHEST

def to_low(value):
    rounded = lax.optimization_barrier(value.astype(jnp.bfloat16)).astype(jnp.float32)
    return value + lax.stop_gradient(rounded - value)

def matmul(left, right):
    return jnp.matmul(left, right, precision=HIGH)

def layer_norm(value):
    mean = lax.optimization_barrier(jnp.mean(value, axis=-1, keepdims=True))
    centred = value - mean
    var = lax.optimization_barrier(jnp.mean(centred * centred, axis=-1, keepdims=True))
    return centred * lax.rsqrt(var + 1e-05)

def pick_rows(rows, picks):
    return rows[picks]

def sect_layer(state, incoming, sources, weights):
    table = jnp.concatenate([state, incoming], axis=1)
    from_src = matmul(table, weights[0])
    to_dst = matmul(state, weights[1])
    joined = jax.vmap(pick_rows)(from_src, sources) + to_dst[:, :, None, :]
    agg = to_low(lax.optimization_barrier(jnp.sum(jax.nn.silu(joined), axis=2)))
    mixed = matmul(state, weights[2]) + matmul(agg, weights[3])
    return to_low(state + jax.nn.silu(layer_norm(mixed)))

def forward(grid, edge_len, g2m_owner, g2m_dst, enc_weight, enc_vec, mesh_init, mesh_weight, halo_send, mesh_src, proc_weight):
    pre = matmul(grid, enc_weight)
    message = to_low(jax.nn.silu(pre[:, None, :] + edge_len[:, :, None] * enc_vec))
    target = (g2m_owner * M_DEV + g2m_dst).reshape(-1).astype(jnp.int32)
    agg = jax.ops.segment_sum(message.reshape(-1, D), target, num_segments=MESH)
    mesh_pre = matmul(to_low(agg), mesh_weight)
    state = to_low(mesh_init.reshape(MESH, D) + jax.nn.silu(mesh_pre))
    state = state.reshape(N_NODE, N_SECT, Q_DEV, D).transpose(1, 0, 2, 3)
    sources = mesh_src.reshape(N_NODE, N_SECT, Q_DEV, KM).transpose(1, 0, 2, 3)
    picks = halo_send.reshape(N_SECT, N_NODE, N_SECT * N_NODE * HCAP)
    for layer in range(LAYERS):
        weights = proc_weight[layer]
        outgoing = jax.vmap(jax.vmap(pick_rows))(state, picks)
        outgoing = outgoing.reshape(N_SECT, N_NODE, N_SECT, N_NODE, HCAP, D)
        incoming = outgoing.transpose(2, 3, 0, 1, 4, 5).reshape(N_SECT, N_NODE, N_SECT * N_NODE * HCAP, D)

        def one_sect(item):
            return sect_layer(item[0], item[1], item[2], weights)
        state = lax.map(one_sect, (state, incoming, sources))
    return state.transpose(1, 0, 2, 3).reshape(N_NODE, M_DEV, D)

def reference(grid_feat, edge_len, g2m_owner, g2m_dst, enc_weight, enc_vec, mesh_init, mesh_weight, halo_send, mesh_src, proc_weight, cot):

    def run(grid):
        return forward(grid, edge_len.astype(jnp.float32), g2m_owner, g2m_dst, enc_weight.astype(jnp.float32), enc_vec.astype(jnp.float32), mesh_init.astype(jnp.float32), mesh_weight.astype(jnp.float32), halo_send, mesh_src, proc_weight.astype(jnp.float32))
    mesh_out, pull = jax.vjp(run, grid_feat.astype(jnp.float32))
    grid_grad = pull(cot.astype(jnp.float32))[0]
    return (mesh_out.astype(jnp.bfloat16), grid_grad.astype(jnp.bfloat16))
```

```python
import functools

import jax
import jax.numpy as jnp
from jax import lax
from jax.experimental import pallas as pl
from jax.experimental.pallas import tpu as pltpu
from jax.sharding import PartitionSpec as P

F32 = jnp.float32
BF16 = jnp.bfloat16
LANES = 128
VMEM_BYTES = 48 * 1024 * 1024


def sigmoid(value):
    return 0.5 * jnp.tanh(0.5 * value) + 0.5


def silu(value):
    return value * sigmoid(value)


def slope(value):
    sig = sigmoid(value)
    return sig * (1.0 + value * (1.0 - sig))


def dot(left, right):
    return jnp.dot(left, right, preferred_element_type=F32)


def dot_t(left, right):
    return lax.dot_general(left, right, (((1,), (1,)), ((), ())), preferred_element_type=F32)


def halves(value):
    high = value.astype(BF16)
    return high, (value - high.astype(F32)).astype(BF16)


def back_dot(grad, weight):
    high, low = halves(grad)
    return dot_t(high, weight) + dot_t(low, weight)


def pick_dot(onehot, rows):
    high, low = halves(rows)
    return dot(onehot, high) + dot(onehot, low)


def mark(equal):
    return jnp.where(equal, 1.0, 0.0).astype(BF16)


def iota(shape, axis):
    return lax.broadcasted_iota(jnp.int32, shape, axis)


def norm_parts(mixed):
    mean = jnp.mean(mixed, axis=-1, keepdims=True)
    centred = mixed - mean
    scale = lax.rsqrt(jnp.mean(centred * centred, axis=-1, keepdims=True) + 1e-05)
    return centred * scale, scale


def norm_back(grad, normed, scale):
    pull = grad * slope(normed)
    return scale * (
        pull
        - jnp.mean(pull, axis=-1, keepdims=True)
        - normed * jnp.mean(pull * normed, axis=-1, keepdims=True)
    )


def spot_of(owner, dst, section, node, nodes, block):
    apart = jnp.bitwise_xor(owner.astype(jnp.int32), node)
    order = lax.shift_right_logical(apart, 1) + jnp.bitwise_and(apart, 1) * (nodes // 2)
    place = dst.astype(jnp.int32) - section * block
    inside = jnp.logical_and(place >= 0, place < block)
    return jnp.where(inside, order * block + place, -1)


def encode_kernel(sects, nodes, block, fanout, who, *refs):
    feats, metas = refs[:sects], refs[sects : 2 * sects]
    weight, vec, keep, cross, message, spots = refs[2 * sects :]
    rows = feats[0].shape[0]
    section, node = who[0], who[1]
    for j in range(sects):
        pre = dot(feats[j][...], weight[...])
        meta = metas[j][...]
        lens = meta.T
        for k in range(fanout):
            at = (j * fanout + k) * rows
            act = pre + lens[:, k : k + 1] * vec[...]
            message[at : at + rows, :] = silu(act).astype(BF16)
            owner = meta[fanout + k : fanout + k + 1]
            dst = meta[2 * fanout + k : 2 * fanout + k + 1]
            spots[:, at : at + rows] = spot_of(owner, dst, section, node, nodes, block)
    half = keep.shape[0]
    step = min(half, 512)
    for out, base in ((cross, half), (keep, 0)):

        def chunk(c, carry, out=out, base=base):
            start = pl.multiple_of(c * step, step)
            ids = iota((step, spots.shape[1]), 0) + (base + start)
            part = dot(mark(ids == spots[...]), message[...])
            out[pl.ds(start, step), :] = part.astype(BF16)
            return carry

        lax.fori_loop(0, half // step, chunk, 0)


def slope_kernel(sects, fanout, *refs):
    feats, metas = refs[:sects], refs[sects : 2 * sects]
    weight, vec = refs[2 * sects : 2 * sects + 2]
    outs = refs[2 * sects + 2 :]
    rows = feats[0].shape[0]
    for j in range(sects):
        pre = dot(feats[j][...], weight[...])
        lens = metas[j][...].T
        for k in range(fanout):
            act = pre + lens[:, k : k + 1] * vec[...]
            outs[j][k * rows : (k + 1) * rows, :] = slope(act).astype(BF16)


def halo_rows(state, picks, parts):
    block = state.shape[0]
    onehot = mark(iota((picks.shape[0], parts * block), 1) == picks)
    stacked = jnp.concatenate(
        [state[:, i * LANES : (i + 1) * LANES] for i in range(parts)], axis=0
    )
    return dot(onehot, stacked).astype(BF16)


def join_pieces(pieces, parts):
    count = pieces.shape[0]
    shape = (count // parts, count)
    return jnp.concatenate(
        [
            dot(mark(iota(shape, 1) == iota(shape, 0) * parts + i), pieces).astype(BF16)
            for i in range(parts)
        ],
        axis=1,
    )


def cut_pieces(rows, parts):
    count = rows.shape[0]
    shape = (count * parts, count)
    total = None
    for i in range(parts):
        onehot = mark(iota(shape, 0) == iota(shape, 1) * parts + i)
        piece = dot(onehot, rows[:, i * LANES : (i + 1) * LANES])
        total = piece if total is None else total + piece
    return total.astype(BF16)


def add_pieces(pieces, picks_row, block, parts):
    onehot = mark(iota((parts * block, picks_row.shape[1]), 0) == picks_row)
    total = dot(onehot, pieces)
    return jnp.concatenate([total[i * block : (i + 1) * block] for i in range(parts)], axis=1)


def start_kernel(parts, sums, *refs):
    received, (init, weight, picks, state, mesh_pre, halo) = refs[:-6], refs[-6:]
    agg = sums[...]
    for ref in received:
        agg = agg + ref[...].astype(F32)
    pre = dot(agg.astype(BF16), weight[...])
    mesh_pre[...] = pre
    new = (init[...].astype(F32) + silu(pre)).astype(BF16)
    state[...] = new
    halo[...] = halo_rows(new, picks[...], parts)


def layer_forward(state, pieces, src, weights, parts):
    block, fan = src.shape
    halo = join_pieces(pieces, parts)
    table = jnp.concatenate([state, halo], axis=0)
    from_src = dot(table, weights[0])
    to_dst = dot(state, weights[1])
    high, low = halves(from_src)
    ids = iota((block, table.shape[0]), 1)
    agg = jnp.zeros(state.shape, F32)
    slopes = []
    for k in range(fan):
        onehot = mark(ids == src[:, k : k + 1])
        joined = dot(onehot, high) + dot(onehot, low) + to_dst
        sig = sigmoid(joined)
        agg = agg + joined * sig
        slopes.append((sig * (1.0 + joined * (1.0 - sig))).astype(BF16))
    mixed = dot(state, weights[2]) + dot(agg.astype(BF16), weights[3])
    return mixed, slopes


def layer_back(grad, mixed, slopes, src_row, weights, table_len):
    block = grad.shape[0]
    normed, scale = norm_parts(mixed)
    grad_mixed = norm_back(grad, normed, scale)
    high, low = halves(grad_mixed)
    grad_state = grad + dot_t(high, weights[2]) + dot_t(low, weights[2])
    grad_agg = dot_t(high, weights[3]) + dot_t(low, weights[3])
    total = jnp.zeros(grad.shape, F32)
    grad_src = jnp.zeros((table_len, grad.shape[1]), F32)
    ids = iota((table_len, block), 0)
    for k in range(src_row.shape[0]):
        piece = grad_agg * slopes[k].astype(F32)
        total = total + piece
        grad_src = grad_src + pick_dot(mark(ids == src_row[k : k + 1]), piece)
    grad_state = grad_state + back_dot(total, weights[1])
    grad_table = back_dot(grad_src, weights[0])
    return grad_state + grad_table[:block], grad_table[block:]


def first_kernel(parts, state, pieces, src, weights, picks, new, mixed, slopes, halo):
    block = state.shape[0]
    own = state[...]
    value, found = layer_forward(own, pieces[...], src[...], weights, parts)
    mixed[...] = value
    for k, part in enumerate(found):
        slopes[k * block : (k + 1) * block, :] = part
    normed, _ = norm_parts(value)
    result = (own.astype(F32) + silu(normed)).astype(BF16)
    new[...] = result
    halo[...] = halo_rows(result, picks[...], parts)


def last_kernel(
    parts, state, pieces, src, src_row, weights, cot, out, grad_own, grad_halo
):
    own = state[...]
    value, found = layer_forward(own, pieces[...], src[...], weights, parts)
    normed, _ = norm_parts(value)
    out[...] = (own.astype(F32) + silu(normed)).astype(BF16)
    table_len = own.shape[0] + pieces.shape[0] // parts
    mine, sent = layer_back(
        cot[...].astype(F32), value, found, src_row[...], weights, table_len
    )
    grad_own[...] = mine
    grad_halo[...] = cut_pieces(sent.astype(BF16), parts)


def back_kernel(
    parts, mine, returned, picks_row, mixed, slopes, src_row, weights, grad_own, grad_halo
):
    block = mine.shape[0]
    grad = mine[...] + add_pieces(returned[...], picks_row[...], block, parts)
    found = [slopes[k * block : (k + 1) * block, :] for k in range(src_row.shape[0])]
    table_len = block + returned.shape[0] // parts
    own, sent = layer_back(grad, mixed[...], found, src_row[...], weights, table_len)
    grad_own[...] = own
    grad_halo[...] = cut_pieces(sent.astype(BF16), parts)


def mesh_back_kernel(parts, mine, returned, picks_row, mesh_pre, weight, out):
    block = mine.shape[0]
    grad = mine[...] + add_pieces(returned[...], picks_row[...], block, parts)
    out[...] = back_dot(grad * slope(mesh_pre[...]), weight[...]).astype(BF16)


def message_back_kernel(nodes, block, fanout, who, meta, slopes, *refs):
    out = refs[-1]
    rows = out.shape[0]
    grads = jnp.concatenate([ref[...] for ref in refs[:-1]], axis=0)
    found = meta[...].T
    total = jnp.zeros(out.shape, F32)
    ids = iota((rows, nodes * block), 1)
    for k in range(fanout):
        owner = found[:, fanout + k : fanout + k + 1]
        dst = found[:, 2 * fanout + k : 2 * fanout + k + 1]
        spot = spot_of(owner, dst, who[0], who[1], nodes, block)
        picked = dot(mark(ids == spot), grads)
        total = total + picked * slopes[k * rows : (k + 1) * rows, :].astype(F32)
    out[...] = total.astype(out.dtype)


def grid_back_kernel(*refs):
    *parts, weight, out = refs
    total = parts[0][...].astype(F32)
    for ref in parts[1:]:
        total = total + ref[...].astype(F32)
    out[...] = back_dot(total, weight[...]).astype(BF16)


def call(kernel, outs, args, smem=0, scratch=(), macs=0, scalars=0):
    specs = [pl.BlockSpec(memory_space=pltpu.SMEM)] * smem
    specs += [pl.BlockSpec(memory_space=pltpu.VMEM)] * (len(args) - smem)
    moved = sum(a.size * a.dtype.itemsize for a in list(args) + list(outs))
    result = pl.pallas_call(
        kernel,
        out_shape=list(outs),
        in_specs=specs,
        out_specs=[pl.BlockSpec(memory_space=pltpu.VMEM)] * len(outs),
        scratch_shapes=list(scratch),
        compiler_params=pltpu.CompilerParams(vmem_limit_bytes=VMEM_BYTES),
        cost_estimate=pl.CostEstimate(
            flops=2 * macs, bytes_accessed=moved, transcendentals=scalars
        ),
    )(*args)
    return result


def shape(dims, dtype):
    return jax.ShapeDtypeStruct(dims, dtype)


def swap(value, axis, apart):
    size = lax.axis_size(axis)
    return lax.ppermute(value, axis, [(i, i ^ apart) for i in range(size)])


def body(
    grid_feat,
    edge_len,
    g2m_owner,
    g2m_dst,
    enc_weight,
    enc_vec,
    mesh_init,
    mesh_weight,
    halo_send,
    mesh_src,
    proc_weight,
    cot,
):
    nodes = lax.axis_size("node")
    sects = lax.axis_size("sect")
    width = grid_feat.shape[1]
    grid_rows, fanout = edge_len.shape
    block = mesh_init.shape[1]
    parts = width // LANES
    both = ("sect", "node")
    who = jnp.stack([lax.axis_index("sect"), lax.axis_index("node")]).astype(jnp.int32)

    meta = jnp.concatenate(
        [edge_len.T, g2m_owner.T.astype(F32), g2m_dst.T.astype(F32)], axis=0
    )
    meta = jnp.pad(meta, ((0, -(3 * fanout) % 8), (0, 0)))
    feats = [grid_feat] + [swap(grid_feat, "sect", j) for j in range(1, sects)]
    metas = [meta] + [swap(meta, "sect", j) for j in range(1, sects)]
    vec = enc_vec[None, :]
    half = nodes // 2
    edges = sects * grid_rows * fanout
    keep, cross = call(
        functools.partial(encode_kernel, sects, nodes, block, fanout),
        [shape((half * block, width), BF16)] * 2,
        [who, *feats, *metas, enc_weight, vec],
        smem=1,
        scratch=[pltpu.VMEM((edges, width), BF16), pltpu.VMEM((1, edges), jnp.int32)],
        macs=sects * grid_rows * width * width + edges * nodes * block * width,
        scalars=edges * width,
    )
    slopes = call(
        functools.partial(slope_kernel, sects, fanout),
        [shape((fanout * grid_rows, width), BF16)] * sects,
        [*feats, *metas, enc_weight, vec],
        macs=sects * grid_rows * width * width,
        scalars=edges * width,
    )

    pair = keep.astype(F32) + swap(cross, "node", 1).astype(F32)
    pair = pair.reshape(half, block, width)
    arrived = [swap(pair[q].astype(BF16), "node", 2 * q) for q in range(1, half)]

    sends = halo_send[0, 0].reshape(-1)
    picks = jnp.repeat(sends, parts) + jnp.tile(
        jnp.arange(parts, dtype=jnp.int32) * block, sends.shape[0]
    )
    picks_col, picks_row = picks[:, None], picks[None, :]
    pieces = picks.shape[0]
    halo_shape = shape((pieces, LANES), BF16)
    row_low, row_high = shape((block, width), BF16), shape((block, width), F32)

    def exchange(value):
        return lax.all_to_all(value, both, split_axis=0, concat_axis=0, tiled=True)

    state, mesh_pre, halo = call(
        functools.partial(start_kernel, parts),
        [row_low, row_high, halo_shape],
        [pair[0], *arrived, mesh_init[0], mesh_weight, picks_col],
        macs=block * width * width,
        scalars=block * width,
    )
    src = mesh_src[0]
    src_row = src.T
    fan = src.shape[1]
    layer_macs = 6 * block * width * width + 2 * fan * block * 2 * block * width
    assert proc_weight.shape[0] == 2
    state, mixed, slope_first, halo = call(
        functools.partial(first_kernel, parts),
        [row_low, row_high, shape((fan * block, width), BF16), halo_shape],
        [state, exchange(halo), src, proc_weight[0], picks_col],
        macs=layer_macs,
        scalars=fan * block * width,
    )
    mesh_out, grad, halo = call(
        functools.partial(last_kernel, parts),
        [row_low, row_high, halo_shape],
        [state, exchange(halo), src, src_row, proc_weight[1], cot[0]],
        macs=3 * layer_macs,
        scalars=fan * block * width,
    )
    grad, halo = call(
        functools.partial(back_kernel, parts),
        [row_high, halo_shape],
        [grad, exchange(halo), picks_row, mixed, slope_first, src_row, proc_weight[0]],
        macs=2 * layer_macs,
        scalars=block * width,
    )
    (grad_sum,) = call(
        functools.partial(mesh_back_kernel, parts),
        [row_low],
        [grad, exchange(halo), picks_row, mesh_pre, mesh_weight],
        macs=2 * block * width * width,
        scalars=block * width,
    )

    same = [grad_sum] + [swap(grad_sum, "node", 2 * q) for q in range(1, half)]
    other = [swap(rows, "node", 1) for rows in same]
    mine, sent = None, []
    for j in reversed(range(sects)):
        (grad_pre,) = call(
            functools.partial(message_back_kernel, nodes, block, fanout),
            [shape((grid_rows, width), BF16)],
            [who, metas[j], slopes[j], *same, *other],
            smem=1,
            macs=fanout * grid_rows * nodes * block * width,
        )
        if j == 0:
            mine = grad_pre
        else:
            sent.append(swap(grad_pre, "sect", j))
    (grid_grad,) = call(
        grid_back_kernel,
        [shape((grid_rows, width), BF16)],
        [mine, *sent, enc_weight],
        macs=2 * grid_rows * width * width,
    )
    return (mesh_out[None], grid_grad)


def solution(mesh):
    return jax.shard_map(
        body,
        mesh=mesh,
        in_specs=(
            P(("sect", "node"), None),
            P(("sect", "node"), None),
            P(("sect", "node"), None),
            P(("sect", "node"), None),
            P(),
            P(),
            P("node", "sect", None),
            P(),
            P("sect", "node", None, None, None),
            P("node", "sect", None),
            P(),
            P("node", "sect", None),
        ),
        out_specs=(P("node", "sect", None), P(("sect", "node"), None)),
        check_vma=False,
    )
```

```python
import functools
import math

import jax
import jax.numpy as jnp
from jax import lax
from jax.experimental import pallas as pl
from jax.experimental.pallas import tpu as pltpu
from jax.sharding import PartitionSpec as P

F32 = jnp.float32
BF16 = jnp.bfloat16
LANES = 128
META_ROWS = 16
MIB = 1024 * 1024


def sigmoid(value):
    return 0.5 * jnp.tanh(0.5 * value) + 0.5


def silu(value):
    return value * sigmoid(value)


def slope(value):
    sig = sigmoid(value)
    return sig * (1.0 + value * (1.0 - sig))


def dot(left, right):
    return jnp.dot(left, right, preferred_element_type=F32)


def dot_t(left, right):
    return lax.dot_general(left, right, (((1,), (1,)), ((), ())), preferred_element_type=F32)


def halves(value):
    high = value.astype(BF16)
    return high, (value - high.astype(F32)).astype(BF16)


def back_dot(grad, weight):
    high, low = halves(grad)
    return dot_t(high, weight) + dot_t(low, weight)


def pick_dot(onehot, rows):
    high, low = halves(rows)
    return dot(onehot, high) + dot(onehot, low)


def mark(equal):
    return jnp.where(equal, 1.0, 0.0).astype(BF16)


def iota(shape, axis):
    return lax.broadcasted_iota(jnp.int32, shape, axis)


def norm_parts(mixed):
    mean = jnp.mean(mixed, axis=-1, keepdims=True)
    centred = mixed - mean
    scale = lax.rsqrt(jnp.mean(centred * centred, axis=-1, keepdims=True) + 1e-05)
    return centred * scale, scale


def norm_back(grad, normed, scale):
    pull = grad * slope(normed)
    return scale * (
        pull
        - jnp.mean(pull, axis=-1, keepdims=True)
        - normed * jnp.mean(pull * normed, axis=-1, keepdims=True)
    )


def pack_kernel(block, feat, lens, owner, dst, out):
    rows = feat.shape[0]
    out[:rows, :] = feat[...]
    high, rest = halves(lens[...])
    middle = rest
    low = (lens[...] - high.astype(F32) - middle.astype(F32)).astype(BF16)
    far = dst[...]
    section = far // block
    found = [high, middle, low] + [
        v.astype(F32).astype(BF16) for v in (owner[...], section, far - section * block)
    ]
    found = [v.astype(F32) for v in found]
    fill = META_ROWS - 6 * lens.shape[0]
    found.append(jnp.zeros((fill, rows), F32))
    meta = jnp.concatenate(found, axis=0).astype(BF16)
    out[rows:, :] = jnp.concatenate(
        [meta, jnp.zeros((META_ROWS, feat.shape[1] - rows), BF16)], axis=1
    )


def edge_data(feat, rows):
    return feat[rows:, :rows].astype(F32)


def edge_length(meta, fanout, k):
    high, middle, low = (meta[:, t * fanout + k : t * fanout + k + 1] for t in range(3))
    return high + middle + low


def spot_of(pick, fanout, k, section, node, nodes, block):
    owner, where, place = (pick((3 + t) * fanout + k).astype(jnp.int32) for t in range(3))
    apart = jnp.bitwise_xor(owner, node)
    order = lax.shift_right_logical(apart, 1) + jnp.bitwise_and(apart, 1) * (nodes // 2)
    return jnp.where(where == section, order * block + place, -1)


def encode_kernel(count, nodes, block, fanout, rows, last, who, *refs):
    feats = refs[:count]
    weight, vec = refs[count : count + 2]
    if last:
        before, keep, cross, message, spots = refs[count + 2 :]
    else:
        total, message, spots = refs[count + 2 :]
    section, node = who[0], who[1]
    for j in range(count):
        pre = dot(feats[j][:rows, :], weight[...])
        meta = edge_data(feats[j], rows)
        turned = meta.T
        for k in range(fanout):
            at = (j * fanout + k) * rows
            act = pre + edge_length(turned, fanout, k) * vec[...]
            message[at : at + rows, :] = silu(act).astype(BF16)
            spots[:, at : at + rows] = spot_of(
                lambda t, meta=meta: meta[t : t + 1], fanout, k, section, node, nodes, block
            )
    half = nodes // 2 * block
    step = min(half, 512)
    for out, base in ((cross, half), (keep, 0)) if last else ((total, 0),):

        def chunk(c, carry, out=out, base=base):
            start = pl.multiple_of(c * step, step)
            ids = iota((step, spots.shape[1]), 0) + (base + start)
            part = dot(mark(ids == spots[...]), message[...])
            if last:
                part = part + before[pl.ds(base + start, step), :]
            out[pl.ds(start, step), :] = part.astype(out.dtype)
            return carry

        lax.fori_loop(0, out.shape[0] // step, chunk, 0)


def slope_kernel(sects, fanout, rows, *refs):
    feats = refs[:sects]
    weight, vec = refs[sects : sects + 2]
    outs = refs[sects + 2 :]
    for j in range(sects):
        pre = dot(feats[j][:rows, :], weight[...])
        turned = edge_data(feats[j], rows).T
        for k in range(fanout):
            act = pre + edge_length(turned, fanout, k) * vec[...]
            outs[j][k * rows : (k + 1) * rows, :] = slope(act).astype(BF16)


def halo_rows(state, picks, parts):
    block = state.shape[0]
    onehot = mark(iota((picks.shape[0], parts * block), 1) == picks)
    stacked = jnp.concatenate(
        [state[:, i * LANES : (i + 1) * LANES] for i in range(parts)], axis=0
    )
    return dot(onehot, stacked).astype(BF16)


def join_pieces(pieces, parts):
    count = pieces.shape[0]
    shape = (count // parts, count)
    return jnp.concatenate(
        [
            dot(mark(iota(shape, 1) == iota(shape, 0) * parts + i), pieces).astype(BF16)
            for i in range(parts)
        ],
        axis=1,
    )


def cut_pieces(rows, parts):
    count = rows.shape[0]
    shape = (count * parts, count)
    total = None
    for i in range(parts):
        onehot = mark(iota(shape, 0) == iota(shape, 1) * parts + i)
        piece = dot(onehot, rows[:, i * LANES : (i + 1) * LANES])
        total = piece if total is None else total + piece
    return total.astype(BF16)


def add_pieces(pieces, picks_row, block, parts):
    onehot = mark(iota((parts * block, picks_row.shape[1]), 0) == picks_row)
    total = dot(onehot, pieces)
    return jnp.concatenate([total[i * block : (i + 1) * block] for i in range(parts)], axis=1)


def start_kernel(parts, sums, *refs):
    received, (init, weight, picks, state, mesh_pre, halo) = refs[:-6], refs[-6:]
    agg = sums[...]
    for ref in received:
        agg = agg + ref[...].astype(F32)
    pre = dot(agg.astype(BF16), weight[...])
    mesh_pre[...] = pre
    new = (init[...].astype(F32) + silu(pre)).astype(BF16)
    state[...] = new
    halo[...] = halo_rows(new, picks[...], parts)


def layer_forward(state, pieces, src, weights, parts):
    block, fan = src.shape
    halo = join_pieces(pieces, parts)
    table = jnp.concatenate([state, halo], axis=0)
    from_src = dot(table, weights(0))
    to_dst = dot(state, weights(1))
    high, low = halves(from_src)
    ids = iota((block, table.shape[0]), 1)
    agg = jnp.zeros(state.shape, F32)
    slopes = []
    for k in range(fan):
        onehot = mark(ids == src[:, k : k + 1])
        joined = dot(onehot, high) + dot(onehot, low) + to_dst
        sig = sigmoid(joined)
        agg = agg + joined * sig
        slopes.append((sig * (1.0 + joined * (1.0 - sig))).astype(BF16))
    mixed = dot(state, weights(2)) + dot(agg.astype(BF16), weights(3))
    return mixed, slopes


def layer_back(grad, mixed, slopes, src_row, weights, table_len):
    block = grad.shape[0]
    normed, scale = norm_parts(mixed)
    grad_mixed = norm_back(grad, normed, scale)
    high, low = halves(grad_mixed)
    grad_state = grad + dot_t(high, weights(2)) + dot_t(low, weights(2))
    grad_agg = dot_t(high, weights(3)) + dot_t(low, weights(3))
    total = jnp.zeros(grad.shape, F32)
    grad_src = jnp.zeros((table_len, grad.shape[1]), F32)
    ids = iota((table_len, block), 0)
    for k in range(src_row.shape[0]):
        piece = grad_agg * slopes[k].astype(F32)
        total = total + piece
        grad_src = grad_src + pick_dot(mark(ids == src_row[k : k + 1]), piece)
    grad_state = grad_state + back_dot(total, weights(1))
    grad_table = back_dot(grad_src, weights(0))
    return grad_state + grad_table[:block], grad_table[block:]


def layer_weights(weights, layer):
    return lambda i: weights[layer, i]


def first_kernel(
    layer, parts, state, pieces, src, weights, picks, new, mixed, slopes, halo
):
    block = state.shape[0]
    own = state[...]
    used = layer_weights(weights, layer)
    value, found = layer_forward(own, pieces[...], src[...], used, parts)
    mixed[...] = value
    for k, part in enumerate(found):
        slopes[k * block : (k + 1) * block, :] = part
    normed, _ = norm_parts(value)
    result = (own.astype(F32) + silu(normed)).astype(BF16)
    new[...] = result
    halo[...] = halo_rows(result, picks[...], parts)


def last_kernel(
    layer, parts, state, pieces, src, src_row, weights, cot, out, grad_own, grad_halo
):
    own = state[...]
    used = layer_weights(weights, layer)
    value, found = layer_forward(own, pieces[...], src[...], used, parts)
    normed, _ = norm_parts(value)
    out[...] = (own.astype(F32) + silu(normed)).astype(BF16)
    table_len = own.shape[0] + pieces.shape[0] // parts
    mine, sent = layer_back(
        cot[...].astype(F32), value, found, src_row[...], used, table_len
    )
    grad_own[...] = mine
    grad_halo[...] = cut_pieces(sent.astype(BF16), parts)


def back_kernel(
    layer,
    parts,
    mine,
    returned,
    picks_row,
    mixed,
    slopes,
    src_row,
    weights,
    grad_own,
    grad_halo,
):
    block = mine.shape[0]
    grad = mine[...] + add_pieces(returned[...], picks_row[...], block, parts)
    found = [slopes[k * block : (k + 1) * block, :] for k in range(src_row.shape[0])]
    table_len = block + returned.shape[0] // parts
    used = layer_weights(weights, layer)
    own, sent = layer_back(grad, mixed[...], found, src_row[...], used, table_len)
    grad_own[...] = own
    grad_halo[...] = cut_pieces(sent.astype(BF16), parts)


def mesh_back_kernel(parts, mine, returned, picks_row, mesh_pre, weight, out):
    block = mine.shape[0]
    grad = mine[...] + add_pieces(returned[...], picks_row[...], block, parts)
    out[...] = back_dot(grad * slope(mesh_pre[...]), weight[...]).astype(BF16)


def message_back_kernel(nodes, block, fanout, who, feat, slopes, *refs):
    out = refs[-1]
    rows = out.shape[0]
    grads = jnp.concatenate([ref[...] for ref in refs[:-1]], axis=0)
    turned = edge_data(feat, rows).T
    total = jnp.zeros(out.shape, F32)
    ids = iota((rows, nodes * block), 1)
    for k in range(fanout):
        spot = spot_of(
            lambda t: turned[:, t : t + 1], fanout, k, who[0], who[1], nodes, block
        )
        picked = dot(mark(ids == spot), grads)
        total = total + picked * slopes[k * rows : (k + 1) * rows, :].astype(F32)
    out[...] = total.astype(out.dtype)


def grid_back_kernel(*refs):
    *parts, weight, out = refs
    total = parts[0][...].astype(F32)
    for ref in parts[1:]:
        total = total + ref[...].astype(F32)
    out[...] = back_dot(total, weight[...]).astype(BF16)


def call(kernel, outs, args, smem=0, scratch=(), macs=0, scalars=0):
    specs = [pl.BlockSpec(memory_space=pltpu.SMEM)] * smem
    specs += [pl.BlockSpec(memory_space=pltpu.VMEM)] * (len(args) - smem)
    moved = sum(a.size * a.dtype.itemsize for a in list(args) + list(outs))
    held = sum(math.prod(a.shape) * jnp.dtype(a.dtype).itemsize for a in scratch)
    limit = 2 * (moved + held) + 6 * MIB
    result = pl.pallas_call(
        kernel,
        out_shape=list(outs),
        in_specs=specs,
        out_specs=[pl.BlockSpec(memory_space=pltpu.VMEM)] * len(outs),
        scratch_shapes=list(scratch),
        compiler_params=pltpu.CompilerParams(vmem_limit_bytes=limit),
        cost_estimate=pl.CostEstimate(
            flops=2 * macs, bytes_accessed=moved, transcendentals=scalars
        ),
    )(*args)
    return result


def shape(dims, dtype):
    return jax.ShapeDtypeStruct(dims, dtype)


def swap(value, axis, apart):
    size = lax.axis_size(axis)
    return lax.ppermute(value, axis, [(i, i ^ apart) for i in range(size)])


def body(
    grid_feat,
    edge_len,
    g2m_owner,
    g2m_dst,
    enc_weight,
    enc_vec,
    mesh_init,
    mesh_weight,
    halo_send,
    mesh_src,
    proc_weight,
    cot,
):
    nodes = lax.axis_size("node")
    sects = lax.axis_size("sect")
    width = grid_feat.shape[1]
    grid_rows, fanout = edge_len.shape
    block = mesh_init.shape[1]
    parts = width // LANES
    both = ("sect", "node")
    who = jnp.stack([lax.axis_index("sect"), lax.axis_index("node")]).astype(jnp.int32)

    (packed,) = call(
        functools.partial(pack_kernel, block),
        [shape((grid_rows + META_ROWS, width), BF16)],
        [grid_feat, edge_len.T, g2m_owner.T, g2m_dst.T],
    )
    feats = [packed] + [swap(packed, "sect", j) for j in range(1, sects)]
    vec = enc_vec[None, :]
    half = nodes // 2

    def encode(used, last, outs, extra):
        edges = len(used) * grid_rows * fanout
        return call(
            functools.partial(
                encode_kernel, len(used), nodes, block, fanout, grid_rows, last
            ),
            outs,
            [who, *used, enc_weight, vec, *extra],
            smem=1,
            scratch=[pltpu.VMEM((edges, width), BF16), pltpu.VMEM((1, edges), jnp.int32)],
            macs=len(used) * grid_rows * width * width + edges * nodes * block * width,
            scalars=edges * width,
        )

    before = encode(feats[:-1], False, [shape((nodes * block, width), F32)], [])
    keep, cross = encode(
        feats[-1:], True, [shape((half * block, width), BF16)] * 2, before
    )
    slopes = call(
        functools.partial(slope_kernel, sects, fanout, grid_rows),
        [shape((fanout * grid_rows, width), BF16)] * sects,
        [*feats, enc_weight, vec],
        macs=sects * grid_rows * width * width,
        scalars=sects * grid_rows * fanout * width,
    )

    pair = keep.astype(F32) + swap(cross, "node", 1).astype(F32)
    pair = pair.reshape(half, block, width)
    arrived = [swap(pair[q].astype(BF16), "node", 2 * q) for q in range(1, half)]

    sends = halo_send[0, 0].reshape(-1)
    picks = jnp.repeat(sends, parts) + jnp.tile(
        jnp.arange(parts, dtype=jnp.int32) * block, sends.shape[0]
    )
    picks_col, picks_row = picks[:, None], picks[None, :]
    pieces = picks.shape[0]
    halo_shape = shape((pieces, LANES), BF16)
    row_low, row_high = shape((block, width), BF16), shape((block, width), F32)

    def exchange(value):
        return lax.all_to_all(value, both, split_axis=0, concat_axis=0, tiled=True)

    state, mesh_pre, halo = call(
        functools.partial(start_kernel, parts),
        [row_low, row_high, halo_shape],
        [pair[0], *arrived, mesh_init[0], mesh_weight, picks_col],
        macs=block * width * width,
        scalars=block * width,
    )
    arrived, *slopes = lax.optimization_barrier((exchange(halo), *slopes))
    src = mesh_src[0]
    src_row = src.T
    fan = src.shape[1]
    layer_macs = 6 * block * width * width + 2 * fan * block * 2 * block * width
    assert proc_weight.shape[0] == 2
    state, mixed, slope_first, halo = call(
        functools.partial(first_kernel, 0, parts),
        [row_low, row_high, shape((fan * block, width), BF16), halo_shape],
        [state, arrived, src, proc_weight, picks_col],
        macs=layer_macs,
        scalars=fan * block * width,
    )
    mesh_out, grad, halo = call(
        functools.partial(last_kernel, 1, parts),
        [row_low, row_high, halo_shape],
        [state, exchange(halo), src, src_row, proc_weight, cot[0]],
        macs=3 * layer_macs,
        scalars=fan * block * width,
    )
    grad, halo = call(
        functools.partial(back_kernel, 0, parts),
        [row_high, halo_shape],
        [grad, exchange(halo), picks_row, mixed, slope_first, src_row, proc_weight],
        macs=2 * layer_macs,
        scalars=block * width,
    )
    (grad_sum,) = call(
        functools.partial(mesh_back_kernel, parts),
        [row_low],
        [grad, exchange(halo), picks_row, mesh_pre, mesh_weight],
        macs=2 * block * width * width,
        scalars=block * width,
    )

    same = [grad_sum] + [swap(grad_sum, "node", 2 * q) for q in range(1, half)]
    other = [swap(rows, "node", 1) for rows in same]
    mine, sent = None, []
    for j in reversed(range(sects)):
        (grad_pre,) = call(
            functools.partial(message_back_kernel, nodes, block, fanout),
            [shape((grid_rows, width), BF16)],
            [who, feats[j], slopes[j], *same, *other],
            smem=1,
            macs=fanout * grid_rows * nodes * block * width,
        )
        if j == 0:
            mine = grad_pre
        else:
            sent.append(swap(grad_pre, "sect", j))
    (grid_grad,) = call(
        grid_back_kernel,
        [shape((grid_rows, width), BF16)],
        [mine, *sent, enc_weight],
        macs=2 * grid_rows * width * width,
    )
    return (mesh_out[None], grid_grad)


def solution(mesh):
    return jax.shard_map(
        body,
        mesh=mesh,
        in_specs=(
            P(("sect", "node"), None),
            P(("sect", "node"), None),
            P(("sect", "node"), None),
            P(("sect", "node"), None),
            P(),
            P(),
            P("node", "sect", None),
            P(),
            P("sect", "node", None, None, None),
            P("node", "sect", None),
            P(),
            P("node", "sect", None),
        ),
        out_specs=(P("node", "sect", None), P(("sect", "node"), None)),
        check_vma=False,
    )
```

```python
import functools
import math

import jax
import jax.numpy as jnp
from jax import lax
from jax.experimental import pallas as pl
from jax.experimental.pallas import tpu as pltpu
from jax.sharding import PartitionSpec as P

F32 = jnp.float32
BF16 = jnp.bfloat16
LANES = 128
META_ROWS = 16
MIB = 1024 * 1024


def sigmoid(value):
    return 0.5 * jnp.tanh(0.5 * value) + 0.5


def silu(value):
    return value * sigmoid(value)


def slope(value):
    sig = sigmoid(value)
    return sig * (1.0 + value * (1.0 - sig))


def dot(left, right):
    return jnp.dot(left, right, preferred_element_type=F32)


def dot_t(left, right):
    return lax.dot_general(left, right, (((1,), (1,)), ((), ())), preferred_element_type=F32)


def halves(value):
    high = value.astype(BF16)
    return high, (value - high.astype(F32)).astype(BF16)


def back_dot(grad, weight):
    rows = grad.shape[0]
    both = dot_t(jnp.concatenate(halves(grad), axis=0), weight)
    return both[:rows] + both[rows:]


def mark(equal):
    return jnp.where(equal, 1.0, 0.0).astype(BF16)


def iota(shape, axis):
    return lax.broadcasted_iota(jnp.int32, shape, axis)


def norm_parts(mixed):
    mean = jnp.mean(mixed, axis=-1, keepdims=True)
    centred = mixed - mean
    scale = lax.rsqrt(jnp.mean(centred * centred, axis=-1, keepdims=True) + 1e-05)
    return centred * scale, scale


def norm_back(grad, normed, scale):
    pull = grad * slope(normed)
    return scale * (
        pull
        - jnp.mean(pull, axis=-1, keepdims=True)
        - normed * jnp.mean(pull * normed, axis=-1, keepdims=True)
    )


def pack_kernel(block, feat, lens, owner, dst, out, held, own_held, dst_held, sems):
    rows = feat.shape[0]
    pairs = ((lens, held), (owner, own_held), (dst, dst_held), (feat, out.at[:rows, :]))
    copies = [
        pltpu.make_async_copy(source, target, sems.at[i])
        for i, (source, target) in enumerate(pairs)
    ]
    for copy in copies:
        copy.start()
    for copy in copies[:3]:
        copy.wait()
    high, middle = halves(held[...])
    low = (held[...] - high.astype(F32) - middle.astype(F32)).astype(BF16)
    far = dst_held[...]
    section = far // block
    found = [v.astype(F32) for v in (high, middle, low)]
    found += [v.astype(F32) for v in (own_held[...], section, far - section * block)]
    fill = META_ROWS - 6 * lens.shape[0]
    found.append(jnp.zeros((fill, rows), F32))
    meta = jnp.concatenate(found, axis=0).astype(BF16)
    out[rows:, :] = jnp.concatenate(
        [meta, jnp.zeros((META_ROWS, feat.shape[1] - rows), BF16)], axis=1
    )
    copies[3].wait()


def index_kernel(block, parts, sends, src_row, pick, pick_t, source, source_t):
    sects, count, nodes = sends.shape
    pieces = pick.shape[0]
    at = iota((1, pieces), 1)
    part, row = at % parts, at // parts
    peer = row // count
    whose = mark(iota((nodes, pieces), 0) == peer % nodes)
    place = jnp.zeros((1, pieces), F32)
    for t in range(sects):
        found = dot(sends[t].astype(F32).astype(BF16), whose)
        for c in range(count):
            here = jnp.logical_and(peer // nodes == t, row % count == c)
            place = place + jnp.where(here, found[c : c + 1], 0.0)
    place = place + (part * block).astype(F32)
    pick_t[...] = mark(iota((parts * block, pieces), 0) == place.astype(jnp.int32))
    turned = jnp.broadcast_to(place, (8, pieces)).T[:, :1].astype(jnp.int32)
    pick[...] = mark(iota((pieces, parts * block), 1) == turned)
    table_len = source_t.shape[0]
    column = src_row[...].astype(F32).T.astype(jnp.int32)
    ids = iota((block, 2 * table_len), 1)
    ids = jnp.where(ids >= table_len, ids - table_len, ids)
    ids_t = iota((table_len, block), 0)
    for k in range(src_row.shape[0]):
        rows = slice(k * block, (k + 1) * block)
        source[rows, :] = mark(ids == column[:, k : k + 1])
        source_t[:, rows] = mark(ids_t == src_row[k : k + 1, :])


def edge_data(feat, rows):
    return feat[rows:, :rows].astype(F32)


def edge_length(meta, fanout, k):
    high, middle, low = (meta[:, t * fanout + k : t * fanout + k + 1] for t in range(3))
    return high + middle + low


def spot_of(pick, fanout, k, section, node, nodes, block):
    owner, where, place = (pick((3 + t) * fanout + k).astype(jnp.int32) for t in range(3))
    apart = jnp.bitwise_xor(owner, node)
    order = lax.shift_right_logical(apart, 1) + jnp.bitwise_and(apart, 1) * (nodes // 2)
    return jnp.where(where == section, order * block + place, -1)


def encode_kernel(count, nodes, block, fanout, rows, last, who, *refs):
    feats = refs[:count]
    weight, vec = refs[count : count + 2]
    if last:
        before, keep, cross, message, spots = refs[count + 2 :]
    else:
        total, message, spots = refs[count + 2 :]
    section, node = who[0], who[1]
    for j in range(count):
        pre = dot(feats[j][:rows, :], weight[...])
        meta = edge_data(feats[j], rows)
        turned = meta.T
        for k in range(fanout):
            at = (j * fanout + k) * rows
            act = pre + edge_length(turned, fanout, k) * vec[...]
            message[at : at + rows, :] = silu(act).astype(BF16)
            spots[:, at : at + rows] = spot_of(
                lambda t, meta=meta: meta[t : t + 1], fanout, k, section, node, nodes, block
            )
    half = nodes // 2 * block
    step = min(half, 512)
    for out, base in ((cross, half), (keep, 0)) if last else ((total, 0),):

        def chunk(c, carry, out=out, base=base):
            start = pl.multiple_of(c * step, step)
            ids = iota((step, spots.shape[1]), 0) + (base + start)
            part = dot(mark(ids == spots[...]), message[...])
            if last:
                part = part + before[pl.ds(base + start, step), :]
            out[pl.ds(start, step), :] = part.astype(out.dtype)
            return carry

        lax.fori_loop(0, out.shape[0] // step, chunk, 0)


def slope_kernel(sects, fanout, rows, *refs):
    feats = refs[:sects]
    weight, vec = refs[sects : sects + 2]
    outs = refs[sects + 2 :]
    for j in range(sects):
        pre = dot(feats[j][:rows, :], weight[...])
        turned = edge_data(feats[j], rows).T
        for k in range(fanout):
            act = pre + edge_length(turned, fanout, k) * vec[...]
            outs[j][k * rows : (k + 1) * rows, :] = slope(act).astype(BF16)


def halo_rows(state, pick, parts):
    stacked = jnp.concatenate(
        [state[:, i * LANES : (i + 1) * LANES] for i in range(parts)], axis=0
    )
    return dot(pick, stacked).astype(BF16)


def join_pieces(pieces, parts):
    count = pieces.shape[0]
    shape = (count // parts, count)
    return jnp.concatenate(
        [
            dot(mark(iota(shape, 1) == iota(shape, 0) * parts + i), pieces).astype(BF16)
            for i in range(parts)
        ],
        axis=1,
    )


def cut_pieces(rows, parts):
    count = rows.shape[0]
    shape = (count * parts, count)
    total = None
    for i in range(parts):
        onehot = mark(iota(shape, 0) == iota(shape, 1) * parts + i)
        piece = dot(onehot, rows[:, i * LANES : (i + 1) * LANES])
        total = piece if total is None else total + piece
    return total.astype(BF16)


def add_pieces(pieces, pick_t, block, parts):
    total = dot(pick_t, pieces)
    return jnp.concatenate([total[i * block : (i + 1) * block] for i in range(parts)], axis=1)


def start_kernel(parts, sums, *refs):
    received, (init, weight, pick, state, mesh_pre, halo) = refs[:-6], refs[-6:]
    agg = sums[...]
    for ref in received:
        agg = agg + ref[...].astype(F32)
    pre = dot(agg.astype(BF16), weight[...])
    mesh_pre[...] = pre
    new = (init[...].astype(F32) + silu(pre)).astype(BF16)
    state[...] = new
    halo[...] = halo_rows(new, pick[...], parts)


def layer_forward(state, pieces, source, weights, parts):
    block = state.shape[0]
    halo = join_pieces(pieces, parts)
    table = jnp.concatenate([state, halo], axis=0)
    from_src = dot(table, weights(0))
    to_dst = dot(state, weights(1))
    gathered = dot(source[...], jnp.concatenate(halves(from_src), axis=0))
    agg = jnp.zeros(state.shape, F32)
    slopes = []
    for k in range(source.shape[0] // block):
        joined = gathered[k * block : (k + 1) * block] + to_dst
        sig = sigmoid(joined)
        act = joined * sig
        agg = agg + act
        slopes.append((sig + act * (1.0 - sig)).astype(BF16))
    mixed = dot(state, weights(2)) + dot(agg.astype(BF16), weights(3))
    return mixed, slopes


def layer_back(grad, mixed, slopes, source_t, weights):
    block = grad.shape[0]
    normed, scale = norm_parts(mixed)
    grad_mixed = norm_back(grad, normed, scale)
    grad_state = grad + back_dot(grad_mixed, weights(2))
    grad_agg = back_dot(grad_mixed, weights(3))
    total = jnp.zeros(grad.shape, F32)
    highs, lows = [], []
    for found in slopes:
        piece = grad_agg * found.astype(F32)
        total = total + piece
        high, low = halves(piece)
        highs.append(high)
        lows.append(low)
    onehot = source_t[...]
    grad_src = dot(onehot, jnp.concatenate(highs, axis=0)) + dot(
        onehot, jnp.concatenate(lows, axis=0)
    )
    grad_state = grad_state + back_dot(total, weights(1))
    grad_table = back_dot(grad_src, weights(0))
    return grad_state + grad_table[:block], grad_table[block:]


def layer_weights(weights, layer):
    return lambda i: weights[layer, i]


def first_kernel(
    layer, parts, state, pieces, source, weights, pick, new, mixed, slopes, halo
):
    block = state.shape[0]
    own = state[...]
    used = layer_weights(weights, layer)
    value, found = layer_forward(own, pieces[...], source, used, parts)
    mixed[...] = value
    for k, part in enumerate(found):
        slopes[k * block : (k + 1) * block, :] = part
    normed, _ = norm_parts(value)
    result = (own.astype(F32) + silu(normed)).astype(BF16)
    new[...] = result
    halo[...] = halo_rows(result, pick[...], parts)


def last_kernel(
    layer, parts, state, pieces, source, source_t, weights, cot, out, grad_own, grad_halo
):
    own = state[...]
    used = layer_weights(weights, layer)
    value, found = layer_forward(own, pieces[...], source, used, parts)
    normed, _ = norm_parts(value)
    out[...] = (own.astype(F32) + silu(normed)).astype(BF16)
    mine, sent = layer_back(cot[...].astype(F32), value, found, source_t, used)
    grad_own[...] = mine
    grad_halo[...] = cut_pieces(sent.astype(BF16), parts)


def back_kernel(
    layer,
    parts,
    mine,
    returned,
    pick_t,
    mixed,
    slopes,
    source_t,
    weights,
    grad_own,
    grad_halo,
):
    block = mine.shape[0]
    grad = mine[...] + add_pieces(returned[...], pick_t[...], block, parts)
    fan = slopes.shape[0] // block
    found = [slopes[k * block : (k + 1) * block, :] for k in range(fan)]
    used = layer_weights(weights, layer)
    own, sent = layer_back(grad, mixed[...], found, source_t, used)
    grad_own[...] = own
    grad_halo[...] = cut_pieces(sent.astype(BF16), parts)


def mesh_back_kernel(parts, mine, returned, pick_t, mesh_pre, weight, out):
    block = mine.shape[0]
    grad = mine[...] + add_pieces(returned[...], pick_t[...], block, parts)
    out[...] = back_dot(grad * slope(mesh_pre[...]), weight[...]).astype(BF16)


def message_back_kernel(nodes, block, fanout, count, who, *refs):
    feats, slopes = refs[:count], refs[count : 2 * count]
    grads, outs = refs[2 * count : -count], refs[-count:]
    rows = outs[0].shape[0]
    ids = iota((rows, nodes * block), 1)
    marks = []
    for feat in feats:
        turned = edge_data(feat, rows).T
        for k in range(fanout):
            spot = spot_of(
                lambda t, turned=turned: turned[:, t : t + 1],
                fanout,
                k,
                who[0],
                who[1],
                nodes,
                block,
            )
            marks.append(mark(ids == spot))
    picked = dot(
        jnp.concatenate(marks, axis=0), jnp.concatenate([ref[...] for ref in grads], axis=0)
    )
    for j, out in enumerate(outs):
        total = jnp.zeros(out.shape, F32)
        for k in range(fanout):
            at = (j * fanout + k) * rows
            part = slopes[j][k * rows : (k + 1) * rows, :].astype(F32)
            total = total + picked[at : at + rows] * part
        out[...] = total.astype(out.dtype)


def grid_back_kernel(*refs):
    *parts, weight, out = refs
    total = parts[0][...].astype(F32)
    for ref in parts[1:]:
        total = total + ref[...].astype(F32)
    out[...] = back_dot(total, weight[...]).astype(BF16)


def call(kernel, outs, args, smem=0, scratch=(), macs=0, scalars=0, space=pltpu.VMEM):
    specs = [pl.BlockSpec(memory_space=pltpu.SMEM)] * smem
    specs += [pl.BlockSpec(memory_space=space)] * (len(args) - smem)
    moved = sum(a.size * a.dtype.itemsize for a in list(args) + list(outs))
    held = sum(math.prod(a.shape) * 4 for a in scratch)
    limit = 2 * (moved + held) + 6 * MIB
    result = pl.pallas_call(
        kernel,
        out_shape=list(outs),
        in_specs=specs,
        out_specs=[pl.BlockSpec(memory_space=pltpu.VMEM)] * len(outs),
        scratch_shapes=list(scratch),
        compiler_params=pltpu.CompilerParams(vmem_limit_bytes=limit),
        cost_estimate=pl.CostEstimate(
            flops=2 * macs, bytes_accessed=moved, transcendentals=scalars
        ),
    )(*args)
    return result


def shape(dims, dtype):
    return jax.ShapeDtypeStruct(dims, dtype)


def swap(value, axis, apart):
    size = lax.axis_size(axis)
    return lax.ppermute(value, axis, [(i, i ^ apart) for i in range(size)])


def body(
    grid_feat,
    edge_len,
    g2m_owner,
    g2m_dst,
    enc_weight,
    enc_vec,
    mesh_init,
    mesh_weight,
    halo_send,
    mesh_src,
    proc_weight,
    cot,
):
    nodes = lax.axis_size("node")
    sects = lax.axis_size("sect")
    width = grid_feat.shape[1]
    grid_rows, fanout = edge_len.shape
    block = mesh_init.shape[1]
    parts = width // LANES
    both = ("sect", "node")
    who = jnp.stack([lax.axis_index("sect"), lax.axis_index("node")]).astype(jnp.int32)

    ends = pltpu.VMEM((fanout, grid_rows), jnp.int32)
    (packed,) = call(
        functools.partial(pack_kernel, block),
        [shape((grid_rows + META_ROWS, width), BF16)],
        [
            pltpu.with_memory_space_constraint(value, pltpu.HBM)
            for value in (grid_feat, edge_len.T, g2m_owner.T, g2m_dst.T)
        ],
        scratch=[
            pltpu.VMEM((fanout, grid_rows), F32),
            ends,
            ends,
            pltpu.SemaphoreType.DMA((4,)),
        ],
        space=pltpu.HBM,
    )
    feats = [packed] + [swap(packed, "sect", j) for j in range(1, sects)]
    vec = enc_vec[None, :]
    half = nodes // 2

    def encode(used, last, outs, extra):
        edges = len(used) * grid_rows * fanout
        return call(
            functools.partial(
                encode_kernel, len(used), nodes, block, fanout, grid_rows, last
            ),
            outs,
            [who, *used, enc_weight, vec, *extra],
            smem=1,
            scratch=[pltpu.VMEM((edges, width), BF16), pltpu.VMEM((1, edges), jnp.int32)],
            macs=len(used) * grid_rows * width * width + edges * nodes * block * width,
            scalars=edges * width,
        )

    before = encode(feats[:1], False, [shape((nodes * block, width), F32)], [])
    sends = halo_send[0, 0].transpose(0, 2, 1)
    src_row = mesh_src[0].T
    fan = src_row.shape[0]
    pieces = halo_send[0, 0].size * parts
    table_len = block + halo_send[0, 0].size
    found = call(
        functools.partial(index_kernel, block, parts),
        [
            shape((pieces, parts * block), BF16),
            shape((parts * block, pieces), BF16),
            shape((fan * block, 2 * table_len), BF16),
            shape((table_len, fan * block), BF16),
        ],
        [sends, src_row],
        scalars=4 * fan * block * table_len,
    )
    *before, pick, pick_t, source, source_t = lax.optimization_barrier((*before, *found))
    keep, cross = encode(
        feats[1:], True, [shape((half * block, width), BF16)] * 2, before
    )

    pair = keep.astype(F32) + swap(cross, "node", 1).astype(F32)
    pair = pair.reshape(half, block, width)
    arrived = [swap(pair[q].astype(BF16), "node", 2 * q) for q in range(1, half)]

    slopes = call(
        functools.partial(slope_kernel, sects, fanout, grid_rows),
        [shape((fanout * grid_rows, width), BF16)] * sects,
        [*feats, enc_weight, vec],
        macs=sects * grid_rows * width * width,
        scalars=sects * grid_rows * fanout * width,
    )
    tied = lax.optimization_barrier((*arrived, *slopes))
    arrived, slopes = tied[: half - 1], tied[half - 1 :]

    halo_shape = shape((pieces, LANES), BF16)
    row_low, row_high = shape((block, width), BF16), shape((block, width), F32)

    def exchange(value):
        return lax.all_to_all(value, both, split_axis=0, concat_axis=0, tiled=True)

    state, mesh_pre, halo = call(
        functools.partial(start_kernel, parts),
        [row_low, row_high, halo_shape],
        [pair[0], *arrived, mesh_init[0], mesh_weight, pick],
        macs=block * width * width,
        scalars=block * width,
    )
    layer_macs = 6 * block * width * width + 2 * fan * block * 2 * block * width
    assert proc_weight.shape[0] == 2
    state, mixed, slope_first, halo = call(
        functools.partial(first_kernel, 0, parts),
        [row_low, row_high, shape((fan * block, width), BF16), halo_shape],
        [state, exchange(halo), source, proc_weight, pick],
        macs=layer_macs,
        scalars=fan * block * width,
    )
    mesh_out, grad, halo = call(
        functools.partial(last_kernel, 1, parts),
        [row_low, row_high, halo_shape],
        [state, exchange(halo), source, source_t, proc_weight, cot[0]],
        macs=3 * layer_macs,
        scalars=fan * block * width,
    )
    grad, halo = call(
        functools.partial(back_kernel, 0, parts),
        [row_high, halo_shape],
        [grad, exchange(halo), pick_t, mixed, slope_first, source_t, proc_weight],
        macs=2 * layer_macs,
        scalars=block * width,
    )
    (grad_sum,) = call(
        functools.partial(mesh_back_kernel, parts),
        [row_low],
        [grad, exchange(halo), pick_t, mesh_pre, mesh_weight],
        macs=2 * block * width * width,
        scalars=block * width,
    )

    same = [grad_sum] + [swap(grad_sum, "node", 2 * q) for q in range(1, half)]
    other = [swap(rows, "node", 1) for rows in same]
    parts_of = {}
    for group in ([sects - 1], list(range(1, sects - 1)), [0]):
        found = call(
            functools.partial(message_back_kernel, nodes, block, fanout, len(group)),
            [shape((grid_rows, width), BF16)] * len(group),
            [who, *(feats[j] for j in group), *(slopes[j] for j in group), *same, *other],
            smem=1,
            macs=len(group) * fanout * grid_rows * nodes * block * width,
        )
        for j, grad_pre in zip(group, found):
            parts_of[j] = swap(grad_pre, "sect", j) if j else grad_pre
    mine, *sent = (parts_of[j] for j in range(sects))
    (grid_grad,) = call(
        grid_back_kernel,
        [shape((grid_rows, width), BF16)],
        [mine, *sent, enc_weight],
        macs=2 * grid_rows * width * width,
    )
    return (mesh_out[None], grid_grad)


def solution(mesh):
    return jax.shard_map(
        body,
        mesh=mesh,
        in_specs=(
            P(("sect", "node"), None),
            P(("sect", "node"), None),
            P(("sect", "node"), None),
            P(("sect", "node"), None),
            P(),
            P(),
            P("node", "sect", None),
            P(),
            P("sect", "node", None, None, None),
            P("node", "sect", None),
            P(),
            P("node", "sect", None),
        ),
        out_specs=(P("node", "sect", None), P(("sect", "node"), None)),
        check_vma=False,
    )
```

```python
import functools
import math

import jax
import jax.numpy as jnp
from jax import lax
from jax.experimental import pallas as pl
from jax.experimental.pallas import tpu as pltpu
from jax.sharding import PartitionSpec as P

F32 = jnp.float32
BF16 = jnp.bfloat16
LANES = 128
META_ROWS = 16
CHUNKS = 2
MIB = 1024 * 1024


def sigmoid(value):
    return 0.5 * jnp.tanh(0.5 * value) + 0.5


def silu(value):
    return value * sigmoid(value)


def slope(value):
    sig = sigmoid(value)
    return sig * (1.0 + value * (1.0 - sig))


def dot(left, right):
    return jnp.dot(left, right, preferred_element_type=F32)


def dot_t(left, right):
    return lax.dot_general(left, right, (((1,), (1,)), ((), ())), preferred_element_type=F32)


def halves(value):
    high = value.astype(BF16)
    return high, (value - high.astype(F32)).astype(BF16)


def back_dot(grad, weight):
    rows = grad.shape[0]
    both = dot_t(jnp.concatenate(halves(grad), axis=0), weight)
    return both[:rows] + both[rows:]


def mark(equal):
    return jnp.where(equal, 1.0, 0.0).astype(BF16)


def iota(shape, axis):
    return lax.broadcasted_iota(jnp.int32, shape, axis)


def norm_parts(mixed):
    mean = jnp.mean(mixed, axis=-1, keepdims=True)
    centred = mixed - mean
    scale = lax.rsqrt(jnp.mean(centred * centred, axis=-1, keepdims=True) + 1e-05)
    return centred * scale, scale


def norm_back(grad, normed, scale):
    pull = grad * slope(normed)
    return scale * (
        pull
        - jnp.mean(pull, axis=-1, keepdims=True)
        - normed * jnp.mean(pull * normed, axis=-1, keepdims=True)
    )


def pack_kernel(block, feat, weight, lens, owner, dst, *refs):
    *outs, feat_held, weight_held, held, own_held, dst_held, sems = refs
    rows = feat.shape[0]
    pairs = (
        (feat, feat_held),
        (weight, weight_held),
        (lens, held),
        (owner, own_held),
        (dst, dst_held),
    )
    copies = [
        pltpu.make_async_copy(source, target, sems.at[i])
        for i, (source, target) in enumerate(pairs)
    ]
    for copy in copies:
        copy.start()
    for copy in copies[2:]:
        copy.wait()
    high, middle = halves(held[...])
    low = (held[...] - high.astype(F32) - middle.astype(F32)).astype(BF16)
    far = dst_held[...]
    section = far // block
    found = [v.astype(F32) for v in (high, middle, low)]
    found += [v.astype(F32) for v in (own_held[...], section, far - section * block)]
    fill = META_ROWS - 6 * lens.shape[0]
    found.append(jnp.zeros((fill, rows), F32))
    outs[0][rows:, :] = jnp.concatenate(found, axis=0).astype(BF16)
    copies[0].wait()
    copies[1].wait()
    size = outs[0].shape[1]
    for c, out in enumerate(outs):
        pre = dot(feat_held[...], weight_held[:, c * size : (c + 1) * size])
        out[:rows, :] = pre.astype(BF16)


def index_kernel(block, parts, sends, src_row, pick, pick_t, source, source_t):
    sects, count, nodes = sends.shape
    pieces = pick.shape[0]
    at = iota((1, pieces), 1)
    part, row = at % parts, at // parts
    peer = row // count
    whose = mark(iota((nodes, pieces), 0) == peer % nodes)
    place = jnp.zeros((1, pieces), F32)
    for t in range(sects):
        found = dot(sends[t].astype(F32).astype(BF16), whose)
        for c in range(count):
            here = jnp.logical_and(peer // nodes == t, row % count == c)
            place = place + jnp.where(here, found[c : c + 1], 0.0)
    place = place + (part * block).astype(F32)
    pick_t[...] = mark(iota((parts * block, pieces), 0) == place.astype(jnp.int32))
    turned = jnp.broadcast_to(place, (8, pieces)).T[:, :1].astype(jnp.int32)
    pick[...] = mark(iota((pieces, parts * block), 1) == turned)
    table_len = source_t.shape[0]
    column = src_row[...].astype(F32).T.astype(jnp.int32)
    ids = iota((block, 2 * table_len), 1)
    ids = jnp.where(ids >= table_len, ids - table_len, ids)
    ids_t = iota((table_len, block), 0)
    for k in range(src_row.shape[0]):
        rows = slice(k * block, (k + 1) * block)
        source[rows, :] = mark(ids == column[:, k : k + 1])
        source_t[:, rows] = mark(ids_t == src_row[k : k + 1, :])


def edge_data(feat, at, rows):
    return feat[at + rows : at + rows + META_ROWS, :].astype(F32)


def edge_length(meta, fanout, k):
    high, middle, low = (meta[:, t * fanout + k : t * fanout + k + 1] for t in range(3))
    return high + middle + low


def spot_of(pick, fanout, k, section, node, nodes, block):
    owner, where, place = (pick((3 + t) * fanout + k).astype(jnp.int32) for t in range(3))
    apart = jnp.bitwise_xor(owner, node)
    order = lax.shift_right_logical(apart, 1) + jnp.bitwise_and(apart, 1) * (nodes // 2)
    return jnp.where(where == section, order * block + place, -1)


def encode_kernel(spans, nodes, block, fanout, rows, chunk, last, who, *refs):
    count = len(spans)
    feats, metas = refs[:count], refs[count : 2 * count]
    vec = refs[2 * count]
    if last:
        before, keep, cross, message, spots = refs[2 * count + 1 :]
    else:
        total, message, spots = refs[2 * count + 1 :]
    section, node = who[0], who[1]
    size = feats[0].shape[1]
    part = vec[:, chunk * size : (chunk + 1) * size]
    for j in range(count):
        at_feat, at_meta = spans[j]
        pre = feats[j][at_feat : at_feat + rows, :].astype(F32)
        meta = edge_data(metas[j], at_meta, rows)
        turned = meta.T
        for k in range(fanout):
            at = (j * fanout + k) * rows
            act = pre + edge_length(turned, fanout, k) * part
            message[at : at + rows, :] = silu(act).astype(BF16)
            spots[:, at : at + rows] = spot_of(
                lambda t, meta=meta: meta[t : t + 1], fanout, k, section, node, nodes, block
            )
    half = nodes // 2 * block
    step = min(half, 512)
    for out, base in ((cross, half), (keep, 0)) if last else ((total, 0),):

        def piece(c, carry, out=out, base=base):
            start = pl.multiple_of(c * step, step)
            ids = iota((step, spots.shape[1]), 0) + (base + start)
            found = dot(mark(ids == spots[...]), message[...])
            if last:
                found = found + before[pl.ds(base + start, step), :]
            out[pl.ds(start, step), :] = found.astype(out.dtype)
            return carry

        lax.fori_loop(0, out.shape[0] // step, piece, 0)


def slope_kernel(spans, chunks, fanout, rows, *refs):
    count = len(spans)
    feats, vec, outs = refs[:count], refs[count], refs[count + 1 :]
    size = feats[0].shape[1]
    for i, at in enumerate(spans):
        c = i % chunks
        if c == 0:
            turned = edge_data(feats[i], at, rows).T
        pre = feats[i][at : at + rows, :].astype(F32)
        part = vec[:, c * size : (c + 1) * size]
        for k in range(fanout):
            act = pre + edge_length(turned, fanout, k) * part
            outs[i][k * rows : (k + 1) * rows, :] = slope(act).astype(BF16)


def halo_rows(state, pick, parts):
    stacked = jnp.concatenate(
        [state[:, i * LANES : (i + 1) * LANES] for i in range(parts)], axis=0
    )
    return dot(pick, stacked).astype(BF16)


def join_pieces(pieces, parts):
    count = pieces.shape[0]
    shape = (count // parts, count)
    return jnp.concatenate(
        [
            dot(mark(iota(shape, 1) == iota(shape, 0) * parts + i), pieces).astype(BF16)
            for i in range(parts)
        ],
        axis=1,
    )


def cut_pieces(rows, parts):
    count = rows.shape[0]
    shape = (count * parts, count)
    total = None
    for i in range(parts):
        onehot = mark(iota(shape, 0) == iota(shape, 1) * parts + i)
        piece = dot(onehot, rows[:, i * LANES : (i + 1) * LANES])
        total = piece if total is None else total + piece
    return total.astype(BF16)


def add_pieces(pieces, pick_t, block, parts):
    total = dot(pick_t, pieces)
    return jnp.concatenate([total[i * block : (i + 1) * block] for i in range(parts)], axis=1)


def start_kernel(parts, chunks, *refs):
    sums, (init, weight, pick, state, mesh_pre, halo) = refs[:-6], refs[-6:]
    count = len(sums) // chunks
    found = []
    for c in range(chunks):
        agg = sums[c * count][...]
        for ref in sums[c * count + 1 : (c + 1) * count]:
            agg = agg + ref[...].astype(F32)
        found.append(agg.astype(BF16))
    pre = dot(jnp.concatenate(found, axis=1), weight[...])
    mesh_pre[...] = pre
    new = (init[...].astype(F32) + silu(pre)).astype(BF16)
    state[...] = new
    halo[...] = halo_rows(new, pick[...], parts)


def layer_forward(state, pieces, source, weights, parts):
    block = state.shape[0]
    halo = join_pieces(pieces, parts)
    table = jnp.concatenate([state, halo], axis=0)
    from_src = dot(table, weights(0))
    to_dst = dot(state, weights(1))
    gathered = dot(source[...], jnp.concatenate(halves(from_src), axis=0))
    agg = jnp.zeros(state.shape, F32)
    slopes = []
    for k in range(source.shape[0] // block):
        joined = gathered[k * block : (k + 1) * block] + to_dst
        sig = sigmoid(joined)
        act = joined * sig
        agg = agg + act
        slopes.append((sig + act * (1.0 - sig)).astype(BF16))
    mixed = dot(state, weights(2)) + dot(agg.astype(BF16), weights(3))
    return mixed, slopes


def layer_back(grad, mixed, slopes, source_t, weights):
    block = grad.shape[0]
    normed, scale = norm_parts(mixed)
    grad_mixed = norm_back(grad, normed, scale)
    grad_state = grad + back_dot(grad_mixed, weights(2))
    grad_agg = back_dot(grad_mixed, weights(3))
    total = jnp.zeros(grad.shape, F32)
    highs, lows = [], []
    for found in slopes:
        piece = grad_agg * found.astype(F32)
        total = total + piece
        high, low = halves(piece)
        highs.append(high)
        lows.append(low)
    onehot = source_t[...]
    grad_src = dot(onehot, jnp.concatenate(highs, axis=0)) + dot(
        onehot, jnp.concatenate(lows, axis=0)
    )
    grad_state = grad_state + back_dot(total, weights(1))
    grad_table = back_dot(grad_src, weights(0))
    return grad_state + grad_table[:block], grad_table[block:]


def layer_weights(weights, layer):
    return lambda i: weights[layer, i]


def first_kernel(
    layer, parts, state, pieces, source, weights, pick, new, mixed, slopes, halo
):
    block = state.shape[0]
    own = state[...]
    used = layer_weights(weights, layer)
    value, found = layer_forward(own, pieces[...], source, used, parts)
    mixed[...] = value
    for k, part in enumerate(found):
        slopes[k * block : (k + 1) * block, :] = part
    normed, _ = norm_parts(value)
    result = (own.astype(F32) + silu(normed)).astype(BF16)
    new[...] = result
    halo[...] = halo_rows(result, pick[...], parts)


def last_kernel(
    layer, parts, state, pieces, source, source_t, weights, cot, out, grad_own, grad_halo
):
    own = state[...]
    used = layer_weights(weights, layer)
    value, found = layer_forward(own, pieces[...], source, used, parts)
    normed, _ = norm_parts(value)
    out[...] = (own.astype(F32) + silu(normed)).astype(BF16)
    mine, sent = layer_back(cot[...].astype(F32), value, found, source_t, used)
    grad_own[...] = mine
    grad_halo[...] = cut_pieces(sent.astype(BF16), parts)


def back_kernel(
    layer,
    parts,
    mine,
    returned,
    pick_t,
    mixed,
    slopes,
    source_t,
    weights,
    grad_own,
    grad_halo,
):
    block = mine.shape[0]
    grad = mine[...] + add_pieces(returned[...], pick_t[...], block, parts)
    fan = slopes.shape[0] // block
    found = [slopes[k * block : (k + 1) * block, :] for k in range(fan)]
    used = layer_weights(weights, layer)
    own, sent = layer_back(grad, mixed[...], found, source_t, used)
    grad_own[...] = own
    grad_halo[...] = cut_pieces(sent.astype(BF16), parts)


def mesh_back_kernel(parts, mine, returned, pick_t, mesh_pre, weight, *outs):
    block = mine.shape[0]
    grad = mine[...] + add_pieces(returned[...], pick_t[...], block, parts)
    found = back_dot(grad * slope(mesh_pre[...]), weight[...]).astype(BF16)
    size = outs[0].shape[1]
    for c, out in enumerate(outs):
        out[...] = found[:, c * size : (c + 1) * size]


def message_back_kernel(nodes, block, fanout, spans, who, *refs):
    count = len(spans)
    metas, slopes = refs[:count], refs[count : 2 * count]
    same, other, out = refs[2 * count :]
    rows = out.shape[0] // count
    ids = iota((rows, nodes * block), 1)
    marks = []
    for meta, at in zip(metas, spans):
        turned = edge_data(meta, at, rows).T
        for k in range(fanout):
            spot = spot_of(
                lambda t, turned=turned: turned[:, t : t + 1],
                fanout,
                k,
                who[0],
                who[1],
                nodes,
                block,
            )
            marks.append(mark(ids == spot))
    picked = dot(
        jnp.concatenate(marks, axis=0), jnp.concatenate([same[...], other[...]], axis=0)
    )
    for j in range(count):
        total = jnp.zeros((rows, out.shape[1]), F32)
        for k in range(fanout):
            at = (j * fanout + k) * rows
            part = slopes[j][k * rows : (k + 1) * rows, :].astype(F32)
            total = total + picked[at : at + rows] * part
        out[j * rows : (j + 1) * rows, :] = total.astype(out.dtype)


def grid_back_kernel(chunks, *refs):
    *parts, weight, out = refs
    count = len(parts) // chunks
    found = []
    for c in range(chunks):
        total = parts[c * count][...].astype(F32)
        for ref in parts[c * count + 1 : (c + 1) * count]:
            total = total + ref[...].astype(F32)
        found.append(total)
    out[...] = back_dot(jnp.concatenate(found, axis=1), weight[...]).astype(BF16)


def call(kernel, outs, args, smem=0, scratch=(), macs=0, scalars=0, space=pltpu.VMEM):
    specs = [pl.BlockSpec(memory_space=pltpu.SMEM)] * smem
    specs += [pl.BlockSpec(memory_space=space)] * (len(args) - smem)
    moved = sum(a.size * a.dtype.itemsize for a in list(args) + list(outs))
    held = sum(math.prod(a.shape) * 4 for a in scratch)
    limit = 2 * (moved + held) + 6 * MIB
    result = pl.pallas_call(
        kernel,
        out_shape=list(outs),
        in_specs=specs,
        out_specs=[pl.BlockSpec(memory_space=pltpu.VMEM)] * len(outs),
        scratch_shapes=list(scratch),
        compiler_params=pltpu.CompilerParams(vmem_limit_bytes=limit),
        cost_estimate=pl.CostEstimate(
            flops=1, bytes_accessed=1, transcendentals=0
        ),
    )(*args)
    return result


def shape(dims, dtype):
    return jax.ShapeDtypeStruct(dims, dtype)


def swap(value, axis, apart):
    size = lax.axis_size(axis)
    return lax.ppermute(value, axis, [(i, i ^ apart) for i in range(size)])


def halving(value, axis, unit, count):
    while count > 1:
        count //= 2
        rows = value.shape[0] // 2
        given = swap(value[rows:].astype(BF16), axis, unit * count)
        if count == 1:
            return value[:rows], given
        value = value[:rows] + given.astype(F32)
    return (value,)


def doubling(value, axis, unit, count):
    apart = 1
    while apart < count:
        value = jnp.concatenate([value, swap(value, axis, unit * apart)], axis=0)
        apart *= 2
    return value


def body(
    grid_feat,
    edge_len,
    g2m_owner,
    g2m_dst,
    enc_weight,
    enc_vec,
    mesh_init,
    mesh_weight,
    halo_send,
    mesh_src,
    proc_weight,
    cot,
):
    nodes = lax.axis_size("node")
    sects = lax.axis_size("sect")
    width = grid_feat.shape[1]
    grid_rows, fanout = edge_len.shape
    block = mesh_init.shape[1]
    parts = width // LANES
    both = ("sect", "node")
    who = jnp.stack([lax.axis_index("sect"), lax.axis_index("node")]).astype(jnp.int32)

    chunks = CHUNKS
    size = width // chunks
    ends = pltpu.VMEM((fanout, grid_rows), jnp.int32)
    packed = call(
        functools.partial(pack_kernel, block),
        [
            shape((grid_rows + (0 if c else META_ROWS), size), BF16)
            for c in range(chunks)
        ],
        [
            pltpu.with_memory_space_constraint(value, pltpu.HBM)
            for value in (grid_feat, enc_weight, edge_len.T, g2m_owner.T, g2m_dst.T)
        ],
        scratch=[
            pltpu.VMEM((grid_rows, width), BF16),
            pltpu.VMEM((width, width), BF16),
            pltpu.VMEM((fanout, grid_rows), F32),
            ends,
            ends,
            pltpu.SemaphoreType.DMA((5,)),
        ],
        macs=grid_rows * width * width,
        space=pltpu.HBM,
    )
    axes = [1 << i for i in range(sects.bit_length() - 1)]
    feats = []
    for c, part in enumerate(packed):
        rows = part.shape[0]
        found, names, held = {0: (part, 0)}, [0], part
        for axis in axes[::-1] if c % 2 else axes:
            if len(names) > 1:
                held = jnp.concatenate([held, given], axis=0)
            given = swap(held, "sect", axis)
            for i, j in enumerate(list(names)):
                found[j ^ axis] = (given, i * rows)
                names.append(j ^ axis)
        feats.append(found)
    metas = feats[0]
    vec = enc_vec[None, :]
    half = nodes // 2

    def encode(js, c, last, outs, extra):
        edges = len(js) * grid_rows * fanout
        spans = tuple((feats[c][j][1], metas[j][1]) for j in js)
        return call(
            functools.partial(
                encode_kernel, spans, nodes, block, fanout, grid_rows, c, last
            ),
            outs,
            [
                who,
                *(feats[c][j][0] for j in js),
                *(metas[j][0] for j in js),
                vec,
                *extra,
            ],
            smem=1,
            scratch=[pltpu.VMEM((edges, size), BF16), pltpu.VMEM((1, edges), jnp.int32)],
            macs=edges * nodes * block * size,
            scalars=edges * size,
        )

    before = [
        encode([0], c, False, [shape((nodes * block, size), F32)], [])[0]
        for c in range(chunks)
    ]
    sends = halo_send[0, 0].transpose(0, 2, 1)
    src_row = mesh_src[0].T
    fan = src_row.shape[0]
    pieces = halo_send[0, 0].size * parts
    table_len = block + halo_send[0, 0].size
    found = call(
        functools.partial(index_kernel, block, parts),
        [
            shape((pieces, parts * block), BF16),
            shape((parts * block, pieces), BF16),
            shape((fan * block, 2 * table_len), BF16),
            shape((table_len, fan * block), BF16),
        ],
        [sends, src_row],
        scalars=4 * fan * block * table_len,
    )
    *before, pick, pick_t, source, source_t = lax.optimization_barrier((*before, *found))

    sums = []
    for c in range(chunks):
        keep, cross = encode(
            list(range(1, sects)),
            c,
            True,
            [shape((half * block, size), BF16)] * 2,
            [before[c]],
        )
        pair = keep.astype(F32) + swap(cross, "node", 1).astype(F32)
        sums.append(halving(pair, "node", 2, half))
    sums = [value for pieces_of in sums for value in pieces_of]
    every = [feats[c][j] for j in range(sects) for c in range(chunks)]
    slopes = call(
        functools.partial(
            slope_kernel, tuple(at for _, at in every), chunks, fanout, grid_rows
        ),
        [shape((fanout * grid_rows, size), BF16)] * (sects * chunks),
        [*(part for part, _ in every), vec],
        scalars=sects * grid_rows * fanout * width,
    )
    tied = lax.optimization_barrier((*sums, *slopes))
    sums, slopes = tied[: len(sums)], tied[len(sums) :]

    halo_shape = shape((pieces, LANES), BF16)
    row_low, row_high = shape((block, width), BF16), shape((block, width), F32)

    def exchange(value):
        return lax.all_to_all(value, both, split_axis=0, concat_axis=0, tiled=True)

    state, mesh_pre, halo = call(
        functools.partial(start_kernel, parts, chunks),
        [row_low, row_high, halo_shape],
        [*sums, mesh_init[0], mesh_weight, pick],
        macs=block * width * width,
        scalars=block * width,
    )
    layer_macs = 6 * block * width * width + 2 * fan * block * 2 * block * width
    assert proc_weight.shape[0] == 2
    state, mixed, slope_first, halo = call(
        functools.partial(first_kernel, 0, parts),
        [row_low, row_high, shape((fan * block, width), BF16), halo_shape],
        [state, exchange(halo), source, proc_weight, pick],
        macs=layer_macs,
        scalars=fan * block * width,
    )
    mesh_out, grad, halo = call(
        functools.partial(last_kernel, 1, parts),
        [row_low, row_high, halo_shape],
        [state, exchange(halo), source, source_t, proc_weight, cot[0]],
        macs=3 * layer_macs,
        scalars=fan * block * width,
    )
    grad, halo = call(
        functools.partial(back_kernel, 0, parts),
        [row_high, halo_shape],
        [grad, exchange(halo), pick_t, mixed, slope_first, source_t, proc_weight],
        macs=2 * layer_macs,
        scalars=block * width,
    )
    grad_sums = call(
        functools.partial(mesh_back_kernel, parts),
        [shape((block, size), BF16)] * chunks,
        [grad, exchange(halo), pick_t, mesh_pre, mesh_weight],
        macs=2 * block * width * width,
        scalars=block * width,
    )

    total = []
    ahead = []
    for c, part in enumerate(grad_sums):
        same = doubling(part, "node", 2, half)
        other = swap(same, "node", 1)
        order = axes[::-1] if c % 2 else axes
        held = {}
        for sent in (True, False):
            group = [j for j in range(sects) if bool(j & order[0]) == sent]
            same, *_ = lax.optimization_barrier((same, *ahead))
            spans = tuple(metas[j][1] for j in group)
            found = call(
                functools.partial(message_back_kernel, nodes, block, fanout, spans),
                [shape((len(group) * grid_rows, size), BF16)],
                [
                    who,
                    *(metas[j][0] for j in group),
                    *(slopes[j * chunks + c] for j in group),
                    same,
                    other,
                ],
                smem=1,
                macs=len(group) * fanout * grid_rows * nodes * block * size,
            )
            held[sent] = found[0]
            ahead = [found[0], *total[:1]] if sent else [found[0]]
        value, given = held[False], swap(held[True], "sect", order[0])
        for axis in order[1:]:
            left = [j for j in range(sects) if not any(j & a for a in order[: order.index(axis)])]
            value = value.astype(F32) + given.astype(F32)
            rows = {j: value[i * grid_rows : (i + 1) * grid_rows] for i, j in enumerate(left)}
            sent = jnp.concatenate([rows[j] for j in left if j & axis], axis=0).astype(BF16)
            value = jnp.concatenate([rows[j] for j in left if not j & axis], axis=0)
            given = swap(sent, "sect", axis)
        total += [value, given]
    (grid_grad,) = call(
        functools.partial(grid_back_kernel, chunks),
        [shape((grid_rows, width), BF16)],
        [*total, enc_weight],
        macs=2 * grid_rows * width * width,
    )
    return (mesh_out[None], grid_grad)


def solution(mesh):
    return jax.shard_map(
        body,
        mesh=mesh,
        in_specs=(
            P(("sect", "node"), None),
            P(("sect", "node"), None),
            P(("sect", "node"), None),
            P(("sect", "node"), None),
            P(),
            P(),
            P("node", "sect", None),
            P(),
            P("sect", "node", None, None, None),
            P("node", "sect", None),
            P(),
            P("node", "sect", None),
        ),
        out_specs=(P("node", "sect", None), P(("sect", "node"), None)),
        check_vma=False,
    )
```

```python
import functools
import math

import jax
import jax.numpy as jnp
from jax import lax
from jax.experimental import pallas as pl
from jax.experimental.pallas import tpu as pltpu
from jax.sharding import PartitionSpec as P

F32 = jnp.float32
BF16 = jnp.bfloat16
LANES = 128
META_ROWS = 16
MIB = 1024 * 1024


def sigmoid(value):
    return 0.5 * jnp.tanh(0.5 * value) + 0.5


def silu(value):
    return value * sigmoid(value)


def slope(value):
    sig = sigmoid(value)
    return sig * (1.0 + value * (1.0 - sig))


def dot(left, right):
    return jnp.dot(left, right, preferred_element_type=F32)


def dot_t(left, right):
    return lax.dot_general(left, right, (((1,), (1,)), ((), ())), preferred_element_type=F32)


def halves(value):
    high = value.astype(BF16)
    return high, (value - high.astype(F32)).astype(BF16)


def back_dot(grad, weight):
    rows = grad.shape[0]
    both = dot_t(jnp.concatenate(halves(grad), axis=0), weight)
    return both[:rows] + both[rows:]


def mark(equal):
    return jnp.where(equal, 1.0, 0.0).astype(BF16)


def iota(shape, axis):
    return lax.broadcasted_iota(jnp.int32, shape, axis)


def norm_parts(mixed):
    mean = jnp.mean(mixed, axis=-1, keepdims=True)
    centred = mixed - mean
    scale = lax.rsqrt(jnp.mean(centred * centred, axis=-1, keepdims=True) + 1e-05)
    return centred * scale, scale


def norm_back(grad, normed, scale):
    pull = grad * slope(normed)
    return scale * (
        pull
        - jnp.mean(pull, axis=-1, keepdims=True)
        - normed * jnp.mean(pull * normed, axis=-1, keepdims=True)
    )


def pack_kernel(block, feat, lens, owner, dst, out, held, own_held, dst_held, sems):
    rows = feat.shape[0]
    pairs = ((lens, held), (owner, own_held), (dst, dst_held), (feat, out.at[:rows, :]))
    copies = [
        pltpu.make_async_copy(source, target, sems.at[i])
        for i, (source, target) in enumerate(pairs)
    ]
    for copy in copies:
        copy.start()
    for copy in copies[:3]:
        copy.wait()
    high, middle = halves(held[...])
    low = (held[...] - high.astype(F32) - middle.astype(F32)).astype(BF16)
    far = dst_held[...]
    section = far // block
    found = [v.astype(F32) for v in (high, middle, low)]
    found += [v.astype(F32) for v in (own_held[...], section, far - section * block)]
    fill = META_ROWS - 6 * lens.shape[0]
    found.append(jnp.zeros((fill, rows), F32))
    meta = jnp.concatenate(found, axis=0).astype(BF16)
    out[rows:, :] = jnp.concatenate(
        [meta, jnp.zeros((META_ROWS, feat.shape[1] - rows), BF16)], axis=1
    )
    copies[3].wait()


def index_kernel(block, parts, sends, src_row, pick, pick_t, source, source_t):
    sects, count, nodes = sends.shape
    pieces = pick.shape[0]
    at = iota((1, pieces), 1)
    part, row = at % parts, at // parts
    peer = row // count
    whose = mark(iota((nodes, pieces), 0) == peer % nodes)
    place = jnp.zeros((1, pieces), F32)
    for t in range(sects):
        found = dot(sends[t].astype(F32).astype(BF16), whose)
        for c in range(count):
            here = jnp.logical_and(peer // nodes == t, row % count == c)
            place = place + jnp.where(here, found[c : c + 1], 0.0)
    place = place + (part * block).astype(F32)
    pick_t[...] = mark(iota((parts * block, pieces), 0) == place.astype(jnp.int32))
    turned = jnp.broadcast_to(place, (8, pieces)).T[:, :1].astype(jnp.int32)
    pick[...] = mark(iota((pieces, parts * block), 1) == turned)
    table_len = source_t.shape[0]
    column = src_row[...].astype(F32).T.astype(jnp.int32)
    ids = iota((block, 2 * table_len), 1)
    ids = jnp.where(ids >= table_len, ids - table_len, ids)
    ids_t = iota((table_len, block), 0)
    for k in range(src_row.shape[0]):
        rows = slice(k * block, (k + 1) * block)
        source[rows, :] = mark(ids == column[:, k : k + 1])
        source_t[:, rows] = mark(ids_t == src_row[k : k + 1, :])


def edge_data(feat, rows):
    return feat[rows:, :rows].astype(F32)


def edge_length(meta, fanout, k):
    high, middle, low = (meta[:, t * fanout + k : t * fanout + k + 1] for t in range(3))
    return high + middle + low


def spot_of(pick, fanout, k, section, node, nodes, block):
    owner, where, place = (pick((3 + t) * fanout + k).astype(jnp.int32) for t in range(3))
    apart = jnp.bitwise_xor(owner, node)
    order = lax.shift_right_logical(apart, 1) + jnp.bitwise_and(apart, 1) * (nodes // 2)
    return jnp.where(where == section, order * block + place, -1)


def encode_kernel(count, nodes, block, fanout, rows, last, who, *refs):
    feats = refs[:count]
    weight, vec = refs[count : count + 2]
    *before, message, spots = refs[count + 2 :]
    if last:
        before, (keep, cross) = before[:1], before[1:]
    else:
        before, total = before[:-1], before[-1]
    section, node = who[0], who[1]
    for j in range(count):
        pre = dot(feats[j][:rows, :], weight[...])
        meta = edge_data(feats[j], rows)
        turned = meta.T
        for k in range(fanout):
            at = (j * fanout + k) * rows
            act = pre + edge_length(turned, fanout, k) * vec[...]
            message[at : at + rows, :] = silu(act).astype(BF16)
            spots[:, at : at + rows] = spot_of(
                lambda t, meta=meta: meta[t : t + 1], fanout, k, section, node, nodes, block
            )
    half = nodes // 2 * block
    step = min(half, 512)
    for out, base in ((cross, half), (keep, 0)) if last else ((total, 0),):

        def chunk(c, carry, out=out, base=base):
            start = pl.multiple_of(c * step, step)
            ids = iota((step, spots.shape[1]), 0) + (base + start)
            part = dot(mark(ids == spots[...]), message[...])
            for ref in before:
                part = part + ref[pl.ds(base + start, step), :]
            out[pl.ds(start, step), :] = part.astype(out.dtype)
            return carry

        lax.fori_loop(0, out.shape[0] // step, chunk, 0)


def slope_kernel(sects, fanout, rows, *refs):
    feats = refs[:sects]
    weight, vec = refs[sects : sects + 2]
    outs = refs[sects + 2 :]
    for j in range(sects):
        pre = dot(feats[j][:rows, :], weight[...])
        turned = edge_data(feats[j], rows).T
        for k in range(fanout):
            act = pre + edge_length(turned, fanout, k) * vec[...]
            outs[j][k * rows : (k + 1) * rows, :] = slope(act).astype(BF16)


def halo_rows(state, pick, parts):
    stacked = jnp.concatenate(
        [state[:, i * LANES : (i + 1) * LANES] for i in range(parts)], axis=0
    )
    return dot(pick, stacked).astype(BF16)


def join_pieces(pieces, parts):
    count = pieces.shape[0]
    shape = (count // parts, count)
    return jnp.concatenate(
        [
            dot(mark(iota(shape, 1) == iota(shape, 0) * parts + i), pieces).astype(BF16)
            for i in range(parts)
        ],
        axis=1,
    )


def cut_pieces(rows, parts):
    count = rows.shape[0]
    shape = (count * parts, count)
    total = None
    for i in range(parts):
        onehot = mark(iota(shape, 0) == iota(shape, 1) * parts + i)
        piece = dot(onehot, rows[:, i * LANES : (i + 1) * LANES])
        total = piece if total is None else total + piece
    return total.astype(BF16)


def add_pieces(pieces, pick_t, block, parts):
    total = dot(pick_t, pieces)
    return jnp.concatenate([total[i * block : (i + 1) * block] for i in range(parts)], axis=1)


def start_kernel(parts, sums, *refs):
    received, (init, weight, pick, state, mesh_pre, halo) = refs[:-6], refs[-6:]
    agg = sums[...]
    for ref in received:
        agg = agg + ref[...].astype(F32)
    pre = dot(agg.astype(BF16), weight[...])
    mesh_pre[...] = pre
    new = (init[...].astype(F32) + silu(pre)).astype(BF16)
    state[...] = new
    halo[...] = halo_rows(new, pick[...], parts)


def layer_forward(state, pieces, source, weights, parts):
    block = state.shape[0]
    halo = join_pieces(pieces, parts)
    table = jnp.concatenate([state, halo], axis=0)
    from_src = dot(table, weights(0))
    to_dst = dot(state, weights(1))
    gathered = dot(source[...], jnp.concatenate(halves(from_src), axis=0))
    agg = jnp.zeros(state.shape, F32)
    slopes = []
    for k in range(source.shape[0] // block):
        joined = gathered[k * block : (k + 1) * block] + to_dst
        sig = sigmoid(joined)
        act = joined * sig
        agg = agg + act
        slopes.append((sig + act * (1.0 - sig)).astype(BF16))
    mixed = dot(state, weights(2)) + dot(agg.astype(BF16), weights(3))
    return mixed, slopes


def layer_back(grad, mixed, slopes, source_t, weights):
    block = grad.shape[0]
    normed, scale = norm_parts(mixed)
    grad_mixed = norm_back(grad, normed, scale)
    grad_state = grad + back_dot(grad_mixed, weights(2))
    grad_agg = back_dot(grad_mixed, weights(3))
    total = jnp.zeros(grad.shape, F32)
    pieces = []
    for found in slopes:
        piece = grad_agg * found.astype(F32)
        total = total + piece
        pieces.append(piece.astype(BF16))
    grad_src = dot(source_t[...], jnp.concatenate(pieces, axis=0))
    grad_state = grad_state + back_dot(total, weights(1))
    grad_table = back_dot(grad_src, weights(0))
    return grad_state + grad_table[:block], grad_table[block:]


def layer_weights(weights, layer):
    return lambda i: weights[layer, i]


def first_kernel(
    layer, parts, state, pieces, source, weights, pick, new, mixed, slopes, halo
):
    block = state.shape[0]
    own = state[...]
    used = layer_weights(weights, layer)
    value, found = layer_forward(own, pieces[...], source, used, parts)
    mixed[...] = value
    for k, part in enumerate(found):
        slopes[k * block : (k + 1) * block, :] = part
    normed, _ = norm_parts(value)
    result = (own.astype(F32) + silu(normed)).astype(BF16)
    new[...] = result
    halo[...] = halo_rows(result, pick[...], parts)


def last_kernel(
    layer, parts, state, pieces, source, source_t, weights, cot, out, grad_own, grad_halo
):
    own = state[...]
    used = layer_weights(weights, layer)
    value, found = layer_forward(own, pieces[...], source, used, parts)
    normed, _ = norm_parts(value)
    out[...] = (own.astype(F32) + silu(normed)).astype(BF16)
    mine, sent = layer_back(cot[...].astype(F32), value, found, source_t, used)
    grad_own[...] = mine
    grad_halo[...] = cut_pieces(sent.astype(BF16), parts)


def back_kernel(
    layer,
    parts,
    mine,
    returned,
    pick_t,
    mixed,
    slopes,
    source_t,
    weights,
    grad_own,
    grad_halo,
):
    block = mine.shape[0]
    grad = mine[...] + add_pieces(returned[...], pick_t[...], block, parts)
    fan = slopes.shape[0] // block
    found = [slopes[k * block : (k + 1) * block, :] for k in range(fan)]
    used = layer_weights(weights, layer)
    own, sent = layer_back(grad, mixed[...], found, source_t, used)
    grad_own[...] = own
    grad_halo[...] = cut_pieces(sent.astype(BF16), parts)


def mesh_back_kernel(parts, mine, returned, pick_t, mesh_pre, weight, out):
    block = mine.shape[0]
    grad = mine[...] + add_pieces(returned[...], pick_t[...], block, parts)
    out[...] = back_dot(grad * slope(mesh_pre[...]), weight[...]).astype(BF16)


def message_back_kernel(nodes, block, fanout, count, who, *refs):
    feats, slopes = refs[:count], refs[count : 2 * count]
    grads, outs = refs[2 * count : -count], refs[-count:]
    rows = slopes[0].shape[0] // fanout
    ids = iota((rows, nodes * block), 1)
    marks = []
    for feat in feats:
        turned = edge_data(feat, rows).T
        for k in range(fanout):
            spot = spot_of(
                lambda t, turned=turned: turned[:, t : t + 1],
                fanout,
                k,
                who[0],
                who[1],
                nodes,
                block,
            )
            marks.append(mark(ids == spot))
    picked = dot(
        jnp.concatenate(marks, axis=0), jnp.concatenate([ref[...] for ref in grads], axis=0)
    )
    for j, out in enumerate(outs):
        total = jnp.zeros((rows, out.shape[1]), F32)
        for k in range(fanout):
            at = (j * fanout + k) * rows
            part = slopes[j][k * rows : (k + 1) * rows, :].astype(F32)
            total = total + picked[at : at + rows] * part
        out[:rows, :] = total.astype(out.dtype)
        if out.shape[0] > rows:
            out[rows:, :] = jnp.zeros((out.shape[0] - rows, out.shape[1]), out.dtype)


def grid_back_kernel(*refs):
    *parts, weight, out = refs
    rows = out.shape[0]
    total = parts[0][:rows, :].astype(F32)
    for ref in parts[1:]:
        total = total + ref[:rows, :].astype(F32)
    out[...] = back_dot(total, weight[...]).astype(BF16)


def call(kernel, outs, args, smem=0, scratch=(), macs=0, scalars=0, space=pltpu.VMEM):
    specs = [pl.BlockSpec(memory_space=pltpu.SMEM)] * smem
    specs += [pl.BlockSpec(memory_space=space)] * (len(args) - smem)
    moved = sum(a.size * a.dtype.itemsize for a in list(args) + list(outs))
    held = sum(math.prod(a.shape) * 4 for a in scratch)
    limit = 2 * (moved + held) + 6 * MIB
    result = pl.pallas_call(
        kernel,
        out_shape=list(outs),
        in_specs=specs,
        out_specs=[pl.BlockSpec(memory_space=pltpu.VMEM)] * len(outs),
        scratch_shapes=list(scratch),
        compiler_params=pltpu.CompilerParams(vmem_limit_bytes=limit),
        cost_estimate=pl.CostEstimate(
            flops=2 * macs, bytes_accessed=moved, transcendentals=scalars
        ),
    )(*args)
    return result


def shape(dims, dtype):
    return jax.ShapeDtypeStruct(dims, dtype)


def swap(value, axis, apart):
    size = lax.axis_size(axis)
    return lax.ppermute(value, axis, [(i, i ^ apart) for i in range(size)])


def body(
    grid_feat,
    edge_len,
    g2m_owner,
    g2m_dst,
    enc_weight,
    enc_vec,
    mesh_init,
    mesh_weight,
    halo_send,
    mesh_src,
    proc_weight,
    cot,
):
    nodes = lax.axis_size("node")
    sects = lax.axis_size("sect")
    width = grid_feat.shape[1]
    grid_rows, fanout = edge_len.shape
    block = mesh_init.shape[1]
    parts = width // LANES
    both = ("sect", "node")
    who = jnp.stack([lax.axis_index("sect"), lax.axis_index("node")]).astype(jnp.int32)

    ends = pltpu.VMEM((fanout, grid_rows), jnp.int32)
    (packed,) = call(
        functools.partial(pack_kernel, block),
        [shape((grid_rows + META_ROWS, width), BF16)],
        [
            pltpu.with_memory_space_constraint(value, pltpu.HBM)
            for value in (grid_feat, edge_len.T, g2m_owner.T, g2m_dst.T)
        ],
        scratch=[
            pltpu.VMEM((fanout, grid_rows), F32),
            ends,
            ends,
            pltpu.SemaphoreType.DMA((4,)),
        ],
        space=pltpu.HBM,
    )
    axes = [1 << i for i in range(sects.bit_length() - 1)]
    feats = [packed] + [swap(packed, "sect", j) for j in range(1, sects)]
    vec = enc_vec[None, :]
    half = nodes // 2

    near = [j for j in range(1, sects) if j.bit_count() < len(axes)]
    far = [j for j in range(1, sects) if j.bit_count() == len(axes)]
    sums_shape = shape((nodes * block, width), F32)

    def encode(js, last, outs, extra):
        used = [feats[j] for j in js]
        edges = len(used) * grid_rows * fanout
        return call(
            functools.partial(
                encode_kernel, len(used), nodes, block, fanout, grid_rows, last
            ),
            outs,
            [who, *used, enc_weight, vec, *extra],
            smem=1,
            scratch=[pltpu.VMEM((edges, width), BF16), pltpu.VMEM((1, edges), jnp.int32)],
            macs=len(used) * grid_rows * width * width + edges * nodes * block * width,
            scalars=edges * width,
        )

    before = encode([0], False, [sums_shape], [])
    sends = halo_send[0, 0].transpose(0, 2, 1)
    src_row = mesh_src[0].T
    fan = src_row.shape[0]
    pieces = halo_send[0, 0].size * parts
    table_len = block + halo_send[0, 0].size
    found = call(
        functools.partial(index_kernel, block, parts),
        [
            shape((pieces, parts * block), BF16),
            shape((parts * block, pieces), BF16),
            shape((fan * block, 2 * table_len), BF16),
            shape((table_len, fan * block), BF16),
        ],
        [sends, src_row],
        scalars=4 * fan * block * table_len,
    )
    *before, pick, pick_t, source, source_t = lax.optimization_barrier((*before, *found))
    if near:
        before = encode(near, False, [sums_shape], before)
    keep, cross = encode(far, True, [shape((half * block, width), BF16)] * 2, before)

    pair = keep.astype(F32) + swap(cross, "node", 1).astype(F32)
    pair = pair.reshape(half, block, width)
    arrived = [swap(pair[q].astype(BF16), "node", 2 * q) for q in range(1, half)]

    slopes = call(
        functools.partial(slope_kernel, sects, fanout, grid_rows),
        [shape((fanout * grid_rows, width), BF16)] * sects,
        [*feats, enc_weight, vec],
        macs=sects * grid_rows * width * width,
        scalars=sects * grid_rows * fanout * width,
    )
    tied = lax.optimization_barrier((*arrived, *slopes))
    arrived, slopes = tied[: half - 1], tied[half - 1 :]

    halo_shape = shape((pieces, LANES), BF16)
    row_low, row_high = shape((block, width), BF16), shape((block, width), F32)

    def exchange(value):
        return lax.all_to_all(value, both, split_axis=0, concat_axis=0, tiled=True)

    state, mesh_pre, halo = call(
        functools.partial(start_kernel, parts),
        [row_low, row_high, halo_shape],
        [pair[0], *arrived, mesh_init[0], mesh_weight, pick],
        macs=block * width * width,
        scalars=block * width,
    )
    layer_macs = 6 * block * width * width + 2 * fan * block * 2 * block * width
    assert proc_weight.shape[0] == 2
    state, mixed, slope_first, halo = call(
        functools.partial(first_kernel, 0, parts),
        [row_low, row_high, shape((fan * block, width), BF16), halo_shape],
        [state, exchange(halo), source, proc_weight, pick],
        macs=layer_macs,
        scalars=fan * block * width,
    )
    mesh_out, grad, halo = call(
        functools.partial(last_kernel, 1, parts),
        [row_low, row_high, halo_shape],
        [state, exchange(halo), source, source_t, proc_weight, cot[0]],
        macs=3 * layer_macs,
        scalars=fan * block * width,
    )
    grad, halo = call(
        functools.partial(back_kernel, 0, parts),
        [row_high, halo_shape],
        [grad, exchange(halo), pick_t, mixed, slope_first, source_t, proc_weight],
        macs=2 * layer_macs,
        scalars=block * width,
    )
    (grad_sum,) = call(
        functools.partial(mesh_back_kernel, parts),
        [row_low],
        [grad, exchange(halo), pick_t, mesh_pre, mesh_weight],
        macs=2 * block * width * width,
        scalars=block * width,
    )

    same = [grad_sum] + [swap(grad_sum, "node", 2 * q) for q in range(1, half)]
    other = [swap(rows, "node", 1) for rows in same]
    parts_of = {}
    ahead = []
    gathered = (*same, *other)
    for group in (far, near, [0]) if near else (far, [0]):
        if ahead:
            gathered = lax.optimization_barrier((*gathered, *ahead))[: len(gathered)]
        found = call(
            functools.partial(message_back_kernel, nodes, block, fanout, len(group)),
            [shape((grid_rows + (META_ROWS if group is far else 0), width), BF16)] * len(group),
            [who, *(feats[j] for j in group), *(slopes[j] for j in group), *gathered],
            smem=1,
            macs=len(group) * fanout * grid_rows * nodes * block * width,
        )
        ahead = found[:1]
        for j, grad_pre in zip(group, found):
            parts_of[j] = swap(grad_pre, "sect", j) if j else grad_pre
    mine, *sent = (parts_of[j] for j in range(sects))
    (grid_grad,) = call(
        grid_back_kernel,
        [shape((grid_rows, width), BF16)],
        [mine, *sent, enc_weight],
        macs=2 * grid_rows * width * width,
    )
    return (mesh_out[None], grid_grad)


def solution(mesh):
    return jax.shard_map(
        body,
        mesh=mesh,
        in_specs=(
            P(("sect", "node"), None),
            P(("sect", "node"), None),
            P(("sect", "node"), None),
            P(("sect", "node"), None),
            P(),
            P(),
            P("node", "sect", None),
            P(),
            P("sect", "node", None, None, None),
            P("node", "sect", None),
            P(),
            P("node", "sect", None),
        ),
        out_specs=(P("node", "sect", None), P(("sect", "node"), None)),
        check_vma=False,
    )
```

```python
import functools
import math

import jax
import jax.numpy as jnp
from jax import lax
from jax.experimental import pallas as pl
from jax.experimental.pallas import tpu as pltpu
from jax.sharding import PartitionSpec as P

F32 = jnp.float32
BF16 = jnp.bfloat16
LANES = 128
META_ROWS = 16
MIB = 1024 * 1024


def sigmoid(value):
    return 0.5 * jnp.tanh(0.5 * value) + 0.5


def silu(value):
    return value * sigmoid(value)


def slope(value):
    sig = sigmoid(value)
    return sig * (1.0 + value * (1.0 - sig))


def dot(left, right):
    return jnp.dot(left, right, preferred_element_type=F32)


def dot_t(left, right):
    return lax.dot_general(left, right, (((1,), (1,)), ((), ())), preferred_element_type=F32)


def halves(value):
    high = value.astype(BF16)
    return high, (value - high.astype(F32)).astype(BF16)


def back_dot(grad, weight):
    rows = grad.shape[0]
    both = dot_t(jnp.concatenate(halves(grad), axis=0), weight)
    return both[:rows] + both[rows:]


def mark(equal):
    return jnp.where(equal, 1.0, 0.0).astype(BF16)


def iota(shape, axis):
    return lax.broadcasted_iota(jnp.int32, shape, axis)


def norm_parts(mixed):
    mean = jnp.mean(mixed, axis=-1, keepdims=True)
    centred = mixed - mean
    scale = lax.rsqrt(jnp.mean(centred * centred, axis=-1, keepdims=True) + 1e-05)
    return centred * scale, scale


def norm_back(grad, normed, scale):
    pull = grad * slope(normed)
    return scale * (
        pull
        - jnp.mean(pull, axis=-1, keepdims=True)
        - normed * jnp.mean(pull * normed, axis=-1, keepdims=True)
    )


def pack_kernel(block, feat, lens, owner, dst, *refs):
    *outs, held, own_held, dst_held, sems = refs
    rows = feat.shape[0] // len(outs)
    pairs = [(lens, held), (owner, own_held), (dst, dst_held)]
    pairs += [
        (feat.at[i * rows : (i + 1) * rows, :], out.at[:rows, :]) for i, out in enumerate(outs)
    ]
    copies = [
        pltpu.make_async_copy(source, target, sems.at[i])
        for i, (source, target) in enumerate(pairs)
    ]
    for copy in copies:
        copy.start()
    for copy in copies[:3]:
        copy.wait()
    high, middle = halves(held[...])
    low = (held[...] - high.astype(F32) - middle.astype(F32)).astype(BF16)
    far = dst_held[...]
    section = far // block
    found = [v.astype(F32) for v in (high, middle, low)]
    found += [v.astype(F32) for v in (own_held[...], section, far - section * block)]
    fill = META_ROWS - 6 * lens.shape[0]
    found.append(jnp.zeros((fill, feat.shape[0]), F32))
    meta = jnp.concatenate(found, axis=0).astype(BF16)
    rest = jnp.zeros((META_ROWS, feat.shape[1] - rows), BF16)
    for i, out in enumerate(outs):
        out[rows:, :] = jnp.concatenate([meta[:, i * rows : (i + 1) * rows], rest], axis=1)
    for copy in copies[3:]:
        copy.wait()


def index_kernel(block, parts, sends, src_row, pick, pick_t, source, source_t):
    sects, count, nodes = sends.shape
    pieces = pick.shape[0]
    at = iota((1, pieces), 1)
    part, row = at % parts, at // parts
    peer = row // count
    whose = mark(iota((nodes, pieces), 0) == peer % nodes)
    place = jnp.zeros((1, pieces), F32)
    for t in range(sects):
        found = dot(sends[t].astype(F32).astype(BF16), whose)
        for c in range(count):
            here = jnp.logical_and(peer // nodes == t, row % count == c)
            place = place + jnp.where(here, found[c : c + 1], 0.0)
    place = place + (part * block).astype(F32)
    pick_t[...] = mark(iota((parts * block, pieces), 0) == place.astype(jnp.int32))
    turned = jnp.broadcast_to(place, (8, pieces)).T[:, :1].astype(jnp.int32)
    pick[...] = mark(iota((pieces, parts * block), 1) == turned)
    table_len = source_t.shape[0]
    column = src_row[...].astype(F32).T.astype(jnp.int32)
    ids = iota((block, 2 * table_len), 1)
    ids = jnp.where(ids >= table_len, ids - table_len, ids)
    ids_t = iota((table_len, block), 0)
    for k in range(src_row.shape[0]):
        rows = slice(k * block, (k + 1) * block)
        source[rows, :] = mark(ids == column[:, k : k + 1])
        source_t[:, rows] = mark(ids_t == src_row[k : k + 1, :])


def edge_data(feat, at, rows):
    return feat[at + rows : at + rows + META_ROWS, :rows].astype(F32)


def edge_length(meta, fanout, k):
    high, middle, low = (meta[:, t * fanout + k : t * fanout + k + 1] for t in range(3))
    return high + middle + low


def spot_of(pick, fanout, k, section, node, nodes, block):
    owner, where, place = (pick((3 + t) * fanout + k).astype(jnp.int32) for t in range(3))
    apart = jnp.bitwise_xor(owner, node)
    order = lax.shift_right_logical(apart, 1) + jnp.bitwise_and(apart, 1) * (nodes // 2)
    return jnp.where(where == section, order * block + place, -1)


def encode_kernel(spans, nodes, block, fanout, rows, last, who, *refs):
    count = len(spans)
    feats = refs[:count]
    weight, vec = refs[count : count + 2]
    *before, message, spots = refs[count + 2 :]
    if last:
        before, (keep, cross) = before[:1], before[1:]
    else:
        before, total = before[:-1], before[-1]
    section, node = who[0], who[1]
    pre = dot(
        jnp.concatenate([feat[at : at + rows, :] for feat, at in zip(feats, spans)], axis=0),
        weight[...],
    )
    for j in range(count):
        meta = edge_data(feats[j], spans[j], rows)
        turned = meta.T
        for k in range(fanout):
            at = (j * fanout + k) * rows
            act = pre[j * rows : (j + 1) * rows] + edge_length(turned, fanout, k) * vec[...]
            message[at : at + rows, :] = silu(act).astype(BF16)
            spots[:, at : at + rows] = spot_of(
                lambda t, meta=meta: meta[t : t + 1], fanout, k, section, node, nodes, block
            )
    half = nodes // 2 * block
    step = min(half, 512)
    for out, base in ((cross, half), (keep, 0)) if last else ((total, 0),):

        def chunk(c, carry, out=out, base=base):
            start = pl.multiple_of(c * step, step)
            ids = iota((step, spots.shape[1]), 0) + (base + start)
            part = dot(mark(ids == spots[...]), message[...])
            for ref in before:
                part = part + ref[pl.ds(base + start, step), :]
            out[pl.ds(start, step), :] = part.astype(out.dtype)
            return carry

        lax.fori_loop(0, out.shape[0] // step, chunk, 0)


def slope_kernel(spans, fanout, rows, *refs):
    count = len(spans)
    feats = refs[:count]
    weight, vec = refs[count : count + 2]
    outs = refs[count + 2 :]
    for feat, at, out in zip(feats, spans, outs):
        pre = dot(feat[at : at + rows, :], weight[...])
        turned = edge_data(feat, at, rows).T
        for k in range(fanout):
            act = pre + edge_length(turned, fanout, k) * vec[...]
            out[k * rows : (k + 1) * rows, :] = slope(act).astype(BF16)


def halo_rows(state, pick, parts):
    stacked = jnp.concatenate(
        [state[:, i * LANES : (i + 1) * LANES] for i in range(parts)], axis=0
    )
    return dot(pick, stacked).astype(BF16)


def join_pieces(pieces, parts):
    count = pieces.shape[0]
    shape = (count // parts, count)
    return jnp.concatenate(
        [
            dot(mark(iota(shape, 1) == iota(shape, 0) * parts + i), pieces).astype(BF16)
            for i in range(parts)
        ],
        axis=1,
    )


def cut_pieces(rows, parts):
    count = rows.shape[0]
    shape = (count * parts, count)
    total = None
    for i in range(parts):
        onehot = mark(iota(shape, 0) == iota(shape, 1) * parts + i)
        piece = dot(onehot, rows[:, i * LANES : (i + 1) * LANES])
        total = piece if total is None else total + piece
    return total.astype(BF16)


def add_pieces(pieces, pick_t, block, parts):
    total = dot(pick_t, pieces)
    return jnp.concatenate([total[i * block : (i + 1) * block] for i in range(parts)], axis=1)


def start_kernel(parts, sums, *refs):
    received, (init, weight, pick, state, mesh_pre, halo) = refs[:-6], refs[-6:]
    agg = sums[...]
    for ref in received:
        agg = agg + ref[...].astype(F32)
    pre = dot(agg.astype(BF16), weight[...])
    mesh_pre[...] = pre
    new = (init[...].astype(F32) + silu(pre)).astype(BF16)
    state[...] = new
    halo[...] = halo_rows(new, pick[...], parts)


def layer_forward(state, pieces, source, weights, parts):
    block = state.shape[0]
    halo = join_pieces(pieces, parts)
    table = jnp.concatenate([state, halo], axis=0)
    from_src = dot(table, weights(0))
    to_dst = dot(state, weights(1))
    gathered = dot(source[...], jnp.concatenate(halves(from_src), axis=0))
    agg = jnp.zeros(state.shape, F32)
    slopes = []
    for k in range(source.shape[0] // block):
        joined = gathered[k * block : (k + 1) * block] + to_dst
        sig = sigmoid(joined)
        act = joined * sig
        agg = agg + act
        slopes.append((sig + act * (1.0 - sig)).astype(BF16))
    mixed = dot(state, weights(2)) + dot(agg.astype(BF16), weights(3))
    return mixed, slopes


def layer_back(grad, mixed, slopes, source_t, weights):
    block = grad.shape[0]
    normed, scale = norm_parts(mixed)
    grad_mixed = norm_back(grad, normed, scale)
    grad_state = grad + back_dot(grad_mixed, weights(2))
    grad_agg = back_dot(grad_mixed, weights(3))
    total = jnp.zeros(grad.shape, F32)
    pieces = []
    for found in slopes:
        piece = grad_agg * found.astype(F32)
        total = total + piece
        pieces.append(piece.astype(BF16))
    grad_src = dot(source_t[...], jnp.concatenate(pieces, axis=0))
    grad_state = grad_state + back_dot(total, weights(1))
    grad_table = back_dot(grad_src, weights(0))
    return grad_state + grad_table[:block], grad_table[block:]


def layer_weights(weights, layer):
    return lambda i: weights[layer, i]


def first_kernel(
    layer, parts, state, pieces, source, weights, pick, new, mixed, slopes, halo
):
    block = state.shape[0]
    own = state[...]
    used = layer_weights(weights, layer)
    value, found = layer_forward(own, pieces[...], source, used, parts)
    mixed[...] = value
    for k, part in enumerate(found):
        slopes[k * block : (k + 1) * block, :] = part
    normed, _ = norm_parts(value)
    result = (own.astype(F32) + silu(normed)).astype(BF16)
    new[...] = result
    halo[...] = halo_rows(result, pick[...], parts)


def last_kernel(
    layer, parts, state, pieces, source, source_t, weights, cot, out, grad_own, grad_halo
):
    own = state[...]
    used = layer_weights(weights, layer)
    value, found = layer_forward(own, pieces[...], source, used, parts)
    normed, _ = norm_parts(value)
    out[...] = (own.astype(F32) + silu(normed)).astype(BF16)
    mine, sent = layer_back(cot[...].astype(F32), value, found, source_t, used)
    grad_own[...] = mine
    grad_halo[...] = cut_pieces(sent.astype(BF16), parts)


def back_kernel(
    layer,
    parts,
    mine,
    returned,
    pick_t,
    mixed,
    slopes,
    source_t,
    weights,
    grad_own,
    grad_halo,
):
    block = mine.shape[0]
    grad = mine[...] + add_pieces(returned[...], pick_t[...], block, parts)
    fan = slopes.shape[0] // block
    found = [slopes[k * block : (k + 1) * block, :] for k in range(fan)]
    used = layer_weights(weights, layer)
    own, sent = layer_back(grad, mixed[...], found, source_t, used)
    grad_own[...] = own
    grad_halo[...] = cut_pieces(sent.astype(BF16), parts)


def mesh_back_kernel(parts, mine, returned, pick_t, mesh_pre, weight, out):
    block = mine.shape[0]
    grad = mine[...] + add_pieces(returned[...], pick_t[...], block, parts)
    out[...] = back_dot(grad * slope(mesh_pre[...]), weight[...]).astype(BF16)


def message_back_kernel(spans, nodes, block, fanout, who, *refs):
    count = len(spans)
    feats, slopes = refs[:count], refs[count : 2 * count]
    rows = slopes[0].shape[0] // fanout
    outs = refs[2 * count :]
    grads, outs = outs[:nodes], outs[nodes:]
    ids = iota((rows, nodes * block), 1)
    marks = []
    for feat, at in zip(feats, spans):
        turned = edge_data(feat, at, rows).T
        for k in range(fanout):
            spot = spot_of(
                lambda t, turned=turned: turned[:, t : t + 1],
                fanout,
                k,
                who[0],
                who[1],
                nodes,
                block,
            )
            marks.append(mark(ids == spot))
    picked = dot(
        jnp.concatenate(marks, axis=0), jnp.concatenate([ref[...] for ref in grads], axis=0)
    )
    per = count // len(outs)
    for i in range(count):
        total = jnp.zeros((rows, outs[0].shape[1]), F32)
        for k in range(fanout):
            at = (i * fanout + k) * rows
            part = slopes[i][k * rows : (k + 1) * rows, :].astype(F32)
            total = total + picked[at : at + rows] * part
        out, at = outs[i // per], i % per * rows
        out[at : at + rows, :] = total.astype(out.dtype)


def grid_back_kernel(*refs):
    *parts, weight, out = refs
    rows = out.shape[0]
    total = parts[0][:rows, :].astype(F32)
    for ref in parts[1:]:
        total = total + ref[:rows, :].astype(F32)
    out[...] = back_dot(total, weight[...]).astype(BF16)


def call(kernel, outs, args, smem=0, scratch=(), macs=0, scalars=0, space=pltpu.VMEM):
    specs = [pl.BlockSpec(memory_space=pltpu.SMEM)] * smem
    specs += [pl.BlockSpec(memory_space=space)] * (len(args) - smem)
    moved = sum(a.size * a.dtype.itemsize for a in list(args) + list(outs))
    held = sum(math.prod(a.shape) * 4 for a in scratch)
    limit = 2 * (moved + held) + 6 * MIB
    result = pl.pallas_call(
        kernel,
        out_shape=list(outs),
        in_specs=specs,
        out_specs=[pl.BlockSpec(memory_space=pltpu.VMEM)] * len(outs),
        scratch_shapes=list(scratch),
        compiler_params=pltpu.CompilerParams(vmem_limit_bytes=limit),
        cost_estimate=pl.CostEstimate(
            flops=2 * macs, bytes_accessed=moved, transcendentals=scalars
        ),
    )(*args)
    return result


def shape(dims, dtype):
    return jax.ShapeDtypeStruct(dims, dtype)


def swap(value, axis, apart):
    size = lax.axis_size(axis)
    return lax.ppermute(value, axis, [(i, i ^ apart) for i in range(size)])


def body(
    grid_feat,
    edge_len,
    g2m_owner,
    g2m_dst,
    enc_weight,
    enc_vec,
    mesh_init,
    mesh_weight,
    halo_send,
    mesh_src,
    proc_weight,
    cot,
):
    nodes = lax.axis_size("node")
    sects = lax.axis_size("sect")
    width = grid_feat.shape[1]
    grid_rows, fanout = edge_len.shape
    block = mesh_init.shape[1]
    parts = width // LANES
    both = ("sect", "node")
    who = jnp.stack([lax.axis_index("sect"), lax.axis_index("node")]).astype(jnp.int32)

    axes = [1 << i for i in range(sects.bit_length() - 1)]
    part_rows = grid_rows // len(axes)
    ends = pltpu.VMEM((fanout, grid_rows), jnp.int32)
    packed = call(
        functools.partial(pack_kernel, block),
        [shape((part_rows + META_ROWS, width), BF16)] * len(axes),
        [
            pltpu.with_memory_space_constraint(value, pltpu.HBM)
            for value in (grid_feat, edge_len.T, g2m_owner.T, g2m_dst.T)
        ],
        scratch=[
            pltpu.VMEM((fanout, grid_rows), F32),
            ends,
            ends,
            pltpu.SemaphoreType.DMA((3 + len(axes),)),
        ],
        space=pltpu.HBM,
    )
    where = {(0, p): (part, 0) for p, part in enumerate(packed)}
    steps = [[(0, p) for p in range(len(axes))]]
    held, names = list(packed), [[0] for _ in axes]
    for step in range(len(axes)):
        given = [
            swap(part, "sect", axes[(p + step) % len(axes)]) for p, part in enumerate(held)
        ]
        steps.append([])
        for p, part in enumerate(given):
            axis = axes[(p + step) % len(axes)]
            for i, j in enumerate(list(names[p])):
                where[j ^ axis, p] = (part, i * packed[0].shape[0])
                names[p].append(j ^ axis)
                steps[-1].append((j ^ axis, p))
        held = [jnp.concatenate(pair, axis=0) for pair in zip(held, given)]
    vec = enc_vec[None, :]
    half = nodes // 2
    sums_shape = shape((nodes * block, width), F32)

    def encode(units, last, outs, extra):
        edges = len(units) * part_rows * fanout
        used = [where[unit] for unit in units]
        return call(
            functools.partial(
                encode_kernel,
                tuple(at for _, at in used),
                nodes,
                block,
                fanout,
                part_rows,
                last,
            ),
            outs,
            [who, *(part for part, _ in used), enc_weight, vec, *extra],
            smem=1,
            scratch=[pltpu.VMEM((edges, width), BF16), pltpu.VMEM((1, edges), jnp.int32)],
        )

    before = []
    for units in steps[:-1]:
        before = encode(units, False, [sums_shape], before)
    sends = halo_send[0, 0].transpose(0, 2, 1)
    src_row = mesh_src[0].T
    fan = src_row.shape[0]
    pieces = halo_send[0, 0].size * parts
    table_len = block + halo_send[0, 0].size
    found = call(
        functools.partial(index_kernel, block, parts),
        [
            shape((pieces, parts * block), BF16),
            shape((parts * block, pieces), BF16),
            shape((fan * block, 2 * table_len), BF16),
            shape((table_len, fan * block), BF16),
        ],
        [sends, src_row],
        scalars=4 * fan * block * table_len,
    )
    *before, pick, pick_t, source, source_t = lax.optimization_barrier((*before, *found))
    keep, cross = encode(
        steps[-1], True, [shape((half * block, width), BF16)] * 2, before
    )

    pair = keep.astype(F32) + swap(cross, "node", 1).astype(F32)
    pair = pair.reshape(half, block, width)
    arrived = [swap(pair[q].astype(BF16), "node", 2 * q) for q in range(1, half)]

    units = [(j, p) for j in range(sects) for p in range(len(axes))]
    slopes = call(
        functools.partial(
            slope_kernel, tuple(where[unit][1] for unit in units), fanout, part_rows
        ),
        [shape((fanout * part_rows, width), BF16)] * len(units),
        [*(where[unit][0] for unit in units), enc_weight, vec],
    )
    tied = lax.optimization_barrier((*arrived, *slopes))
    arrived, slopes = tied[: half - 1], dict(zip(units, tied[half - 1 :]))

    halo_shape = shape((pieces, LANES), BF16)
    row_low, row_high = shape((block, width), BF16), shape((block, width), F32)

    def exchange(value):
        return lax.all_to_all(value, both, split_axis=0, concat_axis=0, tiled=True)

    state, mesh_pre, halo = call(
        functools.partial(start_kernel, parts),
        [row_low, row_high, halo_shape],
        [pair[0], *arrived, mesh_init[0], mesh_weight, pick],
        macs=block * width * width,
        scalars=block * width,
    )
    layer_macs = 6 * block * width * width + 2 * fan * block * 2 * block * width
    assert proc_weight.shape[0] == 2
    state, mixed, slope_first, halo = call(
        functools.partial(first_kernel, 0, parts),
        [row_low, row_high, shape((fan * block, width), BF16), halo_shape],
        [state, exchange(halo), source, proc_weight, pick],
        macs=layer_macs,
        scalars=fan * block * width,
    )
    mesh_out, grad, halo = call(
        functools.partial(last_kernel, 1, parts),
        [row_low, row_high, halo_shape],
        [state, exchange(halo), source, source_t, proc_weight, cot[0]],
        macs=3 * layer_macs,
        scalars=fan * block * width,
    )
    grad, halo = call(
        functools.partial(back_kernel, 0, parts),
        [row_high, halo_shape],
        [grad, exchange(halo), pick_t, mixed, slope_first, source_t, proc_weight],
        macs=2 * layer_macs,
        scalars=block * width,
    )
    (grad_sum,) = call(
        functools.partial(mesh_back_kernel, parts),
        [row_low],
        [grad, exchange(halo), pick_t, mesh_pre, mesh_weight],
        macs=2 * block * width * width,
        scalars=block * width,
    )

    same = [grad_sum] + [swap(grad_sum, "node", 2 * q) for q in range(1, half)]
    other = [swap(rows, "node", 1) for rows in same]
    parts_of = {}
    ahead = []
    gathered = (*same, *other)
    near = [j for j in range(1, sects) if j.bit_count() < len(axes)]
    for group in (near, [sects - 1], [0]):
        if ahead:
            gathered = lax.optimization_barrier((*gathered, *ahead))[: len(gathered)]
        used = [(j, p) for j in group for p in range(len(axes))]
        found = call(
            functools.partial(
                message_back_kernel,
                tuple(where[unit][1] for unit in used),
                nodes,
                block,
                fanout,
            ),
            [shape((grid_rows, width), BF16)] * len(group),
            [
                who,
                *(where[unit][0] for unit in used),
                *(slopes[unit] for unit in used),
                *gathered,
            ],
            smem=1,
        )
        ahead = found[:1]
        for j, grad_pre in zip(group, found):
            parts_of[j] = swap(grad_pre, "sect", j) if j else grad_pre
    mine, *sent = (parts_of[j] for j in range(sects))
    (grid_grad,) = call(
        grid_back_kernel,
        [shape((grid_rows, width), BF16)],
        [mine, *sent, enc_weight],
        macs=2 * grid_rows * width * width,
    )
    return (mesh_out[None], grid_grad)


def solution(mesh):
    return jax.shard_map(
        body,
        mesh=mesh,
        in_specs=(
            P(("sect", "node"), None),
            P(("sect", "node"), None),
            P(("sect", "node"), None),
            P(("sect", "node"), None),
            P(),
            P(),
            P("node", "sect", None),
            P(),
            P("sect", "node", None, None, None),
            P("node", "sect", None),
            P(),
            P("node", "sect", None),
        ),
        out_specs=(P("node", "sect", None), P(("sect", "node"), None)),
        check_vma=False,
    )
```

```python
import functools
import math

import jax
import jax.numpy as jnp
from jax import lax
from jax.experimental import pallas as pl
from jax.experimental.pallas import tpu as pltpu
from jax.sharding import PartitionSpec as P

F32 = jnp.float32
BF16 = jnp.bfloat16
LANES = 128
META_ROWS = 16
MIB = 1024 * 1024


def sigmoid(value):
    return 0.5 * jnp.tanh(0.5 * value) + 0.5


def silu(value):
    return value * sigmoid(value)


def slope(value):
    sig = sigmoid(value)
    return sig * (1.0 + value * (1.0 - sig))


def dot(left, right):
    return jnp.dot(left, right, preferred_element_type=F32)


def dot_t(left, right):
    return lax.dot_general(left, right, (((1,), (1,)), ((), ())), preferred_element_type=F32)


def halves(value):
    high = value.astype(BF16)
    return high, (value - high.astype(F32)).astype(BF16)


def back_dot(grad, weight):
    rows = grad.shape[0]
    both = dot_t(jnp.concatenate(halves(grad), axis=0), weight)
    return both[:rows] + both[rows:]


def mark(equal):
    return jnp.where(equal, 1.0, 0.0).astype(BF16)


def iota(shape, axis):
    return lax.broadcasted_iota(jnp.int32, shape, axis)


def norm_parts(mixed):
    mean = jnp.mean(mixed, axis=-1, keepdims=True)
    centred = mixed - mean
    scale = lax.rsqrt(jnp.mean(centred * centred, axis=-1, keepdims=True) + 1e-05)
    return centred * scale, scale


def norm_back(grad, normed, scale):
    pull = grad * slope(normed)
    return scale * (
        pull
        - jnp.mean(pull, axis=-1, keepdims=True)
        - normed * jnp.mean(pull * normed, axis=-1, keepdims=True)
    )


def pack_kernel(block, feat, lens, owner, dst, *refs):
    *outs, held, own_held, dst_held, sems = refs
    rows = feat.shape[0] // len(outs)
    pairs = [(lens, held), (owner, own_held), (dst, dst_held)]
    pairs += [
        (feat.at[i * rows : (i + 1) * rows, :], out.at[:rows, :]) for i, out in enumerate(outs)
    ]
    copies = [
        pltpu.make_async_copy(source, target, sems.at[i])
        for i, (source, target) in enumerate(pairs)
    ]
    for copy in copies:
        copy.start()
    for copy in copies[:3]:
        copy.wait()
    high, middle = halves(held[...])
    low = (held[...] - high.astype(F32) - middle.astype(F32)).astype(BF16)
    far = dst_held[...]
    section = far // block
    found = [v.astype(F32) for v in (high, middle, low)]
    found += [v.astype(F32) for v in (own_held[...], section, far - section * block)]
    fill = META_ROWS - 6 * lens.shape[0]
    found.append(jnp.zeros((fill, feat.shape[0]), F32))
    meta = jnp.concatenate(found, axis=0).astype(BF16)
    rest = jnp.zeros((META_ROWS, feat.shape[1] - rows), BF16)
    for i, out in enumerate(outs):
        out[rows:, :] = jnp.concatenate([meta[:, i * rows : (i + 1) * rows], rest], axis=1)
    for copy in copies[3:]:
        copy.wait()


def index_kernel(block, parts, sends, src_row, pick, pick_t, source, source_t):
    sects, count, nodes = sends.shape
    pieces = pick.shape[0]
    at = iota((1, pieces), 1)
    part, row = at % parts, at // parts
    peer = row // count
    whose = mark(iota((nodes, pieces), 0) == peer % nodes)
    place = jnp.zeros((1, pieces), F32)
    for t in range(sects):
        found = dot(sends[t].astype(F32).astype(BF16), whose)
        for c in range(count):
            here = jnp.logical_and(peer // nodes == t, row % count == c)
            place = place + jnp.where(here, found[c : c + 1], 0.0)
    place = place + (part * block).astype(F32)
    pick_t[...] = mark(iota((parts * block, pieces), 0) == place.astype(jnp.int32))
    turned = jnp.broadcast_to(place, (8, pieces)).T[:, :1].astype(jnp.int32)
    pick[...] = mark(iota((pieces, parts * block), 1) == turned)
    table_len = source_t.shape[0]
    column = src_row[...].astype(F32).T.astype(jnp.int32)
    ids = iota((block, 2 * table_len), 1)
    ids = jnp.where(ids >= table_len, ids - table_len, ids)
    ids_t = iota((table_len, block), 0)
    for k in range(src_row.shape[0]):
        rows = slice(k * block, (k + 1) * block)
        source[rows, :] = mark(ids == column[:, k : k + 1])
        source_t[:, rows] = mark(ids_t == src_row[k : k + 1, :])


def edge_data(feat, at, rows):
    return feat[at + rows : at + rows + META_ROWS, :rows].astype(F32)


def edge_length(meta, fanout, k):
    high, middle, low = (meta[:, t * fanout + k : t * fanout + k + 1] for t in range(3))
    return high + middle + low


def spot_of(pick, fanout, k, section, node, nodes, block):
    owner, where, place = (pick((3 + t) * fanout + k).astype(jnp.int32) for t in range(3))
    apart = jnp.bitwise_xor(owner, node)
    order = lax.shift_right_logical(apart, 1) + jnp.bitwise_and(apart, 1) * (nodes // 2)
    return jnp.where(where == section, order * block + place, -1)


def add_rows(out, base, message, spots, before):
    step = min(out.shape[0], 512)

    def chunk(c, carry):
        start = pl.multiple_of(c * step, step)
        ids = iota((step, spots.shape[1]), 0) + (base + start)
        part = dot(mark(ids == spots[...]), message[...])
        for ref in before:
            part = part + ref[pl.ds(base + start, step), :]
        out[pl.ds(start, step), :] = part.astype(out.dtype)
        return carry

    lax.fori_loop(0, out.shape[0] // step, chunk, 0)


def encode_kernel(spans, nodes, block, fanout, rows, last, who, *refs):
    count = len(spans)
    feats = refs[:count]
    weight, vec = refs[count : count + 2]
    *before, out, message, spots = refs[count + 2 :]
    section, node = who[0], who[1]
    pre = 0.5 * dot(
        jnp.concatenate([feat[at : at + rows, :] for feat, at in zip(feats, spans)], axis=0),
        weight[...],
    )
    part = 0.5 * vec[...]
    for j in range(count):
        meta = edge_data(feats[j], spans[j], rows)
        turned = meta.T
        for k in range(fanout):
            at = (j * fanout + k) * rows
            act = pre[j * rows : (j + 1) * rows] + edge_length(turned, fanout, k) * part
            message[at : at + rows, :] = (act + act * jnp.tanh(act)).astype(BF16)
            spots[:, at : at + rows] = spot_of(
                lambda t, meta=meta: meta[t : t + 1], fanout, k, section, node, nodes, block
            )
    add_rows(out, nodes // 2 * block if last else 0, message, spots, before)


def keep_kernel(message, spots, before, out):
    add_rows(out, 0, message, spots, [before])


def slope_kernel(spans, fanout, rows, *refs):
    count = len(spans)
    feats = refs[:count]
    weight, vec = refs[count : count + 2]
    outs = refs[count + 2 :]
    for feat, at, out in zip(feats, spans, outs):
        pre = dot(feat[at : at + rows, :], weight[...])
        turned = edge_data(feat, at, rows).T
        for k in range(fanout):
            act = pre + edge_length(turned, fanout, k) * vec[...]
            out[k * rows : (k + 1) * rows, :] = slope(act).astype(BF16)


def halo_rows(state, pick, parts):
    stacked = jnp.concatenate(
        [state[:, i * LANES : (i + 1) * LANES] for i in range(parts)], axis=0
    )
    return dot(pick, stacked).astype(BF16)


def join_pieces(pieces, parts):
    count = pieces.shape[0]
    shape = (count // parts, count)
    return jnp.concatenate(
        [
            dot(mark(iota(shape, 1) == iota(shape, 0) * parts + i), pieces).astype(BF16)
            for i in range(parts)
        ],
        axis=1,
    )


def cut_pieces(rows, parts):
    count = rows.shape[0]
    shape = (count * parts, count)
    total = None
    for i in range(parts):
        onehot = mark(iota(shape, 0) == iota(shape, 1) * parts + i)
        piece = dot(onehot, rows[:, i * LANES : (i + 1) * LANES])
        total = piece if total is None else total + piece
    return total.astype(BF16)


def add_pieces(pieces, pick_t, block, parts):
    total = dot(pick_t, pieces)
    return jnp.concatenate([total[i * block : (i + 1) * block] for i in range(parts)], axis=1)


def start_kernel(parts, sums, *refs):
    received, (init, weight, pick, state, mesh_pre, halo) = refs[:-6], refs[-6:]
    agg = sums[...]
    for ref in received:
        agg = agg + ref[...].astype(F32)
    pre = dot(agg.astype(BF16), weight[...])
    mesh_pre[...] = pre
    new = (init[...].astype(F32) + silu(pre)).astype(BF16)
    state[...] = new
    halo[...] = halo_rows(new, pick[...], parts)


def layer_forward(state, pieces, source, weights, parts):
    block = state.shape[0]
    halo = join_pieces(pieces, parts)
    table = jnp.concatenate([state, halo], axis=0)
    from_src = 0.5 * dot(table, weights(0))
    to_dst = 0.5 * dot(state, weights(1))
    gathered = dot(source[...], jnp.concatenate(halves(from_src), axis=0))
    agg = jnp.zeros(state.shape, F32)
    slopes = []
    for k in range(source.shape[0] // block):
        joined = gathered[k * block : (k + 1) * block] + to_dst
        bend = jnp.tanh(joined)
        agg = agg + (joined + joined * bend)
        slopes.append((1.0 + bend + joined * (1.0 - bend * bend)).astype(BF16))
    mixed = dot(state, weights(2)) + dot(agg.astype(BF16), weights(3))
    return mixed, slopes


def layer_back(grad, mixed, slopes, source_t, weights):
    block = grad.shape[0]
    normed, scale = norm_parts(mixed)
    grad_mixed = norm_back(grad, normed, scale)
    grad_state = grad + back_dot(grad_mixed, weights(2))
    grad_agg = 0.5 * back_dot(grad_mixed, weights(3))
    total = jnp.zeros(grad.shape, F32)
    pieces = []
    for found in slopes:
        piece = grad_agg * found.astype(F32)
        total = total + piece
        pieces.append(piece.astype(BF16))
    grad_src = dot(source_t[...], jnp.concatenate(pieces, axis=0))
    grad_state = grad_state + back_dot(total, weights(1))
    grad_table = back_dot(grad_src, weights(0))
    return grad_state + grad_table[:block], grad_table[block:]


def layer_weights(weights, layer):
    return lambda i: weights[layer, i]


def first_kernel(
    layer, parts, state, pieces, source, weights, pick, new, mixed, slopes, halo
):
    block = state.shape[0]
    own = state[...]
    used = layer_weights(weights, layer)
    value, found = layer_forward(own, pieces[...], source, used, parts)
    mixed[...] = value
    for k, part in enumerate(found):
        slopes[k * block : (k + 1) * block, :] = part
    normed, _ = norm_parts(value)
    result = (own.astype(F32) + silu(normed)).astype(BF16)
    new[...] = result
    halo[...] = halo_rows(result, pick[...], parts)


def last_kernel(
    layer, parts, state, pieces, source, source_t, weights, cot, out, grad_own, grad_halo
):
    own = state[...]
    used = layer_weights(weights, layer)
    value, found = layer_forward(own, pieces[...], source, used, parts)
    normed, _ = norm_parts(value)
    out[...] = (own.astype(F32) + silu(normed)).astype(BF16)
    mine, sent = layer_back(cot[...].astype(F32), value, found, source_t, used)
    grad_own[...] = mine
    grad_halo[...] = cut_pieces(sent.astype(BF16), parts)


def back_kernel(
    layer,
    parts,
    mine,
    returned,
    pick_t,
    mixed,
    slopes,
    source_t,
    weights,
    grad_own,
    grad_halo,
):
    block = mine.shape[0]
    grad = mine[...] + add_pieces(returned[...], pick_t[...], block, parts)
    fan = slopes.shape[0] // block
    found = [slopes[k * block : (k + 1) * block, :] for k in range(fan)]
    used = layer_weights(weights, layer)
    own, sent = layer_back(grad, mixed[...], found, source_t, used)
    grad_own[...] = own
    grad_halo[...] = cut_pieces(sent.astype(BF16), parts)


def mesh_back_kernel(parts, mine, returned, pick_t, mesh_pre, weight, out):
    block = mine.shape[0]
    grad = mine[...] + add_pieces(returned[...], pick_t[...], block, parts)
    out[...] = back_dot(grad * slope(mesh_pre[...]), weight[...]).astype(BF16)


def edge_marks(feat, at, rows, nodes, block, fanout, who):
    turned = edge_data(feat, at, rows).T
    ids = iota((rows, nodes * block), 1)
    return [
        mark(
            ids
            == spot_of(
                lambda t: turned[:, t : t + 1], fanout, k, who[0], who[1], nodes, block
            )
        )
        for k in range(fanout)
    ]


def mark_kernel(spans, rows, nodes, block, fanout, who, *refs):
    feats, outs = refs[: len(spans)], refs[len(spans) :]
    for feat, at, out in zip(feats, spans, outs):
        for k, found in enumerate(edge_marks(feat, at, rows, nodes, block, fanout, who)):
            out[k * rows : (k + 1) * rows, :] = found


def message_back_kernel(spans, rows, ready, nodes, block, fanout, who, *refs):
    count = len(spans)
    feats, slopes = refs[:count], refs[count : 2 * count]
    outs = refs[2 * count :]
    grads, outs = outs[:nodes], outs[nodes:]
    marks = []
    for feat, at in zip(feats, spans):
        if ready:
            marks.append(feat[...])
        else:
            marks += edge_marks(feat, at, rows, nodes, block, fanout, who)
    picked = dot(
        jnp.concatenate(marks, axis=0), jnp.concatenate([ref[...] for ref in grads], axis=0)
    )
    per = count // len(outs)
    for i in range(count):
        total = jnp.zeros((rows, outs[0].shape[1]), F32)
        for k in range(fanout):
            at = (i * fanout + k) * rows
            part = slopes[i][k * rows : (k + 1) * rows, :].astype(F32)
            total = total + picked[at : at + rows] * part
        out, at = outs[i // per], i % per * rows
        out[at : at + rows, :] = total.astype(out.dtype)
    for out in outs:
        spare = out.shape[0] - per * rows
        if spare:
            out[per * rows :, :] = jnp.zeros((spare, out.shape[1]), out.dtype)


def grid_back_kernel(*refs):
    *parts, weight, out = refs
    rows = out.shape[0]
    total = parts[0][:rows, :].astype(F32)
    for ref in parts[1:]:
        total = total + ref[:rows, :].astype(F32)
    out[...] = back_dot(total, weight[...]).astype(BF16)


def call(kernel, outs, args, smem=0, scratch=(), space=pltpu.VMEM, aliases=None):
    specs = [pl.BlockSpec(memory_space=pltpu.SMEM)] * smem
    specs += [pl.BlockSpec(memory_space=space)] * (len(args) - smem)
    moved = sum(a.size * a.dtype.itemsize for a in list(args) + list(outs))
    held = sum(math.prod(a.shape) * 4 for a in scratch)
    limit = 2 * (moved + held) + 6 * MIB
    result = pl.pallas_call(
        kernel,
        out_shape=list(outs),
        in_specs=specs,
        out_specs=[pl.BlockSpec(memory_space=pltpu.VMEM)] * len(outs),
        scratch_shapes=list(scratch),
        input_output_aliases=aliases or {},
        compiler_params=pltpu.CompilerParams(vmem_limit_bytes=limit),
        cost_estimate=pl.CostEstimate(
            flops=0, bytes_accessed=moved, transcendentals=0
        ),
    )(*args)
    return result


def shape(dims, dtype):
    return jax.ShapeDtypeStruct(dims, dtype)


def swap(value, axis, apart):
    size = lax.axis_size(axis)
    return lax.ppermute(value, axis, [(i, i ^ apart) for i in range(size)])


def body(
    grid_feat,
    edge_len,
    g2m_owner,
    g2m_dst,
    enc_weight,
    enc_vec,
    mesh_init,
    mesh_weight,
    halo_send,
    mesh_src,
    proc_weight,
    cot,
):
    nodes = lax.axis_size("node")
    sects = lax.axis_size("sect")
    width = grid_feat.shape[1]
    grid_rows, fanout = edge_len.shape
    block = mesh_init.shape[1]
    parts = width // LANES
    both = ("sect", "node")
    who = jnp.stack([lax.axis_index("sect"), lax.axis_index("node")]).astype(jnp.int32)

    axes = [1 << i for i in range(sects.bit_length() - 1)]
    part_rows = grid_rows // len(axes)
    ends = pltpu.VMEM((fanout, grid_rows), jnp.int32)
    packed = call(
        functools.partial(pack_kernel, block),
        [shape((part_rows + META_ROWS, width), BF16)] * len(axes),
        [
            pltpu.with_memory_space_constraint(value, pltpu.HBM)
            for value in (grid_feat, edge_len.T, g2m_owner.T, g2m_dst.T)
        ],
        scratch=[
            pltpu.VMEM((fanout, grid_rows), F32),
            ends,
            ends,
            pltpu.SemaphoreType.DMA((3 + len(axes),)),
        ],
        space=pltpu.HBM,
    )
    where = {(0, p): (part, 0) for p, part in enumerate(packed)}
    steps = [[(0, p) for p in range(len(axes))]]
    held, names = list(packed), [[0] for _ in axes]
    for step in range(len(axes)):
        given = [
            swap(part, "sect", axes[(p + step) % len(axes)]) for p, part in enumerate(held)
        ]
        steps.append([])
        for p, part in enumerate(given):
            axis = axes[(p + step) % len(axes)]
            for i, j in enumerate(list(names[p])):
                where[j ^ axis, p] = (part, i * packed[0].shape[0])
                names[p].append(j ^ axis)
                steps[-1].append((j ^ axis, p))
        held = [jnp.concatenate(pair, axis=0) for pair in zip(held, given)]
    vec = enc_vec[None, :]
    half = nodes // 2
    sums_shape = shape((nodes * block, width), F32)

    def encode(units, last, before):
        edges = len(units) * part_rows * fanout
        used = [where[unit] for unit in units]
        args = [who, *(part for part, _ in used), enc_weight, vec, *before]
        outs = [
            shape((half * block, width), BF16) if last else sums_shape,
            shape((edges, width), BF16),
            shape((1, edges), jnp.int32),
        ]
        return call(
            functools.partial(
                encode_kernel,
                tuple(at for _, at in used),
                nodes,
                block,
                fanout,
                part_rows,
                last,
            ),
            outs if last else outs[:1],
            args,
            smem=1,
            scratch=() if last else [pltpu.VMEM(s.shape, s.dtype) for s in outs[1:]],
            aliases={len(args) - 1: 0} if before and not last else None,
        )

    before = []
    for units in steps[:-1]:
        before = encode(units, False, before)
    sends = halo_send[0, 0].transpose(0, 2, 1)
    src_row = mesh_src[0].T
    fan = src_row.shape[0]
    pieces = halo_send[0, 0].size * parts
    table_len = block + halo_send[0, 0].size
    found = call(
        functools.partial(index_kernel, block, parts),
        [
            shape((pieces, parts * block), BF16),
            shape((parts * block, pieces), BF16),
            shape((fan * block, 2 * table_len), BF16),
            shape((table_len, fan * block), BF16),
        ],
        [sends, src_row],
    )
    *before, pick, pick_t, source, source_t = lax.optimization_barrier((*before, *found))
    cross, message, spots = encode(steps[-1], True, before)
    (keep,) = call(
        keep_kernel, [shape((half * block, width), BF16)], [message, spots, *before]
    )

    pair = keep.astype(F32) + swap(cross, "node", 1).astype(F32)
    pair = pair.reshape(half, block, width)
    arrived = [swap(pair[q].astype(BF16), "node", 2 * q) for q in range(1, half)]

    units = [(j, p) for j in range(sects) for p in range(len(axes))]
    slopes = call(
        functools.partial(
            slope_kernel, tuple(where[unit][1] for unit in units), fanout, part_rows
        ),
        [shape((fanout * part_rows, width), BF16)] * len(units),
        [*(where[unit][0] for unit in units), enc_weight, vec],
    )
    tied = lax.optimization_barrier((*arrived, *slopes))
    arrived, slopes = tied[: half - 1], dict(zip(units, tied[half - 1 :]))

    halo_shape = shape((pieces, LANES), BF16)
    row_low, row_high = shape((block, width), BF16), shape((block, width), F32)

    def exchange(value):
        return lax.all_to_all(value, both, split_axis=0, concat_axis=0, tiled=True)

    state, mesh_pre, halo = call(
        functools.partial(start_kernel, parts),
        [row_low, row_high, halo_shape],
        [pair[0], *arrived, mesh_init[0], mesh_weight, pick],
    )
    assert proc_weight.shape[0] == 2
    state, mixed, slope_first, halo = call(
        functools.partial(first_kernel, 0, parts),
        [row_low, row_high, shape((fan * block, width), BF16), halo_shape],
        [state, exchange(halo), source, proc_weight, pick],
    )
    mesh_out, grad, halo = call(
        functools.partial(last_kernel, 1, parts),
        [row_low, row_high, halo_shape],
        [state, exchange(halo), source, source_t, proc_weight, cot[0]],
    )
    grad, halo = call(
        functools.partial(back_kernel, 0, parts),
        [row_high, halo_shape],
        [grad, exchange(halo), pick_t, mixed, slope_first, source_t, proc_weight],
    )
    (grad_sum,) = call(
        functools.partial(mesh_back_kernel, parts),
        [row_low],
        [grad, exchange(halo), pick_t, mesh_pre, mesh_weight],
    )

    same = [grad_sum] + [swap(grad_sum, "node", 2 * q) for q in range(1, half)]
    ready = nodes * block <= 8 * LANES
    picks_of = {unit: where[unit] for unit in units}
    if ready:
        seen, _ = lax.optimization_barrier((who, grad_sum))
        found = call(
            functools.partial(
                mark_kernel,
                tuple(where[unit][1] for unit in units),
                part_rows,
                nodes,
                block,
                fanout,
            ),
            [shape((fanout * part_rows, nodes * block), BF16)] * len(units),
            [seen, *(where[unit][0] for unit in units)],
            smem=1,
        )
        same[1] = lax.optimization_barrier((same[1], found[0]))[0]
        picks_of = {unit: (part, 0) for unit, part in zip(units, found)}
    other = [swap(rows, "node", 1) for rows in same]
    parts_of = {}
    ahead = []
    gathered = (*same, *other)
    near = [j for j in range(1, sects) if j.bit_count() < len(axes)]
    for group in (near, [sects - 1], [0]):
        if ahead:
            gathered = lax.optimization_barrier((*gathered, *ahead))[: len(gathered)]
        used = [(j, p) for j in group for p in range(len(axes))]
        spare = META_ROWS if group is near else 0
        found = call(
            functools.partial(
                message_back_kernel,
                tuple(picks_of[unit][1] for unit in used),
                part_rows,
                ready,
                nodes,
                block,
                fanout,
            ),
            [shape((grid_rows + spare, width), BF16)] * len(group),
            [
                who,
                *(picks_of[unit][0] for unit in used),
                *(slopes[unit] for unit in used),
                *gathered,
            ],
            smem=1,
        )
        ahead = found[:1]
        for j, grad_pre in zip(group, found):
            parts_of[j] = swap(grad_pre, "sect", j) if j else grad_pre
    mine, *sent = (parts_of[j] for j in range(sects))
    (grid_grad,) = call(
        grid_back_kernel,
        [shape((grid_rows, width), BF16)],
        [mine, *sent, enc_weight],
    )
    return (mesh_out[None], grid_grad)


def solution(mesh):
    return jax.shard_map(
        body,
        mesh=mesh,
        in_specs=(
            P(("sect", "node"), None),
            P(("sect", "node"), None),
            P(("sect", "node"), None),
            P(("sect", "node"), None),
            P(),
            P(),
            P("node", "sect", None),
            P(),
            P("sect", "node", None, None, None),
            P("node", "sect", None),
            P(),
            P("node", "sect", None),
        ),
        out_specs=(P("node", "sect", None), P(("sect", "node"), None)),
        check_vma=False,
    )
```

```python
import functools
import math

import jax
import jax.numpy as jnp
from jax import lax
from jax.experimental import pallas as pl
from jax.experimental.pallas import tpu as pltpu
from jax.sharding import PartitionSpec as P

F32 = jnp.float32
BF16 = jnp.bfloat16
LANES = 128
META_ROWS = 16
MIB = 1024 * 1024


def sigmoid(value):
    return 0.5 * jnp.tanh(0.5 * value) + 0.5


def silu(value):
    return value * sigmoid(value)


def slope(value):
    sig = sigmoid(value)
    return sig * (1.0 + value * (1.0 - sig))


def dot(left, right):
    return jnp.dot(left, right, preferred_element_type=F32)


def dot_t(left, right):
    return lax.dot_general(left, right, (((1,), (1,)), ((), ())), preferred_element_type=F32)


def halves(value):
    high = value.astype(BF16)
    return high, (value - high.astype(F32)).astype(BF16)


def back_dot(grad, weight):
    rows = grad.shape[0]
    both = dot_t(jnp.concatenate(halves(grad), axis=0), weight)
    return both[:rows] + both[rows:]


def mark(equal):
    return jnp.where(equal, 1.0, 0.0).astype(BF16)


def iota(shape, axis):
    return lax.broadcasted_iota(jnp.int32, shape, axis)


def norm_parts(mixed):
    mean = jnp.mean(mixed, axis=-1, keepdims=True)
    centred = mixed - mean
    scale = lax.rsqrt(jnp.mean(centred * centred, axis=-1, keepdims=True) + 1e-05)
    return centred * scale, scale


def norm_back(grad, normed, scale):
    pull = grad * slope(normed)
    return scale * (
        pull
        - jnp.mean(pull, axis=-1, keepdims=True)
        - normed * jnp.mean(pull * normed, axis=-1, keepdims=True)
    )


def pack_kernel(block, feat, lens, owner, dst, *refs):
    *outs, held, own_held, dst_held, sems = refs
    rows = feat.shape[0] // len(outs)
    pairs = [(lens, held), (owner, own_held), (dst, dst_held)]
    pairs += [
        (feat.at[i * rows : (i + 1) * rows, :], out.at[:rows, :]) for i, out in enumerate(outs)
    ]
    copies = [
        pltpu.make_async_copy(source, target, sems.at[i])
        for i, (source, target) in enumerate(pairs)
    ]
    for copy in copies:
        copy.start()
    for copy in copies[:3]:
        copy.wait()
    high, middle = halves(held[...])
    low = (held[...] - high.astype(F32) - middle.astype(F32)).astype(BF16)
    far = dst_held[...]
    section = far // block
    found = [v.astype(F32) for v in (high, middle, low)]
    found += [v.astype(F32) for v in (own_held[...], section, far - section * block)]
    fill = META_ROWS - 6 * lens.shape[0]
    found.append(jnp.zeros((fill, feat.shape[0]), F32))
    meta = jnp.concatenate(found, axis=0).astype(BF16)
    rest = jnp.zeros((META_ROWS, feat.shape[1] - rows), BF16)
    for i, out in enumerate(outs):
        out[rows:, :] = jnp.concatenate([meta[:, i * rows : (i + 1) * rows], rest], axis=1)
    for copy in copies[3:]:
        copy.wait()


def index_kernel(block, parts, *refs):
    wanted, far_weight, far_vec = refs[:2], refs[2], refs[3]
    pick, pick_t, source, source_t, weight, vec, sends, src_row, sems = refs[4:]
    pairs = ((wanted[0], sends), (wanted[1], src_row), (far_vec, vec), (far_weight, weight))
    copies = [
        pltpu.make_async_copy(start, target, sems.at[i])
        for i, (start, target) in enumerate(pairs)
    ]
    for copy in copies:
        copy.start()
    for copy in copies[:2]:
        copy.wait()
    sects, count, nodes = sends.shape
    pieces = pick.shape[0]
    at = iota((1, pieces), 1)
    part, row = at % parts, at // parts
    peer = row // count
    whose = mark(iota((nodes, pieces), 0) == peer % nodes)
    place = jnp.zeros((1, pieces), F32)
    for t in range(sects):
        found = dot(sends[t].astype(F32).astype(BF16), whose)
        for c in range(count):
            here = jnp.logical_and(peer // nodes == t, row % count == c)
            place = place + jnp.where(here, found[c : c + 1], 0.0)
    place = place + (part * block).astype(F32)
    pick_t[...] = mark(iota((parts * block, pieces), 0) == place.astype(jnp.int32))
    turned = jnp.broadcast_to(place, (8, pieces)).T[:, :1].astype(jnp.int32)
    pick[...] = mark(iota((pieces, parts * block), 1) == turned)
    table_len = source_t.shape[0]
    column = src_row[...].astype(F32).T.astype(jnp.int32)
    ids = iota((block, table_len), 1)
    ids_t = iota((table_len, block), 0)
    for k in range(src_row.shape[0]):
        rows = slice(k * block, (k + 1) * block)
        source[rows, :] = mark(ids == column[:, k : k + 1])
        source_t[:, rows] = mark(ids_t == src_row[k : k + 1, :])
    for copy in copies[2:]:
        copy.wait()


def edge_data(feat, at, rows):
    return feat[at + rows : at + rows + META_ROWS, :rows].astype(F32)


def edge_length(meta, fanout, k):
    high, middle, low = (meta[:, t * fanout + k : t * fanout + k + 1] for t in range(3))
    return high + middle + low


def spot_of(pick, fanout, k, section, node, nodes, block):
    owner, where, place = (pick((3 + t) * fanout + k).astype(jnp.int32) for t in range(3))
    apart = jnp.bitwise_xor(owner, node)
    order = lax.shift_right_logical(apart, 1) + jnp.bitwise_and(apart, 1) * (nodes // 2)
    return jnp.where(where == section, order * block + place, -1)


def add_rows(out, base, message, spots, before):
    step = min(out.shape[0], 512)

    def chunk(c, carry):
        start = pl.multiple_of(c * step, step)
        ids = iota((step, spots.shape[1]), 0) + (base + start)
        part = dot(mark(ids == spots[...]), message[...])
        for ref in before:
            part = part + ref[pl.ds(base + start, step), :]
        out[pl.ds(start, step), :] = part.astype(out.dtype)
        return carry

    lax.fori_loop(0, out.shape[0] // step, chunk, 0)


def encode_kernel(spans, nodes, block, fanout, rows, last, who, *refs):
    count = len(spans)
    feats = refs[:count]
    weight, vec = refs[count : count + 2]
    *before, out, message, spots = refs[count + 2 :]
    section, node = who[0], who[1]
    pre = 0.5 * dot(
        jnp.concatenate([feat[at : at + rows, :] for feat, at in zip(feats, spans)], axis=0),
        weight[...],
    )
    part = 0.5 * vec[...]
    for j in range(count):
        meta = edge_data(feats[j], spans[j], rows)
        turned = meta.T
        for k in range(fanout):
            at = (j * fanout + k) * rows
            act = pre[j * rows : (j + 1) * rows] + edge_length(turned, fanout, k) * part
            message[at : at + rows, :] = (act + act * jnp.tanh(act)).astype(BF16)
            spots[:, at : at + rows] = spot_of(
                lambda t, meta=meta: meta[t : t + 1], fanout, k, section, node, nodes, block
            )
    add_rows(out, nodes // 2 * block if last else 0, message, spots, before)


def keep_kernel(message, spots, before, out):
    add_rows(out, 0, message, spots, [before])


def slope_kernel(spans, fanout, rows, *refs):
    count = len(spans)
    feats = refs[:count]
    weight, vec = refs[count : count + 2]
    outs = refs[count + 2 :]
    for feat, at, out in zip(feats, spans, outs):
        pre = dot(feat[at : at + rows, :], weight[...])
        turned = edge_data(feat, at, rows).T
        for k in range(fanout):
            act = pre + edge_length(turned, fanout, k) * vec[...]
            out[k * rows : (k + 1) * rows, :] = slope(act).astype(BF16)


def halo_rows(state, pick, parts):
    stacked = jnp.concatenate(
        [state[:, i * LANES : (i + 1) * LANES] for i in range(parts)], axis=0
    )
    return dot(pick, stacked).astype(BF16)


def join_pieces(pieces, parts):
    count = pieces.shape[0]
    shape = (count // parts, count)
    return jnp.concatenate(
        [
            dot(mark(iota(shape, 1) == iota(shape, 0) * parts + i), pieces).astype(BF16)
            for i in range(parts)
        ],
        axis=1,
    )


def cut_pieces(rows, parts):
    count = rows.shape[0]
    shape = (count * parts, count)
    total = None
    for i in range(parts):
        onehot = mark(iota(shape, 0) == iota(shape, 1) * parts + i)
        piece = dot(onehot, rows[:, i * LANES : (i + 1) * LANES])
        total = piece if total is None else total + piece
    return total.astype(BF16)


def add_pieces(pieces, pick_t, block, parts):
    total = dot(pick_t, pieces)
    return jnp.concatenate([total[i * block : (i + 1) * block] for i in range(parts)], axis=1)


def start_kernel(parts, sums, *refs):
    received, (init, weight, pick, state, mesh_pre, halo) = refs[:-6], refs[-6:]
    agg = sums[...]
    for ref in received:
        agg = agg + ref[...].astype(F32)
    pre = dot(agg.astype(BF16), weight[...])
    mesh_pre[...] = pre
    new = (init[...].astype(F32) + silu(pre)).astype(BF16)
    state[...] = new
    halo[...] = halo_rows(new, pick[...], parts)


def layer_forward(state, pieces, source, weights, parts):
    block = state.shape[0]
    halo = join_pieces(pieces, parts)
    table = jnp.concatenate([state, halo], axis=0)
    from_src = 0.5 * dot(table, weights(0))
    to_dst = 0.5 * dot(state, weights(1))
    gathered = dot(source[...], from_src.astype(BF16))
    agg = jnp.zeros(state.shape, F32)
    slopes = []
    for k in range(source.shape[0] // block):
        joined = gathered[k * block : (k + 1) * block] + to_dst
        bend = jnp.tanh(joined)
        agg = agg + (joined + joined * bend)
        slopes.append((1.0 + bend + joined * (1.0 - bend * bend)).astype(BF16))
    mixed = dot(state, weights(2)) + dot(agg.astype(BF16), weights(3))
    return mixed, slopes


def layer_back(grad, mixed, slopes, source_t, weights):
    block = grad.shape[0]
    normed, scale = norm_parts(mixed)
    grad_mixed = norm_back(grad, normed, scale)
    grad_state = grad + back_dot(grad_mixed, weights(2))
    grad_agg = 0.5 * back_dot(grad_mixed, weights(3))
    total = jnp.zeros(grad.shape, F32)
    pieces = []
    for found in slopes:
        piece = grad_agg * found.astype(F32)
        total = total + piece
        pieces.append(piece.astype(BF16))
    grad_src = dot(source_t[...], jnp.concatenate(pieces, axis=0))
    grad_state = grad_state + back_dot(total, weights(1))
    grad_table = back_dot(grad_src, weights(0))
    return grad_state + grad_table[:block], grad_table[block:]


def layer_weights(weights, layer):
    return lambda i: weights[layer, i]


def first_kernel(
    layer, parts, state, pieces, source, weights, pick, new, mixed, slopes, halo
):
    block = state.shape[0]
    own = state[...]
    used = layer_weights(weights, layer)
    value, found = layer_forward(own, pieces[...], source, used, parts)
    mixed[...] = value
    for k, part in enumerate(found):
        slopes[k * block : (k + 1) * block, :] = part
    normed, _ = norm_parts(value)
    result = (own.astype(F32) + silu(normed)).astype(BF16)
    new[...] = result
    halo[...] = halo_rows(result, pick[...], parts)


def last_kernel(
    layer, parts, state, pieces, source, source_t, weights, cot, out, grad_own, grad_halo
):
    own = state[...]
    used = layer_weights(weights, layer)
    value, found = layer_forward(own, pieces[...], source, used, parts)
    normed, _ = norm_parts(value)
    out[...] = (own.astype(F32) + silu(normed)).astype(BF16)
    mine, sent = layer_back(cot[...].astype(F32), value, found, source_t, used)
    grad_own[...] = mine
    grad_halo[...] = cut_pieces(sent.astype(BF16), parts)


def back_kernel(
    layer,
    parts,
    mine,
    returned,
    pick_t,
    mixed,
    slopes,
    source_t,
    weights,
    grad_own,
    grad_halo,
):
    block = mine.shape[0]
    grad = mine[...] + add_pieces(returned[...], pick_t[...], block, parts)
    fan = slopes.shape[0] // block
    found = [slopes[k * block : (k + 1) * block, :] for k in range(fan)]
    used = layer_weights(weights, layer)
    own, sent = layer_back(grad, mixed[...], found, source_t, used)
    grad_own[...] = own
    grad_halo[...] = cut_pieces(sent.astype(BF16), parts)


def mesh_back_kernel(parts, mine, returned, pick_t, mesh_pre, weight, out):
    block = mine.shape[0]
    grad = mine[...] + add_pieces(returned[...], pick_t[...], block, parts)
    out[...] = back_dot(grad * slope(mesh_pre[...]), weight[...]).astype(BF16)


def edge_marks(feat, at, rows, nodes, block, fanout, who):
    turned = edge_data(feat, at, rows).T
    ids = iota((rows, nodes * block), 1)
    return [
        mark(
            ids
            == spot_of(
                lambda t: turned[:, t : t + 1], fanout, k, who[0], who[1], nodes, block
            )
        )
        for k in range(fanout)
    ]


def mark_kernel(spans, rows, nodes, block, fanout, who, *refs):
    feats, outs = refs[: len(spans)], refs[len(spans) :]
    for feat, at, out in zip(feats, spans, outs):
        for k, found in enumerate(edge_marks(feat, at, rows, nodes, block, fanout, who)):
            out[k * rows : (k + 1) * rows, :] = found


def message_back_kernel(spans, rows, ready, nodes, block, fanout, who, *refs):
    count = len(spans)
    feats, slopes = refs[:count], refs[count : 2 * count]
    outs = refs[2 * count :]
    grads, outs = outs[:nodes], outs[nodes:]
    marks = []
    for feat, at in zip(feats, spans):
        if ready:
            marks.append(feat[...])
        else:
            marks += edge_marks(feat, at, rows, nodes, block, fanout, who)
    picked = dot(
        jnp.concatenate(marks, axis=0), jnp.concatenate([ref[...] for ref in grads], axis=0)
    )
    per = count // len(outs)
    for i in range(count):
        total = jnp.zeros((rows, outs[0].shape[1]), F32)
        for k in range(fanout):
            at = (i * fanout + k) * rows
            part = slopes[i][k * rows : (k + 1) * rows, :].astype(F32)
            total = total + picked[at : at + rows] * part
        out, at = outs[i // per], i % per * rows
        out[at : at + rows, :] = total.astype(out.dtype)


def grid_back_kernel(*refs):
    *parts, weight, out = refs
    count = len(parts) // 2
    total = [
        mine[...] + given[...].astype(F32) for mine, given in zip(parts[:count], parts[count:])
    ]
    out[...] = back_dot(jnp.concatenate(total, axis=0), weight[...]).astype(BF16)


def call(kernel, outs, args, smem=0, scratch=(), space=pltpu.VMEM, aliases=None):
    specs = [pl.BlockSpec(memory_space=pltpu.SMEM)] * smem
    specs += [pl.BlockSpec(memory_space=space)] * (len(args) - smem)
    moved = sum(a.size * a.dtype.itemsize for a in list(args) + list(outs))
    held = sum(math.prod(a.shape) * 4 for a in scratch)
    limit = 2 * (moved + held) + 6 * MIB
    result = pl.pallas_call(
        kernel,
        out_shape=list(outs),
        in_specs=specs,
        out_specs=[pl.BlockSpec(memory_space=pltpu.VMEM)] * len(outs),
        scratch_shapes=list(scratch),
        input_output_aliases=aliases or {},
        compiler_params=pltpu.CompilerParams(vmem_limit_bytes=limit),
        cost_estimate=pl.CostEstimate(
            flops=0, bytes_accessed=moved, transcendentals=0
        ),
    )(*args)
    return result


def shape(dims, dtype):
    return jax.ShapeDtypeStruct(dims, dtype)


def swap(value, axis, apart):
    size = lax.axis_size(axis)
    return lax.ppermute(value, axis, [(i, i ^ apart) for i in range(size)])


def body(
    grid_feat,
    edge_len,
    g2m_owner,
    g2m_dst,
    enc_weight,
    enc_vec,
    mesh_init,
    mesh_weight,
    halo_send,
    mesh_src,
    proc_weight,
    cot,
):
    nodes = lax.axis_size("node")
    sects = lax.axis_size("sect")
    width = grid_feat.shape[1]
    grid_rows, fanout = edge_len.shape
    block = mesh_init.shape[1]
    parts = width // LANES
    both = ("sect", "node")
    who = jnp.stack([lax.axis_index("sect"), lax.axis_index("node")]).astype(jnp.int32)

    axes = [1 << i for i in range(sects.bit_length() - 1)]
    part_rows = grid_rows // len(axes)
    ends = pltpu.VMEM((fanout, grid_rows), jnp.int32)
    packed = call(
        functools.partial(pack_kernel, block),
        [shape((part_rows + META_ROWS, width), BF16)] * len(axes),
        [
            pltpu.with_memory_space_constraint(value, pltpu.HBM)
            for value in (grid_feat, edge_len.T, g2m_owner.T, g2m_dst.T)
        ],
        scratch=[
            pltpu.VMEM((fanout, grid_rows), F32),
            ends,
            ends,
            pltpu.SemaphoreType.DMA((3 + len(axes),)),
        ],
        space=pltpu.HBM,
    )
    where = {(0, p): (part, 0) for p, part in enumerate(packed)}
    steps = [[(0, p) for p in range(len(axes))]]
    held, names = list(packed), [[0] for _ in axes]
    for step in range(len(axes)):
        given = [
            swap(part, "sect", axes[(p + step) % len(axes)]) for p, part in enumerate(held)
        ]
        steps.append([])
        for p, part in enumerate(given):
            axis = axes[(p + step) % len(axes)]
            for i, j in enumerate(list(names[p])):
                where[j ^ axis, p] = (part, i * packed[0].shape[0])
                names[p].append(j ^ axis)
                steps[-1].append((j ^ axis, p))
        held = [jnp.concatenate(pair, axis=0) for pair in zip(held, given)]
    sends = halo_send[0, 0].transpose(0, 2, 1)
    src_row = mesh_src[0].T
    fan = src_row.shape[0]
    pieces = sends.size * parts
    table_len = block + sends.size
    pick, pick_t, source, source_t, weight, vec = call(
        functools.partial(index_kernel, block, parts),
        [
            shape((pieces, parts * block), BF16),
            shape((parts * block, pieces), BF16),
            shape((fan * block, table_len), BF16),
            shape((table_len, fan * block), BF16),
            shape(enc_weight.shape, BF16),
            shape((1, width), F32),
        ],
        [
            pltpu.with_memory_space_constraint(value, pltpu.HBM)
            for value in (sends, src_row, enc_weight, enc_vec[None, :])
        ],
        scratch=[
            pltpu.VMEM(sends.shape, jnp.int32),
            pltpu.VMEM(src_row.shape, jnp.int32),
            pltpu.SemaphoreType.DMA((4,)),
        ],
        space=pltpu.HBM,
    )

    half = nodes // 2
    sums_shape = shape((nodes * block, width), F32)

    def encode(units, last, before):
        edges = len(units) * part_rows * fanout
        used = [where[unit] for unit in units]
        args = [who, *(part for part, _ in used), weight, vec, *before]
        outs = [
            shape((half * block, width), BF16) if last else sums_shape,
            shape((edges, width), BF16),
            shape((1, edges), jnp.int32),
        ]
        return call(
            functools.partial(
                encode_kernel,
                tuple(at for _, at in used),
                nodes,
                block,
                fanout,
                part_rows,
                last,
            ),
            outs if last else outs[:1],
            args,
            smem=1,
            scratch=() if last else [pltpu.VMEM(s.shape, s.dtype) for s in outs[1:]],
            aliases={len(args) - 1: 0} if before and not last else None,
        )

    before = []
    for units in steps[:-1]:
        before = encode(units, False, before)
    cross, message, spots = encode(steps[-1], True, before)
    (keep,) = call(
        keep_kernel, [shape((half * block, width), BF16)], [message, spots, *before]
    )

    pair = keep.astype(F32) + swap(cross, "node", 1).astype(F32)
    pair = pair.reshape(half, block, width)
    arrived = [swap(pair[q].astype(BF16), "node", 2 * q) for q in range(1, half)]

    units = [(j, p) for j in range(sects) for p in range(len(axes))]
    slopes = call(
        functools.partial(
            slope_kernel, tuple(where[unit][1] for unit in units), fanout, part_rows
        ),
        [shape((fanout * part_rows, width), BF16)] * len(units),
        [*(where[unit][0] for unit in units), weight, vec],
    )
    tied = lax.optimization_barrier((*arrived, *slopes))
    arrived, slopes = tied[: half - 1], dict(zip(units, tied[half - 1 :]))

    halo_shape = shape((pieces, LANES), BF16)
    row_low, row_high = shape((block, width), BF16), shape((block, width), F32)

    def exchange(value):
        return lax.all_to_all(value, both, split_axis=0, concat_axis=0, tiled=True)

    state, mesh_pre, halo = call(
        functools.partial(start_kernel, parts),
        [row_low, row_high, halo_shape],
        [pair[0], *arrived, mesh_init[0], mesh_weight, pick],
    )
    assert proc_weight.shape[0] == 2
    state, mixed, slope_first, halo = call(
        functools.partial(first_kernel, 0, parts),
        [row_low, row_high, shape((fan * block, width), BF16), halo_shape],
        [state, exchange(halo), source, proc_weight, pick],
    )
    mesh_out, grad, halo = call(
        functools.partial(last_kernel, 1, parts),
        [row_low, row_high, halo_shape],
        [state, exchange(halo), source, source_t, proc_weight, cot[0]],
    )
    grad, halo = call(
        functools.partial(back_kernel, 0, parts),
        [row_high, halo_shape],
        [grad, exchange(halo), pick_t, mixed, slope_first, source_t, proc_weight],
    )
    (grad_sum,) = call(
        functools.partial(mesh_back_kernel, parts),
        [row_low],
        [grad, exchange(halo), pick_t, mesh_pre, mesh_weight],
    )

    same = [grad_sum] + [swap(grad_sum, "node", 2 * q) for q in range(1, half)]
    ready = nodes * block <= 8 * LANES
    picks_of = {unit: where[unit] for unit in units}
    if ready:
        seen, _ = lax.optimization_barrier((who, grad_sum))
        found = call(
            functools.partial(
                mark_kernel,
                tuple(where[unit][1] for unit in units),
                part_rows,
                nodes,
                block,
                fanout,
            ),
            [shape((fanout * part_rows, nodes * block), BF16)] * len(units),
            [seen, *(where[unit][0] for unit in units)],
            smem=1,
        )
        same[1] = lax.optimization_barrier((same[1], found[0]))[0]
        picks_of = {unit: (part, 0) for unit, part in zip(units, found)}
    other = [swap(rows, "node", 1) for rows in same]
    gathered = (*same, *other)

    def message_back(groups, dtype):
        used = [unit for group in groups for unit in group]
        return call(
            functools.partial(
                message_back_kernel,
                tuple(picks_of[unit][1] for unit in used),
                part_rows,
                ready,
                nodes,
                block,
                fanout,
            ),
            [shape((len(group) * part_rows, width), dtype) for group in groups],
            [
                who,
                *(picks_of[unit][0] for unit in used),
                *(slopes[unit] for unit in used),
                *gathered,
            ],
            smem=1,
        )

    first = [axes[p] for p in range(len(axes))]
    stay = [[j for j in range(sects) if not j & axis] for axis in first]
    given = message_back(
        [[(j ^ axis, p) for j in stay[p]] for p, axis in enumerate(first)], BF16
    )
    gathered = lax.optimization_barrier((*gathered, given[0]))[:-1]
    kept = message_back([[(j, p) for j in stay[p]] for p in range(len(axes))], F32)
    for step in range(len(axes)):
        order = [axes[(p + step) % len(axes)] for p in range(len(axes))]
        given = [swap(part, "sect", axis) for part, axis in zip(given, order)]
        if step + 1 == len(axes):
            break
        kept = [mine + part.astype(F32) for mine, part in zip(kept, given)]
        given = []
        for p, axis in enumerate(axes[(p + step + 1) % len(axes)] for p in range(len(axes))):
            rows = kept[p].reshape(len(stay[p]), part_rows, width)
            left = [j for j in stay[p] if not j & axis]
            given.append(
                jnp.concatenate([rows[stay[p].index(j ^ axis)] for j in left]).astype(BF16)
            )
            kept[p] = jnp.concatenate([rows[stay[p].index(j)] for j in left])
            stay[p] = left
    (grid_grad,) = call(
        grid_back_kernel,
        [shape((grid_rows, width), BF16)],
        [*kept, *given, enc_weight],
    )
    return (mesh_out[None], grid_grad)


def solution(mesh):
    return jax.shard_map(
        body,
        mesh=mesh,
        in_specs=(
            P(("sect", "node"), None),
            P(("sect", "node"), None),
            P(("sect", "node"), None),
            P(("sect", "node"), None),
            P(),
            P(),
            P("node", "sect", None),
            P(),
            P("sect", "node", None, None, None),
            P("node", "sect", None),
            P(),
            P("node", "sect", None),
        ),
        out_specs=(P("node", "sect", None), P(("sect", "node"), None)),
        check_vma=False,
    )
```

```python
import functools
import math

import jax
import jax.numpy as jnp
from jax import lax
from jax.experimental import pallas as pl
from jax.experimental.pallas import tpu as pltpu
from jax.sharding import PartitionSpec as P

F32 = jnp.float32
BF16 = jnp.bfloat16
LANES = 128
META_ROWS = 16
MIB = 1024 * 1024


def sigmoid(value):
    return 0.5 * jnp.tanh(0.5 * value) + 0.5


def silu(value):
    return value * sigmoid(value)


def slope(value):
    sig = sigmoid(value)
    return sig * (1.0 + value * (1.0 - sig))


def dot(left, right):
    return jnp.dot(left, right, preferred_element_type=F32)


def dot_t(left, right):
    return lax.dot_general(left, right, (((1,), (1,)), ((), ())), preferred_element_type=F32)


def halves(value):
    high = value.astype(BF16)
    return high, (value - high.astype(F32)).astype(BF16)


def back_dot(grad, weight):
    rows = grad.shape[0]
    both = dot_t(jnp.concatenate(halves(grad), axis=0), weight)
    return both[:rows] + both[rows:]


def mark(equal):
    return jnp.where(equal, 1.0, 0.0).astype(BF16)


def iota(shape, axis):
    return lax.broadcasted_iota(jnp.int32, shape, axis)


def norm_parts(mixed):
    mean = jnp.mean(mixed, axis=-1, keepdims=True)
    centred = mixed - mean
    scale = lax.rsqrt(jnp.mean(centred * centred, axis=-1, keepdims=True) + 1e-05)
    return centred * scale, scale


def norm_back(grad, normed, scale):
    pull = grad * slope(normed)
    return scale * (
        pull
        - jnp.mean(pull, axis=-1, keepdims=True)
        - normed * jnp.mean(pull * normed, axis=-1, keepdims=True)
    )


def pack_kernel(block, feat, lens, owner, dst, *refs):
    *outs, held, own_held, dst_held, sems = refs
    rows = feat.shape[0] // len(outs)
    pairs = [(lens, held), (owner, own_held), (dst, dst_held)]
    pairs += [
        (feat.at[i * rows : (i + 1) * rows, :], out.at[:rows, :]) for i, out in enumerate(outs)
    ]
    copies = [
        pltpu.make_async_copy(source, target, sems.at[i])
        for i, (source, target) in enumerate(pairs)
    ]
    for copy in copies:
        copy.start()
    for copy in copies[:3]:
        copy.wait()
    high, middle = halves(held[...])
    low = (held[...] - high.astype(F32) - middle.astype(F32)).astype(BF16)
    far = dst_held[...]
    section = far // block
    found = [v.astype(F32) for v in (high, middle, low)]
    found += [v.astype(F32) for v in (own_held[...], section, far - section * block)]
    fill = META_ROWS - 6 * lens.shape[0]
    found.append(jnp.zeros((fill, feat.shape[0]), F32))
    meta = jnp.concatenate(found, axis=0).astype(BF16)
    rest = jnp.zeros((META_ROWS, feat.shape[1] - rows), BF16)
    for i, out in enumerate(outs):
        out[rows:, :] = jnp.concatenate([meta[:, i * rows : (i + 1) * rows], rest], axis=1)
    for copy in copies[3:]:
        copy.wait()


def index_kernel(block, parts, *refs):
    wanted, far_weight, far_vec = refs[:2], refs[2], refs[3]
    pick, pick_t, source, source_t, weight, vec, sends, src_row, sems = refs[4:]
    pairs = ((wanted[0], sends), (wanted[1], src_row), (far_vec, vec), (far_weight, weight))
    copies = [
        pltpu.make_async_copy(start, target, sems.at[i])
        for i, (start, target) in enumerate(pairs)
    ]
    for copy in copies:
        copy.start()
    for copy in copies[:2]:
        copy.wait()
    sects, count, nodes = sends.shape
    pieces = pick.shape[0]
    at = iota((1, pieces), 1)
    part, row = at % parts, at // parts
    peer = row // count
    whose = mark(iota((nodes, pieces), 0) == peer % nodes)
    place = jnp.zeros((1, pieces), F32)
    for t in range(sects):
        found = dot(sends[t].astype(F32).astype(BF16), whose)
        for c in range(count):
            here = jnp.logical_and(peer // nodes == t, row % count == c)
            place = place + jnp.where(here, found[c : c + 1], 0.0)
    place = place + (part * block).astype(F32)
    pick_t[...] = mark(iota((parts * block, pieces), 0) == place.astype(jnp.int32))
    turned = jnp.broadcast_to(place, (8, pieces)).T[:, :1].astype(jnp.int32)
    pick[...] = mark(iota((pieces, parts * block), 1) == turned)
    table_len = source_t.shape[0]
    column = src_row[...].astype(F32).T.astype(jnp.int32)
    ids = iota((block, table_len), 1)
    ids_t = iota((table_len, block), 0)
    for k in range(src_row.shape[0]):
        rows = slice(k * block, (k + 1) * block)
        source[rows, :] = mark(ids == column[:, k : k + 1])
        source_t[:, rows] = mark(ids_t == src_row[k : k + 1, :])
    for copy in copies[2:]:
        copy.wait()


def edge_data(feat, at, rows):
    return feat[at + rows : at + rows + META_ROWS, :rows].astype(F32)


def edge_length(meta, fanout, k):
    high, middle, low = (meta[:, t * fanout + k : t * fanout + k + 1] for t in range(3))
    return high + middle + low


def spot_of(pick, fanout, k, section, node, nodes, block):
    owner, where, place = (pick((3 + t) * fanout + k).astype(jnp.int32) for t in range(3))
    apart = jnp.bitwise_xor(owner, node)
    order = lax.shift_right_logical(apart, 1) + jnp.bitwise_and(apart, 1) * (nodes // 2)
    return jnp.where(where == section, order * block + place, -1)


def add_rows(out, base, message, spots, before):
    step = min(out.shape[0], 512)

    def chunk(c, carry):
        start = pl.multiple_of(c * step, step)
        ids = iota((step, spots.shape[1]), 0) + (base + start)
        part = dot(mark(ids == spots[...]), message[...])
        for ref in before:
            part = part + ref[pl.ds(base + start, step), :]
        out[pl.ds(start, step), :] = part.astype(out.dtype)
        return carry

    lax.fori_loop(0, out.shape[0] // step, chunk, 0)


def encode_kernel(spans, nodes, block, fanout, rows, last, who, *refs):
    count = len(spans)
    feats = refs[:count]
    weight, vec = refs[count : count + 2]
    *before, out, message, spots = refs[count + 2 :]
    section, node = who[0], who[1]
    pre = 0.5 * dot(
        jnp.concatenate([feat[at : at + rows, :] for feat, at in zip(feats, spans)], axis=0),
        weight[...],
    )
    part = 0.5 * vec[...]
    for j in range(count):
        meta = edge_data(feats[j], spans[j], rows)
        turned = meta.T
        for k in range(fanout):
            at = (j * fanout + k) * rows
            act = pre[j * rows : (j + 1) * rows] + edge_length(turned, fanout, k) * part
            message[at : at + rows, :] = (act + act * jnp.tanh(act)).astype(BF16)
            spots[:, at : at + rows] = spot_of(
                lambda t, meta=meta: meta[t : t + 1], fanout, k, section, node, nodes, block
            )
    add_rows(out, nodes // 2 * block if last else 0, message, spots, before)


def keep_kernel(message, spots, before, out):
    add_rows(out, 0, message, spots, [before])


def slope_kernel(spans, fanout, rows, *refs):
    count = len(spans)
    feats = refs[:count]
    weight, vec = refs[count : count + 2]
    outs = refs[count + 2 :]
    for feat, at, out in zip(feats, spans, outs):
        pre = dot(feat[at : at + rows, :], weight[...])
        turned = edge_data(feat, at, rows).T
        for k in range(fanout):
            act = pre + edge_length(turned, fanout, k) * vec[...]
            out[k * rows : (k + 1) * rows, :] = slope(act).astype(BF16)


def halo_rows(state, pick, parts):
    stacked = jnp.concatenate(
        [state[:, i * LANES : (i + 1) * LANES] for i in range(parts)], axis=0
    )
    return dot(pick, stacked).astype(BF16)


def join_pieces(pieces, parts):
    count = pieces.shape[0]
    shape = (count // parts, count)
    return jnp.concatenate(
        [
            dot(mark(iota(shape, 1) == iota(shape, 0) * parts + i), pieces).astype(BF16)
            for i in range(parts)
        ],
        axis=1,
    )


def cut_pieces(rows, parts):
    count = rows.shape[0]
    shape = (count * parts, count)
    total = None
    for i in range(parts):
        onehot = mark(iota(shape, 0) == iota(shape, 1) * parts + i)
        piece = dot(onehot, rows[:, i * LANES : (i + 1) * LANES])
        total = piece if total is None else total + piece
    return total.astype(BF16)


def add_pieces(pieces, pick_t, block, parts):
    total = dot(pick_t, pieces)
    return jnp.concatenate([total[i * block : (i + 1) * block] for i in range(parts)], axis=1)


def start_kernel(parts, sums, *refs):
    received, (init, weight, pick, state, mesh_pre, halo) = refs[:-6], refs[-6:]
    agg = sums[...]
    for ref in received:
        agg = agg + ref[...].astype(F32)
    pre = dot(agg.astype(BF16), weight[...])
    mesh_pre[...] = pre
    new = (init[...].astype(F32) + silu(pre)).astype(BF16)
    state[...] = new
    halo[...] = halo_rows(new, pick[...], parts)


def layer_forward(state, pieces, source, weights, parts):
    block = state.shape[0]
    halo = join_pieces(pieces, parts)
    table = jnp.concatenate([state, halo], axis=0)
    from_src = 0.5 * dot(table, weights(0))
    to_dst = 0.5 * dot(state, weights(1))
    gathered = dot(source[...], from_src.astype(BF16))
    agg = jnp.zeros(state.shape, F32)
    slopes = []
    for k in range(source.shape[0] // block):
        joined = gathered[k * block : (k + 1) * block] + to_dst
        bend = jnp.tanh(joined)
        agg = agg + (joined + joined * bend)
        slopes.append((1.0 + bend + joined * (1.0 - bend * bend)).astype(BF16))
    mixed = dot(state, weights(2)) + dot(agg.astype(BF16), weights(3))
    return mixed, slopes


def layer_back(grad, mixed, slopes, source_t, weights):
    block = grad.shape[0]
    normed, scale = norm_parts(mixed)
    grad_mixed = norm_back(grad, normed, scale)
    grad_state = grad + back_dot(grad_mixed, weights(2))
    grad_agg = 0.5 * back_dot(grad_mixed, weights(3))
    total = jnp.zeros(grad.shape, F32)
    pieces = []
    for found in slopes:
        piece = grad_agg * found.astype(F32)
        total = total + piece
        pieces.append(piece.astype(BF16))
    grad_src = dot(source_t[...], jnp.concatenate(pieces, axis=0))
    grad_state = grad_state + back_dot(total, weights(1))
    grad_table = back_dot(grad_src, weights(0))
    return grad_state + grad_table[:block], grad_table[block:]


def layer_weights(weights, layer):
    return lambda i: weights[layer, i]


def first_kernel(
    layer, parts, state, pieces, source, weights, pick, new, mixed, slopes, halo
):
    block = state.shape[0]
    own = state[...]
    used = layer_weights(weights, layer)
    value, found = layer_forward(own, pieces[...], source, used, parts)
    mixed[...] = value
    for k, part in enumerate(found):
        slopes[k * block : (k + 1) * block, :] = part
    normed, _ = norm_parts(value)
    result = (own.astype(F32) + silu(normed)).astype(BF16)
    new[...] = result
    halo[...] = halo_rows(result, pick[...], parts)


def last_kernel(
    layer, parts, state, pieces, source, source_t, weights, cot, out, grad_own, grad_halo
):
    own = state[...]
    used = layer_weights(weights, layer)
    value, found = layer_forward(own, pieces[...], source, used, parts)
    normed, _ = norm_parts(value)
    out[...] = (own.astype(F32) + silu(normed)).astype(BF16)
    mine, sent = layer_back(cot[...].astype(F32), value, found, source_t, used)
    grad_own[...] = mine
    grad_halo[...] = cut_pieces(sent.astype(BF16), parts)


def back_kernel(
    layer,
    parts,
    mine,
    returned,
    pick_t,
    mixed,
    slopes,
    source_t,
    weights,
    grad_own,
    grad_halo,
):
    block = mine.shape[0]
    grad = mine[...] + add_pieces(returned[...], pick_t[...], block, parts)
    fan = slopes.shape[0] // block
    found = [slopes[k * block : (k + 1) * block, :] for k in range(fan)]
    used = layer_weights(weights, layer)
    own, sent = layer_back(grad, mixed[...], found, source_t, used)
    grad_own[...] = own
    grad_halo[...] = cut_pieces(sent.astype(BF16), parts)


def mesh_back_kernel(parts, mine, returned, pick_t, mesh_pre, weight, out):
    block = mine.shape[0]
    grad = mine[...] + add_pieces(returned[...], pick_t[...], block, parts)
    out[...] = back_dot(grad * slope(mesh_pre[...]), weight[...]).astype(BF16)


def edge_marks(feat, at, rows, nodes, block, fanout, who):
    turned = edge_data(feat, at, rows).T
    ids = iota((rows, nodes * block), 1)
    return [
        mark(
            ids
            == spot_of(
                lambda t: turned[:, t : t + 1], fanout, k, who[0], who[1], nodes, block
            )
        )
        for k in range(fanout)
    ]


def mark_kernel(spans, rows, nodes, block, fanout, who, *refs):
    feats, state = refs[: len(spans)], refs[len(spans)]
    *outs, final = refs[len(spans) + 1 :]
    final[...] = state[...]
    for feat, at, out in zip(feats, spans, outs):
        for k, found in enumerate(edge_marks(feat, at, rows, nodes, block, fanout, who)):
            out[k * rows : (k + 1) * rows, :] = found


def message_back_kernel(
    spans, used, added, rows, ready, nodes, block, fanout, who, *refs
):
    count = len(spans)
    feats, slopes = refs[:count], refs[count : 2 * count]
    outs = refs[2 * count :]
    grads, outs = outs[: len(used)], outs[len(used) :]
    before, outs = outs[:added], outs[added:]
    marks = []
    for feat, at in zip(feats, spans):
        if ready:
            columns = [feat[:, q * block : (q + 1) * block] for q in used]
            marks.append(jnp.concatenate(columns, axis=1))
        else:
            marks += edge_marks(feat, at, rows, nodes, block, fanout, who)
    picked = dot(
        jnp.concatenate(marks, axis=0), jnp.concatenate([ref[...] for ref in grads], axis=0)
    )
    per = count // len(outs)
    for i in range(count):
        total = jnp.zeros((rows, outs[0].shape[1]), F32)
        for k in range(fanout):
            at = (i * fanout + k) * rows
            part = slopes[i][k * rows : (k + 1) * rows, :].astype(F32)
            total = total + picked[at : at + rows] * part
        out, at = outs[i // per], i % per * rows
        if added:
            total = total + before[i // per][at : at + rows, :]
        out[at : at + rows, :] = total.astype(out.dtype)


def grid_back_kernel(*refs):
    *parts, weight, out = refs
    count = len(parts) // 2
    total = [
        mine[...] + given[...].astype(F32) for mine, given in zip(parts[:count], parts[count:])
    ]
    out[...] = back_dot(jnp.concatenate(total, axis=0), weight[...]).astype(BF16)


def call(kernel, outs, args, smem=0, scratch=(), space=pltpu.VMEM, aliases=None):
    specs = [pl.BlockSpec(memory_space=pltpu.SMEM)] * smem
    specs += [pl.BlockSpec(memory_space=space)] * (len(args) - smem)
    moved = sum(a.size * a.dtype.itemsize for a in list(args) + list(outs))
    held = sum(math.prod(a.shape) * 4 for a in scratch)
    limit = 2 * (moved + held) + 6 * MIB
    result = pl.pallas_call(
        kernel,
        out_shape=list(outs),
        in_specs=specs,
        out_specs=[pl.BlockSpec(memory_space=pltpu.VMEM)] * len(outs),
        scratch_shapes=list(scratch),
        input_output_aliases=aliases or {},
        compiler_params=pltpu.CompilerParams(vmem_limit_bytes=limit),
        cost_estimate=pl.CostEstimate(
            flops=0, bytes_accessed=moved, transcendentals=0
        ),
    )(*args)
    return result


def shape(dims, dtype):
    return jax.ShapeDtypeStruct(dims, dtype)


def swap(value, axis, apart):
    size = lax.axis_size(axis)
    return lax.ppermute(value, axis, [(i, i ^ apart) for i in range(size)])


def body(
    grid_feat,
    edge_len,
    g2m_owner,
    g2m_dst,
    enc_weight,
    enc_vec,
    mesh_init,
    mesh_weight,
    halo_send,
    mesh_src,
    proc_weight,
    cot,
):
    nodes = lax.axis_size("node")
    sects = lax.axis_size("sect")
    width = grid_feat.shape[1]
    grid_rows, fanout = edge_len.shape
    block = mesh_init.shape[1]
    parts = width // LANES
    both = ("sect", "node")
    who = jnp.stack([lax.axis_index("sect"), lax.axis_index("node")]).astype(jnp.int32)

    axes = [1 << i for i in range(sects.bit_length() - 1)]
    part_rows = grid_rows // len(axes)
    ends = pltpu.VMEM((fanout, grid_rows), jnp.int32)
    packed = call(
        functools.partial(pack_kernel, block),
        [shape((part_rows + META_ROWS, width), BF16)] * len(axes),
        [
            pltpu.with_memory_space_constraint(value, pltpu.HBM)
            for value in (grid_feat, edge_len.T, g2m_owner.T, g2m_dst.T)
        ],
        scratch=[
            pltpu.VMEM((fanout, grid_rows), F32),
            ends,
            ends,
            pltpu.SemaphoreType.DMA((3 + len(axes),)),
        ],
        space=pltpu.HBM,
    )
    where = {(0, p): (part, 0) for p, part in enumerate(packed)}
    steps = [[(0, p) for p in range(len(axes))]]
    held, names = list(packed), [[0] for _ in axes]
    for step in range(len(axes)):
        given = [
            swap(part, "sect", axes[(p + step) % len(axes)]) for p, part in enumerate(held)
        ]
        steps.append([])
        for p, part in enumerate(given):
            axis = axes[(p + step) % len(axes)]
            for i, j in enumerate(list(names[p])):
                where[j ^ axis, p] = (part, i * packed[0].shape[0])
                names[p].append(j ^ axis)
                steps[-1].append((j ^ axis, p))
        held = [jnp.concatenate(pair, axis=0) for pair in zip(held, given)]
    sends = halo_send[0, 0].transpose(0, 2, 1)
    src_row = mesh_src[0].T
    fan = src_row.shape[0]
    pieces = sends.size * parts
    table_len = block + sends.size
    pick, pick_t, source, source_t, weight, vec = call(
        functools.partial(index_kernel, block, parts),
        [
            shape((pieces, parts * block), BF16),
            shape((parts * block, pieces), BF16),
            shape((fan * block, table_len), BF16),
            shape((table_len, fan * block), BF16),
            shape(enc_weight.shape, BF16),
            shape((1, width), F32),
        ],
        [
            pltpu.with_memory_space_constraint(value, pltpu.HBM)
            for value in (sends, src_row, enc_weight, enc_vec[None, :])
        ],
        scratch=[
            pltpu.VMEM(sends.shape, jnp.int32),
            pltpu.VMEM(src_row.shape, jnp.int32),
            pltpu.SemaphoreType.DMA((4,)),
        ],
        space=pltpu.HBM,
    )

    half = nodes // 2
    sums_shape = shape((nodes * block, width), F32)

    def encode(units, last, before):
        edges = len(units) * part_rows * fanout
        used = [where[unit] for unit in units]
        args = [who, *(part for part, _ in used), weight, vec, *before]
        outs = [
            shape((half * block, width), BF16) if last else sums_shape,
            shape((edges, width), BF16),
            shape((1, edges), jnp.int32),
        ]
        return call(
            functools.partial(
                encode_kernel,
                tuple(at for _, at in used),
                nodes,
                block,
                fanout,
                part_rows,
                last,
            ),
            outs if last else outs[:1],
            args,
            smem=1,
            scratch=() if last else [pltpu.VMEM(s.shape, s.dtype) for s in outs[1:]],
            aliases={len(args) - 1: 0} if before and not last else None,
        )

    before = []
    for units in steps[:-1]:
        before = encode(units, False, before)
    cross, message, spots = encode(steps[-1], True, before)
    (keep,) = call(
        keep_kernel, [shape((half * block, width), BF16)], [message, spots, *before]
    )

    pair = keep.astype(F32) + swap(cross, "node", 1).astype(F32)
    pair = pair.reshape(half, block, width)
    arrived = [
        swap(pair[q].astype(BF16), "node", 2 * q) for q in reversed(range(1, half))
    ]

    units = [(j, p) for j in range(sects) for p in range(len(axes))]
    slopes = call(
        functools.partial(
            slope_kernel, tuple(where[unit][1] for unit in units), fanout, part_rows
        ),
        [shape((fanout * part_rows, width), BF16)] * len(units),
        [*(where[unit][0] for unit in units), weight, vec],
    )
    tied = lax.optimization_barrier((*arrived, *slopes))
    arrived, slopes = tied[: half - 1], dict(zip(units, tied[half - 1 :]))

    halo_shape = shape((pieces, LANES), BF16)
    row_low, row_high = shape((block, width), BF16), shape((block, width), F32)

    def exchange(value):
        return lax.all_to_all(value, both, split_axis=0, concat_axis=0, tiled=True)

    state, mesh_pre, halo = call(
        functools.partial(start_kernel, parts),
        [row_low, row_high, halo_shape],
        [pair[0], *arrived, mesh_init[0], mesh_weight, pick],
    )
    assert proc_weight.shape[0] == 2
    state, mixed, slope_first, halo = call(
        functools.partial(first_kernel, 0, parts),
        [row_low, row_high, shape((fan * block, width), BF16), halo_shape],
        [state, exchange(halo), source, proc_weight, pick],
    )
    mesh_out, grad, halo = call(
        functools.partial(last_kernel, 1, parts),
        [row_low, row_high, halo_shape],
        [state, exchange(halo), source, source_t, proc_weight, cot[0]],
    )
    grad, halo = call(
        functools.partial(back_kernel, 0, parts),
        [row_high, halo_shape],
        [grad, exchange(halo), pick_t, mixed, slope_first, source_t, proc_weight],
    )
    (grad_sum,) = call(
        functools.partial(mesh_back_kernel, parts),
        [row_low],
        [grad, exchange(halo), pick_t, mesh_pre, mesh_weight],
    )

    same = [grad_sum] + [swap(grad_sum, "node", 2 * q) for q in range(1, half)]
    ready = nodes * block <= 8 * LANES
    picks_of = {unit: where[unit] for unit in units}
    if ready:
        seen, _ = lax.optimization_barrier((who, grad_sum))
        *found, mesh_out = call(
            functools.partial(
                mark_kernel,
                tuple(where[unit][1] for unit in units),
                part_rows,
                nodes,
                block,
                fanout,
            ),
            [shape((fanout * part_rows, nodes * block), BF16)] * len(units) + [row_low],
            [seen, *(where[unit][0] for unit in units), mesh_out],
            smem=1,
        )
        same[1] = lax.optimization_barrier((same[1], found[0]))[0]
        picks_of = {unit: (part, 0) for unit, part in zip(units, found)}
    other = [swap(rows, "node", 1) for rows in same]
    gathered = (*same, *other)

    def message_back(groups, dtype, blocks=range(nodes), added=()):
        used = [unit for group in groups for unit in group]
        return call(
            functools.partial(
                message_back_kernel,
                tuple(picks_of[unit][1] for unit in used),
                tuple(blocks),
                len(added),
                part_rows,
                ready,
                nodes,
                block,
                fanout,
            ),
            [shape((len(group) * part_rows, width), dtype) for group in groups],
            [
                who,
                *(picks_of[unit][0] for unit in used),
                *(slopes[unit] for unit in used),
                *(gathered[q] for q in blocks),
                *added,
            ],
            smem=1,
        )

    first = [axes[p] for p in range(len(axes))]
    stay = [[j for j in range(sects) if not j & axis] for axis in first]
    sent = [[(j ^ axis, p) for j in stay[p]] for p, axis in enumerate(first)]
    if ready:
        late = [half - 1, nodes - 1]
        early = message_back(sent, F32, [q for q in range(nodes) if q not in late])
        given = message_back(sent, BF16, late, early)
    else:
        given = message_back(sent, BF16)
    gathered = lax.optimization_barrier((*gathered, given[0]))[:-1]
    kept = message_back([[(j, p) for j in stay[p]] for p in range(len(axes))], F32)
    for step in range(len(axes)):
        order = [axes[(p + step) % len(axes)] for p in range(len(axes))]
        given = [swap(part, "sect", axis) for part, axis in zip(given, order)]
        if step + 1 == len(axes):
            break
        kept = [mine + part.astype(F32) for mine, part in zip(kept, given)]
        given = []
        for p, axis in enumerate(axes[(p + step + 1) % len(axes)] for p in range(len(axes))):
            rows = kept[p].reshape(len(stay[p]), part_rows, width)
            left = [j for j in stay[p] if not j & axis]
            given.append(
                jnp.concatenate([rows[stay[p].index(j ^ axis)] for j in left]).astype(BF16)
            )
            kept[p] = jnp.concatenate([rows[stay[p].index(j)] for j in left])
            stay[p] = left
    (grid_grad,) = call(
        grid_back_kernel,
        [shape((grid_rows, width), BF16)],
        [*kept, *given, enc_weight],
    )
    return (mesh_out[None], grid_grad)


def solution(mesh):
    return jax.shard_map(
        body,
        mesh=mesh,
        in_specs=(
            P(("sect", "node"), None),
            P(("sect", "node"), None),
            P(("sect", "node"), None),
            P(("sect", "node"), None),
            P(),
            P(),
            P("node", "sect", None),
            P(),
            P("sect", "node", None, None, None),
            P("node", "sect", None),
            P(),
            P("node", "sect", None),
        ),
        out_specs=(P("node", "sect", None), P(("sect", "node"), None)),
        check_vma=False,
    )
```

```python
import functools
import math

import jax
import jax.numpy as jnp
from jax import lax
from jax.experimental import pallas as pl
from jax.experimental.pallas import tpu as pltpu
from jax.sharding import PartitionSpec as P

F32 = jnp.float32
BF16 = jnp.bfloat16
LANES = 128
META_ROWS = 16
MIB = 1024 * 1024


def sigmoid(value):
    return 0.5 * jnp.tanh(0.5 * value) + 0.5


def silu(value):
    return value * sigmoid(value)


def slope(value):
    sig = sigmoid(value)
    return sig * (1.0 + value * (1.0 - sig))


def dot(left, right):
    return jnp.dot(left, right, preferred_element_type=F32)


def dot_t(left, right):
    return lax.dot_general(left, right, (((1,), (1,)), ((), ())), preferred_element_type=F32)


def halves(value):
    high = value.astype(BF16)
    return high, (value - high.astype(F32)).astype(BF16)


def back_dot(grad, weight):
    rows = grad.shape[0]
    both = dot_t(jnp.concatenate(halves(grad), axis=0), weight)
    return both[:rows] + both[rows:]


def mark(equal):
    return jnp.where(equal, 1.0, 0.0).astype(BF16)


def iota(shape, axis):
    return lax.broadcasted_iota(jnp.int32, shape, axis)


def norm_parts(mixed):
    mean = jnp.mean(mixed, axis=-1, keepdims=True)
    centred = mixed - mean
    scale = lax.rsqrt(jnp.mean(centred * centred, axis=-1, keepdims=True) + 1e-05)
    return centred * scale, scale


def norm_back(grad, normed, scale):
    pull = grad * slope(normed)
    return scale * (
        pull
        - jnp.mean(pull, axis=-1, keepdims=True)
        - normed * jnp.mean(pull * normed, axis=-1, keepdims=True)
    )


def pack_kernel(block, feat, lens, owner, dst, *refs):
    *outs, held, own_held, dst_held, sems = refs
    rows = feat.shape[0] // len(outs)
    pairs = [(lens, held), (owner, own_held), (dst, dst_held)]
    pairs += [
        (feat.at[i * rows : (i + 1) * rows, :], out.at[:rows, :]) for i, out in enumerate(outs)
    ]
    copies = [
        pltpu.make_async_copy(source, target, sems.at[i])
        for i, (source, target) in enumerate(pairs)
    ]
    for copy in copies:
        copy.start()
    for copy in copies[:3]:
        copy.wait()
    high, middle = halves(held[...])
    low = (held[...] - high.astype(F32) - middle.astype(F32)).astype(BF16)
    far = dst_held[...]
    section = far // block
    found = [v.astype(F32) for v in (high, middle, low)]
    found += [v.astype(F32) for v in (own_held[...], section, far - section * block)]
    fill = META_ROWS - 6 * lens.shape[0]
    found.append(jnp.zeros((fill, feat.shape[0]), F32))
    meta = jnp.concatenate(found, axis=0).astype(BF16)
    rest = jnp.zeros((META_ROWS, feat.shape[1] - rows), BF16)
    for i, out in enumerate(outs):
        out[rows:, :] = jnp.concatenate([meta[:, i * rows : (i + 1) * rows], rest], axis=1)
    for copy in copies[3:]:
        copy.wait()


def index_kernel(block, parts, *refs):
    wanted, far_weight, far_vec = refs[:2], refs[2], refs[3]
    pick, pick_t, source, source_t, weight, vec, sends, src_row, sems = refs[4:]
    pairs = ((wanted[0], sends), (wanted[1], src_row), (far_vec, vec), (far_weight, weight))
    copies = [
        pltpu.make_async_copy(start, target, sems.at[i])
        for i, (start, target) in enumerate(pairs)
    ]
    for copy in copies:
        copy.start()
    for copy in copies[:2]:
        copy.wait()
    sects, count, nodes = sends.shape
    pieces = pick.shape[0]
    at = iota((1, pieces), 1)
    part, row = at % parts, at // parts
    peer = row // count
    whose = mark(iota((nodes, pieces), 0) == peer % nodes)
    place = jnp.zeros((1, pieces), F32)
    for t in range(sects):
        found = dot(sends[t].astype(F32).astype(BF16), whose)
        for c in range(count):
            here = jnp.logical_and(peer // nodes == t, row % count == c)
            place = place + jnp.where(here, found[c : c + 1], 0.0)
    place = place + (part * block).astype(F32)
    pick_t[...] = mark(iota((parts * block, pieces), 0) == place.astype(jnp.int32))
    turned = jnp.broadcast_to(place, (8, pieces)).T[:, :1].astype(jnp.int32)
    pick[...] = mark(iota((pieces, parts * block), 1) == turned)
    table_len = source_t.shape[0]
    column = src_row[...].astype(F32).T.astype(jnp.int32)
    ids = iota((block, table_len), 1)
    ids_t = iota((table_len, block), 0)
    for k in range(src_row.shape[0]):
        rows = slice(k * block, (k + 1) * block)
        source[rows, :] = mark(ids == column[:, k : k + 1])
        source_t[:, rows] = mark(ids_t == src_row[k : k + 1, :])
    for copy in copies[2:]:
        copy.wait()


def edge_data(feat, at, rows):
    return feat[at + rows : at + rows + META_ROWS, :rows].astype(F32)


def edge_length(meta, fanout, k):
    high, middle, low = (meta[:, t * fanout + k : t * fanout + k + 1] for t in range(3))
    return high + middle + low


def spot_of(pick, fanout, k, section, node, nodes, block):
    owner, where, place = (pick((3 + t) * fanout + k).astype(jnp.int32) for t in range(3))
    apart = jnp.bitwise_xor(owner, node)
    order = lax.shift_right_logical(apart, 1) + jnp.bitwise_and(apart, 1) * (nodes // 2)
    return jnp.where(where == section, order * block + place, -1)


def add_rows(out, base, message, spots, before):
    step = min(out.shape[0], 512)

    def chunk(c, carry):
        start = pl.multiple_of(c * step, step)
        ids = iota((step, spots.shape[1]), 0) + (base + start)
        part = dot(mark(ids == spots[...]), message[...])
        for ref in before:
            part = part + ref[pl.ds(base + start, step), :]
        out[pl.ds(start, step), :] = part.astype(out.dtype)
        return carry

    lax.fori_loop(0, out.shape[0] // step, chunk, 0)


def encode_kernel(spans, nodes, block, fanout, rows, last, who, *refs):
    count = len(spans)
    feats = refs[:count]
    weight, vec = refs[count : count + 2]
    *before, out, message, spots = refs[count + 2 :]
    section, node = who[0], who[1]
    pre = 0.5 * dot(
        jnp.concatenate([feat[at : at + rows, :] for feat, at in zip(feats, spans)], axis=0),
        weight[...],
    )
    part = 0.5 * vec[...]
    for j in range(count):
        meta = edge_data(feats[j], spans[j], rows)
        turned = meta.T
        for k in range(fanout):
            at = (j * fanout + k) * rows
            act = pre[j * rows : (j + 1) * rows] + edge_length(turned, fanout, k) * part
            message[at : at + rows, :] = (act + act * jnp.tanh(act)).astype(BF16)
            spots[:, at : at + rows] = spot_of(
                lambda t, meta=meta: meta[t : t + 1], fanout, k, section, node, nodes, block
            )
    add_rows(out, nodes // 2 * block if last else 0, message, spots, before)


def keep_kernel(message, spots, before, out):
    add_rows(out, 0, message, spots, [before])


def slope_kernel(spans, fanout, rows, *refs):
    count = len(spans)
    feats = refs[:count]
    weight, vec = refs[count : count + 2]
    outs = refs[count + 2 :]
    for feat, at, out in zip(feats, spans, outs):
        pre = dot(feat[at : at + rows, :], weight[...])
        turned = edge_data(feat, at, rows).T
        for k in range(fanout):
            act = pre + edge_length(turned, fanout, k) * vec[...]
            out[k * rows : (k + 1) * rows, :] = slope(act).astype(BF16)


def halo_rows(state, pick, parts):
    stacked = jnp.concatenate(
        [state[:, i * LANES : (i + 1) * LANES] for i in range(parts)], axis=0
    )
    return dot(pick, stacked).astype(BF16)


def join_pieces(pieces, parts):
    count = pieces.shape[0]
    rows = count // parts
    at = iota((count, count), 0)
    onehot = mark(iota((count, count), 1) == at % rows * parts + at // rows)
    found = dot(onehot, pieces).astype(BF16)
    return jnp.concatenate([found[i * rows : (i + 1) * rows] for i in range(parts)], axis=1)


def cut_pieces(rows, parts):
    each, count = rows.shape[0], rows.shape[0] * parts
    at = iota((count, count), 0)
    onehot = mark(iota((count, count), 1) == at % parts * each + at // parts)
    stacked = jnp.concatenate(
        [rows[:, i * LANES : (i + 1) * LANES] for i in range(parts)], axis=0
    )
    return dot(onehot, stacked).astype(BF16)


def add_pieces(pieces, pick_t, block, parts):
    total = dot(pick_t, pieces)
    return jnp.concatenate([total[i * block : (i + 1) * block] for i in range(parts)], axis=1)


def start_kernel(parts, sums, *refs):
    received, (init, weight, pick, state, mesh_pre, halo) = refs[:-6], refs[-6:]
    agg = sums[...]
    for ref in received:
        agg = agg + ref[...].astype(F32)
    pre = dot(agg.astype(BF16), weight[...])
    mesh_pre[...] = pre
    new = (init[...].astype(F32) + silu(pre)).astype(BF16)
    state[...] = new
    halo[...] = halo_rows(new, pick[...], parts)


def layer_forward(state, pieces, source, weights, parts):
    block = state.shape[0]
    halo = join_pieces(pieces, parts)
    table = jnp.concatenate([state, halo], axis=0)
    from_src = 0.5 * dot(table, weights(0))
    to_dst = 0.5 * dot(state, weights(1))
    gathered = dot(source[...], from_src.astype(BF16))
    agg = jnp.zeros(state.shape, F32)
    slopes = []
    for k in range(source.shape[0] // block):
        joined = gathered[k * block : (k + 1) * block] + to_dst
        bend = jnp.tanh(joined)
        agg = agg + (joined + joined * bend)
        joined, bend = joined.astype(BF16), bend.astype(BF16)
        slopes.append(1 + bend + joined * (1 - bend * bend))
    mixed = dot(state, weights(2)) + dot(agg.astype(BF16), weights(3))
    return mixed, slopes


def layer_back(grad, mixed, slopes, source_t, weights):
    block = grad.shape[0]
    normed, scale = norm_parts(mixed)
    grad_mixed = norm_back(grad, normed, scale)
    grad_state = grad + back_dot(grad_mixed, weights(2))
    grad_agg = 0.5 * back_dot(grad_mixed, weights(3))
    low = grad_agg.astype(BF16)
    total = jnp.zeros(grad.shape, F32)
    for found in slopes:
        total = total + found.astype(F32)
    total = grad_agg * total
    pieces = [low * found for found in slopes]
    grad_src = dot(source_t[...], jnp.concatenate(pieces, axis=0))
    grad_state = grad_state + back_dot(total, weights(1))
    grad_table = back_dot(grad_src, weights(0))
    return grad_state + grad_table[:block], grad_table[block:]


def layer_weights(weights, layer):
    return lambda i: weights[layer, i]


def first_kernel(
    layer, parts, state, pieces, source, weights, pick, new, mixed, slopes, halo
):
    block = state.shape[0]
    own = state[...]
    used = layer_weights(weights, layer)
    value, found = layer_forward(own, pieces[...], source, used, parts)
    mixed[...] = value
    for k, part in enumerate(found):
        slopes[k * block : (k + 1) * block, :] = part
    normed, _ = norm_parts(value)
    result = (own.astype(F32) + silu(normed)).astype(BF16)
    new[...] = result
    halo[...] = halo_rows(result, pick[...], parts)


def last_kernel(
    layer, parts, state, pieces, source, source_t, weights, cot, out, grad_own, grad_halo
):
    own = state[...]
    used = layer_weights(weights, layer)
    value, found = layer_forward(own, pieces[...], source, used, parts)
    normed, _ = norm_parts(value)
    out[...] = (own.astype(F32) + silu(normed)).astype(BF16)
    mine, sent = layer_back(cot[...].astype(F32), value, found, source_t, used)
    grad_own[...] = mine
    grad_halo[...] = cut_pieces(sent.astype(BF16), parts)


def back_kernel(
    layer,
    parts,
    mine,
    returned,
    pick_t,
    mixed,
    slopes,
    source_t,
    weights,
    grad_own,
    grad_halo,
):
    block = mine.shape[0]
    grad = mine[...] + add_pieces(returned[...], pick_t[...], block, parts)
    fan = slopes.shape[0] // block
    found = [slopes[k * block : (k + 1) * block, :] for k in range(fan)]
    used = layer_weights(weights, layer)
    own, sent = layer_back(grad, mixed[...], found, source_t, used)
    grad_own[...] = own
    grad_halo[...] = cut_pieces(sent.astype(BF16), parts)


def mesh_back_kernel(parts, mine, returned, pick_t, mesh_pre, weight, out):
    block = mine.shape[0]
    grad = mine[...] + add_pieces(returned[...], pick_t[...], block, parts)
    out[...] = back_dot(grad * slope(mesh_pre[...]), weight[...]).astype(BF16)


def edge_marks(feat, at, rows, nodes, block, fanout, who):
    turned = edge_data(feat, at, rows).T
    ids = iota((rows, nodes * block), 1)
    return [
        mark(
            ids
            == spot_of(
                lambda t: turned[:, t : t + 1], fanout, k, who[0], who[1], nodes, block
            )
        )
        for k in range(fanout)
    ]


def mark_kernel(spans, rows, nodes, block, fanout, who, *refs):
    feats, state = refs[: len(spans)], refs[len(spans)]
    *outs, final = refs[len(spans) + 1 :]
    final[...] = state[...]
    for feat, at, out in zip(feats, spans, outs):
        for k, found in enumerate(edge_marks(feat, at, rows, nodes, block, fanout, who)):
            out[k * rows : (k + 1) * rows, :] = found


def message_back_kernel(spans, rows, ready, nodes, block, fanout, who, *refs):
    count = len(spans)
    feats, slopes = refs[:count], refs[count : 2 * count]
    outs = refs[2 * count :]
    grads, outs = outs[:nodes], outs[nodes:]
    marks = []
    for feat, at in zip(feats, spans):
        if ready:
            marks.append(feat[...])
        else:
            marks += edge_marks(feat, at, rows, nodes, block, fanout, who)
    picked = dot(
        jnp.concatenate(marks, axis=0), jnp.concatenate([ref[...] for ref in grads], axis=0)
    )
    per = count // len(outs)
    for i in range(count):
        total = jnp.zeros((rows, outs[0].shape[1]), F32)
        for k in range(fanout):
            at = (i * fanout + k) * rows
            part = slopes[i][k * rows : (k + 1) * rows, :].astype(F32)
            total = total + picked[at : at + rows] * part
        out, at = outs[i // per], i % per * rows
        out[at : at + rows, :] = total.astype(out.dtype)


def grid_back_kernel(*refs):
    *parts, weight, out = refs
    count = len(parts) // 2
    total = [
        mine[...] + given[...].astype(F32) for mine, given in zip(parts[:count], parts[count:])
    ]
    out[...] = back_dot(jnp.concatenate(total, axis=0), weight[...]).astype(BF16)


def call(kernel, outs, args, smem=0, scratch=(), space=pltpu.VMEM, aliases=None):
    specs = [pl.BlockSpec(memory_space=pltpu.SMEM)] * smem
    specs += [pl.BlockSpec(memory_space=space)] * (len(args) - smem)
    moved = sum(a.size * a.dtype.itemsize for a in list(args) + list(outs))
    held = sum(math.prod(a.shape) * 4 for a in scratch)
    limit = 2 * (moved + held) + 6 * MIB
    result = pl.pallas_call(
        kernel,
        out_shape=list(outs),
        in_specs=specs,
        out_specs=[pl.BlockSpec(memory_space=pltpu.VMEM)] * len(outs),
        scratch_shapes=list(scratch),
        input_output_aliases=aliases or {},
        compiler_params=pltpu.CompilerParams(vmem_limit_bytes=limit),
        cost_estimate=pl.CostEstimate(
            flops=0, bytes_accessed=moved, transcendentals=0
        ),
    )(*args)
    return result


def shape(dims, dtype):
    return jax.ShapeDtypeStruct(dims, dtype)


def swap(value, axis, apart):
    size = lax.axis_size(axis)
    return lax.ppermute(value, axis, [(i, i ^ apart) for i in range(size)])


def body(
    grid_feat,
    edge_len,
    g2m_owner,
    g2m_dst,
    enc_weight,
    enc_vec,
    mesh_init,
    mesh_weight,
    halo_send,
    mesh_src,
    proc_weight,
    cot,
):
    nodes = lax.axis_size("node")
    sects = lax.axis_size("sect")
    width = grid_feat.shape[1]
    grid_rows, fanout = edge_len.shape
    block = mesh_init.shape[1]
    parts = width // LANES
    both = ("sect", "node")
    who = jnp.stack([lax.axis_index("sect"), lax.axis_index("node")]).astype(jnp.int32)

    axes = [1 << i for i in range(sects.bit_length() - 1)]
    part_rows = grid_rows // len(axes)
    ends = pltpu.VMEM((fanout, grid_rows), jnp.int32)
    packed = call(
        functools.partial(pack_kernel, block),
        [shape((part_rows + META_ROWS, width), BF16)] * len(axes),
        [
            pltpu.with_memory_space_constraint(value, pltpu.HBM)
            for value in (grid_feat, edge_len.T, g2m_owner.T, g2m_dst.T)
        ],
        scratch=[
            pltpu.VMEM((fanout, grid_rows), F32),
            ends,
            ends,
            pltpu.SemaphoreType.DMA((3 + len(axes),)),
        ],
        space=pltpu.HBM,
    )
    where = {(0, p): (part, 0) for p, part in enumerate(packed)}
    steps = [[(0, p) for p in range(len(axes))]]
    held, names = list(packed), [[0] for _ in axes]
    for step in range(len(axes)):
        given = [
            swap(part, "sect", axes[(p + step) % len(axes)]) for p, part in enumerate(held)
        ]
        steps.append([])
        for p, part in enumerate(given):
            axis = axes[(p + step) % len(axes)]
            for i, j in enumerate(list(names[p])):
                where[j ^ axis, p] = (part, i * packed[0].shape[0])
                names[p].append(j ^ axis)
                steps[-1].append((j ^ axis, p))
        held = [jnp.concatenate(pair, axis=0) for pair in zip(held, given)]
    sends = halo_send[0, 0].transpose(0, 2, 1)
    src_row = mesh_src[0].T
    fan = src_row.shape[0]
    pieces = sends.size * parts
    table_len = block + sends.size
    pick, pick_t, source, source_t, weight, vec = call(
        functools.partial(index_kernel, block, parts),
        [
            shape((pieces, parts * block), BF16),
            shape((parts * block, pieces), BF16),
            shape((fan * block, table_len), BF16),
            shape((table_len, fan * block), BF16),
            shape(enc_weight.shape, BF16),
            shape((1, width), F32),
        ],
        [
            pltpu.with_memory_space_constraint(value, pltpu.HBM)
            for value in (sends, src_row, enc_weight, enc_vec[None, :])
        ],
        scratch=[
            pltpu.VMEM(sends.shape, jnp.int32),
            pltpu.VMEM(src_row.shape, jnp.int32),
            pltpu.SemaphoreType.DMA((4,)),
        ],
        space=pltpu.HBM,
    )

    half = nodes // 2
    sums_shape = shape((nodes * block, width), F32)

    def encode(units, last, before):
        edges = len(units) * part_rows * fanout
        used = [where[unit] for unit in units]
        args = [who, *(part for part, _ in used), weight, vec, *before]
        outs = [
            shape((half * block, width), BF16) if last else sums_shape,
            shape((edges, width), BF16),
            shape((1, edges), jnp.int32),
        ]
        return call(
            functools.partial(
                encode_kernel,
                tuple(at for _, at in used),
                nodes,
                block,
                fanout,
                part_rows,
                last,
            ),
            outs if last else outs[:1],
            args,
            smem=1,
            scratch=() if last else [pltpu.VMEM(s.shape, s.dtype) for s in outs[1:]],
            aliases={len(args) - 1: 0} if before and not last else None,
        )

    before = []
    for units in steps[:-1]:
        before = encode(units, False, before)
    cross, message, spots = encode(steps[-1], True, before)
    (keep,) = call(
        keep_kernel, [shape((half * block, width), BF16)], [message, spots, *before]
    )

    pair = keep.astype(F32) + swap(cross, "node", 1).astype(F32)
    pair = pair.reshape(half, block, width)
    arrived = [
        swap(pair[q].astype(BF16), "node", 2 * q) for q in reversed(range(1, half))
    ]

    units = [(j, p) for j in range(sects) for p in range(len(axes))]
    slopes = call(
        functools.partial(
            slope_kernel, tuple(where[unit][1] for unit in units), fanout, part_rows
        ),
        [shape((fanout * part_rows, width), BF16)] * len(units),
        [*(where[unit][0] for unit in units), weight, vec],
    )
    tied = lax.optimization_barrier((*arrived, *slopes))
    arrived, slopes = tied[: half - 1], dict(zip(units, tied[half - 1 :]))

    halo_shape = shape((pieces, LANES), BF16)
    row_low, row_high = shape((block, width), BF16), shape((block, width), F32)

    def exchange(value):
        return lax.all_to_all(value, both, split_axis=0, concat_axis=0, tiled=True)

    state, mesh_pre, halo = call(
        functools.partial(start_kernel, parts),
        [row_low, row_high, halo_shape],
        [pair[0], *arrived, mesh_init[0], mesh_weight, pick],
    )
    assert proc_weight.shape[0] == 2
    state, mixed, slope_first, halo = call(
        functools.partial(first_kernel, 0, parts),
        [row_low, row_high, shape((fan * block, width), BF16), halo_shape],
        [state, exchange(halo), source, proc_weight, pick],
    )
    mesh_out, grad, halo = call(
        functools.partial(last_kernel, 1, parts),
        [row_low, row_high, halo_shape],
        [state, exchange(halo), source, source_t, proc_weight, cot[0]],
    )
    grad, halo = call(
        functools.partial(back_kernel, 0, parts),
        [row_high, halo_shape],
        [grad, exchange(halo), pick_t, mixed, slope_first, source_t, proc_weight],
    )
    (grad_sum,) = call(
        functools.partial(mesh_back_kernel, parts),
        [row_low],
        [grad, exchange(halo), pick_t, mesh_pre, mesh_weight],
    )

    same = [grad_sum] + [swap(grad_sum, "node", 2 * q) for q in range(1, half)]
    ready = nodes * block <= 8 * LANES
    picks_of = {unit: where[unit] for unit in units}
    if ready:
        seen, _ = lax.optimization_barrier((who, grad_sum))
        *found, mesh_out = call(
            functools.partial(
                mark_kernel,
                tuple(where[unit][1] for unit in units),
                part_rows,
                nodes,
                block,
                fanout,
            ),
            [shape((fanout * part_rows, nodes * block), BF16)] * len(units) + [row_low],
            [seen, *(where[unit][0] for unit in units), mesh_out],
            smem=1,
        )
        same[1] = lax.optimization_barrier((same[1], found[0]))[0]
        picks_of = {unit: (part, 0) for unit, part in zip(units, found)}
    other = [swap(rows, "node", 1) for rows in same]
    gathered = (*same, *other)

    def message_back(groups, dtype):
        used = [unit for group in groups for unit in group]
        return call(
            functools.partial(
                message_back_kernel,
                tuple(picks_of[unit][1] for unit in used),
                part_rows,
                ready,
                nodes,
                block,
                fanout,
            ),
            [shape((len(group) * part_rows, width), dtype) for group in groups],
            [
                who,
                *(picks_of[unit][0] for unit in used),
                *(slopes[unit] for unit in used),
                *gathered,
            ],
            smem=1,
        )

    first = [axes[p] for p in range(len(axes))]
    stay = [[j for j in range(sects) if not j & axis] for axis in first]
    sent = [[(j ^ axis, p) for j in stay[p]] for p, axis in enumerate(first)]
    given = message_back(sent, BF16)
    gathered = lax.optimization_barrier((*gathered, given[0]))[:-1]
    kept = message_back([[(j, p) for j in stay[p]] for p in range(len(axes))], F32)
    for step in range(len(axes)):
        order = [axes[(p + step) % len(axes)] for p in range(len(axes))]
        given = [swap(part, "sect", axis) for part, axis in zip(given, order)]
        if step + 1 == len(axes):
            break
        kept = [mine + part.astype(F32) for mine, part in zip(kept, given)]
        given = []
        for p, axis in enumerate(axes[(p + step + 1) % len(axes)] for p in range(len(axes))):
            rows = kept[p].reshape(len(stay[p]), part_rows, width)
            left = [j for j in stay[p] if not j & axis]
            given.append(
                jnp.concatenate([rows[stay[p].index(j ^ axis)] for j in left]).astype(BF16)
            )
            kept[p] = jnp.concatenate([rows[stay[p].index(j)] for j in left])
            stay[p] = left
    (grid_grad,) = call(
        grid_back_kernel,
        [shape((grid_rows, width), BF16)],
        [*kept, *given, enc_weight],
    )
    return (mesh_out[None], grid_grad)


def solution(mesh):
    return jax.shard_map(
        body,
        mesh=mesh,
        in_specs=(
            P(("sect", "node"), None),
            P(("sect", "node"), None),
            P(("sect", "node"), None),
            P(("sect", "node"), None),
            P(),
            P(),
            P("node", "sect", None),
            P(),
            P("sect", "node", None, None, None),
            P("node", "sect", None),
            P(),
            P("node", "sect", None),
        ),
        out_specs=(P("node", "sect", None), P(("sect", "node"), None)),
        check_vma=False,
    )
```

```python
import functools
import math

import jax
import jax.numpy as jnp
from jax import lax
from jax.experimental import pallas as pl
from jax.experimental.pallas import tpu as pltpu
from jax.sharding import PartitionSpec as P

F32 = jnp.float32
BF16 = jnp.bfloat16
LANES = 128
META_ROWS = 16
CHUNKS = 2
MIB = 1024 * 1024


def sigmoid(value):
    return 0.5 * jnp.tanh(0.5 * value) + 0.5


def silu(value):
    return value * sigmoid(value)


def slope(value):
    sig = sigmoid(value)
    return sig * (1.0 + value * (1.0 - sig))


def dot(left, right):
    return jnp.dot(left, right, preferred_element_type=F32)


def dot_t(left, right):
    return lax.dot_general(left, right, (((1,), (1,)), ((), ())), preferred_element_type=F32)


def halves(value):
    high = value.astype(BF16)
    return high, (value - high.astype(F32)).astype(BF16)


def back_dot(grad, weight):
    rows = grad.shape[0]
    both = dot_t(jnp.concatenate(halves(grad), axis=0), weight)
    return both[:rows] + both[rows:]


def mark(equal):
    return jnp.where(equal, 1.0, 0.0).astype(BF16)


def iota(shape, axis):
    return lax.broadcasted_iota(jnp.int32, shape, axis)


def norm_parts(mixed):
    mean = jnp.mean(mixed, axis=-1, keepdims=True)
    centred = mixed - mean
    scale = lax.rsqrt(jnp.mean(centred * centred, axis=-1, keepdims=True) + 1e-05)
    return centred * scale, scale


def norm_back(grad, normed, scale):
    pull = grad * slope(normed)
    return scale * (
        pull
        - jnp.mean(pull, axis=-1, keepdims=True)
        - normed * jnp.mean(pull * normed, axis=-1, keepdims=True)
    )


def pack_kernel(block, feat, lens, owner, dst, *refs):
    *outs, held, own_held, dst_held, sems = refs
    rows = feat.shape[0] // len(outs)
    pairs = [(lens, held), (owner, own_held), (dst, dst_held)]
    pairs += [
        (feat.at[i * rows : (i + 1) * rows, :], out.at[:rows, :]) for i, out in enumerate(outs)
    ]
    copies = [
        pltpu.make_async_copy(source, target, sems.at[i])
        for i, (source, target) in enumerate(pairs)
    ]
    for copy in copies:
        copy.start()
    for copy in copies[:3]:
        copy.wait()
    high, middle = halves(held[...])
    low = (held[...] - high.astype(F32) - middle.astype(F32)).astype(BF16)
    far = dst_held[...]
    section = far // block
    found = [v.astype(F32) for v in (high, middle, low)]
    found += [v.astype(F32) for v in (own_held[...], section, far - section * block)]
    fill = META_ROWS - 6 * lens.shape[0]
    found.append(jnp.zeros((fill, feat.shape[0]), F32))
    meta = jnp.concatenate(found, axis=0).astype(BF16)
    rest = jnp.zeros((META_ROWS, feat.shape[1] - rows), BF16)
    for i, out in enumerate(outs):
        out[rows:, :] = jnp.concatenate([meta[:, i * rows : (i + 1) * rows], rest], axis=1)
    for copy in copies[3:]:
        copy.wait()


def index_kernel(block, parts, *refs):
    wanted, far_weight, far_vec = refs[:2], refs[2], refs[3]
    pick, pick_t, source, source_t, weight, vec, sends, src_row, sems = refs[4:]
    pairs = ((wanted[0], sends), (wanted[1], src_row), (far_vec, vec), (far_weight, weight))
    copies = [
        pltpu.make_async_copy(start, target, sems.at[i])
        for i, (start, target) in enumerate(pairs)
    ]
    for copy in copies:
        copy.start()
    for copy in copies[:2]:
        copy.wait()
    sects, count, nodes = sends.shape
    pieces = pick.shape[0]
    at = iota((1, pieces), 1)
    part, row = at % parts, at // parts
    peer = row // count
    whose = mark(iota((nodes, pieces), 0) == peer % nodes)
    place = jnp.zeros((1, pieces), F32)
    for t in range(sects):
        found = dot(sends[t].astype(F32).astype(BF16), whose)
        for c in range(count):
            here = jnp.logical_and(peer // nodes == t, row % count == c)
            place = place + jnp.where(here, found[c : c + 1], 0.0)
    place = place + (part * block).astype(F32)
    pick_t[...] = mark(iota((parts * block, pieces), 0) == place.astype(jnp.int32))
    turned = jnp.broadcast_to(place, (8, pieces)).T[:, :1].astype(jnp.int32)
    pick[...] = mark(iota((pieces, parts * block), 1) == turned)
    table_len = source_t.shape[0]
    column = src_row[...].astype(F32).T.astype(jnp.int32)
    ids = iota((block, table_len), 1)
    ids_t = iota((table_len, block), 0)
    for k in range(src_row.shape[0]):
        rows = slice(k * block, (k + 1) * block)
        source[rows, :] = mark(ids == column[:, k : k + 1])
        source_t[:, rows] = mark(ids_t == src_row[k : k + 1, :])
    for copy in copies[2:]:
        copy.wait()


def edge_data(feat, at, rows):
    return feat[at + rows : at + rows + META_ROWS, :rows].astype(F32)


def edge_length(meta, fanout, k):
    high, middle, low = (meta[:, t * fanout + k : t * fanout + k + 1] for t in range(3))
    return high + middle + low


def spot_of(pick, fanout, k, section, node, nodes, block):
    owner, where, place = (pick((3 + t) * fanout + k).astype(jnp.int32) for t in range(3))
    apart = jnp.bitwise_xor(owner, node)
    order = lax.shift_right_logical(apart, 1) + jnp.bitwise_and(apart, 1) * (nodes // 2)
    return jnp.where(where == section, order * block + place, -1)


def add_rows(out, base, message, spots, before):
    step = min(out.shape[0], 512)

    def chunk(c, carry):
        start = pl.multiple_of(c * step, step)
        ids = iota((step, spots.shape[1]), 0) + (base + start)
        part = dot(mark(ids == spots[...]), message[...])
        for ref in before:
            part = part + ref[pl.ds(base + start, step), :]
        out[pl.ds(start, step), :] = part.astype(out.dtype)
        return carry

    lax.fori_loop(0, out.shape[0] // step, chunk, 0)


def encode_kernel(spans, nodes, block, fanout, rows, last, who, *refs):
    count = len(spans)
    feats = refs[:count]
    weight, vec = refs[count : count + 2]
    *before, out, message, spots = refs[count + 2 :]
    section, node = who[0], who[1]
    pre = 0.5 * dot(
        jnp.concatenate([feat[at : at + rows, :] for feat, at in zip(feats, spans)], axis=0),
        weight[...],
    )
    part = 0.5 * vec[...]
    for j in range(count):
        meta = edge_data(feats[j], spans[j], rows)
        turned = meta.T
        for k in range(fanout):
            at = (j * fanout + k) * rows
            act = pre[j * rows : (j + 1) * rows] + edge_length(turned, fanout, k) * part
            message[at : at + rows, :] = (act + act * jnp.tanh(act)).astype(BF16)
            spots[:, at : at + rows] = spot_of(
                lambda t, meta=meta: meta[t : t + 1], fanout, k, section, node, nodes, block
            )
    add_rows(out, nodes // 2 * block if last else 0, message, spots, before)


def keep_kernel(message, spots, before, out):
    add_rows(out, 0, message, spots, [before])


def slope_kernel(spans, fanout, rows, *refs):
    count = len(spans)
    feats = refs[:count]
    weight, vec = refs[count : count + 2]
    outs = refs[count + 2 :]
    for feat, at, out in zip(feats, spans, outs):
        pre = dot(feat[at : at + rows, :], weight[...])
        turned = edge_data(feat, at, rows).T
        for k in range(fanout):
            act = pre + edge_length(turned, fanout, k) * vec[...]
            out[k * rows : (k + 1) * rows, :] = slope(act).astype(BF16)


def halo_rows(state, pick, parts):
    stacked = jnp.concatenate(
        [state[:, i * LANES : (i + 1) * LANES] for i in range(parts)], axis=0
    )
    return dot(pick, stacked).astype(BF16)


def join_pieces(pieces, parts):
    count = pieces.shape[0]
    rows = count // parts
    at = iota((count, count), 0)
    onehot = mark(iota((count, count), 1) == at % rows * parts + at // rows)
    found = dot(onehot, pieces).astype(BF16)
    return jnp.concatenate([found[i * rows : (i + 1) * rows] for i in range(parts)], axis=1)


def cut_pieces(rows, parts):
    each, count = rows.shape[0], rows.shape[0] * parts
    at = iota((count, count), 0)
    onehot = mark(iota((count, count), 1) == at % parts * each + at // parts)
    stacked = jnp.concatenate(
        [rows[:, i * LANES : (i + 1) * LANES] for i in range(parts)], axis=0
    )
    return dot(onehot, stacked).astype(BF16)


def add_pieces(pieces, pick_t, block, parts):
    total = dot(pick_t, pieces)
    return jnp.concatenate([total[i * block : (i + 1) * block] for i in range(parts)], axis=1)


def start_kernel(parts, sums, *refs):
    received, (init, weight, pick, state, mesh_pre, halo) = refs[:-6], refs[-6:]
    agg = sums[...]
    for ref in received:
        agg = agg + ref[...].astype(F32)
    pre = dot(agg.astype(BF16), weight[...])
    mesh_pre[...] = pre
    new = (init[...].astype(F32) + silu(pre)).astype(BF16)
    state[...] = new
    halo[...] = halo_rows(new, pick[...], parts)


def layer_forward(state, pieces, source, weights, parts):
    block = state.shape[0]
    halo = join_pieces(pieces, parts)
    table = jnp.concatenate([state, halo], axis=0)
    from_src = 0.5 * dot(table, weights(0))
    to_dst = 0.5 * dot(state, weights(1))
    gathered = dot(source[...], from_src.astype(BF16))
    agg = jnp.zeros(state.shape, F32)
    slopes = []
    for k in range(source.shape[0] // block):
        joined = gathered[k * block : (k + 1) * block] + to_dst
        bend = jnp.tanh(joined)
        agg = agg + (joined + joined * bend)
        joined, bend = joined.astype(BF16), bend.astype(BF16)
        slopes.append(1 + bend + joined * (1 - bend * bend))
    mixed = dot(state, weights(2)) + dot(agg.astype(BF16), weights(3))
    return mixed, slopes


def layer_back(grad, mixed, slopes, source_t, weights):
    block = grad.shape[0]
    normed, scale = norm_parts(mixed)
    grad_mixed = norm_back(grad, normed, scale)
    grad_state = grad + back_dot(grad_mixed, weights(2))
    grad_agg = 0.5 * back_dot(grad_mixed, weights(3))
    low = grad_agg.astype(BF16)
    total = jnp.zeros(grad.shape, F32)
    for found in slopes:
        total = total + found.astype(F32)
    total = grad_agg * total
    pieces = [low * found for found in slopes]
    grad_src = dot(source_t[...], jnp.concatenate(pieces, axis=0))
    grad_state = grad_state + back_dot(total, weights(1))
    grad_table = back_dot(grad_src, weights(0))
    return grad_state + grad_table[:block], grad_table[block:]


def layer_weights(weights, layer):
    return lambda i: weights[layer, i]


def first_kernel(
    layer, parts, state, pieces, source, weights, pick, new, mixed, slopes, halo
):
    block = state.shape[0]
    own = state[...]
    used = layer_weights(weights, layer)
    value, found = layer_forward(own, pieces[...], source, used, parts)
    mixed[...] = value
    for k, part in enumerate(found):
        slopes[k * block : (k + 1) * block, :] = part
    normed, _ = norm_parts(value)
    result = (own.astype(F32) + silu(normed)).astype(BF16)
    new[...] = result
    halo[...] = halo_rows(result, pick[...], parts)


def last_kernel(
    layer, parts, state, pieces, source, source_t, weights, cot, out, grad_own, grad_halo
):
    own = state[...]
    used = layer_weights(weights, layer)
    value, found = layer_forward(own, pieces[...], source, used, parts)
    normed, _ = norm_parts(value)
    out[...] = (own.astype(F32) + silu(normed)).astype(BF16)
    mine, sent = layer_back(cot[...].astype(F32), value, found, source_t, used)
    grad_own[...] = mine
    grad_halo[...] = cut_pieces(sent.astype(BF16), parts)


def back_kernel(
    layer,
    parts,
    mine,
    returned,
    pick_t,
    mixed,
    slopes,
    source_t,
    weights,
    grad_own,
    grad_halo,
):
    block = mine.shape[0]
    grad = mine[...] + add_pieces(returned[...], pick_t[...], block, parts)
    fan = slopes.shape[0] // block
    found = [slopes[k * block : (k + 1) * block, :] for k in range(fan)]
    used = layer_weights(weights, layer)
    own, sent = layer_back(grad, mixed[...], found, source_t, used)
    grad_own[...] = own
    grad_halo[...] = cut_pieces(sent.astype(BF16), parts)


def mesh_back_kernel(parts, mine, returned, pick_t, mesh_pre, weight, out):
    block = mine.shape[0]
    grad = mine[...] + add_pieces(returned[...], pick_t[...], block, parts)
    out[...] = back_dot(grad * slope(mesh_pre[...]), weight[...]).astype(BF16)


def edge_marks(feat, at, rows, nodes, block, fanout, who):
    turned = edge_data(feat, at, rows).T
    ids = iota((rows, nodes * block), 1)
    return [
        mark(
            ids
            == spot_of(
                lambda t: turned[:, t : t + 1], fanout, k, who[0], who[1], nodes, block
            )
        )
        for k in range(fanout)
    ]


def mark_kernel(spans, rows, nodes, block, fanout, who, *refs):
    feats, state = refs[: len(spans)], refs[len(spans)]
    *outs, final = refs[len(spans) + 1 :]
    final[...] = state[...]
    for feat, at, out in zip(feats, spans, outs):
        for k, found in enumerate(edge_marks(feat, at, rows, nodes, block, fanout, who)):
            out[k * rows : (k + 1) * rows, :] = found


def message_back_kernel(spans, rows, ready, nodes, block, fanout, who, *refs):
    count = len(spans)
    feats, slopes = refs[:count], refs[count : 2 * count]
    outs = refs[2 * count :]
    grads, outs = outs[:nodes], outs[nodes:]
    marks = []
    for feat, at in zip(feats, spans):
        if ready:
            marks.append(feat[...])
        else:
            marks += edge_marks(feat, at, rows, nodes, block, fanout, who)
    picked = dot(
        jnp.concatenate(marks, axis=0), jnp.concatenate([ref[...] for ref in grads], axis=0)
    )
    size = outs[0].shape[1]
    chunks = slopes[0].shape[1] // size
    per = count * chunks // len(outs)
    for i in range(count):
        total = jnp.zeros((rows, slopes[0].shape[1]), F32)
        for k in range(fanout):
            at = (i * fanout + k) * rows
            part = slopes[i][k * rows : (k + 1) * rows, :].astype(F32)
            total = total + picked[at : at + rows] * part
        at = i % per * rows
        for c, out in enumerate(outs[i // per * chunks : (i // per + 1) * chunks]):
            out[at : at + rows, :] = total[:, c * size : (c + 1) * size].astype(out.dtype)


def grid_back_kernel(chunks, *refs):
    *parts, weight, out = refs
    count = len(parts) // 2
    total = [
        mine[...] + given[...].astype(F32) for mine, given in zip(parts[:count], parts[count:])
    ]
    each = count // chunks
    columns = [
        jnp.concatenate(total[c * each : (c + 1) * each], axis=0) for c in range(chunks)
    ]
    out[...] = back_dot(jnp.concatenate(columns, axis=1), weight[...]).astype(BF16)


def call(kernel, outs, args, smem=0, scratch=(), space=pltpu.VMEM, aliases=None):
    specs = [pl.BlockSpec(memory_space=pltpu.SMEM)] * smem
    specs += [pl.BlockSpec(memory_space=space)] * (len(args) - smem)
    moved = sum(a.size * a.dtype.itemsize for a in list(args) + list(outs))
    held = sum(math.prod(a.shape) * 4 for a in scratch)
    limit = 2 * (moved + held) + 6 * MIB
    result = pl.pallas_call(
        kernel,
        out_shape=list(outs),
        in_specs=specs,
        out_specs=[pl.BlockSpec(memory_space=pltpu.VMEM)] * len(outs),
        scratch_shapes=list(scratch),
        input_output_aliases=aliases or {},
        compiler_params=pltpu.CompilerParams(vmem_limit_bytes=limit),
        cost_estimate=pl.CostEstimate(
            flops=0, bytes_accessed=moved, transcendentals=0
        ),
    )(*args)
    return result


def shape(dims, dtype):
    return jax.ShapeDtypeStruct(dims, dtype)


def swap(value, axis, apart):
    size = lax.axis_size(axis)
    return lax.ppermute(value, axis, [(i, i ^ apart) for i in range(size)])


def body(
    grid_feat,
    edge_len,
    g2m_owner,
    g2m_dst,
    enc_weight,
    enc_vec,
    mesh_init,
    mesh_weight,
    halo_send,
    mesh_src,
    proc_weight,
    cot,
):
    nodes = lax.axis_size("node")
    sects = lax.axis_size("sect")
    width = grid_feat.shape[1]
    grid_rows, fanout = edge_len.shape
    block = mesh_init.shape[1]
    parts = width // LANES
    both = ("sect", "node")
    who = jnp.stack([lax.axis_index("sect"), lax.axis_index("node")]).astype(jnp.int32)

    axes = [1 << i for i in range(sects.bit_length() - 1)]
    part_rows = grid_rows // len(axes)
    ends = pltpu.VMEM((fanout, grid_rows), jnp.int32)
    packed = call(
        functools.partial(pack_kernel, block),
        [shape((part_rows + META_ROWS, width), BF16)] * len(axes),
        [
            pltpu.with_memory_space_constraint(value, pltpu.HBM)
            for value in (grid_feat, edge_len.T, g2m_owner.T, g2m_dst.T)
        ],
        scratch=[
            pltpu.VMEM((fanout, grid_rows), F32),
            ends,
            ends,
            pltpu.SemaphoreType.DMA((3 + len(axes),)),
        ],
        space=pltpu.HBM,
    )
    where = {(0, p): (part, 0) for p, part in enumerate(packed)}
    steps = [[(0, p) for p in range(len(axes))]]
    held, names = list(packed), [[0] for _ in axes]
    for step in range(len(axes)):
        given = [
            swap(part, "sect", axes[(p + step) % len(axes)]) for p, part in enumerate(held)
        ]
        steps.append([])
        for p, part in enumerate(given):
            axis = axes[(p + step) % len(axes)]
            for i, j in enumerate(list(names[p])):
                where[j ^ axis, p] = (part, i * packed[0].shape[0])
                names[p].append(j ^ axis)
                steps[-1].append((j ^ axis, p))
        held = [jnp.concatenate(pair, axis=0) for pair in zip(held, given)]
    sends = halo_send[0, 0].transpose(0, 2, 1)
    src_row = mesh_src[0].T
    fan = src_row.shape[0]
    pieces = sends.size * parts
    table_len = block + sends.size
    pick, pick_t, source, source_t, weight, vec = call(
        functools.partial(index_kernel, block, parts),
        [
            shape((pieces, parts * block), BF16),
            shape((parts * block, pieces), BF16),
            shape((fan * block, table_len), BF16),
            shape((table_len, fan * block), BF16),
            shape(enc_weight.shape, BF16),
            shape((1, width), F32),
        ],
        [
            pltpu.with_memory_space_constraint(value, pltpu.HBM)
            for value in (sends, src_row, enc_weight, enc_vec[None, :])
        ],
        scratch=[
            pltpu.VMEM(sends.shape, jnp.int32),
            pltpu.VMEM(src_row.shape, jnp.int32),
            pltpu.SemaphoreType.DMA((4,)),
        ],
        space=pltpu.HBM,
    )

    half = nodes // 2
    sums_shape = shape((nodes * block, width), F32)

    def encode(units, last, before):
        edges = len(units) * part_rows * fanout
        used = [where[unit] for unit in units]
        args = [who, *(part for part, _ in used), weight, vec, *before]
        outs = [
            shape((half * block, width), BF16) if last else sums_shape,
            shape((edges, width), BF16),
            shape((1, edges), jnp.int32),
        ]
        return call(
            functools.partial(
                encode_kernel,
                tuple(at for _, at in used),
                nodes,
                block,
                fanout,
                part_rows,
                last,
            ),
            outs if last else outs[:1],
            args,
            smem=1,
            scratch=() if last else [pltpu.VMEM(s.shape, s.dtype) for s in outs[1:]],
            aliases={len(args) - 1: 0} if before and not last else None,
        )

    before = []
    for units in steps[:-1]:
        before = encode(units, False, before)
    cross, message, spots = encode(steps[-1], True, before)
    (keep,) = call(
        keep_kernel, [shape((half * block, width), BF16)], [message, spots, *before]
    )

    pair = keep.astype(F32) + swap(cross, "node", 1).astype(F32)
    pair = pair.reshape(half, block, width)
    arrived = [
        swap(pair[q].astype(BF16), "node", 2 * q) for q in reversed(range(1, half))
    ]

    units = [(j, p) for j in range(sects) for p in range(len(axes))]
    slopes = call(
        functools.partial(
            slope_kernel, tuple(where[unit][1] for unit in units), fanout, part_rows
        ),
        [shape((fanout * part_rows, width), BF16)] * len(units),
        [*(where[unit][0] for unit in units), weight, vec],
    )
    tied = lax.optimization_barrier((*arrived, *slopes))
    arrived, slopes = tied[: half - 1], dict(zip(units, tied[half - 1 :]))

    halo_shape = shape((pieces, LANES), BF16)
    row_low, row_high = shape((block, width), BF16), shape((block, width), F32)

    def exchange(value):
        return lax.all_to_all(value, both, split_axis=0, concat_axis=0, tiled=True)

    state, mesh_pre, halo = call(
        functools.partial(start_kernel, parts),
        [row_low, row_high, halo_shape],
        [pair[0], *arrived, mesh_init[0], mesh_weight, pick],
    )
    assert proc_weight.shape[0] == 2
    state, mixed, slope_first, halo = call(
        functools.partial(first_kernel, 0, parts),
        [row_low, row_high, shape((fan * block, width), BF16), halo_shape],
        [state, exchange(halo), source, proc_weight, pick],
    )
    mesh_out, grad, halo = call(
        functools.partial(last_kernel, 1, parts),
        [row_low, row_high, halo_shape],
        [state, exchange(halo), source, source_t, proc_weight, cot[0]],
    )
    grad, halo = call(
        functools.partial(back_kernel, 0, parts),
        [row_high, halo_shape],
        [grad, exchange(halo), pick_t, mixed, slope_first, source_t, proc_weight],
    )
    (grad_sum,) = call(
        functools.partial(mesh_back_kernel, parts),
        [row_low],
        [grad, exchange(halo), pick_t, mesh_pre, mesh_weight],
    )

    same = [grad_sum] + [swap(grad_sum, "node", 2 * q) for q in range(1, half)]
    ready = nodes * block <= 8 * LANES
    picks_of = {unit: where[unit] for unit in units}
    if ready:
        seen, _ = lax.optimization_barrier((who, grad_sum))
        *found, mesh_out = call(
            functools.partial(
                mark_kernel,
                tuple(where[unit][1] for unit in units),
                part_rows,
                nodes,
                block,
                fanout,
            ),
            [shape((fanout * part_rows, nodes * block), BF16)] * len(units) + [row_low],
            [seen, *(where[unit][0] for unit in units), mesh_out],
            smem=1,
        )
        same[1] = lax.optimization_barrier((same[1], found[0]))[0]
        picks_of = {unit: (part, 0) for unit, part in zip(units, found)}
    other = [swap(rows, "node", 1) for rows in same]
    gathered = (*same, *other)

    def message_back(groups, dtype):
        used = [unit for group in groups for unit in group]
        return call(
            functools.partial(
                message_back_kernel,
                tuple(picks_of[unit][1] for unit in used),
                part_rows,
                ready,
                nodes,
                block,
                fanout,
            ),
            [
                shape((len(group) * part_rows, width // CHUNKS), dtype)
                for group in groups
                for _ in range(CHUNKS)
            ],
            [
                who,
                *(picks_of[unit][0] for unit in used),
                *(slopes[unit] for unit in used),
                *gathered,
            ],
            smem=1,
        )

    first = [axes[p] for p in range(len(axes))]
    stay = [[j for j in range(sects) if not j & axis] for axis in first]
    sent = [[(j ^ axis, p) for j in stay[p]] for p, axis in enumerate(first)]
    given = message_back(sent, BF16)
    gathered = lax.optimization_barrier((*gathered, given[0]))[:-1]
    kept = message_back([[(j, p) for j in stay[p]] for p in range(len(axes))], F32)
    turns = [(p, c) for c in range(CHUNKS) for p in range(len(axes))]
    given = [given[p * CHUNKS + c] for p, c in turns]
    kept = [kept[p * CHUNKS + c] for p, c in turns]
    for step in range(len(axes)):
        given = [
            swap(part, "sect", axes[(p + step) % len(axes)])
            for part, (p, _) in zip(given, turns)
        ]
        if step + 1 == len(axes):
            break
        kept = [mine + part.astype(F32) for mine, part in zip(kept, given)]
        given, left = [], []
        for p in range(len(axes)):
            axis = axes[(p + step + 1) % len(axes)]
            left.append([j for j in stay[p] if not j & axis])
        for i, (p, _) in enumerate(turns):
            axis = axes[(p + step + 1) % len(axes)]
            rows = kept[i].reshape(len(stay[p]), part_rows, width // CHUNKS)
            given.append(
                jnp.concatenate([rows[stay[p].index(j ^ axis)] for j in left[p]]).astype(BF16)
            )
            kept[i] = jnp.concatenate([rows[stay[p].index(j)] for j in left[p]])
        stay = left
    (grid_grad,) = call(
        functools.partial(grid_back_kernel, CHUNKS),
        [shape((grid_rows, width), BF16)],
        [*kept, *given, enc_weight],
    )
    return (mesh_out[None], grid_grad)


def solution(mesh):
    return jax.shard_map(
        body,
        mesh=mesh,
        in_specs=(
            P(("sect", "node"), None),
            P(("sect", "node"), None),
            P(("sect", "node"), None),
            P(("sect", "node"), None),
            P(),
            P(),
            P("node", "sect", None),
            P(),
            P("sect", "node", None, None, None),
            P("node", "sect", None),
            P(),
            P("node", "sect", None),
        ),
        out_specs=(P("node", "sect", None), P(("sect", "node"), None)),
        check_vma=False,
    )
```

```python
import functools
import math

import jax
import jax.numpy as jnp
from jax import lax
from jax.experimental import pallas as pl
from jax.experimental.pallas import tpu as pltpu
from jax.sharding import PartitionSpec as P

F32 = jnp.float32
BF16 = jnp.bfloat16
LANES = 128
META_ROWS = 16
CHUNKS = 2
MIB = 1024 * 1024


def sigmoid(value):
    return 0.5 * jnp.tanh(0.5 * value) + 0.5


def silu(value):
    return value * sigmoid(value)


def slope(value):
    sig = sigmoid(value)
    return sig * (1.0 + value * (1.0 - sig))


def dot(left, right):
    return jnp.dot(left, right, preferred_element_type=F32)


def dot_t(left, right):
    return lax.dot_general(left, right, (((1,), (1,)), ((), ())), preferred_element_type=F32)


def halves(value):
    high = value.astype(BF16)
    return high, (value - high.astype(F32)).astype(BF16)


def back_dot(grad, weight):
    rows = grad.shape[0]
    both = dot_t(jnp.concatenate(halves(grad), axis=0), weight)
    return both[:rows] + both[rows:]


def mark(equal):
    return jnp.where(equal, 1.0, 0.0).astype(BF16)


def iota(shape, axis):
    return lax.broadcasted_iota(jnp.int32, shape, axis)


def norm_parts(mixed):
    mean = jnp.mean(mixed, axis=-1, keepdims=True)
    centred = mixed - mean
    scale = lax.rsqrt(jnp.mean(centred * centred, axis=-1, keepdims=True) + 1e-05)
    return centred * scale, scale


def norm_back(grad, normed, scale):
    pull = grad * slope(normed)
    return scale * (
        pull
        - jnp.mean(pull, axis=-1, keepdims=True)
        - normed * jnp.mean(pull * normed, axis=-1, keepdims=True)
    )


def pack_kernel(block, feat, lens, owner, dst, *refs):
    *outs, held, own_held, dst_held, sems = refs
    rows = feat.shape[0] // len(outs)
    pairs = [(lens, held), (owner, own_held), (dst, dst_held)]
    pairs += [
        (feat.at[i * rows : (i + 1) * rows, :], out.at[:rows, :]) for i, out in enumerate(outs)
    ]
    copies = [
        pltpu.make_async_copy(source, target, sems.at[i])
        for i, (source, target) in enumerate(pairs)
    ]
    for copy in copies:
        copy.start()
    for copy in copies[:3]:
        copy.wait()
    high, middle = halves(held[...])
    low = (held[...] - high.astype(F32) - middle.astype(F32)).astype(BF16)
    far = dst_held[...]
    section = far // block
    found = [v.astype(F32) for v in (high, middle, low)]
    found += [v.astype(F32) for v in (own_held[...], section, far - section * block)]
    fill = META_ROWS - 6 * lens.shape[0]
    found.append(jnp.zeros((fill, feat.shape[0]), F32))
    meta = jnp.concatenate(found, axis=0).astype(BF16)
    rest = jnp.zeros((META_ROWS, feat.shape[1] - rows), BF16)
    for i, out in enumerate(outs):
        out[rows:, :] = jnp.concatenate([meta[:, i * rows : (i + 1) * rows], rest], axis=1)
    for copy in copies[3:]:
        copy.wait()


def index_kernel(block, parts, *refs):
    wanted, far_weight, far_vec = refs[:2], refs[2], refs[3]
    pick, pick_t, source, source_t, weight, vec, sends, src_row, sems = refs[4:]
    pairs = ((wanted[0], sends), (wanted[1], src_row), (far_vec, vec), (far_weight, weight))
    copies = [
        pltpu.make_async_copy(start, target, sems.at[i])
        for i, (start, target) in enumerate(pairs)
    ]
    for copy in copies:
        copy.start()
    for copy in copies[:2]:
        copy.wait()
    sects, count, nodes = sends.shape
    pieces = pick.shape[0]
    at = iota((1, pieces), 1)
    part, row = at % parts, at // parts
    peer = row // count
    whose = mark(iota((nodes, pieces), 0) == peer % nodes)
    place = jnp.zeros((1, pieces), F32)
    for t in range(sects):
        found = dot(sends[t].astype(F32).astype(BF16), whose)
        for c in range(count):
            here = jnp.logical_and(peer // nodes == t, row % count == c)
            place = place + jnp.where(here, found[c : c + 1], 0.0)
    place = place + (part * block).astype(F32)
    pick_t[...] = mark(iota((parts * block, pieces), 0) == place.astype(jnp.int32))
    turned = jnp.broadcast_to(place, (8, pieces)).T[:, :1].astype(jnp.int32)
    pick[...] = mark(iota((pieces, parts * block), 1) == turned)
    table_len = source_t.shape[0]
    column = src_row[...].astype(F32).T.astype(jnp.int32)
    ids = iota((block, table_len), 1)
    ids_t = iota((table_len, block), 0)
    for k in range(src_row.shape[0]):
        rows = slice(k * block, (k + 1) * block)
        source[rows, :] = mark(ids == column[:, k : k + 1])
        source_t[:, rows] = mark(ids_t == src_row[k : k + 1, :])
    for copy in copies[2:]:
        copy.wait()


def edge_data(feat, at, rows):
    return feat[at + rows : at + rows + META_ROWS, :rows].astype(F32)


def edge_length(meta, fanout, k):
    high, middle, low = (meta[:, t * fanout + k : t * fanout + k + 1] for t in range(3))
    return high + middle + low


def spot_of(pick, fanout, k, section, node, nodes, block):
    owner, where, place = (pick((3 + t) * fanout + k).astype(jnp.int32) for t in range(3))
    apart = jnp.bitwise_xor(owner, node)
    order = lax.shift_right_logical(apart, 1) + jnp.bitwise_and(apart, 1) * (nodes // 2)
    return jnp.where(where == section, order * block + place, -1)


def add_rows(out, base, message, spots, before):
    step = min(out.shape[0], 512)

    def chunk(c, carry):
        start = pl.multiple_of(c * step, step)
        ids = iota((step, spots.shape[1]), 0) + (base + start)
        part = dot(mark(ids == spots[...]), message[...])
        for ref in before:
            part = part + ref[pl.ds(base + start, step), :]
        out[pl.ds(start, step), :] = part.astype(out.dtype)
        return carry

    lax.fori_loop(0, out.shape[0] // step, chunk, 0)


def encode_kernel(spans, nodes, block, fanout, rows, last, who, *refs):
    count = len(spans)
    feats = refs[:count]
    weight, vec = refs[count : count + 2]
    *before, out, message, spots = refs[count + 2 :]
    section, node = who[0], who[1]
    pre = 0.5 * dot(
        jnp.concatenate([feat[at : at + rows, :] for feat, at in zip(feats, spans)], axis=0),
        weight[...],
    )
    part = 0.5 * vec[...]
    for j in range(count):
        meta = edge_data(feats[j], spans[j], rows)
        turned = meta.T
        for k in range(fanout):
            at = (j * fanout + k) * rows
            act = pre[j * rows : (j + 1) * rows] + edge_length(turned, fanout, k) * part
            message[at : at + rows, :] = (act + act * jnp.tanh(act)).astype(BF16)
            spots[:, at : at + rows] = spot_of(
                lambda t, meta=meta: meta[t : t + 1], fanout, k, section, node, nodes, block
            )
    add_rows(out, nodes // 2 * block if last else 0, message, spots, before)


def keep_kernel(message, spots, before, out):
    add_rows(out, 0, message, spots, [before])


def slope_kernel(spans, fanout, rows, *refs):
    count = len(spans)
    feats = refs[:count]
    weight, vec = refs[count : count + 2]
    outs = refs[count + 2 :]
    for feat, at, out in zip(feats, spans, outs):
        pre = dot(feat[at : at + rows, :], weight[...])
        turned = edge_data(feat, at, rows).T
        for k in range(fanout):
            act = pre + edge_length(turned, fanout, k) * vec[...]
            out[k * rows : (k + 1) * rows, :] = slope(act).astype(BF16)


def halo_rows(state, pick, parts):
    stacked = jnp.concatenate(
        [state[:, i * LANES : (i + 1) * LANES] for i in range(parts)], axis=0
    )
    return dot(pick, stacked).astype(BF16)


def join_pieces(pieces, parts):
    count = pieces.shape[0]
    rows = count // parts
    at = iota((count, count), 0)
    onehot = mark(iota((count, count), 1) == at % rows * parts + at // rows)
    found = dot(onehot, pieces).astype(BF16)
    return jnp.concatenate([found[i * rows : (i + 1) * rows] for i in range(parts)], axis=1)


def cut_pieces(rows, parts):
    each, count = rows.shape[0], rows.shape[0] * parts
    at = iota((count, count), 0)
    onehot = mark(iota((count, count), 1) == at % parts * each + at // parts)
    stacked = jnp.concatenate(
        [rows[:, i * LANES : (i + 1) * LANES] for i in range(parts)], axis=0
    )
    return dot(onehot, stacked).astype(BF16)


def add_pieces(pieces, pick_t, block, parts):
    total = dot(pick_t, pieces)
    return jnp.concatenate([total[i * block : (i + 1) * block] for i in range(parts)], axis=1)


def start_kernel(parts, sums, *refs):
    received, (init, weight, pick, state, mesh_pre, halo) = refs[:-6], refs[-6:]
    agg = sums[...]
    for ref in received:
        agg = agg + ref[...].astype(F32)
    pre = dot(agg.astype(BF16), weight[...])
    mesh_pre[...] = pre
    new = (init[...].astype(F32) + silu(pre)).astype(BF16)
    state[...] = new
    halo[...] = halo_rows(new, pick[...], parts)


def layer_forward(state, pieces, source, weights, parts):
    block = state.shape[0]
    halo = join_pieces(pieces, parts)
    table = jnp.concatenate([state, halo], axis=0)
    from_src = 0.5 * dot(table, weights(0))
    to_dst = 0.5 * dot(state, weights(1))
    gathered = dot(source[...], from_src.astype(BF16))
    agg = jnp.zeros(state.shape, F32)
    slopes = []
    for k in range(source.shape[0] // block):
        joined = gathered[k * block : (k + 1) * block] + to_dst
        bend = jnp.tanh(joined)
        agg = agg + (joined + joined * bend)
        joined, bend = joined.astype(BF16), bend.astype(BF16)
        slopes.append(1 + bend + joined * (1 - bend * bend))
    mixed = dot(state, weights(2)) + dot(agg.astype(BF16), weights(3))
    return mixed, slopes


def layer_back(grad, mixed, slopes, source_t, weights):
    block = grad.shape[0]
    normed, scale = norm_parts(mixed)
    grad_mixed = norm_back(grad, normed, scale)
    grad_state = grad + back_dot(grad_mixed, weights(2))
    grad_agg = 0.5 * back_dot(grad_mixed, weights(3))
    low = grad_agg.astype(BF16)
    total = jnp.zeros(grad.shape, F32)
    for found in slopes:
        total = total + found.astype(F32)
    total = grad_agg * total
    pieces = [low * found for found in slopes]
    grad_src = dot(source_t[...], jnp.concatenate(pieces, axis=0))
    grad_state = grad_state + back_dot(total, weights(1))
    grad_table = back_dot(grad_src, weights(0))
    return grad_state + grad_table[:block], grad_table[block:]


def layer_weights(weights, layer):
    return lambda i: weights[layer, i]


def first_kernel(
    layer, parts, state, pieces, source, weights, pick, new, mixed, slopes, halo
):
    block = state.shape[0]
    own = state[...]
    used = layer_weights(weights, layer)
    value, found = layer_forward(own, pieces[...], source, used, parts)
    mixed[...] = value
    for k, part in enumerate(found):
        slopes[k * block : (k + 1) * block, :] = part
    normed, _ = norm_parts(value)
    result = (own.astype(F32) + silu(normed)).astype(BF16)
    new[...] = result
    halo[...] = halo_rows(result, pick[...], parts)


def last_kernel(
    layer, parts, state, pieces, source, source_t, weights, cot, out, grad_own, grad_halo
):
    own = state[...]
    used = layer_weights(weights, layer)
    value, found = layer_forward(own, pieces[...], source, used, parts)
    normed, _ = norm_parts(value)
    out[...] = (own.astype(F32) + silu(normed)).astype(BF16)
    mine, sent = layer_back(cot[...].astype(F32), value, found, source_t, used)
    grad_own[...] = mine
    grad_halo[...] = cut_pieces(sent.astype(BF16), parts)


def back_kernel(
    layer,
    parts,
    mine,
    returned,
    pick_t,
    mixed,
    slopes,
    source_t,
    weights,
    grad_own,
    grad_halo,
):
    block = mine.shape[0]
    grad = mine[...] + add_pieces(returned[...], pick_t[...], block, parts)
    fan = slopes.shape[0] // block
    found = [slopes[k * block : (k + 1) * block, :] for k in range(fan)]
    used = layer_weights(weights, layer)
    own, sent = layer_back(grad, mixed[...], found, source_t, used)
    grad_own[...] = own
    grad_halo[...] = cut_pieces(sent.astype(BF16), parts)


def mesh_back_kernel(parts, mine, returned, pick_t, mesh_pre, weight, out):
    block = mine.shape[0]
    grad = mine[...] + add_pieces(returned[...], pick_t[...], block, parts)
    out[...] = back_dot(grad * slope(mesh_pre[...]), weight[...]).astype(BF16)


def edge_marks(feat, at, rows, nodes, block, fanout, who):
    turned = edge_data(feat, at, rows).T
    ids = iota((rows, nodes * block), 1)
    return [
        mark(
            ids
            == spot_of(
                lambda t: turned[:, t : t + 1], fanout, k, who[0], who[1], nodes, block
            )
        )
        for k in range(fanout)
    ]


def mark_kernel(spans, rows, nodes, block, fanout, who, *refs):
    feats, state = refs[: len(spans)], refs[len(spans)]
    *outs, final = refs[len(spans) + 1 :]
    final[...] = state[...]
    for feat, at, out in zip(feats, spans, outs):
        for k, found in enumerate(edge_marks(feat, at, rows, nodes, block, fanout, who)):
            out[k * rows : (k + 1) * rows, :] = found


def message_back_kernel(spans, rows, ready, nodes, block, fanout, who, *refs):
    count = len(spans)
    feats, slopes = refs[:count], refs[count : 2 * count]
    outs = refs[2 * count :]
    grads, outs = outs[:nodes], outs[nodes:]
    marks = []
    for feat, at in zip(feats, spans):
        if ready:
            marks.append(feat[...])
        else:
            marks += edge_marks(feat, at, rows, nodes, block, fanout, who)
    picked = dot(
        jnp.concatenate(marks, axis=0), jnp.concatenate([ref[...] for ref in grads], axis=0)
    )
    size = outs[0].shape[1]
    chunks = slopes[0].shape[1] // size
    per = count * chunks // len(outs)
    for i in range(count):
        total = jnp.zeros((rows, slopes[0].shape[1]), F32)
        for k in range(fanout):
            at = (i * fanout + k) * rows
            part = slopes[i][k * rows : (k + 1) * rows, :].astype(F32)
            total = total + picked[at : at + rows] * part
        at = i % per * rows
        for c, out in enumerate(outs[i // per * chunks : (i // per + 1) * chunks]):
            out[at : at + rows, :] = total[:, c * size : (c + 1) * size].astype(out.dtype)


def grid_back_kernel(chunks, *refs):
    *parts, weight, out = refs
    count = len(parts) // 3
    rows = parts[0].shape[0]
    total = [
        parts[i][...]
        + parts[count + i][:rows, :].astype(F32)
        + parts[2 * count + i][...].astype(F32)
        for i in range(count)
    ]
    each = count // chunks
    columns = [
        jnp.concatenate(total[c * each : (c + 1) * each], axis=0) for c in range(chunks)
    ]
    out[...] = back_dot(jnp.concatenate(columns, axis=1), weight[...]).astype(BF16)


def call(kernel, outs, args, smem=0, scratch=(), space=pltpu.VMEM, aliases=None):
    specs = [pl.BlockSpec(memory_space=pltpu.SMEM)] * smem
    specs += [pl.BlockSpec(memory_space=space)] * (len(args) - smem)
    moved = sum(a.size * a.dtype.itemsize for a in list(args) + list(outs))
    held = sum(math.prod(a.shape) * 4 for a in scratch)
    limit = 2 * (moved + held) + 6 * MIB
    result = pl.pallas_call(
        kernel,
        out_shape=list(outs),
        in_specs=specs,
        out_specs=[pl.BlockSpec(memory_space=pltpu.VMEM)] * len(outs),
        scratch_shapes=list(scratch),
        input_output_aliases=aliases or {},
        compiler_params=pltpu.CompilerParams(vmem_limit_bytes=limit),
        cost_estimate=pl.CostEstimate(
            flops=0, bytes_accessed=moved, transcendentals=0
        ),
    )(*args)
    return result


def shape(dims, dtype):
    return jax.ShapeDtypeStruct(dims, dtype)


def swap(value, axis, apart):
    size = lax.axis_size(axis)
    return lax.ppermute(value, axis, [(i, i ^ apart) for i in range(size)])


def body(
    grid_feat,
    edge_len,
    g2m_owner,
    g2m_dst,
    enc_weight,
    enc_vec,
    mesh_init,
    mesh_weight,
    halo_send,
    mesh_src,
    proc_weight,
    cot,
):
    nodes = lax.axis_size("node")
    sects = lax.axis_size("sect")
    width = grid_feat.shape[1]
    grid_rows, fanout = edge_len.shape
    block = mesh_init.shape[1]
    parts = width // LANES
    both = ("sect", "node")
    who = jnp.stack([lax.axis_index("sect"), lax.axis_index("node")]).astype(jnp.int32)

    axes = [1 << i for i in range(sects.bit_length() - 1)]
    part_rows = grid_rows // len(axes)
    assert len(axes) == 2
    ends = pltpu.VMEM((fanout, grid_rows), jnp.int32)
    packed = call(
        functools.partial(pack_kernel, block),
        [shape((part_rows + META_ROWS, width), BF16)] * len(axes),
        [
            pltpu.with_memory_space_constraint(value, pltpu.HBM)
            for value in (grid_feat, edge_len.T, g2m_owner.T, g2m_dst.T)
        ],
        scratch=[
            pltpu.VMEM((fanout, grid_rows), F32),
            ends,
            ends,
            pltpu.SemaphoreType.DMA((3 + len(axes),)),
        ],
        space=pltpu.HBM,
    )
    where = {(0, p): (part, 0) for p, part in enumerate(packed)}
    steps = [[(0, p) for p in range(len(axes))]]
    held, names = list(packed), [[0] for _ in axes]
    for step in range(len(axes)):
        given = [
            swap(part, "sect", axes[(p + step) % len(axes)]) for p, part in enumerate(held)
        ]
        steps.append([])
        for p, part in enumerate(given):
            axis = axes[(p + step) % len(axes)]
            for i, j in enumerate(list(names[p])):
                where[j ^ axis, p] = (part, i * packed[0].shape[0])
                names[p].append(j ^ axis)
                steps[-1].append((j ^ axis, p))
        held = [jnp.concatenate(pair, axis=0) for pair in zip(held, given)]
    sends = halo_send[0, 0].transpose(0, 2, 1)
    src_row = mesh_src[0].T
    fan = src_row.shape[0]
    pieces = sends.size * parts
    table_len = block + sends.size
    pick, pick_t, source, source_t, weight, vec = call(
        functools.partial(index_kernel, block, parts),
        [
            shape((pieces, parts * block), BF16),
            shape((parts * block, pieces), BF16),
            shape((fan * block, table_len), BF16),
            shape((table_len, fan * block), BF16),
            shape(enc_weight.shape, BF16),
            shape((1, width), F32),
        ],
        [
            pltpu.with_memory_space_constraint(value, pltpu.HBM)
            for value in (sends, src_row, enc_weight, enc_vec[None, :])
        ],
        scratch=[
            pltpu.VMEM(sends.shape, jnp.int32),
            pltpu.VMEM(src_row.shape, jnp.int32),
            pltpu.SemaphoreType.DMA((4,)),
        ],
        space=pltpu.HBM,
    )

    half = nodes // 2
    sums_shape = shape((nodes * block, width), F32)

    def encode(units, last, before):
        edges = len(units) * part_rows * fanout
        used = [where[unit] for unit in units]
        args = [who, *(part for part, _ in used), weight, vec, *before]
        outs = [
            shape((half * block, width), BF16) if last else sums_shape,
            shape((edges, width), BF16),
            shape((1, edges), jnp.int32),
        ]
        return call(
            functools.partial(
                encode_kernel,
                tuple(at for _, at in used),
                nodes,
                block,
                fanout,
                part_rows,
                last,
            ),
            outs if last else outs[:1],
            args,
            smem=1,
            scratch=() if last else [pltpu.VMEM(s.shape, s.dtype) for s in outs[1:]],
            aliases={len(args) - 1: 0} if before and not last else None,
        )

    before = []
    for units in steps[:-1]:
        before = encode(units, False, before)
    cross, message, spots = encode(steps[-1], True, before)
    (keep,) = call(
        keep_kernel, [shape((half * block, width), BF16)], [message, spots, *before]
    )

    pair = keep.astype(F32) + swap(cross, "node", 1).astype(F32)
    pair = pair.reshape(half, block, width)
    arrived = [
        swap(pair[q].astype(BF16), "node", 2 * q) for q in reversed(range(1, half))
    ]

    units = [(j, p) for j in range(sects) for p in range(len(axes))]
    slopes = call(
        functools.partial(
            slope_kernel, tuple(where[unit][1] for unit in units), fanout, part_rows
        ),
        [shape((fanout * part_rows, width), BF16)] * len(units),
        [*(where[unit][0] for unit in units), weight, vec],
    )
    tied = lax.optimization_barrier((*arrived, *slopes))
    arrived, slopes = tied[: half - 1], dict(zip(units, tied[half - 1 :]))

    halo_shape = shape((pieces, LANES), BF16)
    row_low, row_high = shape((block, width), BF16), shape((block, width), F32)

    def exchange(value):
        return lax.all_to_all(value, both, split_axis=0, concat_axis=0, tiled=True)

    state, mesh_pre, halo = call(
        functools.partial(start_kernel, parts),
        [row_low, row_high, halo_shape],
        [pair[0], *arrived, mesh_init[0], mesh_weight, pick],
    )
    assert proc_weight.shape[0] == 2
    state, mixed, slope_first, halo = call(
        functools.partial(first_kernel, 0, parts),
        [row_low, row_high, shape((fan * block, width), BF16), halo_shape],
        [state, exchange(halo), source, proc_weight, pick],
    )
    mesh_out, grad, halo = call(
        functools.partial(last_kernel, 1, parts),
        [row_low, row_high, halo_shape],
        [state, exchange(halo), source, source_t, proc_weight, cot[0]],
    )
    grad, halo = call(
        functools.partial(back_kernel, 0, parts),
        [row_high, halo_shape],
        [grad, exchange(halo), pick_t, mixed, slope_first, source_t, proc_weight],
    )
    (grad_sum,) = call(
        functools.partial(mesh_back_kernel, parts),
        [row_low],
        [grad, exchange(halo), pick_t, mesh_pre, mesh_weight],
    )

    same = [swap(grad_sum, "node", 2 * q) for q in reversed(range(1, half))]
    same = [grad_sum, *same[::-1]]
    ready = nodes * block <= 8 * LANES
    picks_of = {unit: where[unit] for unit in units}
    if ready:
        seen, _ = lax.optimization_barrier((who, grad_sum))
        *found, mesh_out = call(
            functools.partial(
                mark_kernel,
                tuple(where[unit][1] for unit in units),
                part_rows,
                nodes,
                block,
                fanout,
            ),
            [shape((fanout * part_rows, nodes * block), BF16)] * len(units) + [row_low],
            [seen, *(where[unit][0] for unit in units), mesh_out],
            smem=1,
        )
        same[-1] = lax.optimization_barrier((same[-1], found[0]))[0]
        picks_of = {unit: (part, 0) for unit, part in zip(units, found)}
    other = [swap(rows, "node", 1) for rows in same[::-1]][::-1]
    gathered = (*same, *other)

    def message_back(groups, dtype):
        used = [unit for group in groups for unit in group]
        return call(
            functools.partial(
                message_back_kernel,
                tuple(picks_of[unit][1] for unit in used),
                part_rows,
                ready,
                nodes,
                block,
                fanout,
            ),
            [
                shape((len(group) * part_rows, width // CHUNKS), dtype)
                for group in groups
                for _ in range(CHUNKS)
            ],
            [
                who,
                *(picks_of[unit][0] for unit in used),
                *(slopes[unit] for unit in used),
                *gathered,
            ],
            smem=1,
        )

    first, then = axes, axes[::-1]
    chunks = [(p, c) for c in range(CHUNKS) for p in range(len(axes))]

    def ordered(found):
        return [found[p * CHUNKS + c] for p, c in chunks]

    given = ordered(
        message_back(
            [[(a, p), (a ^ b, p)] for p, (a, b) in enumerate(zip(first, then))], BF16
        )
    )
    gathered = lax.optimization_barrier((*gathered, *given))[: len(gathered)]
    passed = ordered(message_back([[(b, p)] for p, b in enumerate(then)], F32))
    gathered = lax.optimization_barrier((*gathered, *passed))[: len(gathered)]
    given = [swap(part, "sect", first[p]) for part, (p, _) in zip(given, chunks)]
    passed = [
        (mine + part[part_rows:].astype(F32)).astype(BF16)
        for mine, part in zip(passed, given)
    ]
    kept = ordered(message_back([[(0, p)] for p in range(len(axes))], F32))
    passed = [swap(part, "sect", then[p]) for part, (p, _) in zip(passed, chunks)]
    (grid_grad,) = call(
        functools.partial(grid_back_kernel, CHUNKS),
        [shape((grid_rows, width), BF16)],
        [*kept, *given, *passed, enc_weight],
    )
    return (mesh_out[None], grid_grad)


def solution(mesh):
    return jax.shard_map(
        body,
        mesh=mesh,
        in_specs=(
            P(("sect", "node"), None),
            P(("sect", "node"), None),
            P(("sect", "node"), None),
            P(("sect", "node"), None),
            P(),
            P(),
            P("node", "sect", None),
            P(),
            P("sect", "node", None, None, None),
            P("node", "sect", None),
            P(),
            P("node", "sect", None),
        ),
        out_specs=(P("node", "sect", None), P(("sect", "node"), None)),
        check_vma=False,
    )
```

```python
import functools
import math

import jax
import jax.numpy as jnp
from jax import lax
from jax.experimental import pallas as pl
from jax.experimental.pallas import tpu as pltpu
from jax.sharding import PartitionSpec as P

F32 = jnp.float32
BF16 = jnp.bfloat16
LANES = 128
META_ROWS = 16
CHUNKS = 2
MIB = 1024 * 1024


def sigmoid(value):
    return 0.5 * jnp.tanh(0.5 * value) + 0.5


def silu(value):
    return value * sigmoid(value)


def slope(value):
    sig = sigmoid(value)
    return sig * (1.0 + value * (1.0 - sig))


def dot(left, right):
    return jnp.dot(left, right, preferred_element_type=F32)


def dot_t(left, right):
    return lax.dot_general(left, right, (((1,), (1,)), ((), ())), preferred_element_type=F32)


def halves(value):
    high = value.astype(BF16)
    return high, (value - high.astype(F32)).astype(BF16)


def back_dot(grad, weight):
    rows = grad.shape[0]
    both = dot_t(jnp.concatenate(halves(grad), axis=0), weight)
    return both[:rows] + both[rows:]


def mark(equal):
    return jnp.where(equal, 1.0, 0.0).astype(BF16)


def iota(shape, axis):
    return lax.broadcasted_iota(jnp.int32, shape, axis)


def norm_parts(mixed):
    mean = jnp.mean(mixed, axis=-1, keepdims=True)
    centred = mixed - mean
    scale = lax.rsqrt(jnp.mean(centred * centred, axis=-1, keepdims=True) + 1e-05)
    return centred * scale, scale


def norm_back(grad, normed, scale):
    pull = grad * slope(normed)
    return scale * (
        pull
        - jnp.mean(pull, axis=-1, keepdims=True)
        - normed * jnp.mean(pull * normed, axis=-1, keepdims=True)
    )


def pack_kernel(block, feat, lens, owner, dst, *refs):
    *outs, held, own_held, dst_held, sems = refs
    rows = feat.shape[0] // len(outs)
    pairs = [(lens, held), (owner, own_held), (dst, dst_held)]
    pairs += [
        (feat.at[i * rows : (i + 1) * rows, :], out.at[:rows, :]) for i, out in enumerate(outs)
    ]
    copies = [
        pltpu.make_async_copy(source, target, sems.at[i])
        for i, (source, target) in enumerate(pairs)
    ]
    for copy in copies:
        copy.start()
    for copy in copies[:3]:
        copy.wait()
    high, middle = halves(held[...])
    low = (held[...] - high.astype(F32) - middle.astype(F32)).astype(BF16)
    far = dst_held[...]
    section = far // block
    found = [v.astype(F32) for v in (high, middle, low)]
    found += [v.astype(F32) for v in (own_held[...], section, far - section * block)]
    fill = META_ROWS - 6 * lens.shape[0]
    found.append(jnp.zeros((fill, feat.shape[0]), F32))
    meta = jnp.concatenate(found, axis=0).astype(BF16)
    rest = jnp.zeros((META_ROWS, feat.shape[1] - rows), BF16)
    for i, out in enumerate(outs):
        out[rows:, :] = jnp.concatenate([meta[:, i * rows : (i + 1) * rows], rest], axis=1)
    for copy in copies[3:]:
        copy.wait()


def index_kernel(block, parts, *refs):
    wanted, far_weight, far_vec = refs[:2], refs[2], refs[3]
    pick, pick_t, source, source_t, weight, vec, sends, src_row, sems = refs[4:]
    pairs = ((wanted[0], sends), (wanted[1], src_row), (far_vec, vec), (far_weight, weight))
    copies = [
        pltpu.make_async_copy(start, target, sems.at[i])
        for i, (start, target) in enumerate(pairs)
    ]
    for copy in copies:
        copy.start()
    for copy in copies[:2]:
        copy.wait()
    sects, count, nodes = sends.shape
    pieces = pick.shape[0]
    at = iota((1, pieces), 1)
    part, row = at % parts, at // parts
    peer = row // count
    whose = mark(iota((nodes, pieces), 0) == peer % nodes)
    place = jnp.zeros((1, pieces), F32)
    for t in range(sects):
        found = dot(sends[t].astype(F32).astype(BF16), whose)
        for c in range(count):
            here = jnp.logical_and(peer // nodes == t, row % count == c)
            place = place + jnp.where(here, found[c : c + 1], 0.0)
    place = place + (part * block).astype(F32)
    pick_t[...] = mark(iota((parts * block, pieces), 0) == place.astype(jnp.int32))
    turned = jnp.broadcast_to(place, (8, pieces)).T[:, :1].astype(jnp.int32)
    pick[...] = mark(iota((pieces, parts * block), 1) == turned)
    table_len = source_t.shape[0]
    column = src_row[...].astype(F32).T.astype(jnp.int32)
    ids = iota((block, table_len), 1)
    ids_t = iota((table_len, block), 0)
    for k in range(src_row.shape[0]):
        rows = slice(k * block, (k + 1) * block)
        source[rows, :] = mark(ids == column[:, k : k + 1])
        source_t[:, rows] = mark(ids_t == src_row[k : k + 1, :])
    for copy in copies[2:]:
        copy.wait()


def edge_data(feat, at, rows):
    return feat[at + rows : at + rows + META_ROWS, :rows].astype(F32)


def edge_length(meta, fanout, k):
    high, middle, low = (meta[:, t * fanout + k : t * fanout + k + 1] for t in range(3))
    return high + middle + low


def spot_of(pick, fanout, k, section, node, nodes, block):
    owner, where, place = (pick((3 + t) * fanout + k).astype(jnp.int32) for t in range(3))
    apart = jnp.bitwise_xor(owner, node)
    order = lax.shift_right_logical(apart, 1) + jnp.bitwise_and(apart, 1) * (nodes // 2)
    return jnp.where(where == section, order * block + place, -1)


def add_rows(out, base, message, spots, before):
    step = min(out.shape[0], 512)

    def chunk(c, carry):
        start = pl.multiple_of(c * step, step)
        ids = iota((step, spots.shape[1]), 0) + (base + start)
        part = dot(mark(ids == spots[...]), message[...])
        for ref in before:
            part = part + ref[pl.ds(base + start, step), :]
        out[pl.ds(start, step), :] = part.astype(out.dtype)
        return carry

    lax.fori_loop(0, out.shape[0] // step, chunk, 0)


def encode_kernel(spans, nodes, block, fanout, rows, last, who, *refs):
    count = len(spans)
    feats = refs[:count]
    weight, vec = refs[count : count + 2]
    *before, out, message, spots = refs[count + 2 :]
    section, node = who[0], who[1]
    pre = 0.5 * dot(
        jnp.concatenate([feat[at : at + rows, :] for feat, at in zip(feats, spans)], axis=0),
        weight[...],
    )
    part = 0.5 * vec[...]
    for j in range(count):
        meta = edge_data(feats[j], spans[j], rows)
        turned = meta.T
        for k in range(fanout):
            at = (j * fanout + k) * rows
            act = pre[j * rows : (j + 1) * rows] + edge_length(turned, fanout, k) * part
            message[at : at + rows, :] = (act + act * jnp.tanh(act)).astype(BF16)
            spots[:, at : at + rows] = spot_of(
                lambda t, meta=meta: meta[t : t + 1], fanout, k, section, node, nodes, block
            )
    add_rows(out, nodes // 2 * block if last else 0, message, spots, before)


def keep_kernel(message, spots, before, out):
    add_rows(out, 0, message, spots, [before])


def slope_kernel(spans, fanout, rows, *refs):
    count = len(spans)
    feats = refs[:count]
    weight, vec = refs[count : count + 2]
    outs = refs[count + 2 :]
    for feat, at, out in zip(feats, spans, outs):
        pre = dot(feat[at : at + rows, :], weight[...])
        turned = edge_data(feat, at, rows).T
        for k in range(fanout):
            act = pre + edge_length(turned, fanout, k) * vec[...]
            out[k * rows : (k + 1) * rows, :] = slope(act).astype(BF16)


def halo_rows(state, pick, parts):
    stacked = jnp.concatenate(
        [state[:, i * LANES : (i + 1) * LANES] for i in range(parts)], axis=0
    )
    return dot(pick, stacked).astype(BF16)


def join_pieces(pieces, parts):
    count = pieces.shape[0]
    rows = count // parts
    at = iota((count, count), 0)
    onehot = mark(iota((count, count), 1) == at % rows * parts + at // rows)
    found = dot(onehot, pieces).astype(BF16)
    return jnp.concatenate([found[i * rows : (i + 1) * rows] for i in range(parts)], axis=1)


def cut_pieces(rows, parts):
    each, count = rows.shape[0], rows.shape[0] * parts
    at = iota((count, count), 0)
    onehot = mark(iota((count, count), 1) == at % parts * each + at // parts)
    stacked = jnp.concatenate(
        [rows[:, i * LANES : (i + 1) * LANES] for i in range(parts)], axis=0
    )
    return dot(onehot, stacked).astype(BF16)


def add_pieces(pieces, pick_t, block, parts):
    total = dot(pick_t, pieces)
    return jnp.concatenate([total[i * block : (i + 1) * block] for i in range(parts)], axis=1)


def start_kernel(parts, sums, *refs):
    received, (init, weight, pick, state, mesh_pre, halo) = refs[:-6], refs[-6:]
    agg = sums[...]
    for ref in received:
        agg = agg + ref[...].astype(F32)
    pre = dot(agg.astype(BF16), weight[...])
    mesh_pre[...] = pre
    new = (init[...].astype(F32) + silu(pre)).astype(BF16)
    state[...] = new
    halo[...] = halo_rows(new, pick[...], parts)


def layer_forward(state, pieces, source, weights, parts):
    block = state.shape[0]
    halo = join_pieces(pieces, parts)
    table = jnp.concatenate([state, halo], axis=0)
    from_src = 0.5 * dot(table, weights(0))
    to_dst = 0.5 * dot(state, weights(1))
    gathered = dot(source[...], from_src.astype(BF16))
    agg = jnp.zeros(state.shape, F32)
    slopes = []
    for k in range(source.shape[0] // block):
        joined = gathered[k * block : (k + 1) * block] + to_dst
        bend = jnp.tanh(joined)
        agg = agg + (joined + joined * bend)
        joined, bend = joined.astype(BF16), bend.astype(BF16)
        slopes.append(1 + bend + joined * (1 - bend * bend))
    mixed = dot(state, weights(2)) + dot(agg.astype(BF16), weights(3))
    return mixed, slopes


def layer_back(grad, mixed, slopes, source_t, weights):
    block = grad.shape[0]
    normed, scale = norm_parts(mixed)
    grad_mixed = norm_back(grad, normed, scale)
    grad_state = grad + back_dot(grad_mixed, weights(2))
    grad_agg = 0.5 * dot_t(grad_mixed.astype(BF16), weights(3))
    low = grad_agg.astype(BF16)
    total = jnp.zeros(grad.shape, F32)
    for found in slopes:
        total = total + found.astype(F32)
    total = grad_agg * total
    pieces = [low * found for found in slopes]
    grad_src = dot(source_t[...], jnp.concatenate(pieces, axis=0))
    grad_state = grad_state + back_dot(total, weights(1))
    grad_table = dot_t(grad_src.astype(BF16), weights(0))
    return grad_state + grad_table[:block], grad_table[block:]


def layer_weights(weights, layer):
    return lambda i: weights[layer, i]


def first_kernel(
    layer, parts, state, pieces, source, weights, pick, new, mixed, slopes, halo
):
    block = state.shape[0]
    own = state[...]
    used = layer_weights(weights, layer)
    value, found = layer_forward(own, pieces[...], source, used, parts)
    mixed[...] = value
    for k, part in enumerate(found):
        slopes[k * block : (k + 1) * block, :] = part
    normed, _ = norm_parts(value)
    result = (own.astype(F32) + silu(normed)).astype(BF16)
    new[...] = result
    halo[...] = halo_rows(result, pick[...], parts)


def last_kernel(
    layer, parts, state, pieces, source, source_t, weights, cot, out, grad_own, grad_halo
):
    own = state[...]
    used = layer_weights(weights, layer)
    value, found = layer_forward(own, pieces[...], source, used, parts)
    normed, _ = norm_parts(value)
    out[...] = (own.astype(F32) + silu(normed)).astype(BF16)
    mine, sent = layer_back(cot[...].astype(F32), value, found, source_t, used)
    grad_own[...] = mine
    grad_halo[...] = cut_pieces(sent.astype(BF16), parts)


def back_kernel(
    layer,
    parts,
    mine,
    returned,
    pick_t,
    mixed,
    slopes,
    source_t,
    weights,
    grad_own,
    grad_halo,
):
    block = mine.shape[0]
    grad = mine[...] + add_pieces(returned[...], pick_t[...], block, parts)
    fan = slopes.shape[0] // block
    found = [slopes[k * block : (k + 1) * block, :] for k in range(fan)]
    used = layer_weights(weights, layer)
    own, sent = layer_back(grad, mixed[...], found, source_t, used)
    grad_own[...] = own
    grad_halo[...] = cut_pieces(sent.astype(BF16), parts)


def mesh_back_kernel(parts, mine, returned, pick_t, mesh_pre, weight, out):
    block = mine.shape[0]
    grad = mine[...] + add_pieces(returned[...], pick_t[...], block, parts)
    out[...] = back_dot(grad * slope(mesh_pre[...]), weight[...]).astype(BF16)


def edge_marks(feat, at, rows, nodes, block, fanout, who):
    turned = edge_data(feat, at, rows).T
    ids = iota((rows, nodes * block), 1)
    return [
        mark(
            ids
            == spot_of(
                lambda t: turned[:, t : t + 1], fanout, k, who[0], who[1], nodes, block
            )
        )
        for k in range(fanout)
    ]


def mark_kernel(spans, rows, nodes, block, fanout, who, *refs):
    feats, state = refs[: len(spans)], refs[len(spans)]
    *outs, final = refs[len(spans) + 1 :]
    final[...] = state[...]
    for feat, at, out in zip(feats, spans, outs):
        for k, found in enumerate(edge_marks(feat, at, rows, nodes, block, fanout, who)):
            out[k * rows : (k + 1) * rows, :] = found


def message_back_kernel(spans, rows, ready, nodes, block, fanout, who, *refs):
    count = len(spans)
    feats, slopes = refs[:count], refs[count : 2 * count]
    outs = refs[2 * count :]
    grads, outs = outs[:nodes], outs[nodes:]
    marks = []
    for feat, at in zip(feats, spans):
        if ready:
            marks.append(feat[...])
        else:
            marks += edge_marks(feat, at, rows, nodes, block, fanout, who)
    same, other = grads[: nodes // 2][::-1], grads[nodes // 2 :][::-1]
    picked = dot(
        jnp.concatenate(marks, axis=0),
        jnp.concatenate([ref[...] for ref in (*same, *other)], axis=0),
    )
    size = outs[0].shape[1]
    chunks = slopes[0].shape[1] // size
    per = count * chunks // len(outs)
    for i in range(count):
        total = jnp.zeros((rows, slopes[0].shape[1]), F32)
        for k in range(fanout):
            at = (i * fanout + k) * rows
            part = slopes[i][k * rows : (k + 1) * rows, :].astype(F32)
            total = total + picked[at : at + rows] * part
        at = i % per * rows
        for c, out in enumerate(outs[i // per * chunks : (i // per + 1) * chunks]):
            out[at : at + rows, :] = total[:, c * size : (c + 1) * size].astype(out.dtype)


def grid_back_kernel(chunks, *refs):
    *parts, weight, out = refs
    count = len(parts) // 3
    rows = parts[0].shape[0]
    total = [
        parts[i][...]
        + parts[count + i][:rows, :].astype(F32)
        + parts[2 * count + i][...].astype(F32)
        for i in range(count)
    ]
    each = count // chunks
    columns = [
        jnp.concatenate(total[c * each : (c + 1) * each], axis=0) for c in range(chunks)
    ]
    out[...] = back_dot(jnp.concatenate(columns, axis=1), weight[...]).astype(BF16)


def call(kernel, outs, args, smem=0, scratch=(), space=pltpu.VMEM, aliases=None):
    specs = [pl.BlockSpec(memory_space=pltpu.SMEM)] * smem
    specs += [pl.BlockSpec(memory_space=space)] * (len(args) - smem)
    moved = sum(a.size * a.dtype.itemsize for a in list(args) + list(outs))
    held = sum(math.prod(a.shape) * 4 for a in scratch)
    limit = 2 * (moved + held) + 6 * MIB
    result = pl.pallas_call(
        kernel,
        out_shape=list(outs),
        in_specs=specs,
        out_specs=[pl.BlockSpec(memory_space=pltpu.VMEM)] * len(outs),
        scratch_shapes=list(scratch),
        input_output_aliases=aliases or {},
        compiler_params=pltpu.CompilerParams(vmem_limit_bytes=limit),
        cost_estimate=pl.CostEstimate(
            flops=0, bytes_accessed=moved, transcendentals=0
        ),
    )(*args)
    return result


def shape(dims, dtype):
    return jax.ShapeDtypeStruct(dims, dtype)


def swap(value, axis, apart):
    size = lax.axis_size(axis)
    return lax.ppermute(value, axis, [(i, i ^ apart) for i in range(size)])


def body(
    grid_feat,
    edge_len,
    g2m_owner,
    g2m_dst,
    enc_weight,
    enc_vec,
    mesh_init,
    mesh_weight,
    halo_send,
    mesh_src,
    proc_weight,
    cot,
):
    nodes = lax.axis_size("node")
    sects = lax.axis_size("sect")
    width = grid_feat.shape[1]
    grid_rows, fanout = edge_len.shape
    block = mesh_init.shape[1]
    parts = width // LANES
    both = ("sect", "node")
    who = jnp.stack([lax.axis_index("sect"), lax.axis_index("node")]).astype(jnp.int32)

    axes = [1 << i for i in range(sects.bit_length() - 1)]
    part_rows = grid_rows // len(axes)
    assert len(axes) == 2
    ends = pltpu.VMEM((fanout, grid_rows), jnp.int32)
    packed = call(
        functools.partial(pack_kernel, block),
        [shape((part_rows + META_ROWS, width), BF16)] * len(axes),
        [
            pltpu.with_memory_space_constraint(value, pltpu.HBM)
            for value in (grid_feat, edge_len.T, g2m_owner.T, g2m_dst.T)
        ],
        scratch=[
            pltpu.VMEM((fanout, grid_rows), F32),
            ends,
            ends,
            pltpu.SemaphoreType.DMA((3 + len(axes),)),
        ],
        space=pltpu.HBM,
    )
    where = {(0, p): (part, 0) for p, part in enumerate(packed)}
    steps = [[(0, p) for p in range(len(axes))]]
    held, names = list(packed), [[0] for _ in axes]
    for step in range(len(axes)):
        given = [
            swap(part, "sect", axes[(p + step) % len(axes)]) for p, part in enumerate(held)
        ]
        steps.append([])
        for p, part in enumerate(given):
            axis = axes[(p + step) % len(axes)]
            for i, j in enumerate(list(names[p])):
                where[j ^ axis, p] = (part, i * packed[0].shape[0])
                names[p].append(j ^ axis)
                steps[-1].append((j ^ axis, p))
        held = [jnp.concatenate(pair, axis=0) for pair in zip(held, given)]
    sends = halo_send[0, 0].transpose(0, 2, 1)
    src_row = mesh_src[0].T
    fan = src_row.shape[0]
    pieces = sends.size * parts
    table_len = block + sends.size
    pick, pick_t, source, source_t, weight, vec = call(
        functools.partial(index_kernel, block, parts),
        [
            shape((pieces, parts * block), BF16),
            shape((parts * block, pieces), BF16),
            shape((fan * block, table_len), BF16),
            shape((table_len, fan * block), BF16),
            shape(enc_weight.shape, BF16),
            shape((1, width), F32),
        ],
        [
            pltpu.with_memory_space_constraint(value, pltpu.HBM)
            for value in (sends, src_row, enc_weight, enc_vec[None, :])
        ],
        scratch=[
            pltpu.VMEM(sends.shape, jnp.int32),
            pltpu.VMEM(src_row.shape, jnp.int32),
            pltpu.SemaphoreType.DMA((4,)),
        ],
        space=pltpu.HBM,
    )

    half = nodes // 2
    sums_shape = shape((nodes * block, width), F32)

    def encode(units, last, before):
        edges = len(units) * part_rows * fanout
        used = [where[unit] for unit in units]
        args = [who, *(part for part, _ in used), weight, vec, *before]
        outs = [
            shape((half * block, width), BF16) if last else sums_shape,
            shape((edges, width), BF16),
            shape((1, edges), jnp.int32),
        ]
        return call(
            functools.partial(
                encode_kernel,
                tuple(at for _, at in used),
                nodes,
                block,
                fanout,
                part_rows,
                last,
            ),
            outs if last else outs[:1],
            args,
            smem=1,
            scratch=() if last else [pltpu.VMEM(s.shape, s.dtype) for s in outs[1:]],
            aliases={len(args) - 1: 0} if before and not last else None,
        )

    before = []
    for units in steps[:-1]:
        before = encode(units, False, before)
    cross, message, spots = encode(steps[-1], True, before)
    (keep,) = call(
        keep_kernel, [shape((half * block, width), BF16)], [message, spots, *before]
    )

    pair = keep.astype(F32) + swap(cross, "node", 1).astype(F32)
    pair = pair.reshape(half, block, width)
    arrived = [
        swap(pair[q].astype(BF16), "node", 2 * q) for q in reversed(range(1, half))
    ]

    units = [(j, p) for j in range(sects) for p in range(len(axes))]
    slopes = call(
        functools.partial(
            slope_kernel, tuple(where[unit][1] for unit in units), fanout, part_rows
        ),
        [shape((fanout * part_rows, width), BF16)] * len(units),
        [*(where[unit][0] for unit in units), weight, vec],
    )
    tied = lax.optimization_barrier((*arrived, *slopes))
    arrived, slopes = tied[: half - 1], dict(zip(units, tied[half - 1 :]))

    halo_shape = shape((pieces, LANES), BF16)
    row_low, row_high = shape((block, width), BF16), shape((block, width), F32)

    def exchange(value):
        return lax.all_to_all(value, both, split_axis=0, concat_axis=0, tiled=True)

    state, mesh_pre, halo = call(
        functools.partial(start_kernel, parts),
        [row_low, row_high, halo_shape],
        [pair[0], *arrived, mesh_init[0], mesh_weight, pick],
    )
    assert proc_weight.shape[0] == 2
    state, mixed, slope_first, halo = call(
        functools.partial(first_kernel, 0, parts),
        [row_low, row_high, shape((fan * block, width), BF16), halo_shape],
        [state, exchange(halo), source, proc_weight, pick],
    )
    mesh_out, grad, halo = call(
        functools.partial(last_kernel, 1, parts),
        [row_low, row_high, halo_shape],
        [state, exchange(halo), source, source_t, proc_weight, cot[0]],
    )
    grad, halo = call(
        functools.partial(back_kernel, 0, parts),
        [row_high, halo_shape],
        [grad, exchange(halo), pick_t, mixed, slope_first, source_t, proc_weight],
    )
    (grad_sum,) = call(
        functools.partial(mesh_back_kernel, parts),
        [row_low],
        [grad, exchange(halo), pick_t, mesh_pre, mesh_weight],
    )

    same = [swap(grad_sum, "node", 2 * q) for q in reversed(range(1, half))]
    same = [grad_sum, *same[::-1]]
    ready = nodes * block <= 8 * LANES
    picks_of = {unit: where[unit] for unit in units}
    if ready:
        seen, _ = lax.optimization_barrier((who, grad_sum))
        *found, mesh_out = call(
            functools.partial(
                mark_kernel,
                tuple(where[unit][1] for unit in units),
                part_rows,
                nodes,
                block,
                fanout,
            ),
            [shape((fanout * part_rows, nodes * block), BF16)] * len(units) + [row_low],
            [seen, *(where[unit][0] for unit in units), mesh_out],
            smem=1,
        )
        same[-1] = lax.optimization_barrier((same[-1], found[0]))[0]
        picks_of = {unit: (part, 0) for unit, part in zip(units, found)}
    other = [swap(rows, "node", 1) for rows in same[::-1]][::-1]
    gathered = (*same[::-1], *other[::-1])

    def message_back(groups, dtype):
        used = [unit for group in groups for unit in group]
        return call(
            functools.partial(
                message_back_kernel,
                tuple(picks_of[unit][1] for unit in used),
                part_rows,
                ready,
                nodes,
                block,
                fanout,
            ),
            [
                shape((len(group) * part_rows, width // CHUNKS), dtype)
                for group in groups
                for _ in range(CHUNKS)
            ],
            [
                who,
                *(picks_of[unit][0] for unit in used),
                *(slopes[unit] for unit in used),
                *gathered,
            ],
            smem=1,
        )

    first, then = axes, axes[::-1]
    chunks = [(p, c) for c in range(CHUNKS) for p in range(len(axes))]

    def ordered(found):
        return [found[p * CHUNKS + c] for p, c in chunks]

    given = ordered(
        message_back(
            [[(a, p), (a ^ b, p)] for p, (a, b) in enumerate(zip(first, then))], BF16
        )
    )
    gathered = lax.optimization_barrier((*gathered, *given))[: len(gathered)]
    passed = ordered(message_back([[(b, p)] for p, b in enumerate(then)], F32))
    gathered = lax.optimization_barrier((*gathered, *passed))[: len(gathered)]
    given = [swap(part, "sect", first[p]) for part, (p, _) in zip(given, chunks)]
    passed = [
        (mine + part[part_rows:].astype(F32)).astype(BF16)
        for mine, part in zip(passed, given)
    ]
    kept = ordered(message_back([[(0, p)] for p in range(len(axes))], F32))
    passed = [swap(part, "sect", then[p]) for part, (p, _) in zip(passed, chunks)]
    (grid_grad,) = call(
        functools.partial(grid_back_kernel, CHUNKS),
        [shape((grid_rows, width), BF16)],
        [*kept, *given, *passed, enc_weight],
    )
    return (mesh_out[None], grid_grad)


def solution(mesh):
    return jax.shard_map(
        body,
        mesh=mesh,
        in_specs=(
            P(("sect", "node"), None),
            P(("sect", "node"), None),
            P(("sect", "node"), None),
            P(("sect", "node"), None),
            P(),
            P(),
            P("node", "sect", None),
            P(),
            P("sect", "node", None, None, None),
            P("node", "sect", None),
            P(),
            P("node", "sect", None),
        ),
        out_specs=(P("node", "sect", None), P(("sect", "node"), None)),
        check_vma=False,
    )
```

```python
import functools
import math

import jax
import jax.numpy as jnp
from jax import lax
from jax.experimental import pallas as pl
from jax.experimental.pallas import tpu as pltpu
from jax.sharding import PartitionSpec as P

F32 = jnp.float32
BF16 = jnp.bfloat16
LANES = 128
META_ROWS = 16
CHUNKS = 2
MIB = 1024 * 1024


def sigmoid(value):
    return 0.5 * jnp.tanh(0.5 * value) + 0.5


def silu(value):
    return value * sigmoid(value)


def slope(value):
    sig = sigmoid(value)
    return sig * (1.0 + value * (1.0 - sig))


def dot(left, right):
    return jnp.dot(left, right, preferred_element_type=F32)


def dot_t(left, right):
    return lax.dot_general(left, right, (((1,), (1,)), ((), ())), preferred_element_type=F32)


def halves(value):
    high = value.astype(BF16)
    return high, (value - high.astype(F32)).astype(BF16)


def back_dot(grad, weight):
    rows = grad.shape[0]
    both = dot_t(jnp.concatenate(halves(grad), axis=0), weight)
    return both[:rows] + both[rows:]


def mark(equal):
    return jnp.where(equal, 1.0, 0.0).astype(BF16)


def iota(shape, axis):
    return lax.broadcasted_iota(jnp.int32, shape, axis)


def norm_parts(mixed):
    mean = jnp.mean(mixed, axis=-1, keepdims=True)
    centred = mixed - mean
    scale = lax.rsqrt(jnp.mean(centred * centred, axis=-1, keepdims=True) + 1e-05)
    return centred * scale, scale


def norm_back(grad, normed, scale):
    pull = grad * slope(normed)
    return scale * (
        pull
        - jnp.mean(pull, axis=-1, keepdims=True)
        - normed * jnp.mean(pull * normed, axis=-1, keepdims=True)
    )


def pack_kernel(block, feat, lens, owner, dst, *refs):
    *outs, held, own_held, dst_held, sems = refs
    rows = feat.shape[0] // len(outs)
    pairs = [(lens, held), (owner, own_held), (dst, dst_held)]
    pairs += [
        (feat.at[i * rows : (i + 1) * rows, :], out.at[:rows, :]) for i, out in enumerate(outs)
    ]
    copies = [
        pltpu.make_async_copy(source, target, sems.at[i])
        for i, (source, target) in enumerate(pairs)
    ]
    for copy in copies:
        copy.start()
    for copy in copies[:3]:
        copy.wait()
    high, middle = halves(held[...])
    low = (held[...] - high.astype(F32) - middle.astype(F32)).astype(BF16)
    far = dst_held[...]
    section = far // block
    found = [v.astype(F32) for v in (high, middle, low)]
    found += [v.astype(F32) for v in (own_held[...], section, far - section * block)]
    fill = META_ROWS - 6 * lens.shape[0]
    found.append(jnp.zeros((fill, feat.shape[0]), F32))
    meta = jnp.concatenate(found, axis=0).astype(BF16)
    rest = jnp.zeros((META_ROWS, feat.shape[1] - rows), BF16)
    for i, out in enumerate(outs):
        out[rows:, :] = jnp.concatenate([meta[:, i * rows : (i + 1) * rows], rest], axis=1)
    for copy in copies[3:]:
        copy.wait()


def load_kernel(far_weight, far_vec, weight, vec, sems):
    copies = [
        pltpu.make_async_copy(far_vec, vec, sems.at[0]),
        pltpu.make_async_copy(far_weight, weight, sems.at[1]),
    ]
    for copy in copies:
        copy.start()
    for copy in copies:
        copy.wait()


def index_kernel(block, parts, sends, src_row, pick, pick_t, source, source_t):
    sects, count, nodes = sends.shape
    pieces = pick.shape[0]
    at = iota((1, pieces), 1)
    part, row = at % parts, at // parts
    peer = row // count
    whose = mark(iota((nodes, pieces), 0) == peer % nodes)
    place = jnp.zeros((1, pieces), F32)
    for t in range(sects):
        found = dot(sends[t].astype(F32).astype(BF16), whose)
        for c in range(count):
            here = jnp.logical_and(peer // nodes == t, row % count == c)
            place = place + jnp.where(here, found[c : c + 1], 0.0)
    place = place + (part * block).astype(F32)
    pick_t[...] = mark(iota((parts * block, pieces), 0) == place.astype(jnp.int32))
    turned = jnp.broadcast_to(place, (8, pieces)).T[:, :1].astype(jnp.int32)
    pick[...] = mark(iota((pieces, parts * block), 1) == turned)
    table_len = source_t.shape[0]
    column = src_row[...].astype(F32).T.astype(jnp.int32)
    ids = iota((block, table_len), 1)
    ids_t = iota((table_len, block), 0)
    for k in range(src_row.shape[0]):
        rows = slice(k * block, (k + 1) * block)
        source[rows, :] = mark(ids == column[:, k : k + 1])
        source_t[:, rows] = mark(ids_t == src_row[k : k + 1, :])


def edge_data(feat, at, rows):
    return feat[at + rows : at + rows + META_ROWS, :rows].astype(F32)


def edge_length(meta, fanout, k):
    high, middle, low = (meta[:, t * fanout + k : t * fanout + k + 1] for t in range(3))
    return high + middle + low


def spot_of(pick, fanout, k, section, node, nodes, block):
    owner, where, place = (pick((3 + t) * fanout + k).astype(jnp.int32) for t in range(3))
    apart = jnp.bitwise_xor(owner, node)
    order = lax.shift_right_logical(apart, 1) + jnp.bitwise_and(apart, 1) * (nodes // 2)
    return jnp.where(where == section, order * block + place, -1)


def add_rows(out, base, message, spots, before):
    step = min(out.shape[0], 512)

    def chunk(c, carry):
        start = pl.multiple_of(c * step, step)
        ids = iota((step, spots.shape[1]), 0) + (base + start)
        part = dot(mark(ids == spots[...]), message[...])
        for ref in before:
            part = part + ref[pl.ds(base + start, step), :]
        out[pl.ds(start, step), :] = part.astype(out.dtype)
        return carry

    lax.fori_loop(0, out.shape[0] // step, chunk, 0)


def encode_kernel(spans, nodes, block, fanout, rows, last, who, *refs):
    count = len(spans)
    feats = refs[:count]
    weight, vec = refs[count : count + 2]
    *before, out, message, spots = refs[count + 2 :]
    section, node = who[0], who[1]
    pre = 0.5 * dot(
        jnp.concatenate([feat[at : at + rows, :] for feat, at in zip(feats, spans)], axis=0),
        weight[...],
    )
    part = 0.5 * vec[...]
    for j in range(count):
        meta = edge_data(feats[j], spans[j], rows)
        turned = meta.T
        for k in range(fanout):
            at = (j * fanout + k) * rows
            act = pre[j * rows : (j + 1) * rows] + edge_length(turned, fanout, k) * part
            message[at : at + rows, :] = (act + act * jnp.tanh(act)).astype(BF16)
            spots[:, at : at + rows] = spot_of(
                lambda t, meta=meta: meta[t : t + 1], fanout, k, section, node, nodes, block
            )
    add_rows(out, nodes // 2 * block if last else 0, message, spots, before)


def keep_kernel(message, spots, before, out):
    add_rows(out, 0, message, spots, [before])


def slope_kernel(spans, block, parts, fanout, rows, *refs):
    count = len(spans)
    feats = refs[:count]
    weight, vec, sends, src_row = refs[count : count + 4]
    outs, found = refs[count + 4 : -4], refs[-4:]
    for feat, at, out in zip(feats, spans, outs):
        pre = dot(feat[at : at + rows, :], weight[...])
        turned = edge_data(feat, at, rows).T
        for k in range(fanout):
            act = pre + edge_length(turned, fanout, k) * vec[...]
            out[k * rows : (k + 1) * rows, :] = slope(act).astype(BF16)
    index_kernel(block, parts, sends, src_row, *found)


def halo_rows(state, pick, parts):
    stacked = jnp.concatenate(
        [state[:, i * LANES : (i + 1) * LANES] for i in range(parts)], axis=0
    )
    return dot(pick, stacked).astype(BF16)


def join_pieces(pieces, parts):
    count = pieces.shape[0]
    rows = count // parts
    at = iota((count, count), 0)
    onehot = mark(iota((count, count), 1) == at % rows * parts + at // rows)
    found = dot(onehot, pieces).astype(BF16)
    return jnp.concatenate([found[i * rows : (i + 1) * rows] for i in range(parts)], axis=1)


def cut_pieces(rows, parts):
    each, count = rows.shape[0], rows.shape[0] * parts
    at = iota((count, count), 0)
    onehot = mark(iota((count, count), 1) == at % parts * each + at // parts)
    stacked = jnp.concatenate(
        [rows[:, i * LANES : (i + 1) * LANES] for i in range(parts)], axis=0
    )
    return dot(onehot, stacked).astype(BF16)


def add_pieces(pieces, pick_t, block, parts):
    total = dot(pick_t, pieces)
    return jnp.concatenate([total[i * block : (i + 1) * block] for i in range(parts)], axis=1)


def start_kernel(parts, sums, *refs):
    received, (init, weight, pick, state, mesh_pre, halo) = refs[:-6], refs[-6:]
    agg = sums[...]
    for ref in received:
        agg = agg + ref[...].astype(F32)
    pre = dot(agg.astype(BF16), weight[...])
    mesh_pre[...] = pre
    new = (init[...].astype(F32) + silu(pre)).astype(BF16)
    state[...] = new
    halo[...] = halo_rows(new, pick[...], parts)


def layer_forward(state, pieces, source, weights, parts):
    block = state.shape[0]
    halo = join_pieces(pieces, parts)
    table = jnp.concatenate([state, halo], axis=0)
    from_src = 0.5 * dot(table, weights(0))
    to_dst = 0.5 * dot(state, weights(1))
    gathered = dot(source[...], from_src.astype(BF16))
    agg = jnp.zeros(state.shape, F32)
    slopes = []
    for k in range(source.shape[0] // block):
        joined = gathered[k * block : (k + 1) * block] + to_dst
        bend = jnp.tanh(joined)
        agg = agg + (joined + joined * bend)
        joined, bend = joined.astype(BF16), bend.astype(BF16)
        slopes.append(1 + bend + joined * (1 - bend * bend))
    mixed = dot(state, weights(2)) + dot(agg.astype(BF16), weights(3))
    return mixed, slopes


def layer_back(grad, mixed, slopes, source_t, weights):
    block = grad.shape[0]
    normed, scale = norm_parts(mixed)
    grad_mixed = norm_back(grad, normed, scale)
    grad_state = grad + back_dot(grad_mixed, weights(2))
    grad_agg = 0.5 * dot_t(grad_mixed.astype(BF16), weights(3))
    low = grad_agg.astype(BF16)
    total = jnp.zeros(grad.shape, F32)
    for found in slopes:
        total = total + found.astype(F32)
    total = grad_agg * total
    pieces = [low * found for found in slopes]
    grad_src = dot(source_t[...], jnp.concatenate(pieces, axis=0))
    grad_state = grad_state + back_dot(total, weights(1))
    grad_table = dot_t(grad_src.astype(BF16), weights(0))
    return grad_state + grad_table[:block], grad_table[block:]


def layer_weights(weights, layer):
    return lambda i: weights[layer, i]


def first_kernel(
    layer, parts, state, pieces, source, weights, pick, new, mixed, slopes, halo
):
    block = state.shape[0]
    own = state[...]
    used = layer_weights(weights, layer)
    value, found = layer_forward(own, pieces[...], source, used, parts)
    mixed[...] = value
    for k, part in enumerate(found):
        slopes[k * block : (k + 1) * block, :] = part
    normed, _ = norm_parts(value)
    result = (own.astype(F32) + silu(normed)).astype(BF16)
    new[...] = result
    halo[...] = halo_rows(result, pick[...], parts)


def last_kernel(
    layer, parts, state, pieces, source, source_t, weights, cot, out, grad_own, grad_halo
):
    own = state[...]
    used = layer_weights(weights, layer)
    value, found = layer_forward(own, pieces[...], source, used, parts)
    normed, _ = norm_parts(value)
    out[...] = (own.astype(F32) + silu(normed)).astype(BF16)
    mine, sent = layer_back(cot[...].astype(F32), value, found, source_t, used)
    grad_own[...] = mine
    grad_halo[...] = cut_pieces(sent.astype(BF16), parts)


def back_kernel(
    layer,
    parts,
    mine,
    returned,
    pick_t,
    mixed,
    slopes,
    source_t,
    weights,
    grad_own,
    grad_halo,
):
    block = mine.shape[0]
    grad = mine[...] + add_pieces(returned[...], pick_t[...], block, parts)
    fan = slopes.shape[0] // block
    found = [slopes[k * block : (k + 1) * block, :] for k in range(fan)]
    used = layer_weights(weights, layer)
    own, sent = layer_back(grad, mixed[...], found, source_t, used)
    grad_own[...] = own
    grad_halo[...] = cut_pieces(sent.astype(BF16), parts)


def mesh_back_kernel(parts, mine, returned, pick_t, mesh_pre, weight, out):
    block = mine.shape[0]
    grad = mine[...] + add_pieces(returned[...], pick_t[...], block, parts)
    out[...] = back_dot(grad * slope(mesh_pre[...]), weight[...]).astype(BF16)


def edge_marks(feat, at, rows, nodes, block, fanout, who):
    turned = edge_data(feat, at, rows).T
    ids = iota((rows, nodes * block), 1)
    return [
        mark(
            ids
            == spot_of(
                lambda t: turned[:, t : t + 1], fanout, k, who[0], who[1], nodes, block
            )
        )
        for k in range(fanout)
    ]


def mark_kernel(spans, rows, nodes, block, fanout, who, *refs):
    feats, state = refs[: len(spans)], refs[len(spans)]
    *outs, final = refs[len(spans) + 1 :]
    final[...] = state[...]
    for feat, at, out in zip(feats, spans, outs):
        for k, found in enumerate(edge_marks(feat, at, rows, nodes, block, fanout, who)):
            out[k * rows : (k + 1) * rows, :] = found


def message_back_kernel(spans, rows, ready, nodes, block, fanout, who, *refs):
    count = len(spans)
    feats, slopes = refs[:count], refs[count : 2 * count]
    outs = refs[2 * count :]
    grads, outs = outs[:nodes], outs[nodes:]
    marks = []
    for feat, at in zip(feats, spans):
        if ready:
            marks.append(feat[...])
        else:
            marks += edge_marks(feat, at, rows, nodes, block, fanout, who)
    same, other = grads[: nodes // 2][::-1], grads[nodes // 2 :][::-1]
    picked = dot(
        jnp.concatenate(marks, axis=0),
        jnp.concatenate([ref[...] for ref in (*same, *other)], axis=0),
    )
    size = outs[0].shape[1]
    chunks = slopes[0].shape[1] // size
    per = count * chunks // len(outs)
    for i in range(count):
        total = jnp.zeros((rows, slopes[0].shape[1]), F32)
        for k in range(fanout):
            at = (i * fanout + k) * rows
            part = slopes[i][k * rows : (k + 1) * rows, :].astype(F32)
            total = total + picked[at : at + rows] * part
        at = i % per * rows
        for c, out in enumerate(outs[i // per * chunks : (i // per + 1) * chunks]):
            out[at : at + rows, :] = total[:, c * size : (c + 1) * size].astype(out.dtype)


def grid_back_kernel(chunks, *refs):
    *parts, weight, out = refs
    count = len(parts) // 3
    rows = parts[0].shape[0]
    total = [
        parts[i][...]
        + parts[count + i][:rows, :].astype(F32)
        + parts[2 * count + i][...].astype(F32)
        for i in range(count)
    ]
    each = count // chunks
    columns = [
        jnp.concatenate(total[c * each : (c + 1) * each], axis=0) for c in range(chunks)
    ]
    out[...] = back_dot(jnp.concatenate(columns, axis=1), weight[...]).astype(BF16)


def call(kernel, outs, args, smem=0, scratch=(), space=pltpu.VMEM, aliases=None):
    specs = [pl.BlockSpec(memory_space=pltpu.SMEM)] * smem
    specs += [pl.BlockSpec(memory_space=space)] * (len(args) - smem)
    moved = sum(a.size * a.dtype.itemsize for a in list(args) + list(outs))
    held = sum(math.prod(a.shape) * 4 for a in scratch)
    limit = 2 * (moved + held) + 6 * MIB
    result = pl.pallas_call(
        kernel,
        out_shape=list(outs),
        in_specs=specs,
        out_specs=[pl.BlockSpec(memory_space=pltpu.VMEM)] * len(outs),
        scratch_shapes=list(scratch),
        input_output_aliases=aliases or {},
        compiler_params=pltpu.CompilerParams(vmem_limit_bytes=limit),
        cost_estimate=pl.CostEstimate(
            flops=0, bytes_accessed=moved, transcendentals=0
        ),
    )(*args)
    return result


def shape(dims, dtype):
    return jax.ShapeDtypeStruct(dims, dtype)


def swap(value, axis, apart):
    size = lax.axis_size(axis)
    return lax.ppermute(value, axis, [(i, i ^ apart) for i in range(size)])


def body(
    grid_feat,
    edge_len,
    g2m_owner,
    g2m_dst,
    enc_weight,
    enc_vec,
    mesh_init,
    mesh_weight,
    halo_send,
    mesh_src,
    proc_weight,
    cot,
):
    nodes = lax.axis_size("node")
    sects = lax.axis_size("sect")
    width = grid_feat.shape[1]
    grid_rows, fanout = edge_len.shape
    block = mesh_init.shape[1]
    parts = width // LANES
    both = ("sect", "node")
    who = jnp.stack([lax.axis_index("sect"), lax.axis_index("node")]).astype(jnp.int32)

    axes = [1 << i for i in range(sects.bit_length() - 1)]
    part_rows = grid_rows // len(axes)
    assert len(axes) == 2
    ends = pltpu.VMEM((fanout, grid_rows), jnp.int32)
    packed = call(
        functools.partial(pack_kernel, block),
        [shape((part_rows + META_ROWS, width), BF16)] * len(axes),
        [
            pltpu.with_memory_space_constraint(value, pltpu.HBM)
            for value in (grid_feat, edge_len.T, g2m_owner.T, g2m_dst.T)
        ],
        scratch=[
            pltpu.VMEM((fanout, grid_rows), F32),
            ends,
            ends,
            pltpu.SemaphoreType.DMA((3 + len(axes),)),
        ],
        space=pltpu.HBM,
    )
    where = {(0, p): (part, 0) for p, part in enumerate(packed)}
    steps = [[(0, p) for p in range(len(axes))]]
    held, names = list(packed), [[0] for _ in axes]
    for step in range(len(axes)):
        given = [
            swap(part, "sect", axes[(p + step) % len(axes)]) for p, part in enumerate(held)
        ]
        steps.append([])
        for p, part in enumerate(given):
            axis = axes[(p + step) % len(axes)]
            for i, j in enumerate(list(names[p])):
                where[j ^ axis, p] = (part, i * packed[0].shape[0])
                names[p].append(j ^ axis)
                steps[-1].append((j ^ axis, p))
        held = [jnp.concatenate(pair, axis=0) for pair in zip(held, given)]
    sends = halo_send[0, 0].transpose(0, 2, 1)
    src_row = mesh_src[0].T
    fan = src_row.shape[0]
    pieces = sends.size * parts
    table_len = block + sends.size
    weight, vec = call(
        load_kernel,
        [shape(enc_weight.shape, BF16), shape((1, width), F32)],
        [
            pltpu.with_memory_space_constraint(value, pltpu.HBM)
            for value in (enc_weight, enc_vec[None, :])
        ],
        scratch=[pltpu.SemaphoreType.DMA((2,))],
        space=pltpu.HBM,
    )

    half = nodes // 2
    sums_shape = shape((nodes * block, width), F32)

    def encode(units, last, before):
        edges = len(units) * part_rows * fanout
        used = [where[unit] for unit in units]
        args = [who, *(part for part, _ in used), weight, vec, *before]
        outs = [
            shape((half * block, width), BF16) if last else sums_shape,
            shape((edges, width), BF16),
            shape((1, edges), jnp.int32),
        ]
        return call(
            functools.partial(
                encode_kernel,
                tuple(at for _, at in used),
                nodes,
                block,
                fanout,
                part_rows,
                last,
            ),
            outs if last else outs[:1],
            args,
            smem=1,
            scratch=() if last else [pltpu.VMEM(s.shape, s.dtype) for s in outs[1:]],
            aliases={len(args) - 1: 0} if before and not last else None,
        )

    before = encode([unit for units in steps[:-1] for unit in units], False, [])
    for p in range(len(axes) - 1):
        before = encode([unit for unit in steps[-1] if unit[1] == p], False, before)
    cross, message, spots = encode(
        [unit for unit in steps[-1] if unit[1] == len(axes) - 1], True, before
    )
    (keep,) = call(
        keep_kernel, [shape((half * block, width), BF16)], [message, spots, *before]
    )

    pair = keep.astype(F32) + swap(cross, "node", 1).astype(F32)
    pair = pair.reshape(half, block, width)
    arrived = [
        swap(pair[q].astype(BF16), "node", 2 * q) for q in reversed(range(1, half))
    ]

    units = [(j, p) for j in range(sects) for p in range(len(axes))]
    found = call(
        functools.partial(
            slope_kernel,
            tuple(where[unit][1] for unit in units),
            block,
            parts,
            fanout,
            part_rows,
        ),
        [shape((fanout * part_rows, width), BF16)] * len(units)
        + [
            shape((pieces, parts * block), BF16),
            shape((parts * block, pieces), BF16),
            shape((fan * block, table_len), BF16),
            shape((table_len, fan * block), BF16),
        ],
        [*(where[unit][0] for unit in units), weight, vec, sends, src_row],
    )
    tied = lax.optimization_barrier((*arrived, *found))
    arrived, slopes = tied[: half - 1], dict(zip(units, tied[half - 1 : -4]))
    pick, pick_t, source, source_t = tied[-4:]

    halo_shape = shape((pieces, LANES), BF16)
    row_low, row_high = shape((block, width), BF16), shape((block, width), F32)

    def exchange(value):
        return lax.all_to_all(value, both, split_axis=0, concat_axis=0, tiled=True)

    state, mesh_pre, halo = call(
        functools.partial(start_kernel, parts),
        [row_low, row_high, halo_shape],
        [pair[0], *arrived, mesh_init[0], mesh_weight, pick],
    )
    assert proc_weight.shape[0] == 2
    state, mixed, slope_first, halo = call(
        functools.partial(first_kernel, 0, parts),
        [row_low, row_high, shape((fan * block, width), BF16), halo_shape],
        [state, exchange(halo), source, proc_weight, pick],
    )
    mesh_out, grad, halo = call(
        functools.partial(last_kernel, 1, parts),
        [row_low, row_high, halo_shape],
        [state, exchange(halo), source, source_t, proc_weight, cot[0]],
    )
    grad, halo = call(
        functools.partial(back_kernel, 0, parts),
        [row_high, halo_shape],
        [grad, exchange(halo), pick_t, mixed, slope_first, source_t, proc_weight],
    )
    (grad_sum,) = call(
        functools.partial(mesh_back_kernel, parts),
        [row_low],
        [grad, exchange(halo), pick_t, mesh_pre, mesh_weight],
    )

    same = [swap(grad_sum, "node", 2 * q) for q in reversed(range(1, half))]
    same = [grad_sum, *same[::-1]]
    ready = nodes * block <= 8 * LANES
    picks_of = {unit: where[unit] for unit in units}
    if ready:
        seen, _ = lax.optimization_barrier((who, grad_sum))
        *found, mesh_out = call(
            functools.partial(
                mark_kernel,
                tuple(where[unit][1] for unit in units),
                part_rows,
                nodes,
                block,
                fanout,
            ),
            [shape((fanout * part_rows, nodes * block), BF16)] * len(units) + [row_low],
            [seen, *(where[unit][0] for unit in units), mesh_out],
            smem=1,
        )
        same[-1] = lax.optimization_barrier((same[-1], found[0]))[0]
        picks_of = {unit: (part, 0) for unit, part in zip(units, found)}
    other = [swap(rows, "node", 1) for rows in same[::-1]][::-1]
    gathered = (*same[::-1], *other[::-1])

    def message_back(groups, dtype):
        used = [unit for group in groups for unit in group]
        return call(
            functools.partial(
                message_back_kernel,
                tuple(picks_of[unit][1] for unit in used),
                part_rows,
                ready,
                nodes,
                block,
                fanout,
            ),
            [
                shape((len(group) * part_rows, width // CHUNKS), dtype)
                for group in groups
                for _ in range(CHUNKS)
            ],
            [
                who,
                *(picks_of[unit][0] for unit in used),
                *(slopes[unit] for unit in used),
                *gathered,
            ],
            smem=1,
        )

    first, then = axes, axes[::-1]
    chunks = [(p, c) for c in range(CHUNKS) for p in range(len(axes))]

    def ordered(found):
        return [found[p * CHUNKS + c] for p, c in chunks]

    given = ordered(
        message_back(
            [[(a, p), (a ^ b, p)] for p, (a, b) in enumerate(zip(first, then))], BF16
        )
    )
    gathered = lax.optimization_barrier((*gathered, *given))[: len(gathered)]
    passed = ordered(message_back([[(b, p)] for p, b in enumerate(then)], F32))
    gathered = lax.optimization_barrier((*gathered, *passed))[: len(gathered)]
    given = [swap(part, "sect", first[p]) for part, (p, _) in zip(given, chunks)]
    passed = [
        (mine + part[part_rows:].astype(F32)).astype(BF16)
        for mine, part in zip(passed, given)
    ]
    kept = ordered(message_back([[(0, p)] for p in range(len(axes))], F32))
    passed = [swap(part, "sect", then[p]) for part, (p, _) in zip(passed, chunks)]
    (grid_grad,) = call(
        functools.partial(grid_back_kernel, CHUNKS),
        [shape((grid_rows, width), BF16)],
        [*kept, *given, *passed, enc_weight],
    )
    return (mesh_out[None], grid_grad)


def solution(mesh):
    return jax.shard_map(
        body,
        mesh=mesh,
        in_specs=(
            P(("sect", "node"), None),
            P(("sect", "node"), None),
            P(("sect", "node"), None),
            P(("sect", "node"), None),
            P(),
            P(),
            P("node", "sect", None),
            P(),
            P("sect", "node", None, None, None),
            P("node", "sect", None),
            P(),
            P("node", "sect", None),
        ),
        out_specs=(P("node", "sect", None), P(("sect", "node"), None)),
        check_vma=False,
    )
```

```python
import functools
import math

import jax
import jax.numpy as jnp
from jax import lax
from jax.experimental import pallas as pl
from jax.experimental.pallas import tpu as pltpu
from jax.sharding import PartitionSpec as P

F32 = jnp.float32
BF16 = jnp.bfloat16
LANES = 128
META_ROWS = 16
CHUNKS = 2
MIB = 1024 * 1024


def sigmoid(value):
    return 0.5 * jnp.tanh(0.5 * value) + 0.5


def silu(value):
    return value * sigmoid(value)


def slope(value):
    sig = sigmoid(value)
    return sig * (1.0 + value * (1.0 - sig))


def dot(left, right):
    return jnp.dot(left, right, preferred_element_type=F32)


def dot_t(left, right):
    return lax.dot_general(left, right, (((1,), (1,)), ((), ())), preferred_element_type=F32)


def halves(value):
    high = value.astype(BF16)
    return high, (value - high.astype(F32)).astype(BF16)


def back_dot(grad, weight):
    rows = grad.shape[0]
    both = dot_t(jnp.concatenate(halves(grad), axis=0), weight)
    return both[:rows] + both[rows:]


def mark(equal):
    return jnp.where(equal, 1.0, 0.0).astype(BF16)


def iota(shape, axis):
    return lax.broadcasted_iota(jnp.int32, shape, axis)


def norm_parts(mixed):
    mean = jnp.mean(mixed, axis=-1, keepdims=True)
    centred = mixed - mean
    scale = lax.rsqrt(jnp.mean(centred * centred, axis=-1, keepdims=True) + 1e-05)
    return centred * scale, scale


def norm_back(grad, normed, scale):
    pull = grad * slope(normed)
    return scale * (
        pull
        - jnp.mean(pull, axis=-1, keepdims=True)
        - normed * jnp.mean(pull * normed, axis=-1, keepdims=True)
    )


def pack_kernel(block, feat, lens, owner, dst, *refs):
    *outs, held, own_held, dst_held, sems = refs
    rows = feat.shape[0] // len(outs)
    pairs = [(lens, held), (owner, own_held), (dst, dst_held)]
    pairs += [
        (feat.at[i * rows : (i + 1) * rows, :], out.at[:rows, :]) for i, out in enumerate(outs)
    ]
    copies = [
        pltpu.make_async_copy(source, target, sems.at[i])
        for i, (source, target) in enumerate(pairs)
    ]
    for copy in copies:
        copy.start()
    for copy in copies[:3]:
        copy.wait()
    high, middle = halves(held[...])
    low = (held[...] - high.astype(F32) - middle.astype(F32)).astype(BF16)
    far = dst_held[...]
    section = far // block
    found = [v.astype(F32) for v in (high, middle, low)]
    found += [v.astype(F32) for v in (own_held[...], section, far - section * block)]
    fill = META_ROWS - 6 * lens.shape[0]
    found.append(jnp.zeros((fill, feat.shape[0]), F32))
    meta = jnp.concatenate(found, axis=0).astype(BF16)
    rest = jnp.zeros((META_ROWS, feat.shape[1] - rows), BF16)
    for i, out in enumerate(outs):
        out[rows:, :] = jnp.concatenate([meta[:, i * rows : (i + 1) * rows], rest], axis=1)
    for copy in copies[3:]:
        copy.wait()


def index_kernel(block, parts, *refs):
    wanted, far_weight, far_vec = refs[:2], refs[2], refs[3]
    pick, pick_t, source, source_t, weight, vec, sends, src_row, sems = refs[4:]
    pairs = ((wanted[0], sends), (wanted[1], src_row), (far_vec, vec), (far_weight, weight))
    copies = [
        pltpu.make_async_copy(start, target, sems.at[i])
        for i, (start, target) in enumerate(pairs)
    ]
    for copy in copies:
        copy.start()
    for copy in copies[:2]:
        copy.wait()
    sects, count, nodes = sends.shape
    pieces = pick.shape[0]
    at = iota((1, pieces), 1)
    part, row = at % parts, at // parts
    peer = row // count
    whose = mark(iota((nodes, pieces), 0) == peer % nodes)
    place = jnp.zeros((1, pieces), F32)
    for t in range(sects):
        found = dot(sends[t].astype(F32).astype(BF16), whose)
        for c in range(count):
            here = jnp.logical_and(peer // nodes == t, row % count == c)
            place = place + jnp.where(here, found[c : c + 1], 0.0)
    place = place + (part * block).astype(F32)
    pick_t[...] = mark(iota((parts * block, pieces), 0) == place.astype(jnp.int32))
    turned = jnp.broadcast_to(place, (8, pieces)).T[:, :1].astype(jnp.int32)
    pick[...] = mark(iota((pieces, parts * block), 1) == turned)
    table_len = source_t.shape[0]
    column = src_row[...].astype(F32).T.astype(jnp.int32)
    ids = iota((block, table_len), 1)
    ids_t = iota((table_len, block), 0)
    for k in range(src_row.shape[0]):
        rows = slice(k * block, (k + 1) * block)
        source[rows, :] = mark(ids == column[:, k : k + 1])
        source_t[:, rows] = mark(ids_t == src_row[k : k + 1, :])
    for copy in copies[2:]:
        copy.wait()


def edge_data(feat, at, rows):
    return feat[at + rows : at + rows + META_ROWS, :rows].astype(F32)


def edge_length(meta, fanout, k):
    high, middle, low = (meta[:, t * fanout + k : t * fanout + k + 1] for t in range(3))
    return high + middle + low


def spot_of(pick, fanout, k, section, node, nodes, block):
    owner, where, place = (pick((3 + t) * fanout + k).astype(jnp.int32) for t in range(3))
    apart = jnp.bitwise_xor(owner, node)
    order = lax.shift_right_logical(apart, 1) + jnp.bitwise_and(apart, 1) * (nodes // 2)
    return jnp.where(where == section, order * block + place, -1)


def add_rows(out, base, found, before):
    step = min(out.shape[0], 512)

    def chunk(c, carry):
        start = pl.multiple_of(c * step, step)
        part = None
        for message, spots in found:
            ids = iota((step, spots.shape[1]), 0) + (base + start)
            more = dot(mark(ids == spots[...]), message[...])
            part = more if part is None else part + more
        for ref in before:
            part = part + ref[pl.ds(base + start, step), :]
        out[pl.ds(start, step), :] = part.astype(out.dtype)
        return carry

    lax.fori_loop(0, out.shape[0] // step, chunk, 0)


def make_messages(spans, nodes, block, fanout, rows, who, feats, weight, vec, message, spots):
    section, node = who[0], who[1]
    pre = 0.5 * dot(
        jnp.concatenate([feat[at : at + rows, :] for feat, at in zip(feats, spans)], axis=0),
        weight[...],
    )
    part = 0.5 * vec[...]
    for j in range(len(spans)):
        meta = edge_data(feats[j], spans[j], rows)
        turned = meta.T
        for k in range(fanout):
            at = (j * fanout + k) * rows
            act = pre[j * rows : (j + 1) * rows] + edge_length(turned, fanout, k) * part
            message[at : at + rows, :] = (act + act * jnp.tanh(act)).astype(BF16)
            spots[:, at : at + rows] = spot_of(
                lambda t, meta=meta: meta[t : t + 1], fanout, k, section, node, nodes, block
            )


def message_kernel(spans, nodes, block, fanout, rows, who, *refs):
    feats, rest = refs[: len(spans)], refs[len(spans) :]
    make_messages(spans, nodes, block, fanout, rows, who, feats, *rest)


def encode_kernel(spans, nodes, block, fanout, rows, last, who, *refs):
    count = len(spans)
    feats = refs[:count]
    weight, vec = refs[count : count + 2]
    *before, out, message, spots = refs[count + 2 :]
    make_messages(
        spans, nodes, block, fanout, rows, who, feats, weight, vec, message, spots
    )
    found = [(message, spots)]
    if last:
        found.append((before[0], before[1]))
        before = before[2:]
    add_rows(out, nodes // 2 * block if last else 0, found, before)


def keep_kernel(message, spots, more, more_spots, before, out):
    add_rows(out, 0, [(message, spots), (more, more_spots)], [before])


def slope_kernel(spans, fanout, rows, *refs):
    count = len(spans)
    feats = refs[:count]
    weight, vec = refs[count : count + 2]
    outs = refs[count + 2 :]
    for feat, at, out in zip(feats, spans, outs):
        pre = dot(feat[at : at + rows, :], weight[...])
        turned = edge_data(feat, at, rows).T
        for k in range(fanout):
            act = pre + edge_length(turned, fanout, k) * vec[...]
            out[k * rows : (k + 1) * rows, :] = slope(act).astype(BF16)


def halo_rows(state, pick, parts):
    stacked = jnp.concatenate(
        [state[:, i * LANES : (i + 1) * LANES] for i in range(parts)], axis=0
    )
    return dot(pick, stacked).astype(BF16)


def join_pieces(pieces, parts):
    count = pieces.shape[0]
    rows = count // parts
    at = iota((count, count), 0)
    onehot = mark(iota((count, count), 1) == at % rows * parts + at // rows)
    found = dot(onehot, pieces).astype(BF16)
    return jnp.concatenate([found[i * rows : (i + 1) * rows] for i in range(parts)], axis=1)


def cut_pieces(rows, parts):
    each, count = rows.shape[0], rows.shape[0] * parts
    at = iota((count, count), 0)
    onehot = mark(iota((count, count), 1) == at % parts * each + at // parts)
    stacked = jnp.concatenate(
        [rows[:, i * LANES : (i + 1) * LANES] for i in range(parts)], axis=0
    )
    return dot(onehot, stacked).astype(BF16)


def add_pieces(pieces, pick_t, block, parts):
    total = dot(pick_t, pieces)
    return jnp.concatenate([total[i * block : (i + 1) * block] for i in range(parts)], axis=1)


def start_kernel(parts, sums, *refs):
    received, (init, weight, pick, state, mesh_pre, halo) = refs[:-6], refs[-6:]
    agg = sums[...]
    for ref in received:
        agg = agg + ref[...].astype(F32)
    pre = dot(agg.astype(BF16), weight[...])
    mesh_pre[...] = pre
    new = (init[...].astype(F32) + silu(pre)).astype(BF16)
    state[...] = new
    halo[...] = halo_rows(new, pick[...], parts)


def layer_forward(state, pieces, source, weights, parts):
    block = state.shape[0]
    halo = join_pieces(pieces, parts)
    table = jnp.concatenate([state, halo], axis=0)
    from_src = 0.5 * dot(table, weights(0))
    to_dst = 0.5 * dot(state, weights(1))
    gathered = dot(source[...], from_src.astype(BF16))
    agg = jnp.zeros(state.shape, F32)
    slopes = []
    for k in range(source.shape[0] // block):
        joined = gathered[k * block : (k + 1) * block] + to_dst
        bend = jnp.tanh(joined)
        agg = agg + (joined + joined * bend)
        joined, bend = joined.astype(BF16), bend.astype(BF16)
        slopes.append(1 + bend + joined * (1 - bend * bend))
    mixed = dot(state, weights(2)) + dot(agg.astype(BF16), weights(3))
    return mixed, slopes


def layer_back(grad, mixed, slopes, source_t, weights):
    block = grad.shape[0]
    normed, scale = norm_parts(mixed)
    grad_mixed = norm_back(grad, normed, scale)
    grad_state = grad + back_dot(grad_mixed, weights(2))
    grad_agg = 0.5 * dot_t(grad_mixed.astype(BF16), weights(3))
    low = grad_agg.astype(BF16)
    total = jnp.zeros(grad.shape, F32)
    for found in slopes:
        total = total + found.astype(F32)
    total = grad_agg * total
    pieces = [low * found for found in slopes]
    grad_src = dot(source_t[...], jnp.concatenate(pieces, axis=0))
    grad_state = grad_state + back_dot(total, weights(1))
    grad_table = dot_t(grad_src.astype(BF16), weights(0))
    return grad_state + grad_table[:block], grad_table[block:]


def layer_weights(weights, layer):
    return lambda i: weights[layer, i]


def first_kernel(
    layer, parts, state, pieces, source, weights, pick, new, mixed, slopes, halo
):
    block = state.shape[0]
    own = state[...]
    used = layer_weights(weights, layer)
    value, found = layer_forward(own, pieces[...], source, used, parts)
    mixed[...] = value
    for k, part in enumerate(found):
        slopes[k * block : (k + 1) * block, :] = part
    normed, _ = norm_parts(value)
    result = (own.astype(F32) + silu(normed)).astype(BF16)
    new[...] = result
    halo[...] = halo_rows(result, pick[...], parts)


def last_kernel(
    layer, parts, state, pieces, source, source_t, weights, cot, out, grad_own, grad_halo
):
    own = state[...]
    used = layer_weights(weights, layer)
    value, found = layer_forward(own, pieces[...], source, used, parts)
    normed, _ = norm_parts(value)
    out[...] = (own.astype(F32) + silu(normed)).astype(BF16)
    mine, sent = layer_back(cot[...].astype(F32), value, found, source_t, used)
    grad_own[...] = mine
    grad_halo[...] = cut_pieces(sent.astype(BF16), parts)


def back_kernel(
    layer,
    parts,
    mine,
    returned,
    pick_t,
    mixed,
    slopes,
    source_t,
    weights,
    grad_own,
    grad_halo,
):
    block = mine.shape[0]
    grad = mine[...] + add_pieces(returned[...], pick_t[...], block, parts)
    fan = slopes.shape[0] // block
    found = [slopes[k * block : (k + 1) * block, :] for k in range(fan)]
    used = layer_weights(weights, layer)
    own, sent = layer_back(grad, mixed[...], found, source_t, used)
    grad_own[...] = own
    grad_halo[...] = cut_pieces(sent.astype(BF16), parts)


def mesh_back_kernel(parts, mine, returned, pick_t, mesh_pre, weight, out):
    block = mine.shape[0]
    grad = mine[...] + add_pieces(returned[...], pick_t[...], block, parts)
    out[...] = back_dot(grad * slope(mesh_pre[...]), weight[...]).astype(BF16)


def edge_marks(feat, at, rows, nodes, block, fanout, who):
    turned = edge_data(feat, at, rows).T
    ids = iota((rows, nodes * block), 1)
    return [
        mark(
            ids
            == spot_of(
                lambda t: turned[:, t : t + 1], fanout, k, who[0], who[1], nodes, block
            )
        )
        for k in range(fanout)
    ]


def mark_kernel(spans, rows, nodes, block, fanout, who, *refs):
    feats, state = refs[: len(spans)], refs[len(spans)]
    *outs, final = refs[len(spans) + 1 :]
    final[...] = state[...]
    for feat, at, out in zip(feats, spans, outs):
        for k, found in enumerate(edge_marks(feat, at, rows, nodes, block, fanout, who)):
            out[k * rows : (k + 1) * rows, :] = found


def message_back_kernel(spans, rows, ready, nodes, block, fanout, who, *refs):
    count = len(spans)
    feats, slopes = refs[:count], refs[count : 2 * count]
    outs = refs[2 * count :]
    grads, outs = outs[:nodes], outs[nodes:]
    marks = []
    for feat, at in zip(feats, spans):
        if ready:
            marks.append(feat[...])
        else:
            marks += edge_marks(feat, at, rows, nodes, block, fanout, who)
    same, other = grads[: nodes // 2][::-1], grads[nodes // 2 :][::-1]
    picked = dot(
        jnp.concatenate(marks, axis=0),
        jnp.concatenate([ref[...] for ref in (*same, *other)], axis=0),
    )
    size = outs[0].shape[1]
    chunks = slopes[0].shape[1] // size
    per = count * chunks // len(outs)
    for i in range(count):
        total = jnp.zeros((rows, slopes[0].shape[1]), F32)
        for k in range(fanout):
            at = (i * fanout + k) * rows
            part = slopes[i][k * rows : (k + 1) * rows, :].astype(F32)
            total = total + picked[at : at + rows] * part
        at = i % per * rows
        for c, out in enumerate(outs[i // per * chunks : (i // per + 1) * chunks]):
            out[at : at + rows, :] = total[:, c * size : (c + 1) * size].astype(out.dtype)


def grid_back_kernel(chunks, *refs):
    *parts, weight, out = refs
    count = len(parts) // 3
    rows = parts[0].shape[0]
    total = [
        parts[i][...]
        + parts[count + i][:rows, :].astype(F32)
        + parts[2 * count + i][...].astype(F32)
        for i in range(count)
    ]
    each = count // chunks
    columns = [
        jnp.concatenate(total[c * each : (c + 1) * each], axis=0) for c in range(chunks)
    ]
    out[...] = back_dot(jnp.concatenate(columns, axis=1), weight[...]).astype(BF16)


def call(kernel, outs, args, smem=0, scratch=(), space=pltpu.VMEM, aliases=None):
    specs = [pl.BlockSpec(memory_space=pltpu.SMEM)] * smem
    specs += [pl.BlockSpec(memory_space=space)] * (len(args) - smem)
    moved = sum(a.size * a.dtype.itemsize for a in list(args) + list(outs))
    held = sum(math.prod(a.shape) * 4 for a in scratch)
    limit = 2 * (moved + held) + 6 * MIB
    result = pl.pallas_call(
        kernel,
        out_shape=list(outs),
        in_specs=specs,
        out_specs=[pl.BlockSpec(memory_space=pltpu.VMEM)] * len(outs),
        scratch_shapes=list(scratch),
        input_output_aliases=aliases or {},
        compiler_params=pltpu.CompilerParams(vmem_limit_bytes=limit),
        cost_estimate=pl.CostEstimate(
            flops=0, bytes_accessed=moved, transcendentals=0
        ),
    )(*args)
    return result


def shape(dims, dtype):
    return jax.ShapeDtypeStruct(dims, dtype)


def swap(value, axis, apart):
    size = lax.axis_size(axis)
    return lax.ppermute(value, axis, [(i, i ^ apart) for i in range(size)])


def body(
    grid_feat,
    edge_len,
    g2m_owner,
    g2m_dst,
    enc_weight,
    enc_vec,
    mesh_init,
    mesh_weight,
    halo_send,
    mesh_src,
    proc_weight,
    cot,
):
    nodes = lax.axis_size("node")
    sects = lax.axis_size("sect")
    width = grid_feat.shape[1]
    grid_rows, fanout = edge_len.shape
    block = mesh_init.shape[1]
    parts = width // LANES
    both = ("sect", "node")
    who = jnp.stack([lax.axis_index("sect"), lax.axis_index("node")]).astype(jnp.int32)

    axes = [1 << i for i in range(sects.bit_length() - 1)]
    part_rows = grid_rows // len(axes)
    assert len(axes) == 2
    ends = pltpu.VMEM((fanout, grid_rows), jnp.int32)
    packed = call(
        functools.partial(pack_kernel, block),
        [shape((part_rows + META_ROWS, width), BF16)] * len(axes),
        [
            pltpu.with_memory_space_constraint(value, pltpu.HBM)
            for value in (grid_feat, edge_len.T, g2m_owner.T, g2m_dst.T)
        ],
        scratch=[
            pltpu.VMEM((fanout, grid_rows), F32),
            ends,
            ends,
            pltpu.SemaphoreType.DMA((3 + len(axes),)),
        ],
        space=pltpu.HBM,
    )
    where = {(0, p): (part, 0) for p, part in enumerate(packed)}
    steps = [[(0, p) for p in range(len(axes))]]
    held, names = list(packed), [[0] for _ in axes]
    for step in range(len(axes)):
        given = [
            swap(part, "sect", axes[(p + step) % len(axes)]) for p, part in enumerate(held)
        ]
        steps.append([])
        for p, part in enumerate(given):
            axis = axes[(p + step) % len(axes)]
            for i, j in enumerate(list(names[p])):
                where[j ^ axis, p] = (part, i * packed[0].shape[0])
                names[p].append(j ^ axis)
                steps[-1].append((j ^ axis, p))
        held = [jnp.concatenate(pair, axis=0) for pair in zip(held, given)]
    sends = halo_send[0, 0].transpose(0, 2, 1)
    src_row = mesh_src[0].T
    fan = src_row.shape[0]
    pieces = sends.size * parts
    table_len = block + sends.size
    pick, pick_t, source, source_t, weight, vec = call(
        functools.partial(index_kernel, block, parts),
        [
            shape((pieces, parts * block), BF16),
            shape((parts * block, pieces), BF16),
            shape((fan * block, table_len), BF16),
            shape((table_len, fan * block), BF16),
            shape(enc_weight.shape, BF16),
            shape((1, width), F32),
        ],
        [
            pltpu.with_memory_space_constraint(value, pltpu.HBM)
            for value in (sends, src_row, enc_weight, enc_vec[None, :])
        ],
        scratch=[
            pltpu.VMEM(sends.shape, jnp.int32),
            pltpu.VMEM(src_row.shape, jnp.int32),
            pltpu.SemaphoreType.DMA((4,)),
        ],
        space=pltpu.HBM,
    )

    half = nodes // 2
    sums_shape = shape((nodes * block, width), F32)

    def encode(units, kind, before):
        edges = len(units) * part_rows * fanout
        used = [where[unit] for unit in units]
        args = [who, *(part for part, _ in used), weight, vec, *before]
        outs = [shape((edges, width), BF16), shape((1, edges), jnp.int32)]
        fixed = (tuple(at for _, at in used), nodes, block, fanout, part_rows)
        if kind == "messages":
            return call(functools.partial(message_kernel, *fixed), outs, args, smem=1)
        last = kind == "last"
        sums = shape((half * block, width), BF16) if last else sums_shape
        return call(
            functools.partial(encode_kernel, *fixed, last),
            [sums, *outs] if last else [sums],
            args,
            smem=1,
            scratch=() if last else [pltpu.VMEM(s.shape, s.dtype) for s in outs],
            aliases={len(args) - 1: 0} if before and not last else None,
        )

    before = []
    for units in steps[:-1]:
        before = encode(units, "sums", before)
    early = encode([unit for unit in steps[-1] if unit[1] == 0], "messages", [])
    cross, message, spots = encode(
        [unit for unit in steps[-1] if unit[1]], "last", [*early, *before]
    )
    (keep,) = call(
        keep_kernel,
        [shape((half * block, width), BF16)],
        [message, spots, *early, *before],
    )

    pair = keep.astype(F32) + swap(cross, "node", 1).astype(F32)
    pair = pair.reshape(half, block, width)
    arrived = [
        swap(pair[q].astype(BF16), "node", 2 * q) for q in reversed(range(1, half))
    ]

    units = [(j, p) for j in range(sects) for p in range(len(axes))]
    slopes = call(
        functools.partial(
            slope_kernel, tuple(where[unit][1] for unit in units), fanout, part_rows
        ),
        [shape((fanout * part_rows, width), BF16)] * len(units),
        [*(where[unit][0] for unit in units), weight, vec],
    )
    tied = lax.optimization_barrier((*arrived, *slopes))
    arrived, slopes = tied[: half - 1], dict(zip(units, tied[half - 1 :]))

    halo_shape = shape((pieces, LANES), BF16)
    row_low, row_high = shape((block, width), BF16), shape((block, width), F32)

    def exchange(value):
        return lax.all_to_all(value, both, split_axis=0, concat_axis=0, tiled=True)

    state, mesh_pre, halo = call(
        functools.partial(start_kernel, parts),
        [row_low, row_high, halo_shape],
        [pair[0], *arrived, mesh_init[0], mesh_weight, pick],
    )
    assert proc_weight.shape[0] == 2
    state, mixed, slope_first, halo = call(
        functools.partial(first_kernel, 0, parts),
        [row_low, row_high, shape((fan * block, width), BF16), halo_shape],
        [state, exchange(halo), source, proc_weight, pick],
    )
    mesh_out, grad, halo = call(
        functools.partial(last_kernel, 1, parts),
        [row_low, row_high, halo_shape],
        [state, exchange(halo), source, source_t, proc_weight, cot[0]],
    )
    grad, halo = call(
        functools.partial(back_kernel, 0, parts),
        [row_high, halo_shape],
        [grad, exchange(halo), pick_t, mixed, slope_first, source_t, proc_weight],
    )
    (grad_sum,) = call(
        functools.partial(mesh_back_kernel, parts),
        [row_low],
        [grad, exchange(halo), pick_t, mesh_pre, mesh_weight],
    )

    same = [swap(grad_sum, "node", 2 * q) for q in reversed(range(1, half))]
    same = [grad_sum, *same[::-1]]
    ready = nodes * block <= 8 * LANES
    picks_of = {unit: where[unit] for unit in units}
    if ready:
        seen, _ = lax.optimization_barrier((who, grad_sum))
        *found, mesh_out = call(
            functools.partial(
                mark_kernel,
                tuple(where[unit][1] for unit in units),
                part_rows,
                nodes,
                block,
                fanout,
            ),
            [shape((fanout * part_rows, nodes * block), BF16)] * len(units) + [row_low],
            [seen, *(where[unit][0] for unit in units), mesh_out],
            smem=1,
        )
        same[-1] = lax.optimization_barrier((same[-1], found[0]))[0]
        picks_of = {unit: (part, 0) for unit, part in zip(units, found)}
    other = [swap(rows, "node", 1) for rows in same[::-1]][::-1]
    gathered = (*same[::-1], *other[::-1])

    def message_back(groups, dtype):
        used = [unit for group in groups for unit in group]
        return call(
            functools.partial(
                message_back_kernel,
                tuple(picks_of[unit][1] for unit in used),
                part_rows,
                ready,
                nodes,
                block,
                fanout,
            ),
            [
                shape((len(group) * part_rows, width // CHUNKS), dtype)
                for group in groups
                for _ in range(CHUNKS)
            ],
            [
                who,
                *(picks_of[unit][0] for unit in used),
                *(slopes[unit] for unit in used),
                *gathered,
            ],
            smem=1,
        )

    first, then = axes, axes[::-1]
    chunks = [(p, c) for c in range(CHUNKS) for p in range(len(axes))]

    def ordered(found):
        return [found[p * CHUNKS + c] for p, c in chunks]

    given = ordered(
        message_back(
            [[(a, p), (a ^ b, p)] for p, (a, b) in enumerate(zip(first, then))], BF16
        )
    )
    gathered = lax.optimization_barrier((*gathered, *given))[: len(gathered)]
    passed = ordered(message_back([[(b, p)] for p, b in enumerate(then)], F32))
    gathered = lax.optimization_barrier((*gathered, *passed))[: len(gathered)]
    given = [swap(part, "sect", first[p]) for part, (p, _) in zip(given, chunks)]
    passed = [
        (mine + part[part_rows:].astype(F32)).astype(BF16)
        for mine, part in zip(passed, given)
    ]
    kept = ordered(message_back([[(0, p)] for p in range(len(axes))], F32))
    passed = [swap(part, "sect", then[p]) for part, (p, _) in zip(passed, chunks)]
    (grid_grad,) = call(
        functools.partial(grid_back_kernel, CHUNKS),
        [shape((grid_rows, width), BF16)],
        [*kept, *given, *passed, enc_weight],
    )
    return (mesh_out[None], grid_grad)


def solution(mesh):
    return jax.shard_map(
        body,
        mesh=mesh,
        in_specs=(
            P(("sect", "node"), None),
            P(("sect", "node"), None),
            P(("sect", "node"), None),
            P(("sect", "node"), None),
            P(),
            P(),
            P("node", "sect", None),
            P(),
            P("sect", "node", None, None, None),
            P("node", "sect", None),
            P(),
            P("node", "sect", None),
        ),
        out_specs=(P("node", "sect", None), P(("sect", "node"), None)),
        check_vma=False,
    )
```

```python
import functools
import math

import jax
import jax.numpy as jnp
from jax import lax
from jax.experimental import pallas as pl
from jax.experimental.pallas import tpu as pltpu
from jax.sharding import PartitionSpec as P

F32 = jnp.float32
BF16 = jnp.bfloat16
LANES = 128
META_ROWS = 16
HALO_ROWS = 2
CHUNKS = 2
MIB = 1024 * 1024


def sigmoid(value):
    return 0.5 * jnp.tanh(0.5 * value) + 0.5


def silu(value):
    return value * sigmoid(value)


def slope(value):
    sig = sigmoid(value)
    return sig * (1.0 + value * (1.0 - sig))


def dot(left, right):
    return jnp.dot(left, right, preferred_element_type=F32)


def dot_t(left, right):
    return lax.dot_general(left, right, (((1,), (1,)), ((), ())), preferred_element_type=F32)


def halves(value):
    high = value.astype(BF16)
    return high, (value - high.astype(F32)).astype(BF16)


def back_dot(grad, weight):
    rows = grad.shape[0]
    both = dot_t(jnp.concatenate(halves(grad), axis=0), weight)
    return both[:rows] + both[rows:]


def mark(equal):
    return jnp.where(equal, 1.0, 0.0).astype(BF16)


def iota(shape, axis):
    return lax.broadcasted_iota(jnp.int32, shape, axis)


def norm_parts(mixed):
    mean = jnp.mean(mixed, axis=-1, keepdims=True)
    centred = mixed - mean
    scale = lax.rsqrt(jnp.mean(centred * centred, axis=-1, keepdims=True) + 1e-05)
    return centred * scale, scale


def norm_back(grad, normed, scale):
    pull = grad * slope(normed)
    return scale * (
        pull
        - jnp.mean(pull, axis=-1, keepdims=True)
        - normed * jnp.mean(pull * normed, axis=-1, keepdims=True)
    )


def pack_kernel(block, feat, lens, owner, dst, *refs):
    *outs, held, own_held, dst_held, sems = refs
    rows = feat.shape[0] // len(outs)
    pairs = [(lens, held), (owner, own_held), (dst, dst_held)]
    pairs += [
        (feat.at[i * rows : (i + 1) * rows, :], out.at[:rows, :]) for i, out in enumerate(outs)
    ]
    copies = [
        pltpu.make_async_copy(source, target, sems.at[i])
        for i, (source, target) in enumerate(pairs)
    ]
    for copy in copies:
        copy.start()
    for copy in copies[:3]:
        copy.wait()
    high, middle = halves(held[...])
    low = (held[...] - high.astype(F32) - middle.astype(F32)).astype(BF16)
    far = dst_held[...]
    section = far // block
    found = [v.astype(F32) for v in (high, middle, low)]
    found += [v.astype(F32) for v in (own_held[...], section, far - section * block)]
    fill = META_ROWS - 6 * lens.shape[0]
    found.append(jnp.zeros((fill, feat.shape[0]), F32))
    meta = jnp.concatenate(found, axis=0).astype(BF16)
    rest = jnp.zeros((META_ROWS, feat.shape[1] - rows), BF16)
    for i, out in enumerate(outs):
        out[rows:, :] = jnp.concatenate([meta[:, i * rows : (i + 1) * rows], rest], axis=1)
    for copy in copies[3:]:
        copy.wait()


def index_kernel(block, parts, *refs):
    wanted, far_weight, far_vec = refs[:2], refs[2], refs[3]
    pick, pick_t, source, source_t, weight, vec, sends, src_row, sems = refs[4:]
    pairs = ((wanted[0], sends), (wanted[1], src_row), (far_vec, vec), (far_weight, weight))
    copies = [
        pltpu.make_async_copy(start, target, sems.at[i])
        for i, (start, target) in enumerate(pairs)
    ]
    for copy in copies:
        copy.start()
    for copy in copies[:2]:
        copy.wait()
    sects, count, nodes = sends.shape
    pieces = pick.shape[0]
    at = iota((1, pieces), 1)
    part, row = at % parts, at // parts
    peer = row // count
    whose = mark(iota((nodes, pieces), 0) == peer // sects)
    place = jnp.zeros((1, pieces), F32)
    for t in range(sects):
        found = dot(sends[t].astype(F32).astype(BF16), whose)
        for c in range(count):
            here = jnp.logical_and(peer % sects == t, row % count == c)
            place = place + jnp.where(here, found[c : c + 1], 0.0)
    place = place + (part * block).astype(F32)
    pick_t[...] = mark(iota((parts * block, pieces), 0) == place.astype(jnp.int32))
    turned = jnp.broadcast_to(place, (8, pieces)).T[:, :1].astype(jnp.int32)
    pick[...] = mark(iota((pieces, parts * block), 1) == turned)
    table_len = source_t.shape[0]
    column = src_row[...].astype(F32).T.astype(jnp.int32)
    ids = iota((block, table_len), 1)
    ids_t = iota((table_len, block), 0)
    for k in range(src_row.shape[0]):
        rows = slice(k * block, (k + 1) * block)
        source[rows, :] = mark(ids == column[:, k : k + 1])
        source_t[:, rows] = mark(ids_t == src_row[k : k + 1, :])
    for copy in copies[2:]:
        copy.wait()


def edge_data(feat, at, rows):
    return feat[at + rows : at + rows + META_ROWS, :rows].astype(F32)


def edge_length(meta, fanout, k):
    high, middle, low = (meta[:, t * fanout + k : t * fanout + k + 1] for t in range(3))
    return high + middle + low


def spot_of(pick, fanout, k, section, node, nodes, block):
    owner, where, place = (pick((3 + t) * fanout + k).astype(jnp.int32) for t in range(3))
    apart = jnp.bitwise_xor(owner, node)
    order = lax.shift_right_logical(apart, 1) + jnp.bitwise_and(apart, 1) * (nodes // 2)
    return jnp.where(where == section, order * block + place, -1)


def add_rows(out, base, message, spots, before):
    step = min(out.shape[0], 512)

    def chunk(c, carry):
        start = pl.multiple_of(c * step, step)
        ids = iota((step, spots.shape[1]), 0) + (base + start)
        part = dot(mark(ids == spots[...]), message[...])
        for ref in before:
            part = part + ref[pl.ds(base + start, step), :]
        out[pl.ds(start, step), :] = part.astype(out.dtype)
        return carry

    lax.fori_loop(0, out.shape[0] // step, chunk, 0)


def encode_kernel(spans, nodes, block, fanout, rows, last, who, *refs):
    count = len(spans)
    feats = refs[:count]
    weight, vec = refs[count : count + 2]
    *before, out, message, spots = refs[count + 2 :]
    section, node = who[0], who[1]
    pre = 0.5 * dot(
        jnp.concatenate([feat[at : at + rows, :] for feat, at in zip(feats, spans)], axis=0),
        weight[...],
    )
    part = 0.5 * vec[...]
    for j in range(count):
        meta = edge_data(feats[j], spans[j], rows)
        turned = meta.T
        for k in range(fanout):
            at = (j * fanout + k) * rows
            act = pre[j * rows : (j + 1) * rows] + edge_length(turned, fanout, k) * part
            message[at : at + rows, :] = (act + act * jnp.tanh(act)).astype(BF16)
            spots[:, at : at + rows] = spot_of(
                lambda t, meta=meta: meta[t : t + 1], fanout, k, section, node, nodes, block
            )
    add_rows(out, nodes // 2 * block if last else 0, message, spots, before)


def keep_kernel(message, spots, before, out):
    add_rows(out, 0, message, spots, [before])


def slope_kernel(spans, fanout, rows, *refs):
    count = len(spans)
    feats = refs[:count]
    weight, vec = refs[count : count + 2]
    outs = refs[count + 2 :]
    for feat, at, out in zip(feats, spans, outs):
        pre = dot(feat[at : at + rows, :], weight[...])
        turned = edge_data(feat, at, rows).T
        for k in range(fanout):
            act = pre + edge_length(turned, fanout, k) * vec[...]
            out[k * rows : (k + 1) * rows, :] = slope(act).astype(BF16)


def halo_rows(state, pick, parts):
    stacked = jnp.concatenate(
        [state[:, i * LANES : (i + 1) * LANES] for i in range(parts)], axis=0
    )
    return dot(pick, stacked).astype(BF16)


def piece_of(row, part, parts, sects, per):
    count = HALO_ROWS
    node, which = row % per // count, row % count
    return ((node * sects + row // per) * count + which) * parts + part


def join_pieces(pieces, parts, sects):
    count = pieces.shape[0]
    rows = count // parts
    at = iota((count, count), 0)
    wanted = piece_of(at % rows, at // rows, parts, sects, rows // sects)
    found = dot(mark(iota((count, count), 1) == wanted), pieces).astype(BF16)
    return jnp.concatenate([found[i * rows : (i + 1) * rows] for i in range(parts)], axis=1)


def cut_pieces(rows, parts, sects):
    each, count = rows.shape[0], rows.shape[0] * parts
    at = iota((count, count), 1)
    wanted = piece_of(at % each, at // each, parts, sects, each // sects)
    stacked = jnp.concatenate(
        [rows[:, i * LANES : (i + 1) * LANES] for i in range(parts)], axis=0
    )
    return dot(mark(iota((count, count), 0) == wanted), stacked).astype(BF16)


def add_pieces(pieces, pick_t, block, parts):
    total = dot(pick_t, pieces)
    return jnp.concatenate([total[i * block : (i + 1) * block] for i in range(parts)], axis=1)


def start_kernel(parts, sums, *refs):
    received, (init, weight, pick, state, mesh_pre, halo) = refs[:-6], refs[-6:]
    agg = sums[...]
    for ref in received:
        agg = agg + ref[...].astype(F32)
    pre = dot(agg.astype(BF16), weight[...])
    mesh_pre[...] = pre
    new = (init[...].astype(F32) + silu(pre)).astype(BF16)
    state[...] = new
    halo[...] = halo_rows(new, pick[...], parts)


def layer_forward(state, pieces, source, weights, parts, sects):
    block = state.shape[0]
    halo = join_pieces(pieces, parts, sects)
    table = jnp.concatenate([state, halo], axis=0)
    from_src = 0.5 * dot(table, weights(0))
    to_dst = 0.5 * dot(state, weights(1))
    gathered = dot(source[...], from_src.astype(BF16))
    agg = jnp.zeros(state.shape, F32)
    slopes = []
    for k in range(source.shape[0] // block):
        joined = gathered[k * block : (k + 1) * block] + to_dst
        bend = jnp.tanh(joined)
        agg = agg + (joined + joined * bend)
        joined, bend = joined.astype(BF16), bend.astype(BF16)
        slopes.append(1 + bend + joined * (1 - bend * bend))
    mixed = dot(state, weights(2)) + dot(agg.astype(BF16), weights(3))
    return mixed, slopes


def layer_back(grad, mixed, slopes, source_t, weights):
    block = grad.shape[0]
    normed, scale = norm_parts(mixed)
    grad_mixed = norm_back(grad, normed, scale)
    grad_state = grad + back_dot(grad_mixed, weights(2))
    grad_agg = 0.5 * dot_t(grad_mixed.astype(BF16), weights(3))
    low = grad_agg.astype(BF16)
    total = jnp.zeros(grad.shape, F32)
    for found in slopes:
        total = total + found.astype(F32)
    total = grad_agg * total
    pieces = [low * found for found in slopes]
    grad_src = dot(source_t[...], jnp.concatenate(pieces, axis=0))
    grad_state = grad_state + back_dot(total, weights(1))
    grad_table = dot_t(grad_src.astype(BF16), weights(0))
    return grad_state + grad_table[:block], grad_table[block:]


def layer_weights(weights, layer):
    return lambda i: weights[layer, i]


def first_kernel(
    layer, parts, sects, state, pieces, source, weights, pick, new, mixed, slopes, halo
):
    block = state.shape[0]
    own = state[...]
    used = layer_weights(weights, layer)
    value, found = layer_forward(own, pieces[...], source, used, parts, sects)
    mixed[...] = value
    for k, part in enumerate(found):
        slopes[k * block : (k + 1) * block, :] = part
    normed, _ = norm_parts(value)
    result = (own.astype(F32) + silu(normed)).astype(BF16)
    new[...] = result
    halo[...] = halo_rows(result, pick[...], parts)


def last_kernel(
    layer, parts, sects, state, pieces, source, source_t, weights, cot, out, grad_own, grad_halo
):
    own = state[...]
    used = layer_weights(weights, layer)
    value, found = layer_forward(own, pieces[...], source, used, parts, sects)
    normed, _ = norm_parts(value)
    out[...] = (own.astype(F32) + silu(normed)).astype(BF16)
    mine, sent = layer_back(cot[...].astype(F32), value, found, source_t, used)
    grad_own[...] = mine
    grad_halo[...] = cut_pieces(sent.astype(BF16), parts, sects)


def back_kernel(
    layer,
    parts,
    sects,
    mine,
    returned,
    pick_t,
    mixed,
    slopes,
    source_t,
    weights,
    grad_own,
    grad_halo,
):
    block = mine.shape[0]
    grad = mine[...] + add_pieces(returned[...], pick_t[...], block, parts)
    fan = slopes.shape[0] // block
    found = [slopes[k * block : (k + 1) * block, :] for k in range(fan)]
    used = layer_weights(weights, layer)
    own, sent = layer_back(grad, mixed[...], found, source_t, used)
    grad_own[...] = own
    grad_halo[...] = cut_pieces(sent.astype(BF16), parts, sects)


def mesh_back_kernel(parts, mine, returned, pick_t, mesh_pre, weight, out):
    block = mine.shape[0]
    grad = mine[...] + add_pieces(returned[...], pick_t[...], block, parts)
    out[...] = back_dot(grad * slope(mesh_pre[...]), weight[...]).astype(BF16)


def edge_marks(feat, at, rows, nodes, block, fanout, who):
    turned = edge_data(feat, at, rows).T
    ids = iota((rows, nodes * block), 1)
    return [
        mark(
            ids
            == spot_of(
                lambda t: turned[:, t : t + 1], fanout, k, who[0], who[1], nodes, block
            )
        )
        for k in range(fanout)
    ]


def mark_kernel(spans, rows, nodes, block, fanout, who, *refs):
    feats, state = refs[: len(spans)], refs[len(spans)]
    *outs, final = refs[len(spans) + 1 :]
    final[...] = state[...]
    for feat, at, out in zip(feats, spans, outs):
        for k, found in enumerate(edge_marks(feat, at, rows, nodes, block, fanout, who)):
            out[k * rows : (k + 1) * rows, :] = found


def message_back_kernel(spans, rows, ready, nodes, block, fanout, who, *refs):
    count = len(spans)
    feats, slopes = refs[:count], refs[count : 2 * count]
    outs = refs[2 * count :]
    grads, outs = outs[:nodes], outs[nodes:]
    marks = []
    for feat, at in zip(feats, spans):
        if ready:
            marks.append(feat[...])
        else:
            marks += edge_marks(feat, at, rows, nodes, block, fanout, who)
    same, other = grads[: nodes // 2][::-1], grads[nodes // 2 :][::-1]
    picked = dot(
        jnp.concatenate(marks, axis=0),
        jnp.concatenate([ref[...] for ref in (*same, *other)], axis=0),
    )
    size = outs[0].shape[1]
    chunks = slopes[0].shape[1] // size
    per = count * chunks // len(outs)
    for i in range(count):
        total = jnp.zeros((rows, slopes[0].shape[1]), F32)
        for k in range(fanout):
            at = (i * fanout + k) * rows
            part = slopes[i][k * rows : (k + 1) * rows, :].astype(F32)
            total = total + picked[at : at + rows] * part
        at = i % per * rows
        for c, out in enumerate(outs[i // per * chunks : (i // per + 1) * chunks]):
            out[at : at + rows, :] = total[:, c * size : (c + 1) * size].astype(out.dtype)


def grid_back_kernel(chunks, *refs):
    *parts, weight, out = refs
    count = len(parts) // 3
    rows = parts[0].shape[0]
    total = [
        parts[i][...]
        + parts[count + i][:rows, :].astype(F32)
        + parts[2 * count + i][...].astype(F32)
        for i in range(count)
    ]
    each = count // chunks
    columns = [
        jnp.concatenate(total[c * each : (c + 1) * each], axis=0) for c in range(chunks)
    ]
    out[...] = back_dot(jnp.concatenate(columns, axis=1), weight[...]).astype(BF16)


def call(kernel, outs, args, smem=0, scratch=(), space=pltpu.VMEM, aliases=None):
    specs = [pl.BlockSpec(memory_space=pltpu.SMEM)] * smem
    specs += [pl.BlockSpec(memory_space=space)] * (len(args) - smem)
    moved = sum(a.size * a.dtype.itemsize for a in list(args) + list(outs))
    held = sum(math.prod(a.shape) * 4 for a in scratch)
    limit = 2 * (moved + held) + 6 * MIB
    result = pl.pallas_call(
        kernel,
        out_shape=list(outs),
        in_specs=specs,
        out_specs=[pl.BlockSpec(memory_space=pltpu.VMEM)] * len(outs),
        scratch_shapes=list(scratch),
        input_output_aliases=aliases or {},
        compiler_params=pltpu.CompilerParams(vmem_limit_bytes=limit),
        cost_estimate=pl.CostEstimate(
            flops=0, bytes_accessed=moved, transcendentals=0
        ),
    )(*args)
    return result


def shape(dims, dtype):
    return jax.ShapeDtypeStruct(dims, dtype)


def swap(value, axis, apart):
    size = lax.axis_size(axis)
    return lax.ppermute(value, axis, [(i, i ^ apart) for i in range(size)])


def body(
    grid_feat,
    edge_len,
    g2m_owner,
    g2m_dst,
    enc_weight,
    enc_vec,
    mesh_init,
    mesh_weight,
    halo_send,
    mesh_src,
    proc_weight,
    cot,
):
    nodes = lax.axis_size("node")
    sects = lax.axis_size("sect")
    width = grid_feat.shape[1]
    grid_rows, fanout = edge_len.shape
    block = mesh_init.shape[1]
    parts = width // LANES
    both = ("node", "sect")
    assert halo_send.shape[-1] == HALO_ROWS
    who = jnp.stack([lax.axis_index("sect"), lax.axis_index("node")]).astype(jnp.int32)

    axes = [1 << i for i in range(sects.bit_length() - 1)]
    part_rows = grid_rows // len(axes)
    assert len(axes) == 2
    ends = pltpu.VMEM((fanout, grid_rows), jnp.int32)
    packed = call(
        functools.partial(pack_kernel, block),
        [shape((part_rows + META_ROWS, width), BF16)] * len(axes),
        [
            pltpu.with_memory_space_constraint(value, pltpu.HBM)
            for value in (grid_feat, edge_len.T, g2m_owner.T, g2m_dst.T)
        ],
        scratch=[
            pltpu.VMEM((fanout, grid_rows), F32),
            ends,
            ends,
            pltpu.SemaphoreType.DMA((3 + len(axes),)),
        ],
        space=pltpu.HBM,
    )
    where = {(0, p): (part, 0) for p, part in enumerate(packed)}
    steps = [[(0, p) for p in range(len(axes))]]
    held, names = list(packed), [[0] for _ in axes]
    for step in range(len(axes)):
        given = [
            swap(part, "sect", axes[(p + step) % len(axes)]) for p, part in enumerate(held)
        ]
        steps.append([])
        for p, part in enumerate(given):
            axis = axes[(p + step) % len(axes)]
            for i, j in enumerate(list(names[p])):
                where[j ^ axis, p] = (part, i * packed[0].shape[0])
                names[p].append(j ^ axis)
                steps[-1].append((j ^ axis, p))
        held = [jnp.concatenate(pair, axis=0) for pair in zip(held, given)]
    sends = halo_send[0, 0].transpose(0, 2, 1)
    src_row = mesh_src[0].T
    fan = src_row.shape[0]
    pieces = sends.size * parts
    table_len = block + sends.size
    pick, pick_t, source, source_t, weight, vec = call(
        functools.partial(index_kernel, block, parts),
        [
            shape((pieces, parts * block), BF16),
            shape((parts * block, pieces), BF16),
            shape((fan * block, table_len), BF16),
            shape((table_len, fan * block), BF16),
            shape(enc_weight.shape, BF16),
            shape((1, width), F32),
        ],
        [
            pltpu.with_memory_space_constraint(value, pltpu.HBM)
            for value in (sends, src_row, enc_weight, enc_vec[None, :])
        ],
        scratch=[
            pltpu.VMEM(sends.shape, jnp.int32),
            pltpu.VMEM(src_row.shape, jnp.int32),
            pltpu.SemaphoreType.DMA((4,)),
        ],
        space=pltpu.HBM,
    )

    half = nodes // 2
    sums_shape = shape((nodes * block, width), F32)

    def encode(units, last, before):
        edges = len(units) * part_rows * fanout
        used = [where[unit] for unit in units]
        args = [who, *(part for part, _ in used), weight, vec, *before]
        outs = [
            shape((half * block, width), BF16) if last else sums_shape,
            shape((edges, width), BF16),
            shape((1, edges), jnp.int32),
        ]
        return call(
            functools.partial(
                encode_kernel,
                tuple(at for _, at in used),
                nodes,
                block,
                fanout,
                part_rows,
                last,
            ),
            outs if last else outs[:1],
            args,
            smem=1,
            scratch=() if last else [pltpu.VMEM(s.shape, s.dtype) for s in outs[1:]],
            aliases={len(args) - 1: 0} if before and not last else None,
        )

    before = []
    for units in steps[:-1]:
        before = encode(units, False, before)
    cross, message, spots = encode(steps[-1], True, before)
    (keep,) = call(
        keep_kernel, [shape((half * block, width), BF16)], [message, spots, *before]
    )

    pair = keep.astype(F32) + swap(cross, "node", 1).astype(F32)
    pair = pair.reshape(half, block, width)
    arrived = [
        swap(pair[q].astype(BF16), "node", 2 * q) for q in reversed(range(1, half))
    ]

    units = [(j, p) for j in range(sects) for p in range(len(axes))]
    slopes = call(
        functools.partial(
            slope_kernel, tuple(where[unit][1] for unit in units), fanout, part_rows
        ),
        [shape((fanout * part_rows, width), BF16)] * len(units),
        [*(where[unit][0] for unit in units), weight, vec],
    )
    tied = lax.optimization_barrier((*arrived, *slopes))
    arrived, slopes = tied[: half - 1], dict(zip(units, tied[half - 1 :]))

    halo_shape = shape((pieces, LANES), BF16)
    row_low, row_high = shape((block, width), BF16), shape((block, width), F32)

    def exchange(value):
        return lax.all_to_all(value, both, split_axis=0, concat_axis=0, tiled=True)

    state, mesh_pre, halo = call(
        functools.partial(start_kernel, parts),
        [row_low, row_high, halo_shape],
        [pair[0], *arrived, mesh_init[0], mesh_weight, pick],
    )
    assert proc_weight.shape[0] == 2
    state, mixed, slope_first, halo = call(
        functools.partial(first_kernel, 0, parts, sects),
        [row_low, row_high, shape((fan * block, width), BF16), halo_shape],
        [state, exchange(halo), source, proc_weight, pick],
    )
    mesh_out, grad, halo = call(
        functools.partial(last_kernel, 1, parts, sects),
        [row_low, row_high, halo_shape],
        [state, exchange(halo), source, source_t, proc_weight, cot[0]],
    )
    grad, halo = call(
        functools.partial(back_kernel, 0, parts, sects),
        [row_high, halo_shape],
        [grad, exchange(halo), pick_t, mixed, slope_first, source_t, proc_weight],
    )
    (grad_sum,) = call(
        functools.partial(mesh_back_kernel, parts),
        [row_low],
        [grad, exchange(halo), pick_t, mesh_pre, mesh_weight],
    )

    same = [swap(grad_sum, "node", 2 * q) for q in reversed(range(1, half))]
    same = [grad_sum, *same[::-1]]
    ready = nodes * block <= 8 * LANES
    picks_of = {unit: where[unit] for unit in units}
    if ready:
        seen, _ = lax.optimization_barrier((who, grad_sum))
        *found, mesh_out = call(
            functools.partial(
                mark_kernel,
                tuple(where[unit][1] for unit in units),
                part_rows,
                nodes,
                block,
                fanout,
            ),
            [shape((fanout * part_rows, nodes * block), BF16)] * len(units) + [row_low],
            [seen, *(where[unit][0] for unit in units), mesh_out],
            smem=1,
        )
        same[-1] = lax.optimization_barrier((same[-1], found[0]))[0]
        picks_of = {unit: (part, 0) for unit, part in zip(units, found)}
    other = [swap(rows, "node", 1) for rows in same[::-1]][::-1]
    gathered = (*same[::-1], *other[::-1])

    def message_back(groups, dtype):
        used = [unit for group in groups for unit in group]
        return call(
            functools.partial(
                message_back_kernel,
                tuple(picks_of[unit][1] for unit in used),
                part_rows,
                ready,
                nodes,
                block,
                fanout,
            ),
            [
                shape((len(group) * part_rows, width // CHUNKS), dtype)
                for group in groups
                for _ in range(CHUNKS)
            ],
            [
                who,
                *(picks_of[unit][0] for unit in used),
                *(slopes[unit] for unit in used),
                *gathered,
            ],
            smem=1,
        )

    first, then = axes, axes[::-1]
    chunks = [(p, c) for c in range(CHUNKS) for p in range(len(axes))]

    def ordered(found):
        return [found[p * CHUNKS + c] for p, c in chunks]

    given = ordered(
        message_back(
            [[(a, p), (a ^ b, p)] for p, (a, b) in enumerate(zip(first, then))], BF16
        )
    )
    gathered = lax.optimization_barrier((*gathered, *given))[: len(gathered)]
    passed = ordered(message_back([[(b, p)] for p, b in enumerate(then)], F32))
    gathered = lax.optimization_barrier((*gathered, *passed))[: len(gathered)]
    given = [swap(part, "sect", first[p]) for part, (p, _) in zip(given, chunks)]
    passed = [
        (mine + part[part_rows:].astype(F32)).astype(BF16)
        for mine, part in zip(passed, given)
    ]
    kept = ordered(message_back([[(0, p)] for p in range(len(axes))], F32))
    passed = [swap(part, "sect", then[p]) for part, (p, _) in zip(passed, chunks)]
    (grid_grad,) = call(
        functools.partial(grid_back_kernel, CHUNKS),
        [shape((grid_rows, width), BF16)],
        [*kept, *given, *passed, enc_weight],
    )
    return (mesh_out[None], grid_grad)


def solution(mesh):
    return jax.shard_map(
        body,
        mesh=mesh,
        in_specs=(
            P(("sect", "node"), None),
            P(("sect", "node"), None),
            P(("sect", "node"), None),
            P(("sect", "node"), None),
            P(),
            P(),
            P("node", "sect", None),
            P(),
            P("sect", "node", None, None, None),
            P("node", "sect", None),
            P(),
            P("node", "sect", None),
        ),
        out_specs=(P("node", "sect", None), P(("sect", "node"), None)),
        check_vma=False,
    )
```

```python
import functools
import math

import jax
import jax.numpy as jnp
from jax import lax
from jax.experimental import pallas as pl
from jax.experimental.pallas import tpu as pltpu
from jax.sharding import PartitionSpec as P

F32 = jnp.float32
BF16 = jnp.bfloat16
LANES = 128
META_ROWS = 16
CHUNKS = 2
MIB = 1024 * 1024


def sigmoid(value):
    return 0.5 * jnp.tanh(0.5 * value) + 0.5


def silu(value):
    return value * sigmoid(value)


def slope(value):
    sig = sigmoid(value)
    return sig * (1.0 + value * (1.0 - sig))


def dot(left, right):
    return jnp.dot(left, right, preferred_element_type=F32)


def dot_t(left, right):
    return lax.dot_general(left, right, (((1,), (1,)), ((), ())), preferred_element_type=F32)


def halves(value):
    high = value.astype(BF16)
    return high, (value - high.astype(F32)).astype(BF16)


def back_dot(grad, weight):
    rows = grad.shape[0]
    both = dot_t(jnp.concatenate(halves(grad), axis=0), weight)
    return both[:rows] + both[rows:]


def mark(equal):
    return jnp.where(equal, 1.0, 0.0).astype(BF16)


def iota(shape, axis):
    return lax.broadcasted_iota(jnp.int32, shape, axis)


def norm_parts(mixed):
    mean = jnp.mean(mixed, axis=-1, keepdims=True)
    centred = mixed - mean
    scale = lax.rsqrt(jnp.mean(centred * centred, axis=-1, keepdims=True) + 1e-05)
    return centred * scale, scale


def norm_back(grad, normed, scale):
    pull = grad * slope(normed)
    return scale * (
        pull
        - jnp.mean(pull, axis=-1, keepdims=True)
        - normed * jnp.mean(pull * normed, axis=-1, keepdims=True)
    )


def pack_kernel(block, feat, lens, owner, dst, *refs):
    *outs, held, own_held, dst_held, sems = refs
    rows = feat.shape[0] // len(outs)
    pairs = [(lens, held), (owner, own_held), (dst, dst_held)]
    pairs += [
        (feat.at[i * rows : (i + 1) * rows, :], out.at[:rows, :]) for i, out in enumerate(outs)
    ]
    copies = [
        pltpu.make_async_copy(source, target, sems.at[i])
        for i, (source, target) in enumerate(pairs)
    ]
    for copy in copies:
        copy.start()
    for copy in copies[:3]:
        copy.wait()
    high, middle = halves(held[...])
    low = (held[...] - high.astype(F32) - middle.astype(F32)).astype(BF16)
    far = dst_held[...]
    section = far // block
    found = [v.astype(F32) for v in (high, middle, low)]
    found += [v.astype(F32) for v in (own_held[...], section, far - section * block)]
    fill = META_ROWS - 6 * lens.shape[0]
    found.append(jnp.zeros((fill, feat.shape[0]), F32))
    meta = jnp.concatenate(found, axis=0).astype(BF16)
    rest = jnp.zeros((META_ROWS, feat.shape[1] - rows), BF16)
    for i, out in enumerate(outs):
        out[rows:, :] = jnp.concatenate([meta[:, i * rows : (i + 1) * rows], rest], axis=1)
    for copy in copies[3:]:
        copy.wait()


def index_kernel(block, parts, *refs):
    wanted, far_weight, far_vec = refs[:2], refs[2], refs[3]
    pick, pick_t, source, source_t, weight, vec, sends, src_row, sems = refs[4:]
    pairs = ((wanted[0], sends), (wanted[1], src_row), (far_vec, vec), (far_weight, weight))
    copies = [
        pltpu.make_async_copy(start, target, sems.at[i])
        for i, (start, target) in enumerate(pairs)
    ]
    for copy in copies:
        copy.start()
    for copy in copies[:2]:
        copy.wait()
    sects, count, nodes = sends.shape
    pieces = pick.shape[0]
    at = iota((1, pieces), 1)
    part, row = at % parts, at // parts
    peer = row // count
    whose = mark(iota((nodes, pieces), 0) == peer % nodes)
    place = jnp.zeros((1, pieces), F32)
    for t in range(sects):
        found = dot(sends[t].astype(F32).astype(BF16), whose)
        for c in range(count):
            here = jnp.logical_and(peer // nodes == t, row % count == c)
            place = place + jnp.where(here, found[c : c + 1], 0.0)
    place = place + (part * block).astype(F32)
    pick_t[...] = mark(iota((parts * block, pieces), 0) == place.astype(jnp.int32))
    turned = jnp.broadcast_to(place, (8, pieces)).T[:, :1].astype(jnp.int32)
    pick[...] = mark(iota((pieces, parts * block), 1) == turned)
    table_len = source_t.shape[0]
    column = src_row[...].astype(F32).T.astype(jnp.int32)
    ids = iota((block, table_len), 1)
    ids_t = iota((table_len, block), 0)
    for k in range(src_row.shape[0]):
        rows = slice(k * block, (k + 1) * block)
        source[rows, :] = mark(ids == column[:, k : k + 1])
        source_t[:, rows] = mark(ids_t == src_row[k : k + 1, :])
    for copy in copies[2:]:
        copy.wait()


def edge_data(feat, at, rows):
    return feat[at + rows : at + rows + META_ROWS, :rows].astype(F32)


def edge_length(meta, fanout, k):
    high, middle, low = (meta[:, t * fanout + k : t * fanout + k + 1] for t in range(3))
    return high + middle + low


def spot_of(pick, fanout, k, section, node, nodes, block):
    owner, where, place = (pick((3 + t) * fanout + k).astype(jnp.int32) for t in range(3))
    apart = jnp.bitwise_xor(owner, node)
    order = lax.shift_right_logical(apart, 1) + jnp.bitwise_and(apart, 1) * (nodes // 2)
    return jnp.where(where == section, order * block + place, -1)


def add_rows(out, base, message, spots, before):
    step = min(out.shape[0], 512)

    def chunk(c, carry):
        start = pl.multiple_of(c * step, step)
        ids = iota((step, spots.shape[1]), 0) + (base + start)
        part = dot(mark(ids == spots[...]), message[...])
        for ref in before:
            part = part + ref[pl.ds(base + start, step), :]
        out[pl.ds(start, step), :] = part.astype(out.dtype)
        return carry

    lax.fori_loop(0, out.shape[0] // step, chunk, 0)


def encode_kernel(spans, nodes, block, fanout, rows, last, who, *refs):
    count = len(spans)
    feats = refs[:count]
    weight, vec = refs[count : count + 2]
    *before, out, message, spots = refs[count + 2 :]
    section, node = who[0], who[1]
    pre = 0.5 * dot(
        jnp.concatenate([feat[at : at + rows, :] for feat, at in zip(feats, spans)], axis=0),
        weight[...],
    )
    part = 0.5 * vec[...]
    for j in range(count):
        meta = edge_data(feats[j], spans[j], rows)
        turned = meta.T
        for k in range(fanout):
            at = (j * fanout + k) * rows
            act = pre[j * rows : (j + 1) * rows] + edge_length(turned, fanout, k) * part
            message[at : at + rows, :] = (act + act * jnp.tanh(act)).astype(BF16)
            spots[:, at : at + rows] = spot_of(
                lambda t, meta=meta: meta[t : t + 1], fanout, k, section, node, nodes, block
            )
    add_rows(out, nodes // 2 * block if last else 0, message, spots, before)


def keep_kernel(message, spots, before, out):
    add_rows(out, 0, message, spots, [before])


def slope_kernel(spans, fanout, rows, *refs):
    count = len(spans)
    feats = refs[:count]
    weight, vec = refs[count : count + 2]
    outs = refs[count + 2 :]
    for feat, at, out in zip(feats, spans, outs):
        pre = dot(feat[at : at + rows, :], weight[...])
        turned = edge_data(feat, at, rows).T
        for k in range(fanout):
            act = pre + edge_length(turned, fanout, k) * vec[...]
            out[k * rows : (k + 1) * rows, :] = slope(act).astype(BF16)


def halo_rows(state, pick, parts):
    stacked = jnp.concatenate(
        [state[:, i * LANES : (i + 1) * LANES] for i in range(parts)], axis=0
    )
    return dot(pick, stacked).astype(BF16)


def join_pieces(pieces, parts):
    count = pieces.shape[0]
    rows = count // parts
    at = iota((count, count), 0)
    onehot = mark(iota((count, count), 1) == at % rows * parts + at // rows)
    found = dot(onehot, pieces).astype(BF16)
    return jnp.concatenate([found[i * rows : (i + 1) * rows] for i in range(parts)], axis=1)


def cut_pieces(rows, parts):
    each, count = rows.shape[0], rows.shape[0] * parts
    at = iota((count, count), 0)
    onehot = mark(iota((count, count), 1) == at % parts * each + at // parts)
    stacked = jnp.concatenate(
        [rows[:, i * LANES : (i + 1) * LANES] for i in range(parts)], axis=0
    )
    return dot(onehot, stacked).astype(BF16)


def add_pieces(pieces, pick_t, block, parts):
    total = dot(pick_t, pieces)
    return jnp.concatenate([total[i * block : (i + 1) * block] for i in range(parts)], axis=1)


def start_kernel(parts, sums, *refs):
    received, (init, weight, pick, state, mesh_pre, halo) = refs[:-6], refs[-6:]
    agg = sums[...]
    for ref in received:
        agg = agg + ref[...].astype(F32)
    pre = dot(agg.astype(BF16), weight[...])
    mesh_pre[...] = pre
    new = (init[...].astype(F32) + silu(pre)).astype(BF16)
    state[...] = new
    halo[...] = halo_rows(new, pick[...], parts)


def layer_forward(state, pieces, source, weights, parts):
    block = state.shape[0]
    halo = join_pieces(pieces, parts)
    table = jnp.concatenate([state, halo], axis=0)
    from_src = 0.5 * dot(table, weights(0))
    to_dst = 0.5 * dot(state, weights(1))
    gathered = dot(source[...], from_src.astype(BF16))
    agg = jnp.zeros(state.shape, F32)
    slopes = []
    for k in range(source.shape[0] // block):
        joined = gathered[k * block : (k + 1) * block] + to_dst
        bend = jnp.tanh(joined)
        agg = agg + (joined + joined * bend)
        joined, bend = joined.astype(BF16), bend.astype(BF16)
        slopes.append(1 + bend + joined * (1 - bend * bend))
    mixed = dot(state, weights(2)) + dot(agg.astype(BF16), weights(3))
    return mixed, slopes


def layer_back(grad, mixed, slopes, source_t, weights):
    block = grad.shape[0]
    normed, scale = norm_parts(mixed)
    grad_mixed = norm_back(grad, normed, scale)
    grad_state = grad + back_dot(grad_mixed, weights(2))
    grad_agg = 0.5 * dot_t(grad_mixed.astype(BF16), weights(3))
    low = grad_agg.astype(BF16)
    total = jnp.zeros(grad.shape, F32)
    for found in slopes:
        total = total + found.astype(F32)
    total = grad_agg * total
    pieces = [low * found for found in slopes]
    grad_src = dot(source_t[...], jnp.concatenate(pieces, axis=0))
    grad_state = grad_state + back_dot(total, weights(1))
    grad_table = dot_t(grad_src.astype(BF16), weights(0))
    return grad_state + grad_table[:block], grad_table[block:]


def layer_weights(weights, layer):
    return lambda i: weights[layer, i]


def first_kernel(
    layer, parts, state, pieces, source, weights, pick, new, mixed, slopes, halo
):
    block = state.shape[0]
    own = state[...]
    used = layer_weights(weights, layer)
    value, found = layer_forward(own, pieces[...], source, used, parts)
    mixed[...] = value
    for k, part in enumerate(found):
        slopes[k * block : (k + 1) * block, :] = part
    normed, _ = norm_parts(value)
    result = (own.astype(F32) + silu(normed)).astype(BF16)
    new[...] = result
    halo[...] = halo_rows(result, pick[...], parts)


def last_kernel(
    layer, parts, state, pieces, source, source_t, weights, cot, out, grad_own, grad_halo
):
    own = state[...]
    used = layer_weights(weights, layer)
    value, found = layer_forward(own, pieces[...], source, used, parts)
    normed, _ = norm_parts(value)
    out[...] = (own.astype(F32) + silu(normed)).astype(BF16)
    mine, sent = layer_back(cot[...].astype(F32), value, found, source_t, used)
    grad_own[...] = mine
    grad_halo[...] = cut_pieces(sent.astype(BF16), parts)


def back_kernel(
    layer,
    parts,
    mine,
    returned,
    pick_t,
    mixed,
    slopes,
    source_t,
    weights,
    grad_own,
    grad_halo,
):
    block = mine.shape[0]
    grad = mine[...] + add_pieces(returned[...], pick_t[...], block, parts)
    fan = slopes.shape[0] // block
    found = [slopes[k * block : (k + 1) * block, :] for k in range(fan)]
    used = layer_weights(weights, layer)
    own, sent = layer_back(grad, mixed[...], found, source_t, used)
    grad_own[...] = own
    grad_halo[...] = cut_pieces(sent.astype(BF16), parts)


def mesh_back_kernel(parts, mine, returned, pick_t, mesh_pre, weight, out):
    block = mine.shape[0]
    grad = mine[...] + add_pieces(returned[...], pick_t[...], block, parts)
    out[...] = back_dot(grad * slope(mesh_pre[...]), weight[...]).astype(BF16)


def edge_marks(feat, at, rows, nodes, block, fanout, who):
    turned = edge_data(feat, at, rows).T
    ids = iota((rows, nodes * block), 1)
    return [
        mark(
            ids
            == spot_of(
                lambda t: turned[:, t : t + 1], fanout, k, who[0], who[1], nodes, block
            )
        )
        for k in range(fanout)
    ]


def mark_kernel(spans, rows, nodes, block, fanout, who, *refs):
    feats, state = refs[: len(spans)], refs[len(spans)]
    *outs, final = refs[len(spans) + 1 :]
    final[...] = state[...]
    for feat, at, out in zip(feats, spans, outs):
        for k, found in enumerate(edge_marks(feat, at, rows, nodes, block, fanout, who)):
            out[k * rows : (k + 1) * rows, :] = found


def message_back_kernel(spans, rows, ready, nodes, block, fanout, who, *refs):
    count = len(spans)
    feats, slopes = refs[:count], refs[count : 2 * count]
    outs = refs[2 * count :]
    grads, outs = outs[:nodes], outs[nodes:]
    marks = []
    for feat, at in zip(feats, spans):
        if ready:
            marks.append(feat[...])
        else:
            marks += edge_marks(feat, at, rows, nodes, block, fanout, who)
    same, other = grads[: nodes // 2][::-1], grads[nodes // 2 :][::-1]
    picked = dot(
        jnp.concatenate(marks, axis=0),
        jnp.concatenate([ref[...] for ref in (*same, *other)], axis=0),
    )
    size = outs[0].shape[1]
    chunks = slopes[0].shape[1] // size
    per = count * chunks // len(outs)
    for i in range(count):
        total = jnp.zeros((rows, slopes[0].shape[1]), F32)
        for k in range(fanout):
            at = (i * fanout + k) * rows
            part = slopes[i][k * rows : (k + 1) * rows, :].astype(F32)
            total = total + picked[at : at + rows] * part
        at = i % per * rows
        for c, out in enumerate(outs[i // per * chunks : (i // per + 1) * chunks]):
            out[at : at + rows, :] = total[:, c * size : (c + 1) * size].astype(out.dtype)


def grid_back_kernel(chunks, *refs):
    *parts, weight, out = refs
    count = len(parts) // 3
    rows = parts[0].shape[0]
    total = [
        parts[i][...]
        + parts[count + i][:rows, :].astype(F32)
        + parts[2 * count + i][...].astype(F32)
        for i in range(count)
    ]
    each = count // chunks
    columns = [
        jnp.concatenate(total[c * each : (c + 1) * each], axis=0) for c in range(chunks)
    ]
    out[...] = back_dot(jnp.concatenate(columns, axis=1), weight[...]).astype(BF16)


def call(kernel, outs, args, smem=0, scratch=(), space=pltpu.VMEM, aliases=None):
    specs = [pl.BlockSpec(memory_space=pltpu.SMEM)] * smem
    specs += [pl.BlockSpec(memory_space=space)] * (len(args) - smem)
    moved = sum(a.size * a.dtype.itemsize for a in list(args) + list(outs))
    held = sum(math.prod(a.shape) * 4 for a in scratch)
    limit = 2 * (moved + held) + 6 * MIB
    result = pl.pallas_call(
        kernel,
        out_shape=list(outs),
        in_specs=specs,
        out_specs=[pl.BlockSpec(memory_space=pltpu.VMEM)] * len(outs),
        scratch_shapes=list(scratch),
        input_output_aliases=aliases or {},
        compiler_params=pltpu.CompilerParams(vmem_limit_bytes=limit),
        cost_estimate=pl.CostEstimate(
            flops=0, bytes_accessed=moved, transcendentals=0
        ),
    )(*args)
    return result


def shape(dims, dtype):
    return jax.ShapeDtypeStruct(dims, dtype)


def swap(value, axis, apart):
    size = lax.axis_size(axis)
    return lax.ppermute(value, axis, [(i, i ^ apart) for i in range(size)])


def body(
    grid_feat,
    edge_len,
    g2m_owner,
    g2m_dst,
    enc_weight,
    enc_vec,
    mesh_init,
    mesh_weight,
    halo_send,
    mesh_src,
    proc_weight,
    cot,
):
    nodes = lax.axis_size("node")
    sects = lax.axis_size("sect")
    width = grid_feat.shape[1]
    grid_rows, fanout = edge_len.shape
    block = mesh_init.shape[1]
    parts = width // LANES
    both = ("sect", "node")
    who = jnp.stack([lax.axis_index("sect"), lax.axis_index("node")]).astype(jnp.int32)

    axes = [1 << i for i in range(sects.bit_length() - 1)]
    part_rows = grid_rows // len(axes)
    assert len(axes) == 2
    ends = pltpu.VMEM((fanout, grid_rows), jnp.int32)
    packed = call(
        functools.partial(pack_kernel, block),
        [shape((part_rows + META_ROWS, width), BF16)] * len(axes),
        [
            pltpu.with_memory_space_constraint(value, pltpu.HBM)
            for value in (grid_feat, edge_len.T, g2m_owner.T, g2m_dst.T)
        ],
        scratch=[
            pltpu.VMEM((fanout, grid_rows), F32),
            ends,
            ends,
            pltpu.SemaphoreType.DMA((3 + len(axes),)),
        ],
        space=pltpu.HBM,
    )
    where = {(0, p): (part, 0) for p, part in enumerate(packed)}
    steps = [[(0, p) for p in range(len(axes))]]
    held, names = list(packed), [[0] for _ in axes]
    for step in range(len(axes)):
        given = [
            swap(part, "sect", axes[(p + step) % len(axes)]) for p, part in enumerate(held)
        ]
        steps.append([])
        for p, part in enumerate(given):
            axis = axes[(p + step) % len(axes)]
            for i, j in enumerate(list(names[p])):
                where[j ^ axis, p] = (part, i * packed[0].shape[0])
                names[p].append(j ^ axis)
                steps[-1].append((j ^ axis, p))
        held = [jnp.concatenate(pair, axis=0) for pair in zip(held, given)]
    sends = halo_send[0, 0].transpose(0, 2, 1)
    src_row = mesh_src[0].T
    fan = src_row.shape[0]
    pieces = sends.size * parts
    table_len = block + sends.size
    pick, pick_t, source, source_t, weight, vec = call(
        functools.partial(index_kernel, block, parts),
        [
            shape((pieces, parts * block), BF16),
            shape((parts * block, pieces), BF16),
            shape((fan * block, table_len), BF16),
            shape((table_len, fan * block), BF16),
            shape(enc_weight.shape, BF16),
            shape((1, width), F32),
        ],
        [
            pltpu.with_memory_space_constraint(value, pltpu.HBM)
            for value in (sends, src_row, enc_weight, enc_vec[None, :])
        ],
        scratch=[
            pltpu.VMEM(sends.shape, jnp.int32),
            pltpu.VMEM(src_row.shape, jnp.int32),
            pltpu.SemaphoreType.DMA((4,)),
        ],
        space=pltpu.HBM,
    )

    half = nodes // 2
    sums_shape = shape((nodes * block, width), F32)

    def encode(units, last, before):
        edges = len(units) * part_rows * fanout
        used = [where[unit] for unit in units]
        args = [who, *(part for part, _ in used), weight, vec, *before]
        outs = [
            shape((half * block, width), BF16) if last else sums_shape,
            shape((edges, width), BF16),
            shape((1, edges), jnp.int32),
        ]
        return call(
            functools.partial(
                encode_kernel,
                tuple(at for _, at in used),
                nodes,
                block,
                fanout,
                part_rows,
                last,
            ),
            outs if last else outs[:1],
            args,
            smem=1,
            scratch=() if last else [pltpu.VMEM(s.shape, s.dtype) for s in outs[1:]],
            aliases={len(args) - 1: 0} if before and not last else None,
        )

    before = []
    for units in steps[:-1]:
        before = encode(units, False, before)
    cross, message, spots = encode(steps[-1], True, before)
    (keep,) = call(
        keep_kernel, [shape((half * block, width), BF16)], [message, spots, *before]
    )

    pair = keep.astype(F32) + swap(cross, "node", 1).astype(F32)
    pair = pair.reshape(half, block, width)
    turns = sorted(range(1, half), key=lambda q: (q.bit_length() == 1, -q))
    turns = turns[1:2] + turns[:1] + turns[2:]
    arrived = [swap(pair[q].astype(BF16), "node", 2 * q) for q in turns]

    units = [(j, p) for j in range(sects) for p in range(len(axes))]
    slopes = call(
        functools.partial(
            slope_kernel, tuple(where[unit][1] for unit in units), fanout, part_rows
        ),
        [shape((fanout * part_rows, width), BF16)] * len(units),
        [*(where[unit][0] for unit in units), weight, vec],
    )
    tied = lax.optimization_barrier((*arrived, *slopes))
    arrived, slopes = tied[: half - 1], dict(zip(units, tied[half - 1 :]))

    halo_shape = shape((pieces, LANES), BF16)
    row_low, row_high = shape((block, width), BF16), shape((block, width), F32)

    def exchange(value):
        return lax.all_to_all(value, both, split_axis=0, concat_axis=0, tiled=True)

    state, mesh_pre, halo = call(
        functools.partial(start_kernel, parts),
        [row_low, row_high, halo_shape],
        [pair[0], *arrived, mesh_init[0], mesh_weight, pick],
    )
    assert proc_weight.shape[0] == 2
    state, mixed, slope_first, halo = call(
        functools.partial(first_kernel, 0, parts),
        [row_low, row_high, shape((fan * block, width), BF16), halo_shape],
        [state, exchange(halo), source, proc_weight, pick],
    )
    mesh_out, grad, halo = call(
        functools.partial(last_kernel, 1, parts),
        [row_low, row_high, halo_shape],
        [state, exchange(halo), source, source_t, proc_weight, cot[0]],
    )
    grad, halo = call(
        functools.partial(back_kernel, 0, parts),
        [row_high, halo_shape],
        [grad, exchange(halo), pick_t, mixed, slope_first, source_t, proc_weight],
    )
    (grad_sum,) = call(
        functools.partial(mesh_back_kernel, parts),
        [row_low],
        [grad, exchange(halo), pick_t, mesh_pre, mesh_weight],
    )

    same = [swap(grad_sum, "node", 2 * q) for q in reversed(range(1, half))]
    same = [grad_sum, *same[::-1]]
    ready = nodes * block <= 8 * LANES
    picks_of = {unit: where[unit] for unit in units}
    if ready:
        seen, _ = lax.optimization_barrier((who, grad_sum))
        *found, mesh_out = call(
            functools.partial(
                mark_kernel,
                tuple(where[unit][1] for unit in units),
                part_rows,
                nodes,
                block,
                fanout,
            ),
            [shape((fanout * part_rows, nodes * block), BF16)] * len(units) + [row_low],
            [seen, *(where[unit][0] for unit in units), mesh_out],
            smem=1,
        )
        same[-1] = lax.optimization_barrier((same[-1], found[0]))[0]
        picks_of = {unit: (part, 0) for unit, part in zip(units, found)}
    other = [swap(rows, "node", 1) for rows in same[::-1]][::-1]
    gathered = (*same[::-1], *other[::-1])

    def message_back(groups, dtype):
        used = [unit for group in groups for unit in group]
        return call(
            functools.partial(
                message_back_kernel,
                tuple(picks_of[unit][1] for unit in used),
                part_rows,
                ready,
                nodes,
                block,
                fanout,
            ),
            [
                shape((len(group) * part_rows, width // CHUNKS), dtype)
                for group in groups
                for _ in range(CHUNKS)
            ],
            [
                who,
                *(picks_of[unit][0] for unit in used),
                *(slopes[unit] for unit in used),
                *gathered,
            ],
            smem=1,
        )

    first, then = axes, axes[::-1]
    chunks = [(p, c) for c in range(CHUNKS) for p in range(len(axes))]

    def ordered(found):
        return [found[p * CHUNKS + c] for p, c in chunks]

    given = ordered(
        message_back(
            [[(a, p), (a ^ b, p)] for p, (a, b) in enumerate(zip(first, then))], BF16
        )
    )
    gathered = lax.optimization_barrier((*gathered, *given))[: len(gathered)]
    passed = ordered(message_back([[(b, p)] for p, b in enumerate(then)], F32))
    gathered = lax.optimization_barrier((*gathered, *passed))[: len(gathered)]
    given = [swap(part, "sect", first[p]) for part, (p, _) in zip(given, chunks)]
    passed = [
        (mine + part[part_rows:].astype(F32)).astype(BF16)
        for mine, part in zip(passed, given)
    ]
    kept = ordered(message_back([[(0, p)] for p in range(len(axes))], F32))
    passed = [swap(part, "sect", then[p]) for part, (p, _) in zip(passed, chunks)]
    (grid_grad,) = call(
        functools.partial(grid_back_kernel, CHUNKS),
        [shape((grid_rows, width), BF16)],
        [*kept, *given, *passed, enc_weight],
    )
    return (mesh_out[None], grid_grad)


def solution(mesh):
    return jax.shard_map(
        body,
        mesh=mesh,
        in_specs=(
            P(("sect", "node"), None),
            P(("sect", "node"), None),
            P(("sect", "node"), None),
            P(("sect", "node"), None),
            P(),
            P(),
            P("node", "sect", None),
            P(),
            P("sect", "node", None, None, None),
            P("node", "sect", None),
            P(),
            P("node", "sect", None),
        ),
        out_specs=(P("node", "sect", None), P(("sect", "node"), None)),
        check_vma=False,
    )
```

```python
import functools
import math

import jax
import jax.numpy as jnp
from jax import lax
from jax.experimental import pallas as pl
from jax.experimental.pallas import tpu as pltpu
from jax.sharding import PartitionSpec as P

F32 = jnp.float32
BF16 = jnp.bfloat16
LANES = 128
META_ROWS = 16
CHUNKS = 2
MIB = 1024 * 1024


def sigmoid(value):
    return 0.5 * jnp.tanh(0.5 * value) + 0.5


def silu(value):
    return value * sigmoid(value)


def slope(value):
    sig = sigmoid(value)
    return sig * (1.0 + value * (1.0 - sig))


def dot(left, right):
    return jnp.dot(left, right, preferred_element_type=F32)


def dot_t(left, right):
    return lax.dot_general(left, right, (((1,), (1,)), ((), ())), preferred_element_type=F32)


def halves(value):
    high = value.astype(BF16)
    return high, (value - high.astype(F32)).astype(BF16)


def back_dot(grad, weight):
    rows = grad.shape[0]
    both = dot_t(jnp.concatenate(halves(grad), axis=0), weight)
    return both[:rows] + both[rows:]


def mark(equal):
    return jnp.where(equal, 1.0, 0.0).astype(BF16)


def iota(shape, axis):
    return lax.broadcasted_iota(jnp.int32, shape, axis)


def norm_parts(mixed):
    mean = jnp.mean(mixed, axis=-1, keepdims=True)
    centred = mixed - mean
    scale = lax.rsqrt(jnp.mean(centred * centred, axis=-1, keepdims=True) + 1e-05)
    return centred * scale, scale


def norm_back(grad, normed, scale):
    pull = grad * slope(normed)
    return scale * (
        pull
        - jnp.mean(pull, axis=-1, keepdims=True)
        - normed * jnp.mean(pull * normed, axis=-1, keepdims=True)
    )


def pack_kernel(block, feat, lens, owner, dst, *refs):
    *outs, held, own_held, dst_held, sems = refs
    rows = feat.shape[0] // len(outs)
    pairs = [(lens, held), (owner, own_held), (dst, dst_held)]
    pairs += [
        (feat.at[i * rows : (i + 1) * rows, :], out.at[:rows, :]) for i, out in enumerate(outs)
    ]
    copies = [
        pltpu.make_async_copy(source, target, sems.at[i])
        for i, (source, target) in enumerate(pairs)
    ]
    for copy in copies:
        copy.start()
    for copy in copies[:3]:
        copy.wait()
    high, middle = halves(held[...])
    low = (held[...] - high.astype(F32) - middle.astype(F32)).astype(BF16)
    far = dst_held[...]
    section = far // block
    found = [v.astype(F32) for v in (high, middle, low)]
    found += [v.astype(F32) for v in (own_held[...], section, far - section * block)]
    fill = META_ROWS - 6 * lens.shape[0]
    found.append(jnp.zeros((fill, feat.shape[0]), F32))
    meta = jnp.concatenate(found, axis=0).astype(BF16)
    rest = jnp.zeros((META_ROWS, feat.shape[1] - rows), BF16)
    for i, out in enumerate(outs):
        out[rows:, :] = jnp.concatenate([meta[:, i * rows : (i + 1) * rows], rest], axis=1)
    for copy in copies[3:]:
        copy.wait()


def index_kernel(block, parts, *refs):
    wanted, far_weight, far_vec = refs[:2], refs[2], refs[3]
    pick, pick_t, source, source_t, weight, vec, sends, src_row, sems = refs[4:]
    pairs = ((wanted[0], sends), (wanted[1], src_row), (far_vec, vec), (far_weight, weight))
    copies = [
        pltpu.make_async_copy(start, target, sems.at[i])
        for i, (start, target) in enumerate(pairs)
    ]
    for copy in copies:
        copy.start()
    for copy in copies[:2]:
        copy.wait()
    sects, count, nodes = sends.shape
    pieces = pick.shape[0]
    at = iota((1, pieces), 1)
    part, row = at % parts, at // parts
    peer = row // count
    whose = mark(iota((nodes, pieces), 0) == peer % nodes)
    place = jnp.zeros((1, pieces), F32)
    for t in range(sects):
        found = dot(sends[t].astype(F32).astype(BF16), whose)
        for c in range(count):
            here = jnp.logical_and(peer // nodes == t, row % count == c)
            place = place + jnp.where(here, found[c : c + 1], 0.0)
    place = place + (part * block).astype(F32)
    pick_t[...] = mark(iota((parts * block, pieces), 0) == place.astype(jnp.int32))
    turned = jnp.broadcast_to(place, (8, pieces)).T[:, :1].astype(jnp.int32)
    pick[...] = mark(iota((pieces, parts * block), 1) == turned)
    table_len = source_t.shape[0]
    column = src_row[...].astype(F32).T.astype(jnp.int32)
    ids = iota((block, table_len), 1)
    ids_t = iota((table_len, block), 0)
    for k in range(src_row.shape[0]):
        rows = slice(k * block, (k + 1) * block)
        source[rows, :] = mark(ids == column[:, k : k + 1])
        source_t[:, rows] = mark(ids_t == src_row[k : k + 1, :])
    for copy in copies[2:]:
        copy.wait()


def edge_data(feat, at, rows):
    return feat[at + rows : at + rows + META_ROWS, :rows].astype(F32)


def edge_length(meta, fanout, k):
    high, middle, low = (meta[:, t * fanout + k : t * fanout + k + 1] for t in range(3))
    return high + middle + low


def spot_of(pick, fanout, k, section, node, nodes, block):
    owner, where, place = (pick((3 + t) * fanout + k).astype(jnp.int32) for t in range(3))
    apart = jnp.bitwise_xor(owner, node)
    order = lax.shift_right_logical(apart, 1) + jnp.bitwise_and(apart, 1) * (nodes // 2)
    return jnp.where(where == section, order * block + place, -1)


def add_rows(out, base, message, spots, before):
    step = min(out.shape[0], 512)

    def chunk(c, carry):
        start = pl.multiple_of(c * step, step)
        ids = iota((step, spots.shape[1]), 0) + (base + start)
        part = dot(mark(ids == spots[...]), message[...])
        for ref in before:
            part = part + ref[pl.ds(base + start, step), :]
        out[pl.ds(start, step), :] = part.astype(out.dtype)
        return carry

    lax.fori_loop(0, out.shape[0] // step, chunk, 0)


def encode_kernel(spans, nodes, block, fanout, rows, last, who, *refs):
    count = len(spans)
    feats = refs[:count]
    weight, vec = refs[count : count + 2]
    *before, out, message, spots = refs[count + 2 :]
    section, node = who[0], who[1]
    pre = 0.5 * dot(
        jnp.concatenate([feat[at : at + rows, :] for feat, at in zip(feats, spans)], axis=0),
        weight[...],
    )
    part = 0.5 * vec[...]
    for j in range(count):
        meta = edge_data(feats[j], spans[j], rows)
        turned = meta.T
        for k in range(fanout):
            at = (j * fanout + k) * rows
            act = pre[j * rows : (j + 1) * rows] + edge_length(turned, fanout, k) * part
            act = act.astype(BF16)
            message[at : at + rows, :] = act + act * jnp.tanh(act)
            spots[:, at : at + rows] = spot_of(
                lambda t, meta=meta: meta[t : t + 1], fanout, k, section, node, nodes, block
            )
    add_rows(out, nodes // 2 * block if last else 0, message, spots, before)


def keep_kernel(message, spots, before, out):
    add_rows(out, 0, message, spots, [before])


def slope_kernel(spans, fanout, rows, *refs):
    count = len(spans)
    feats = refs[:count]
    weight, vec = refs[count : count + 2]
    outs = refs[count + 2 :]
    for feat, at, out in zip(feats, spans, outs):
        pre = dot(feat[at : at + rows, :], weight[...])
        turned = edge_data(feat, at, rows).T
        for k in range(fanout):
            act = pre + edge_length(turned, fanout, k) * vec[...]
            out[k * rows : (k + 1) * rows, :] = slope(act).astype(BF16)


def halo_rows(state, pick, parts):
    stacked = jnp.concatenate(
        [state[:, i * LANES : (i + 1) * LANES] for i in range(parts)], axis=0
    )
    return dot(pick, stacked).astype(BF16)


def join_pieces(pieces, parts):
    count = pieces.shape[0]
    rows = count // parts
    at = iota((count, count), 0)
    onehot = mark(iota((count, count), 1) == at % rows * parts + at // rows)
    found = dot(onehot, pieces).astype(BF16)
    return jnp.concatenate([found[i * rows : (i + 1) * rows] for i in range(parts)], axis=1)


def cut_pieces(rows, parts):
    each, count = rows.shape[0], rows.shape[0] * parts
    at = iota((count, count), 0)
    onehot = mark(iota((count, count), 1) == at % parts * each + at // parts)
    stacked = jnp.concatenate(
        [rows[:, i * LANES : (i + 1) * LANES] for i in range(parts)], axis=0
    )
    return dot(onehot, stacked).astype(BF16)


def add_pieces(pieces, pick_t, block, parts):
    total = dot(pick_t, pieces)
    return jnp.concatenate([total[i * block : (i + 1) * block] for i in range(parts)], axis=1)


def start_kernel(parts, sums, *refs):
    received, (init, weight, pick, state, mesh_pre, halo) = refs[:-6], refs[-6:]
    agg = sums[...]
    for ref in received:
        agg = agg + ref[...].astype(F32)
    pre = dot(agg.astype(BF16), weight[...])
    mesh_pre[...] = pre
    new = (init[...].astype(F32) + silu(pre)).astype(BF16)
    state[...] = new
    halo[...] = halo_rows(new, pick[...], parts)


def layer_forward(state, pieces, source, weights, parts):
    block = state.shape[0]
    halo = join_pieces(pieces, parts)
    table = jnp.concatenate([state, halo], axis=0)
    from_src = 0.5 * dot(table, weights(0))
    to_dst = 0.5 * dot(state, weights(1))
    gathered = dot(source[...], from_src.astype(BF16))
    agg = jnp.zeros(state.shape, F32)
    slopes = []
    for k in range(source.shape[0] // block):
        joined = gathered[k * block : (k + 1) * block] + to_dst
        bend = jnp.tanh(joined)
        agg = agg + (joined + joined * bend)
        joined, bend = joined.astype(BF16), bend.astype(BF16)
        slopes.append(1 + bend + joined * (1 - bend * bend))
    mixed = dot(state, weights(2)) + dot(agg.astype(BF16), weights(3))
    return mixed, slopes


def layer_back(grad, mixed, slopes, source_t, weights):
    block = grad.shape[0]
    normed, scale = norm_parts(mixed)
    grad_mixed = norm_back(grad, normed, scale)
    grad_state = grad + back_dot(grad_mixed, weights(2))
    grad_agg = 0.5 * dot_t(grad_mixed.astype(BF16), weights(3))
    low = grad_agg.astype(BF16)
    total = jnp.zeros(grad.shape, F32)
    for found in slopes:
        total = total + found.astype(F32)
    total = grad_agg * total
    pieces = [low * found for found in slopes]
    grad_src = dot(source_t[...], jnp.concatenate(pieces, axis=0))
    grad_state = grad_state + back_dot(total, weights(1))
    grad_table = dot_t(grad_src.astype(BF16), weights(0))
    return grad_state + grad_table[:block], grad_table[block:]


def layer_weights(weights, layer):
    return lambda i: weights[layer, i]


def first_kernel(
    layer, parts, state, pieces, source, weights, pick, new, mixed, slopes, halo
):
    block = state.shape[0]
    own = state[...]
    used = layer_weights(weights, layer)
    value, found = layer_forward(own, pieces[...], source, used, parts)
    mixed[...] = value
    for k, part in enumerate(found):
        slopes[k * block : (k + 1) * block, :] = part
    normed, _ = norm_parts(value)
    result = (own.astype(F32) + silu(normed)).astype(BF16)
    new[...] = result
    halo[...] = halo_rows(result, pick[...], parts)


def last_kernel(
    layer, parts, state, pieces, source, source_t, weights, cot, out, grad_own, grad_halo
):
    own = state[...]
    used = layer_weights(weights, layer)
    value, found = layer_forward(own, pieces[...], source, used, parts)
    normed, _ = norm_parts(value)
    out[...] = (own.astype(F32) + silu(normed)).astype(BF16)
    mine, sent = layer_back(cot[...].astype(F32), value, found, source_t, used)
    grad_own[...] = mine
    grad_halo[...] = cut_pieces(sent.astype(BF16), parts)


def back_kernel(
    layer,
    parts,
    mine,
    returned,
    pick_t,
    mixed,
    slopes,
    source_t,
    weights,
    grad_own,
    grad_halo,
):
    block = mine.shape[0]
    grad = mine[...] + add_pieces(returned[...], pick_t[...], block, parts)
    fan = slopes.shape[0] // block
    found = [slopes[k * block : (k + 1) * block, :] for k in range(fan)]
    used = layer_weights(weights, layer)
    own, sent = layer_back(grad, mixed[...], found, source_t, used)
    grad_own[...] = own
    grad_halo[...] = cut_pieces(sent.astype(BF16), parts)


def mesh_back_kernel(parts, mine, returned, pick_t, mesh_pre, weight, out):
    block = mine.shape[0]
    grad = mine[...] + add_pieces(returned[...], pick_t[...], block, parts)
    out[...] = back_dot(grad * slope(mesh_pre[...]), weight[...]).astype(BF16)


def edge_marks(feat, at, rows, nodes, block, fanout, who):
    turned = edge_data(feat, at, rows).T
    ids = iota((rows, nodes * block), 1)
    return [
        mark(
            ids
            == spot_of(
                lambda t: turned[:, t : t + 1], fanout, k, who[0], who[1], nodes, block
            )
        )
        for k in range(fanout)
    ]


def mark_kernel(spans, rows, nodes, block, fanout, who, *refs):
    feats, state = refs[: len(spans)], refs[len(spans)]
    *outs, final = refs[len(spans) + 1 :]
    final[...] = state[...]
    for feat, at, out in zip(feats, spans, outs):
        for k, found in enumerate(edge_marks(feat, at, rows, nodes, block, fanout, who)):
            out[k * rows : (k + 1) * rows, :] = found


def message_back_kernel(spans, rows, ready, nodes, block, fanout, who, *refs):
    count = len(spans)
    feats, slopes = refs[:count], refs[count : 2 * count]
    outs = refs[2 * count :]
    grads, outs = outs[:nodes], outs[nodes:]
    marks = []
    for feat, at in zip(feats, spans):
        if ready:
            marks.append(feat[...])
        else:
            marks += edge_marks(feat, at, rows, nodes, block, fanout, who)
    same, other = grads[: nodes // 2][::-1], grads[nodes // 2 :][::-1]
    picked = dot(
        jnp.concatenate(marks, axis=0),
        jnp.concatenate([ref[...] for ref in (*same, *other)], axis=0),
    )
    size = outs[0].shape[1]
    chunks = slopes[0].shape[1] // size
    per = count * chunks // len(outs)
    for i in range(count):
        total = jnp.zeros((rows, slopes[0].shape[1]), F32)
        for k in range(fanout):
            at = (i * fanout + k) * rows
            part = slopes[i][k * rows : (k + 1) * rows, :].astype(F32)
            total = total + picked[at : at + rows] * part
        at = i % per * rows
        for c, out in enumerate(outs[i // per * chunks : (i // per + 1) * chunks]):
            out[at : at + rows, :] = total[:, c * size : (c + 1) * size].astype(out.dtype)


def grid_back_kernel(chunks, *refs):
    *parts, weight, out = refs
    count = len(parts) // 3
    rows = parts[0].shape[0]
    total = [
        parts[i][...]
        + parts[count + i][:rows, :].astype(F32)
        + parts[2 * count + i][...].astype(F32)
        for i in range(count)
    ]
    each = count // chunks
    columns = [
        jnp.concatenate(total[c * each : (c + 1) * each], axis=0) for c in range(chunks)
    ]
    whole = jnp.concatenate(columns, axis=1).astype(BF16)
    out[...] = dot_t(whole, weight[...]).astype(BF16)


def call(kernel, outs, args, smem=0, scratch=(), space=pltpu.VMEM, aliases=None):
    specs = [pl.BlockSpec(memory_space=pltpu.SMEM)] * smem
    specs += [pl.BlockSpec(memory_space=space)] * (len(args) - smem)
    moved = sum(a.size * a.dtype.itemsize for a in list(args) + list(outs))
    held = sum(math.prod(a.shape) * 4 for a in scratch)
    limit = 2 * (moved + held) + 6 * MIB
    result = pl.pallas_call(
        kernel,
        out_shape=list(outs),
        in_specs=specs,
        out_specs=[pl.BlockSpec(memory_space=pltpu.VMEM)] * len(outs),
        scratch_shapes=list(scratch),
        input_output_aliases=aliases or {},
        compiler_params=pltpu.CompilerParams(vmem_limit_bytes=limit),
        cost_estimate=pl.CostEstimate(
            flops=0, bytes_accessed=moved, transcendentals=0
        ),
    )(*args)
    return result


def shape(dims, dtype):
    return jax.ShapeDtypeStruct(dims, dtype)


def swap(value, axis, apart):
    size = lax.axis_size(axis)
    return lax.ppermute(value, axis, [(i, i ^ apart) for i in range(size)])


def body(
    grid_feat,
    edge_len,
    g2m_owner,
    g2m_dst,
    enc_weight,
    enc_vec,
    mesh_init,
    mesh_weight,
    halo_send,
    mesh_src,
    proc_weight,
    cot,
):
    nodes = lax.axis_size("node")
    sects = lax.axis_size("sect")
    width = grid_feat.shape[1]
    grid_rows, fanout = edge_len.shape
    block = mesh_init.shape[1]
    parts = width // LANES
    both = ("sect", "node")
    who = jnp.stack([lax.axis_index("sect"), lax.axis_index("node")]).astype(jnp.int32)

    axes = [1 << i for i in range(sects.bit_length() - 1)]
    part_rows = grid_rows // len(axes)
    assert len(axes) == 2
    ends = pltpu.VMEM((fanout, grid_rows), jnp.int32)
    packed = call(
        functools.partial(pack_kernel, block),
        [shape((part_rows + META_ROWS, width), BF16)] * len(axes),
        [
            pltpu.with_memory_space_constraint(value, pltpu.HBM)
            for value in (grid_feat, edge_len.T, g2m_owner.T, g2m_dst.T)
        ],
        scratch=[
            pltpu.VMEM((fanout, grid_rows), F32),
            ends,
            ends,
            pltpu.SemaphoreType.DMA((3 + len(axes),)),
        ],
        space=pltpu.HBM,
    )
    where = {(0, p): (part, 0) for p, part in enumerate(packed)}
    steps = [[(0, p) for p in range(len(axes))]]
    held, names = list(packed), [[0] for _ in axes]
    for step in range(len(axes)):
        given = [
            swap(part, "sect", axes[(p + step) % len(axes)]) for p, part in enumerate(held)
        ]
        steps.append([])
        for p, part in enumerate(given):
            axis = axes[(p + step) % len(axes)]
            for i, j in enumerate(list(names[p])):
                where[j ^ axis, p] = (part, i * packed[0].shape[0])
                names[p].append(j ^ axis)
                steps[-1].append((j ^ axis, p))
        held = [jnp.concatenate(pair, axis=0) for pair in zip(held, given)]
    sends = halo_send[0, 0].transpose(0, 2, 1)
    src_row = mesh_src[0].T
    fan = src_row.shape[0]
    pieces = sends.size * parts
    table_len = block + sends.size
    pick, pick_t, source, source_t, weight, vec = call(
        functools.partial(index_kernel, block, parts),
        [
            shape((pieces, parts * block), BF16),
            shape((parts * block, pieces), BF16),
            shape((fan * block, table_len), BF16),
            shape((table_len, fan * block), BF16),
            shape(enc_weight.shape, BF16),
            shape((1, width), F32),
        ],
        [
            pltpu.with_memory_space_constraint(value, pltpu.HBM)
            for value in (sends, src_row, enc_weight, enc_vec[None, :])
        ],
        scratch=[
            pltpu.VMEM(sends.shape, jnp.int32),
            pltpu.VMEM(src_row.shape, jnp.int32),
            pltpu.SemaphoreType.DMA((4,)),
        ],
        space=pltpu.HBM,
    )

    half = nodes // 2
    sums_shape = shape((nodes * block, width), F32)

    def encode(units, last, before):
        edges = len(units) * part_rows * fanout
        used = [where[unit] for unit in units]
        args = [who, *(part for part, _ in used), weight, vec, *before]
        outs = [
            shape((half * block, width), BF16) if last else sums_shape,
            shape((edges, width), BF16),
            shape((1, edges), jnp.int32),
        ]
        return call(
            functools.partial(
                encode_kernel,
                tuple(at for _, at in used),
                nodes,
                block,
                fanout,
                part_rows,
                last,
            ),
            outs if last else outs[:1],
            args,
            smem=1,
            scratch=() if last else [pltpu.VMEM(s.shape, s.dtype) for s in outs[1:]],
            aliases={len(args) - 1: 0} if before and not last else None,
        )

    before = []
    for units in steps[:-1]:
        before = encode(units, False, before)
    cross, message, spots = encode(steps[-1], True, before)
    (keep,) = call(
        keep_kernel, [shape((half * block, width), BF16)], [message, spots, *before]
    )

    pair = keep.astype(F32) + swap(cross, "node", 1).astype(F32)
    pair = pair.reshape(half, block, width)
    arrived = [
        swap(pair[q].astype(BF16), "node", 2 * q) for q in reversed(range(1, half))
    ]

    units = [(j, p) for j in range(sects) for p in range(len(axes))]
    slopes = call(
        functools.partial(
            slope_kernel, tuple(where[unit][1] for unit in units), fanout, part_rows
        ),
        [shape((fanout * part_rows, width), BF16)] * len(units),
        [*(where[unit][0] for unit in units), weight, vec],
    )
    tied = lax.optimization_barrier((*arrived, *slopes))
    arrived, slopes = tied[: half - 1], dict(zip(units, tied[half - 1 :]))

    halo_shape = shape((pieces, LANES), BF16)
    row_low, row_high = shape((block, width), BF16), shape((block, width), F32)

    def exchange(value):
        return lax.all_to_all(value, both, split_axis=0, concat_axis=0, tiled=True)

    state, mesh_pre, halo = call(
        functools.partial(start_kernel, parts),
        [row_low, row_high, halo_shape],
        [pair[0], *arrived, mesh_init[0], mesh_weight, pick],
    )
    assert proc_weight.shape[0] == 2
    state, mixed, slope_first, halo = call(
        functools.partial(first_kernel, 0, parts),
        [row_low, row_high, shape((fan * block, width), BF16), halo_shape],
        [state, exchange(halo), source, proc_weight, pick],
    )
    mesh_out, grad, halo = call(
        functools.partial(last_kernel, 1, parts),
        [row_low, row_high, halo_shape],
        [state, exchange(halo), source, source_t, proc_weight, cot[0]],
    )
    grad, halo = call(
        functools.partial(back_kernel, 0, parts),
        [row_high, halo_shape],
        [grad, exchange(halo), pick_t, mixed, slope_first, source_t, proc_weight],
    )
    (grad_sum,) = call(
        functools.partial(mesh_back_kernel, parts),
        [row_low],
        [grad, exchange(halo), pick_t, mesh_pre, mesh_weight],
    )

    same = [swap(grad_sum, "node", 2 * q) for q in reversed(range(1, half))]
    same = [grad_sum, *same[::-1]]
    ready = nodes * block <= 8 * LANES
    picks_of = {unit: where[unit] for unit in units}
    if ready:
        seen, _ = lax.optimization_barrier((who, grad_sum))
        *found, mesh_out = call(
            functools.partial(
                mark_kernel,
                tuple(where[unit][1] for unit in units),
                part_rows,
                nodes,
                block,
                fanout,
            ),
            [shape((fanout * part_rows, nodes * block), BF16)] * len(units) + [row_low],
            [seen, *(where[unit][0] for unit in units), mesh_out],
            smem=1,
        )
        same[-1] = lax.optimization_barrier((same[-1], found[0]))[0]
        picks_of = {unit: (part, 0) for unit, part in zip(units, found)}
    other = [swap(rows, "node", 1) for rows in same[::-1]][::-1]
    gathered = (*same[::-1], *other[::-1])

    def message_back(groups, dtype):
        used = [unit for group in groups for unit in group]
        return call(
            functools.partial(
                message_back_kernel,
                tuple(picks_of[unit][1] for unit in used),
                part_rows,
                ready,
                nodes,
                block,
                fanout,
            ),
            [
                shape((len(group) * part_rows, width // CHUNKS), dtype)
                for group in groups
                for _ in range(CHUNKS)
            ],
            [
                who,
                *(picks_of[unit][0] for unit in used),
                *(slopes[unit] for unit in used),
                *gathered,
            ],
            smem=1,
        )

    first, then = axes, axes[::-1]
    chunks = [(p, c) for c in range(CHUNKS) for p in range(len(axes))]

    def ordered(found):
        return [found[p * CHUNKS + c] for p, c in chunks]

    given = ordered(
        message_back(
            [[(a, p), (a ^ b, p)] for p, (a, b) in enumerate(zip(first, then))], BF16
        )
    )
    gathered = lax.optimization_barrier((*gathered, *given))[: len(gathered)]
    passed = ordered(message_back([[(b, p)] for p, b in enumerate(then)], F32))
    gathered = lax.optimization_barrier((*gathered, *passed))[: len(gathered)]
    given = [swap(part, "sect", first[p]) for part, (p, _) in zip(given, chunks)]
    passed = [
        (mine + part[part_rows:].astype(F32)).astype(BF16)
        for mine, part in zip(passed, given)
    ]
    kept = ordered(message_back([[(0, p)] for p in range(len(axes))], F32))
    passed = [swap(part, "sect", then[p]) for part, (p, _) in zip(passed, chunks)]
    (grid_grad,) = call(
        functools.partial(grid_back_kernel, CHUNKS),
        [shape((grid_rows, width), BF16)],
        [*kept, *given, *passed, enc_weight],
    )
    return (mesh_out[None], grid_grad)


def solution(mesh):
    return jax.shard_map(
        body,
        mesh=mesh,
        in_specs=(
            P(("sect", "node"), None),
            P(("sect", "node"), None),
            P(("sect", "node"), None),
            P(("sect", "node"), None),
            P(),
            P(),
            P("node", "sect", None),
            P(),
            P("sect", "node", None, None, None),
            P("node", "sect", None),
            P(),
            P("node", "sect", None),
        ),
        out_specs=(P("node", "sect", None), P(("sect", "node"), None)),
        check_vma=False,
    )
```

```python
import functools
import math

import jax
import jax.numpy as jnp
from jax import lax
from jax.experimental import pallas as pl
from jax.experimental.pallas import tpu as pltpu
from jax.sharding import PartitionSpec as P

F32 = jnp.float32
BF16 = jnp.bfloat16
LANES = 128
META_ROWS = 16
CHUNKS = 2
MIB = 1024 * 1024


def sigmoid(value):
    return 0.5 * jnp.tanh(0.5 * value) + 0.5


def silu(value):
    return value * sigmoid(value)


def slope(value):
    sig = sigmoid(value)
    return sig * (1.0 + value * (1.0 - sig))


def dot(left, right):
    return jnp.dot(left, right, preferred_element_type=F32)


def dot_t(left, right):
    return lax.dot_general(left, right, (((1,), (1,)), ((), ())), preferred_element_type=F32)


def halves(value):
    high = value.astype(BF16)
    return high, (value - high.astype(F32)).astype(BF16)


def back_dot(grad, weight):
    return dot_t(grad.astype(BF16), weight)


def mark(equal):
    return jnp.where(equal, 1.0, 0.0).astype(BF16)


def iota(shape, axis):
    return lax.broadcasted_iota(jnp.int32, shape, axis)


def norm_parts(mixed):
    mean = jnp.mean(mixed, axis=-1, keepdims=True)
    centred = mixed - mean
    scale = lax.rsqrt(jnp.mean(centred * centred, axis=-1, keepdims=True) + 1e-05)
    return centred * scale, scale


def norm_back(grad, normed, scale):
    pull = grad * slope(normed)
    return scale * (
        pull
        - jnp.mean(pull, axis=-1, keepdims=True)
        - normed * jnp.mean(pull * normed, axis=-1, keepdims=True)
    )


def pack_kernel(block, feat, lens, owner, dst, *refs):
    *outs, held, own_held, dst_held, sems = refs
    rows = feat.shape[0] // len(outs)
    pairs = [(lens, held), (owner, own_held), (dst, dst_held)]
    pairs += [
        (feat.at[i * rows : (i + 1) * rows, :], out.at[:rows, :]) for i, out in enumerate(outs)
    ]
    copies = [
        pltpu.make_async_copy(source, target, sems.at[i])
        for i, (source, target) in enumerate(pairs)
    ]
    for copy in copies:
        copy.start()
    for copy in copies[:3]:
        copy.wait()
    high, middle = halves(held[...])
    low = (held[...] - high.astype(F32) - middle.astype(F32)).astype(BF16)
    far = dst_held[...]
    section = far // block
    found = [v.astype(F32) for v in (high, middle, low)]
    found += [v.astype(F32) for v in (own_held[...], section, far - section * block)]
    fill = META_ROWS - 6 * lens.shape[0]
    found.append(jnp.zeros((fill, feat.shape[0]), F32))
    meta = jnp.concatenate(found, axis=0).astype(BF16)
    rest = jnp.zeros((META_ROWS, feat.shape[1] - rows), BF16)
    for i, out in enumerate(outs):
        out[rows:, :] = jnp.concatenate([meta[:, i * rows : (i + 1) * rows], rest], axis=1)
    for copy in copies[3:]:
        copy.wait()


def index_kernel(block, parts, *refs):
    wanted, far_weight, far_vec = refs[:2], refs[2], refs[3]
    pick, pick_t, source, source_t, weight, vec, sends, src_row, sems = refs[4:]
    pairs = ((wanted[0], sends), (wanted[1], src_row), (far_vec, vec), (far_weight, weight))
    copies = [
        pltpu.make_async_copy(start, target, sems.at[i])
        for i, (start, target) in enumerate(pairs)
    ]
    for copy in copies:
        copy.start()
    for copy in copies[:2]:
        copy.wait()
    sects, count, nodes = sends.shape
    pieces = pick.shape[0]
    at = iota((1, pieces), 1)
    part, row = at % parts, at // parts
    peer = row // count
    whose = mark(iota((nodes, pieces), 0) == peer % nodes)
    place = jnp.zeros((1, pieces), F32)
    for t in range(sects):
        found = dot(sends[t].astype(F32).astype(BF16), whose)
        for c in range(count):
            here = jnp.logical_and(peer // nodes == t, row % count == c)
            place = place + jnp.where(here, found[c : c + 1], 0.0)
    place = place + (part * block).astype(F32)
    pick_t[...] = mark(iota((parts * block, pieces), 0) == place.astype(jnp.int32))
    turned = jnp.broadcast_to(place, (8, pieces)).T[:, :1].astype(jnp.int32)
    pick[...] = mark(iota((pieces, parts * block), 1) == turned)
    table_len = source_t.shape[0]
    column = src_row[...].astype(F32).T.astype(jnp.int32)
    ids = iota((block, table_len), 1)
    ids_t = iota((table_len, block), 0)
    for k in range(src_row.shape[0]):
        rows = slice(k * block, (k + 1) * block)
        source[rows, :] = mark(ids == column[:, k : k + 1])
        source_t[:, rows] = mark(ids_t == src_row[k : k + 1, :])
    for copy in copies[2:]:
        copy.wait()


def edge_data(feat, at, rows):
    return feat[at + rows : at + rows + META_ROWS, :rows].astype(F32)


def edge_length(meta, fanout, k):
    high, middle, low = (meta[:, t * fanout + k : t * fanout + k + 1] for t in range(3))
    return high + middle + low


def spot_of(pick, fanout, k, section, node, nodes, block):
    owner, where, place = (pick((3 + t) * fanout + k).astype(jnp.int32) for t in range(3))
    apart = jnp.bitwise_xor(owner, node)
    order = lax.shift_right_logical(apart, 1) + jnp.bitwise_and(apart, 1) * (nodes // 2)
    return jnp.where(where == section, order * block + place, -1)


def add_rows(out, base, message, spots, before):
    step = min(out.shape[0], 512)

    def chunk(c, carry):
        start = pl.multiple_of(c * step, step)
        ids = iota((step, spots.shape[1]), 0) + (base + start)
        part = dot(mark(ids == spots[...]), message[...])
        for ref in before:
            part = part + ref[pl.ds(base + start, step), :]
        out[pl.ds(start, step), :] = part.astype(out.dtype)
        return carry

    lax.fori_loop(0, out.shape[0] // step, chunk, 0)


def encode_kernel(spans, nodes, block, fanout, rows, last, who, *refs):
    count = len(spans)
    feats = refs[:count]
    weight, vec = refs[count : count + 2]
    *before, out, message, spots = refs[count + 2 :]
    section, node = who[0], who[1]
    pre = 0.5 * dot(
        jnp.concatenate([feat[at : at + rows, :] for feat, at in zip(feats, spans)], axis=0),
        weight[...],
    )
    part = 0.5 * vec[...]
    for j in range(count):
        meta = edge_data(feats[j], spans[j], rows)
        turned = meta.T
        for k in range(fanout):
            at = (j * fanout + k) * rows
            act = pre[j * rows : (j + 1) * rows] + edge_length(turned, fanout, k) * part
            message[at : at + rows, :] = (act + act * jnp.tanh(act)).astype(BF16)
            spots[:, at : at + rows] = spot_of(
                lambda t, meta=meta: meta[t : t + 1], fanout, k, section, node, nodes, block
            )
    add_rows(out, nodes // 2 * block if last else 0, message, spots, before)


def keep_kernel(message, spots, before, out):
    add_rows(out, 0, message, spots, [before])


def slope_kernel(spans, fanout, rows, *refs):
    count = len(spans)
    feats = refs[:count]
    weight, vec = refs[count : count + 2]
    outs = refs[count + 2 :]
    for feat, at, out in zip(feats, spans, outs):
        pre = dot(feat[at : at + rows, :], weight[...])
        turned = edge_data(feat, at, rows).T
        for k in range(fanout):
            act = pre + edge_length(turned, fanout, k) * vec[...]
            out[k * rows : (k + 1) * rows, :] = slope(act).astype(BF16)


def halo_rows(state, pick, parts):
    stacked = jnp.concatenate(
        [state[:, i * LANES : (i + 1) * LANES] for i in range(parts)], axis=0
    )
    return dot(pick, stacked).astype(BF16)


def join_pieces(pieces, parts):
    count = pieces.shape[0]
    rows = count // parts
    at = iota((count, count), 0)
    onehot = mark(iota((count, count), 1) == at % rows * parts + at // rows)
    found = dot(onehot, pieces).astype(BF16)
    return jnp.concatenate([found[i * rows : (i + 1) * rows] for i in range(parts)], axis=1)


def cut_pieces(rows, parts):
    each, count = rows.shape[0], rows.shape[0] * parts
    at = iota((count, count), 0)
    onehot = mark(iota((count, count), 1) == at % parts * each + at // parts)
    stacked = jnp.concatenate(
        [rows[:, i * LANES : (i + 1) * LANES] for i in range(parts)], axis=0
    )
    return dot(onehot, stacked).astype(BF16)


def add_pieces(pieces, pick_t, block, parts):
    total = dot(pick_t, pieces)
    return jnp.concatenate([total[i * block : (i + 1) * block] for i in range(parts)], axis=1)


def start_kernel(parts, sums, *refs):
    received, (init, weight, pick, state, mesh_pre, halo) = refs[:-6], refs[-6:]
    agg = sums[...]
    for ref in received:
        agg = agg + ref[...].astype(F32)
    pre = dot(agg.astype(BF16), weight[...])
    mesh_pre[...] = pre
    new = (init[...].astype(F32) + silu(pre)).astype(BF16)
    state[...] = new
    halo[...] = halo_rows(new, pick[...], parts)


def layer_forward(state, pieces, source, weights, parts):
    block = state.shape[0]
    halo = join_pieces(pieces, parts)
    table = jnp.concatenate([state, halo], axis=0)
    from_src = 0.5 * dot(table, weights(0))
    to_dst = 0.5 * dot(state, weights(1))
    gathered = dot(source[...], from_src.astype(BF16))
    agg = jnp.zeros(state.shape, F32)
    slopes = []
    for k in range(source.shape[0] // block):
        joined = gathered[k * block : (k + 1) * block] + to_dst
        bend = jnp.tanh(joined)
        agg = agg + (joined + joined * bend)
        joined, bend = joined.astype(BF16), bend.astype(BF16)
        slopes.append(1 + bend + joined * (1 - bend * bend))
    mixed = dot(state, weights(2)) + dot(agg.astype(BF16), weights(3))
    return mixed, slopes


def layer_back(grad, mixed, slopes, source_t, weights):
    block = grad.shape[0]
    normed, scale = norm_parts(mixed)
    grad_mixed = norm_back(grad, normed, scale)
    grad_state = grad + back_dot(grad_mixed, weights(2))
    grad_agg = 0.5 * dot_t(grad_mixed.astype(BF16), weights(3))
    low = grad_agg.astype(BF16)
    total = jnp.zeros(grad.shape, F32)
    for found in slopes:
        total = total + found.astype(F32)
    total = grad_agg * total
    pieces = [low * found for found in slopes]
    grad_src = dot(source_t[...], jnp.concatenate(pieces, axis=0))
    grad_state = grad_state + back_dot(total, weights(1))
    grad_table = dot_t(grad_src.astype(BF16), weights(0))
    return grad_state + grad_table[:block], grad_table[block:]


def layer_weights(weights, layer):
    return lambda i: weights[layer, i]


def first_kernel(
    layer, parts, state, pieces, source, weights, pick, new, mixed, slopes, halo
):
    block = state.shape[0]
    own = state[...]
    used = layer_weights(weights, layer)
    value, found = layer_forward(own, pieces[...], source, used, parts)
    mixed[...] = value
    for k, part in enumerate(found):
        slopes[k * block : (k + 1) * block, :] = part
    normed, _ = norm_parts(value)
    result = (own.astype(F32) + silu(normed)).astype(BF16)
    new[...] = result
    halo[...] = halo_rows(result, pick[...], parts)


def last_kernel(
    layer, parts, state, pieces, source, source_t, weights, cot, out, grad_own, grad_halo
):
    own = state[...]
    used = layer_weights(weights, layer)
    value, found = layer_forward(own, pieces[...], source, used, parts)
    normed, _ = norm_parts(value)
    out[...] = (own.astype(F32) + silu(normed)).astype(BF16)
    mine, sent = layer_back(cot[...].astype(F32), value, found, source_t, used)
    grad_own[...] = mine
    grad_halo[...] = cut_pieces(sent.astype(BF16), parts)


def back_kernel(
    layer,
    parts,
    mine,
    returned,
    pick_t,
    mixed,
    slopes,
    source_t,
    weights,
    grad_own,
    grad_halo,
):
    block = mine.shape[0]
    grad = mine[...] + add_pieces(returned[...], pick_t[...], block, parts)
    fan = slopes.shape[0] // block
    found = [slopes[k * block : (k + 1) * block, :] for k in range(fan)]
    used = layer_weights(weights, layer)
    own, sent = layer_back(grad, mixed[...], found, source_t, used)
    grad_own[...] = own
    grad_halo[...] = cut_pieces(sent.astype(BF16), parts)


def mesh_back_kernel(parts, mine, returned, pick_t, mesh_pre, weight, out):
    block = mine.shape[0]
    grad = mine[...] + add_pieces(returned[...], pick_t[...], block, parts)
    out[...] = back_dot(grad * slope(mesh_pre[...]), weight[...]).astype(BF16)


def edge_marks(feat, at, rows, nodes, block, fanout, who):
    turned = edge_data(feat, at, rows).T
    ids = iota((rows, nodes * block), 1)
    return [
        mark(
            ids
            == spot_of(
                lambda t: turned[:, t : t + 1], fanout, k, who[0], who[1], nodes, block
            )
        )
        for k in range(fanout)
    ]


def mark_kernel(spans, rows, nodes, block, fanout, who, *refs):
    feats, state = refs[: len(spans)], refs[len(spans)]
    *outs, final = refs[len(spans) + 1 :]
    final[...] = state[...]
    for feat, at, out in zip(feats, spans, outs):
        for k, found in enumerate(edge_marks(feat, at, rows, nodes, block, fanout, who)):
            out[k * rows : (k + 1) * rows, :] = found


def message_back_kernel(spans, rows, ready, nodes, block, fanout, who, *refs):
    count = len(spans)
    feats, slopes = refs[:count], refs[count : 2 * count]
    outs = refs[2 * count :]
    grads, outs = outs[:nodes], outs[nodes:]
    marks = []
    for feat, at in zip(feats, spans):
        if ready:
            marks.append(feat[...])
        else:
            marks += edge_marks(feat, at, rows, nodes, block, fanout, who)
    same, other = grads[: nodes // 2][::-1], grads[nodes // 2 :][::-1]
    picked = dot(
        jnp.concatenate(marks, axis=0),
        jnp.concatenate([ref[...] for ref in (*same, *other)], axis=0),
    )
    size = outs[0].shape[1]
    chunks = slopes[0].shape[1] // size
    per = count * chunks // len(outs)
    for i in range(count):
        total = jnp.zeros((rows, slopes[0].shape[1]), F32)
        for k in range(fanout):
            at = (i * fanout + k) * rows
            part = slopes[i][k * rows : (k + 1) * rows, :].astype(F32)
            total = total + picked[at : at + rows] * part
        at = i % per * rows
        for c, out in enumerate(outs[i // per * chunks : (i // per + 1) * chunks]):
            out[at : at + rows, :] = total[:, c * size : (c + 1) * size].astype(out.dtype)


def grid_back_kernel(chunks, *refs):
    *parts, weight, out = refs
    count = len(parts) // 3
    rows = parts[0].shape[0]
    total = [
        parts[i][...]
        + parts[count + i][:rows, :].astype(F32)
        + parts[2 * count + i][...].astype(F32)
        for i in range(count)
    ]
    each = count // chunks
    columns = [
        jnp.concatenate(total[c * each : (c + 1) * each], axis=0) for c in range(chunks)
    ]
    out[...] = back_dot(jnp.concatenate(columns, axis=1), weight[...]).astype(BF16)


def call(kernel, outs, args, smem=0, scratch=(), space=pltpu.VMEM, aliases=None):
    specs = [pl.BlockSpec(memory_space=pltpu.SMEM)] * smem
    specs += [pl.BlockSpec(memory_space=space)] * (len(args) - smem)
    moved = sum(a.size * a.dtype.itemsize for a in list(args) + list(outs))
    held = sum(math.prod(a.shape) * 4 for a in scratch)
    limit = 2 * (moved + held) + 6 * MIB
    result = pl.pallas_call(
        kernel,
        out_shape=list(outs),
        in_specs=specs,
        out_specs=[pl.BlockSpec(memory_space=pltpu.VMEM)] * len(outs),
        scratch_shapes=list(scratch),
        input_output_aliases=aliases or {},
        compiler_params=pltpu.CompilerParams(vmem_limit_bytes=limit),
        cost_estimate=pl.CostEstimate(
            flops=0, bytes_accessed=moved, transcendentals=0
        ),
    )(*args)
    return result


def shape(dims, dtype):
    return jax.ShapeDtypeStruct(dims, dtype)


def swap(value, axis, apart):
    size = lax.axis_size(axis)
    return lax.ppermute(value, axis, [(i, i ^ apart) for i in range(size)])


def body(
    grid_feat,
    edge_len,
    g2m_owner,
    g2m_dst,
    enc_weight,
    enc_vec,
    mesh_init,
    mesh_weight,
    halo_send,
    mesh_src,
    proc_weight,
    cot,
):
    nodes = lax.axis_size("node")
    sects = lax.axis_size("sect")
    width = grid_feat.shape[1]
    grid_rows, fanout = edge_len.shape
    block = mesh_init.shape[1]
    parts = width // LANES
    both = ("sect", "node")
    who = jnp.stack([lax.axis_index("sect"), lax.axis_index("node")]).astype(jnp.int32)

    axes = [1 << i for i in range(sects.bit_length() - 1)]
    part_rows = grid_rows // len(axes)
    assert len(axes) == 2
    ends = pltpu.VMEM((fanout, grid_rows), jnp.int32)
    packed = call(
        functools.partial(pack_kernel, block),
        [shape((part_rows + META_ROWS, width), BF16)] * len(axes),
        [
            pltpu.with_memory_space_constraint(value, pltpu.HBM)
            for value in (grid_feat, edge_len.T, g2m_owner.T, g2m_dst.T)
        ],
        scratch=[
            pltpu.VMEM((fanout, grid_rows), F32),
            ends,
            ends,
            pltpu.SemaphoreType.DMA((3 + len(axes),)),
        ],
        space=pltpu.HBM,
    )
    where = {(0, p): (part, 0) for p, part in enumerate(packed)}
    steps = [[(0, p) for p in range(len(axes))]]
    held, names = list(packed), [[0] for _ in axes]
    for step in range(len(axes)):
        given = [
            swap(part, "sect", axes[(p + step) % len(axes)]) for p, part in enumerate(held)
        ]
        steps.append([])
        for p, part in enumerate(given):
            axis = axes[(p + step) % len(axes)]
            for i, j in enumerate(list(names[p])):
                where[j ^ axis, p] = (part, i * packed[0].shape[0])
                names[p].append(j ^ axis)
                steps[-1].append((j ^ axis, p))
        held = [jnp.concatenate(pair, axis=0) for pair in zip(held, given)]
    sends = halo_send[0, 0].transpose(0, 2, 1)
    src_row = mesh_src[0].T
    fan = src_row.shape[0]
    pieces = sends.size * parts
    table_len = block + sends.size
    pick, pick_t, source, source_t, weight, vec = call(
        functools.partial(index_kernel, block, parts),
        [
            shape((pieces, parts * block), BF16),
            shape((parts * block, pieces), BF16),
            shape((fan * block, table_len), BF16),
            shape((table_len, fan * block), BF16),
            shape(enc_weight.shape, BF16),
            shape((1, width), F32),
        ],
        [
            pltpu.with_memory_space_constraint(value, pltpu.HBM)
            for value in (sends, src_row, enc_weight, enc_vec[None, :])
        ],
        scratch=[
            pltpu.VMEM(sends.shape, jnp.int32),
            pltpu.VMEM(src_row.shape, jnp.int32),
            pltpu.SemaphoreType.DMA((4,)),
        ],
        space=pltpu.HBM,
    )

    half = nodes // 2
    sums_shape = shape((nodes * block, width), F32)

    def encode(units, last, before):
        edges = len(units) * part_rows * fanout
        used = [where[unit] for unit in units]
        args = [who, *(part for part, _ in used), weight, vec, *before]
        outs = [
            shape((half * block, width), BF16) if last else sums_shape,
            shape((edges, width), BF16),
            shape((1, edges), jnp.int32),
        ]
        return call(
            functools.partial(
                encode_kernel,
                tuple(at for _, at in used),
                nodes,
                block,
                fanout,
                part_rows,
                last,
            ),
            outs if last else outs[:1],
            args,
            smem=1,
            scratch=() if last else [pltpu.VMEM(s.shape, s.dtype) for s in outs[1:]],
            aliases={len(args) - 1: 0} if before and not last else None,
        )

    before = []
    for units in steps[:-1]:
        before = encode(units, False, before)
    cross, message, spots = encode(steps[-1], True, before)
    (keep,) = call(
        keep_kernel, [shape((half * block, width), BF16)], [message, spots, *before]
    )

    pair = keep.astype(F32) + swap(cross, "node", 1).astype(F32)
    pair = pair.reshape(half, block, width)
    arrived = [
        swap(pair[q].astype(BF16), "node", 2 * q) for q in reversed(range(1, half))
    ]

    units = [(j, p) for j in range(sects) for p in range(len(axes))]
    slopes = call(
        functools.partial(
            slope_kernel, tuple(where[unit][1] for unit in units), fanout, part_rows
        ),
        [shape((fanout * part_rows, width), BF16)] * len(units),
        [*(where[unit][0] for unit in units), weight, vec],
    )
    tied = lax.optimization_barrier((*arrived, *slopes))
    arrived, slopes = tied[: half - 1], dict(zip(units, tied[half - 1 :]))

    halo_shape = shape((pieces, LANES), BF16)
    row_low, row_high = shape((block, width), BF16), shape((block, width), F32)

    def exchange(value):
        return lax.all_to_all(value, both, split_axis=0, concat_axis=0, tiled=True)

    state, mesh_pre, halo = call(
        functools.partial(start_kernel, parts),
        [row_low, row_high, halo_shape],
        [pair[0], *arrived, mesh_init[0], mesh_weight, pick],
    )
    assert proc_weight.shape[0] == 2
    state, mixed, slope_first, halo = call(
        functools.partial(first_kernel, 0, parts),
        [row_low, row_high, shape((fan * block, width), BF16), halo_shape],
        [state, exchange(halo), source, proc_weight, pick],
    )
    mesh_out, grad, halo = call(
        functools.partial(last_kernel, 1, parts),
        [row_low, row_high, halo_shape],
        [state, exchange(halo), source, source_t, proc_weight, cot[0]],
    )
    grad, halo = call(
        functools.partial(back_kernel, 0, parts),
        [row_high, halo_shape],
        [grad, exchange(halo), pick_t, mixed, slope_first, source_t, proc_weight],
    )
    (grad_sum,) = call(
        functools.partial(mesh_back_kernel, parts),
        [row_low],
        [grad, exchange(halo), pick_t, mesh_pre, mesh_weight],
    )

    same = [swap(grad_sum, "node", 2 * q) for q in reversed(range(1, half))]
    same = [grad_sum, *same[::-1]]
    ready = nodes * block <= 8 * LANES
    picks_of = {unit: where[unit] for unit in units}
    if ready:
        seen, _ = lax.optimization_barrier((who, grad_sum))
        *found, mesh_out = call(
            functools.partial(
                mark_kernel,
                tuple(where[unit][1] for unit in units),
                part_rows,
                nodes,
                block,
                fanout,
            ),
            [shape((fanout * part_rows, nodes * block), BF16)] * len(units) + [row_low],
            [seen, *(where[unit][0] for unit in units), mesh_out],
            smem=1,
        )
        same[-1] = lax.optimization_barrier((same[-1], found[0]))[0]
        picks_of = {unit: (part, 0) for unit, part in zip(units, found)}
    other = [swap(rows, "node", 1) for rows in same[::-1]][::-1]
    gathered = (*same[::-1], *other[::-1])

    def message_back(groups, dtype):
        used = [unit for group in groups for unit in group]
        return call(
            functools.partial(
                message_back_kernel,
                tuple(picks_of[unit][1] for unit in used),
                part_rows,
                ready,
                nodes,
                block,
                fanout,
            ),
            [
                shape((len(group) * part_rows, width // CHUNKS), dtype)
                for group in groups
                for _ in range(CHUNKS)
            ],
            [
                who,
                *(picks_of[unit][0] for unit in used),
                *(slopes[unit] for unit in used),
                *gathered,
            ],
            smem=1,
        )

    first, then = axes, axes[::-1]
    chunks = [(p, c) for c in range(CHUNKS) for p in range(len(axes))]

    def ordered(found):
        return [found[p * CHUNKS + c] for p, c in chunks]

    given = ordered(
        message_back(
            [[(a, p), (a ^ b, p)] for p, (a, b) in enumerate(zip(first, then))], BF16
        )
    )
    gathered = lax.optimization_barrier((*gathered, *given))[: len(gathered)]
    passed = ordered(message_back([[(b, p)] for p, b in enumerate(then)], F32))
    gathered = lax.optimization_barrier((*gathered, *passed))[: len(gathered)]
    given = [swap(part, "sect", first[p]) for part, (p, _) in zip(given, chunks)]
    passed = [
        (mine + part[part_rows:].astype(F32)).astype(BF16)
        for mine, part in zip(passed, given)
    ]
    kept = ordered(message_back([[(0, p)] for p in range(len(axes))], F32))
    passed = [swap(part, "sect", then[p]) for part, (p, _) in zip(passed, chunks)]
    (grid_grad,) = call(
        functools.partial(grid_back_kernel, CHUNKS),
        [shape((grid_rows, width), BF16)],
        [*kept, *given, *passed, enc_weight],
    )
    return (mesh_out[None], grid_grad)


def solution(mesh):
    return jax.shard_map(
        body,
        mesh=mesh,
        in_specs=(
            P(("sect", "node"), None),
            P(("sect", "node"), None),
            P(("sect", "node"), None),
            P(("sect", "node"), None),
            P(),
            P(),
            P("node", "sect", None),
            P(),
            P("sect", "node", None, None, None),
            P("node", "sect", None),
            P(),
            P("node", "sect", None),
        ),
        out_specs=(P("node", "sect", None), P(("sect", "node"), None)),
        check_vma=False,
    )
```
